32 devices in a mesh: groups: 2 (over y), blk: 4 (over z), col: 2 (over x), ch: 2 (over core).
Axes of the slice: x: 2, y: 2, z: 4, core: 2. Of those that a mesh axis runs over, the one named last changes fastest.
Arguments:
- grad_out: bfloat16 [512, 64, 256], P(('groups', 'blk'), 'col', 'ch'), parts along dimension 0, may hold values from -6 to 6
- saved_input: bfloat16 [4, 4, 16, 12, 12, 256], P(('groups', 'col'), 'blk', None, None, None, 'ch'), parts along dimension 0, may hold values from -6 to 6
- saved_pre: bfloat16 [4, 4, 16, 10, 10, 256], P(('groups', 'col'), 'blk', None, None, None, 'ch'), parts along dimension 0, may hold values from -6 to 6
- first_weight: bfloat16 [9, 256, 256], P(None, 'ch'), may hold values from -0.125 to 0.125
- second_weight: bfloat16 [9, 256, 256], P(None, 'ch'), may hold values from -0.125 to 0.125
- assignment: int32 [4, 4, 16], P(('groups', 'col')), parts along dimension 0, may hold values from 0 to 127, as said below
Outputs:
- grad_in: bfloat16 [512, 64, 256], P(('groups', 'blk'), 'col', 'ch'), parts along dimension 0
- grad_first: float32 [18, 256, 256], P('groups', 'ch'), parts along dimension 0
- grad_second: float32 [18, 256, 256], P('groups', 'ch'), parts along dimension 0
The draws below stay inside these ranges and needn't reach their ends.
There are 2 independent parts, one for each index of `groups`. The reference program is written for one: setup_inputs(seed, part) draws one part's arguments, and reference() takes and returns one part's arrays. A program takes and returns all parts, laid end to end along the dimension named above; an argument that names none is the same for every part. Nothing has to cross between parts.
Inputs may be any that keep to these rules, and one draw needn't show every extreme that they name: `assignment`: an entry r * 32 + p of column c names the block at position p (row-major over the 8 x 4 blocks) of the tile at owner row r of column c. Within one column every block is named at most once and exactly half of the column's blocks are named. In the list of one worker no owner row appears more than 8 times, and in every draw some owner row appears exactly 8 times in some worker's list.
All inputs are finite; a program needn't handle non-finite values.
Results may differ from the reference program's by a relative error of at most 0.0044.
Values may be sent and summed in bfloat16 or wider, within the bound.
No kernel may reach another device: no remote copies, remote signals or barrier semaphores. Data moves between devices by JAX's collectives and lax.ppermute only.
A program may use at most 64 MiB of HBM per device.

```python
import math
import jax
import jax.numpy as jnp
from jax import lax

CHANNELS = 256
BLOCK = 8
TILE_ROWS = 8
TILE_COLS = 4
TILE_BLOCKS = 32
PER_WORKER = 16
MIDDLE = 10
OUTER = 12
HEIGHT = 256
BREADTH = 64
ACTIVE = 128
N_BLK = 4
N_COL = 2


def draw_assignment(key, part):
    key = jax.random.fold_in(key, 11)
    key_weight, key_jitter = jax.random.split(key)
    block_total = N_BLK * TILE_BLOCKS
    capacity = max(2, TILE_BLOCKS // N_BLK)
    weights = jax.random.randint(key_weight, (N_COL, N_BLK, 1), 0, 4)
    jitter = jax.random.randint(key_jitter, (N_COL, N_BLK, TILE_BLOCKS), 0, 2 ** 14)
    scores = (weights * 2 ** 13 + jitter).reshape(N_COL, block_total)
    positions = jnp.arange(block_total, dtype=jnp.int32)
    distinct = scores * block_total + positions[None, :]
    ranked = jnp.argsort(-distinct, axis=1)[:, :block_total // 2]
    active = jnp.sort(ranked, axis=1)
    slot_ids = jnp.arange(TILE_BLOCKS // 2)
    worker = jnp.arange(N_BLK)
    pick_index = capacity * (N_BLK * (slot_ids[None, :] // capacity) + worker[:, None]) + slot_ids[None, :] % capacity
    return active[:, pick_index].astype(jnp.int32)


def levels(own_key, dims, cuts, least, largest):
    factor_of, own = 1.0, jax.random.fold_in(own_key, 6)
    for position, shards_of in cuts:
        heights = jnp.exp(jax.random.uniform(jax.random.fold_in(own, position), (shards_of,), jnp.float32, least / len(cuts), largest / len(cuts)))
        factor_of = factor_of * jnp.repeat(heights, dims[position] // shards_of).reshape([-1 if axis == position else 1 for axis in range(len(dims))])
    return factor_of


def centred(own_key, shape, scale, most, cuts=(), kind=jnp.bfloat16):
    drawn = jax.random.normal(own_key, shape, jnp.float32) * scale
    if len(cuts) > 0:
        drawn = levels(own_key, shape, cuts, -0.22, 0.18) * drawn
    return jnp.clip(drawn, min=-most, max=most).astype(kind)


def setup_inputs(seed: int = 0, part: int = 0) -> dict:
    seeds = jax.random.split(jax.random.key(seed), 7)
    part_splits = jax.random.split(jax.random.fold_in(seeds[6], part), 7)
    return {
        "grad_out": centred(part_splits[0], (HEIGHT, BREADTH, CHANNELS), 1.0, 6.0, ((0, 4), (1, 2), (2, 2))),
        "saved_input": centred(part_splits[1], (N_COL, N_BLK, PER_WORKER, OUTER, OUTER, CHANNELS), 1.0, 6.0, ((0, 2), (1, 4), (5, 2))),
        "saved_pre": centred(part_splits[2], (N_COL, N_BLK, PER_WORKER, MIDDLE, MIDDLE, CHANNELS), 1.0, 6.0, ((0, 2), (1, 4), (5, 2))),
        "first_weight": centred(seeds[3], (9, CHANNELS, CHANNELS), (9 * CHANNELS) ** -0.5, 0.125, ((1, 2),)),
        "second_weight": centred(seeds[4], (9, CHANNELS, CHANNELS), (9 * CHANNELS) ** -0.5, 0.125, ((1, 2),)),
        "assignment": draw_assignment(jax.random.fold_in(jax.random.fold_in(seeds[6], part), 71), part),
    }


def tap_slices(padded, extent):
    return [padded[:, row_off:row_off + extent, col_off:col_off + extent, :] for row_off in range(3) for col_off in range(3)]

def transposed_conv(values, weight, extent):
    padded = jnp.pad(values, ((0, 0), (2, 2), (2, 2), (0, 0)))
    pieces = tap_slices(padded, extent)
    running = jnp.einsum('bpqo,io->bpqi', pieces[0], weight[8], precision=lax.Precision.HIGHEST)
    for number in range(1, 9):
        running = running + jnp.einsum('bpqo,io->bpqi', pieces[number], weight[8 - number], precision=lax.Precision.HIGHEST)
    return running

def weight_terms(inputs, gradients, extent):
    pieces = tap_slices(inputs, extent)
    return jnp.stack([jnp.einsum('bpqi,bpqo->io', shifted, gradients, precision=lax.Precision.HIGHEST) for shifted in pieces])

def reference(grad_out, saved_input, saved_pre, first_weight, second_weight, assignment):
    channels = grad_out.shape[2]
    group_total = N_COL * N_BLK
    routing = assignment.reshape(group_total, PER_WORKER).astype(jnp.int32)
    column_ids = (jnp.arange(group_total) // N_BLK).astype(jnp.int32)
    saved_all = saved_input.reshape(group_total, PER_WORKER, OUTER, OUTER, channels)
    pre_all = saved_pre.reshape(group_total, PER_WORKER, MIDDLE, MIDDLE, channels)
    first_float = first_weight.astype(jnp.float32)
    second_float = second_weight.astype(jnp.float32)
    offsets = jnp.arange(MIDDLE).astype(jnp.int32) - 1
    zero_index = jnp.zeros((), jnp.int32)

    def cut_block(row_start, col_start):
        return lax.dynamic_slice(grad_out, (row_start, col_start, zero_index), (BLOCK, BLOCK, channels))

    def tile_group(state_in, scanned):
        canvas, first_sum, second_sum = state_in
        slot_codes, column, saved_tiles, pre_act = scanned
        owner_ids = slot_codes // TILE_BLOCKS
        places = slot_codes % TILE_BLOCKS
        block_row = (owner_ids * TILE_ROWS + places // TILE_COLS).astype(jnp.int32)
        block_col = (column * TILE_COLS + places % TILE_COLS).astype(jnp.int32)
        grad_blocks = jax.vmap(cut_block)(block_row * BLOCK, block_col * BLOCK).astype(jnp.float32)
        row_global = block_row[:, None] * BLOCK + offsets[None, :]
        col_global = block_col[:, None] * BLOCK + offsets[None, :]
        row_ok = (row_global >= 0) & (row_global < HEIGHT)
        col_ok = (col_global >= 0) & (col_global < BREADTH)
        inside = (row_ok[:, :, None] & col_ok[:, None, :])[..., None]
        pre_float = pre_act.astype(jnp.float32)
        live_mask = (pre_float > 0) & inside
        act_grad = transposed_conv(grad_blocks, second_float, MIDDLE)
        pre_grad = lax.optimization_barrier(jnp.where(live_mask, act_grad, 0.0).astype(jnp.bfloat16)).astype(jnp.float32)
        relu_act = jnp.where(live_mask, pre_float, 0.0)
        second_sum = second_sum + weight_terms(relu_act, grad_blocks, BLOCK)
        first_sum = first_sum + weight_terms(saved_tiles.astype(jnp.float32), pre_grad, MIDDLE)
        input_grad = lax.optimization_barrier(transposed_conv(pre_grad, first_float, OUTER).astype(jnp.bfloat16)).astype(jnp.float32)

        def place_tile(number, running):
            anchor = (block_row[number] * BLOCK, block_col[number] * BLOCK, zero_index)
            current = lax.dynamic_slice(running, anchor, (OUTER, OUTER, channels))
            return lax.dynamic_update_slice(running, current + input_grad[number], anchor)
        canvas = lax.fori_loop(0, PER_WORKER, place_tile, canvas)
        return ((canvas, first_sum, second_sum), None)
    start_state = (jnp.zeros((HEIGHT + 4, BREADTH + 4, channels), jnp.float32), jnp.zeros((9, channels, channels), jnp.float32), jnp.zeros((9, channels, channels), jnp.float32))
    final_state, unused = lax.scan(tile_group, start_state, (routing, column_ids, saved_all, pre_all))
    canvas, first_sum, second_sum = final_state
    grad_in = (grad_out.astype(jnp.float32) + canvas[2:-2, 2:-2]).astype(jnp.bfloat16)
    grad_scale = 1.0 / math.sqrt(ACTIVE * BLOCK * BLOCK)
    return (grad_in, first_sum * grad_scale, second_sum * grad_scale)
```

```python
import functools
import math

import jax
import jax.numpy as jnp
from jax import lax
from jax.experimental import pallas as pl
from jax.experimental.pallas import tpu as pltpu
from jax.sharding import PartitionSpec as P

BLOCK = 8
TILE_ROWS = 8
TILE_COLS = 4
TILE_BLOCKS = 32
PER_WORKER = 16
MIDDLE = 10
OUTER = 12
HALF = 128
FULL = 256
DEAD = -4096
WIDE = 40

BF16 = jnp.bfloat16
F32 = jnp.float32
I32 = jnp.int32

VMEM = pl.BlockSpec(memory_space=pltpu.VMEM)
SMEM = pl.BlockSpec(memory_space=pltpu.SMEM)


def call(body, outs, specs, scratch, cost, name):
    return pl.pallas_call(
        body,
        out_shape=outs,
        in_specs=specs,
        out_specs=jax.tree.map(lambda _: VMEM, outs),
        scratch_shapes=scratch,
        compiler_params=pltpu.CompilerParams(vmem_limit_bytes=48 * 1024 * 1024),
        cost_estimate=pl.CostEstimate(flops=cost[0], bytes_accessed=cost[1], transcendentals=0),
        name=name,
    )


def iota(shape, dim):
    return lax.broadcasted_iota(I32, shape, dim)


def one_hot(hits):
    return jnp.where(hits, 1.0, 0.0).astype(BF16)


def dot(a, b):
    return jnp.dot(a, b, preferred_element_type=F32)


def dot_nt(a, b):
    return lax.dot_general(a, b, (((1,), (1,)), ((), ())), preferred_element_type=F32)


def dot_tn(a, b):
    return lax.dot_general(a, b, (((0,), (0,)), ((), ())), preferred_element_type=F32)


def owner_table(routing, table, owners, capacity):
    me = lax.axis_index("blk")

    def clear(number, carry):
        table[number] = DEAD
        return carry

    lax.fori_loop(0, owners * capacity, clear, 0)

    def worker(number, carry):
        count = jnp.int32(0)
        for slot in range(PER_WORKER):
            code = routing[number, slot]
            hit = (code // TILE_BLOCKS) == me
            table[jnp.where(hit, number * capacity + count, owners * capacity)] = code % TILE_BLOCKS
            count = count + jnp.where(hit, 1, 0)
        return carry

    lax.fori_loop(0, owners, worker, 0)


def worker_codes(routing, counts, owners):
    me = lax.axis_index("blk")

    def clear(number, carry):
        counts[number] = 0
        return carry

    lax.fori_loop(0, owners, clear, 0)
    slots = []
    for slot in range(PER_WORKER):
        code = routing[me, slot]
        owner = code // TILE_BLOCKS
        rank = counts[owner]
        counts[owner] = rank + 1
        slots.append((owner, code % TILE_BLOCKS, rank))
    return slots


def pack_cotangents(owners, capacity, routing, tile, out, table):
    owner_table(routing, table, owners, capacity)
    rows = BLOCK * capacity
    row, lane = iota((rows, FULL), 0), iota((rows, FULL), 1)
    picks = []
    for worker in range(owners):
        target = jnp.full((rows, FULL), DEAD, I32)
        for rank in range(capacity):
            place = table[worker * capacity + rank] * BLOCK
            target = jnp.where(row % capacity == rank, place, target)
        picks.append(one_hot(lane == target + row // capacity))
    pick = jnp.concatenate(picks, axis=0)
    for u in range(0, BLOCK, 2):
        pair = [
            jnp.concatenate([tile[r, u + k] for r in range(TILE_ROWS)], axis=0) for k in range(2)
        ]
        moved = dot(pick, jnp.concatenate(pair, axis=1)).astype(BF16)
        for worker in range(owners):
            part = moved[worker * rows : (worker + 1) * rows]
            out[worker, u] = part[:, :HALF]
            out[worker, u + 1] = part[:, HALF:]


def pack_saved(owners, columns, capacity, wide, routing, saved, masked, out, counts, table):
    column = lax.axis_index("col")

    def clear(number, carry):
        table[number] = DEAD
        return carry

    lax.fori_loop(0, owners * capacity, clear, 0)
    slots = worker_codes(routing, counts, owners)
    rows = MIDDLE * PER_WORKER
    row = iota((rows, HALF), 0)
    flags = jnp.zeros((rows, HALF), I32)
    for slot, (owner, place, rank) in enumerate(slots):
        table[owner * capacity + rank] = slot
        block_row, block_col = place // TILE_COLS, place % TILE_COLS
        flag = (
            jnp.where((owner == 0) & (block_row == 0), 1, 0)
            + jnp.where((owner == owners - 1) & (block_row == TILE_ROWS - 1), 2, 0)
            + jnp.where((column == 0) & (block_col == 0), 4, 0)
            + jnp.where((column == columns - 1) & (block_col == TILE_COLS - 1), 8, 0)
        )
        flags = jnp.where(row % PER_WORKER == slot, flag, flags)
    across = row // PER_WORKER
    outside = (((flags & 4) != 0) & (across == 0)) | (((flags & 8) != 0) & (across == MIDDLE - 1))
    for m in range(MIDDLE):
        here = outside
        if m == 0:
            here = here | ((flags & 1) != 0)
        if m == MIDDLE - 1:
            here = here | ((flags & 2) != 0)
        masked[m] = jnp.where(here, 0.0, saved[m].astype(F32)).astype(BF16)
    size = wide * capacity
    row, lane = iota((size, FULL), 0), iota((size, FULL), 1)
    picks = []
    for owner in range(owners):
        target = jnp.full((size, FULL), DEAD, I32)
        for rank in range(capacity):
            target = jnp.where(row % capacity == rank, table[owner * capacity + rank], target)
        at = row // capacity
        picks.append(one_hot((lane == target + at * PER_WORKER) & (at < MIDDLE)))
    pick = jnp.concatenate(picks, axis=0)
    filler = jnp.zeros((FULL - rows, FULL), BF16)
    for m in range(0, MIDDLE, 2):
        pair = jnp.concatenate([masked[m], masked[m + 1]], axis=1)
        moved = dot(pick, jnp.concatenate([pair, filler], axis=0)).astype(BF16)
        for owner in range(owners):
            part = moved[owner * size : (owner + 1) * size]
            out[owner, m] = part[:, :HALF]
            out[owner, m + 1] = part[:, HALF:]


def ordered(own, other, axis):
    first = lax.axis_index("ch") == 0
    return jnp.concatenate(
        [jnp.where(first, own, other), jnp.where(first, other, own)], axis=axis
    )


def second_gradient(scale, owners, capacity, routing, own, other, masked, cot, out, counts):
    slots = worker_codes(routing, counts, owners)
    rows, inner = BLOCK * PER_WORKER, owners * BLOCK * capacity
    row, lane = iota((rows, inner), 0), iota((rows, inner), 1)
    target = jnp.full((rows, inner), DEAD, I32)
    for slot, (owner, place, rank) in enumerate(slots):
        target = jnp.where(
            row % PER_WORKER == slot, owner * (BLOCK * capacity) + rank, target
        )
    pick = one_hot(lane == target + (row // PER_WORKER) * capacity)
    for u in range(BLOCK):
        got = jnp.concatenate(
            [ordered(own[o, u], other[o, u], 1) for o in range(owners)], axis=0
        )
        cot[u] = dot(pick, got).astype(BF16)
    grads = cot[...].reshape(BLOCK * rows, FULL)
    for tap in range(9):
        dy, dx = tap // 3, tap % 3
        window = masked[dy : dy + BLOCK, dx : dx + BLOCK].reshape(BLOCK * rows, HALF)
        window = jnp.maximum(window, jnp.zeros_like(window))
        out[tap] = (dot_tn(window, grads) * scale).astype(BF16)


def first_gradient(
    scale, cot, masked, masked_other, weight, weight_other, saved, out, total, pre, full
):
    rows = BLOCK * BLOCK * PER_WORKER
    full[...] = ordered(weight[...], weight_other[...], 1)
    total[...] = jnp.zeros_like(total)
    for tap in range(9):
        dy, dx = tap // 3, tap % 3
        part = dot_nt(cot[...].reshape(rows, FULL), full[tap])
        spot = (slice(dy, dy + BLOCK), slice(dx, dx + BLOCK))
        total[spot] = total[spot] + part.reshape(BLOCK, BLOCK, PER_WORKER, FULL)
    for m in range(MIDDLE):
        live = ordered(masked[m], masked_other[m], 2).astype(F32) > 0
        pre[m] = jnp.where(live, total[m], 0.0).astype(BF16)
    size = MIDDLE * MIDDLE * PER_WORKER
    grads = pre[...].reshape(size, FULL)
    for tap in range(9):
        dy, dx = tap // 3, tap % 3
        window = saved[dy : dy + MIDDLE, dx : dx + MIDDLE].reshape(size, HALF)
        out[tap] = (dot_tn(window, grads) * scale).astype(BF16)


def owner_canvas(
    owners, capacity, wide, routing, tile, tile_other, got, got_other, second, second_other, first,
    canvas, table, cot, total, pre, full, grown,
):
    owner_table(routing, table, owners, capacity)
    row, lane = iota((FULL, FULL), 0), iota((FULL, FULL), 1)
    turn = one_hot(lane == (row % TILE_BLOCKS) * BLOCK + row // TILE_BLOCKS)
    for u in range(BLOCK):
        block = jnp.concatenate(
            [ordered(tile[r, u], tile_other[r, u], 1) for r in range(TILE_ROWS)], axis=0
        )
        cot[u] = dot(turn, block).astype(BF16)
    full[...] = ordered(second[...], second_other[...], 1)
    rows = BLOCK * BLOCK * TILE_BLOCKS
    total[...] = jnp.zeros_like(total)
    for tap in range(9):
        dy, dx = tap // 3, tap % 3
        part = dot_nt(cot[...].reshape(rows, FULL), full[tap])
        spot = (slice(dy, dy + BLOCK), slice(dx, dx + BLOCK))
        total[spot] = total[spot] + part.reshape(BLOCK, BLOCK, TILE_BLOCKS, FULL)
    size, into = wide * capacity, MIDDLE * TILE_BLOCKS
    row, lane = iota((size, into), 0), iota((size, into), 1)
    picks = []
    for worker in range(owners):
        target = jnp.full((size, into), DEAD, I32)
        for rank in range(capacity):
            target = jnp.where(row % capacity == rank, table[worker * capacity + rank], target)
        at = row // capacity
        hits = (lane == target + at * TILE_BLOCKS) & (at < MIDDLE)
        picks.append(jnp.where(hits, 1.0, 0.0))
    pick = jnp.concatenate(picks, axis=0).T.astype(BF16)
    for m in range(MIDDLE):
        block = jnp.concatenate(
            [ordered(got[w, m], got_other[w, m], 1) for w in range(owners)], axis=0
        )
        live = dot(pick, block).reshape(MIDDLE, TILE_BLOCKS, FULL) > 0
        pre[m] = jnp.where(live, total[m], 0.0).astype(BF16)
    size = MIDDLE * MIDDLE * TILE_BLOCKS
    grown[...] = jnp.zeros_like(grown)
    for tap in range(9):
        dy, dx = tap // 3, tap % 3
        part = dot_nt(pre[...].reshape(size, FULL), first[tap])
        spot = (slice(dy, dy + MIDDLE), slice(dx, dx + MIDDLE))
        grown[spot] = grown[spot] + part.reshape(MIDDLE, MIDDLE, TILE_BLOCKS, HALF)
    height, depth = TILE_ROWS * WIDE, OUTER * TILE_BLOCKS
    row, lane = iota((height, depth), 0), iota((height, depth), 1)
    at_row, at_col = row // WIDE, row % WIDE
    n, place = lane // TILE_BLOCKS, lane % TILE_BLOCKS
    column = (place % TILE_COLS) * BLOCK + n - 2
    column = jnp.where(column < 0, column + 36, column)
    fold = one_hot((at_row == place // TILE_COLS) & (at_col == column))
    canvas[...] = jnp.zeros_like(canvas)
    for m in range(0, OUTER, 2):
        pair = jnp.concatenate(
            [grown[m + k].reshape(depth, HALF).astype(BF16) for k in range(2)], axis=1
        )
        laid = dot(fold, pair).reshape(TILE_ROWS, WIDE, FULL)
        for r in range(TILE_ROWS):
            for k in range(2):
                canvas[r * BLOCK + m + k] += laid[r, :, k * HALF : (k + 1) * HALF]


def swap(value):
    return lax.ppermute(value, "ch", [(0, 1), (1, 0)])


def neighbours(axis):
    size = lax.axis_size(axis)
    up = [(i, (i + 1) % size) for i in range(size - 1)]
    return up, [(j, i) for i, j in up]


def shards(grad_out, saved_input, saved_pre, first_weight, second_weight, assignment):
    owners = lax.axis_size("blk")
    columns = lax.axis_size("col")
    capacity = max(2, TILE_BLOCKS // owners)
    wide = MIDDLE if (MIDDLE * capacity) % 16 == 0 else 16
    scale = 1.0 / math.sqrt(owners * columns * PER_WORKER * BLOCK * BLOCK)
    routing = assignment[0]
    shape = jax.ShapeDtypeStruct
    tables = [pltpu.SMEM((owners * capacity + 1,), I32)]
    counts = [pltpu.SMEM((owners,), I32)]

    tile = grad_out.reshape(TILE_ROWS, BLOCK, TILE_COLS * BLOCK, HALF)
    outgoing = call(
        functools.partial(pack_cotangents, owners, capacity),
        shape((owners, BLOCK, BLOCK * capacity, HALF), BF16),
        [SMEM, VMEM], tables, (2**28, 2**20), "pack_cotangents",
    )(routing, tile)
    incoming = lax.all_to_all(outgoing, "blk", split_axis=0, concat_axis=0, tiled=True)

    saved_slots = saved_pre[0, 0].transpose(1, 2, 0, 3)
    masked, to_owners = call(
        functools.partial(pack_saved, owners, columns, capacity, wide),
        (
            shape((MIDDLE, MIDDLE * PER_WORKER, HALF), BF16),
            shape((owners, MIDDLE, wide * capacity, HALF), BF16),
        ),
        [SMEM, VMEM], counts + tables, (2**28, 2**20), "pack_saved",
    )(routing, saved_slots.reshape(MIDDLE, MIDDLE * PER_WORKER, HALF))
    masked = masked.reshape(MIDDLE, MIDDLE, PER_WORKER, HALF)
    second_other = swap(second_weight)
    masked_other = swap(masked)
    tile_other = swap(tile)

    incoming_other = swap(incoming)
    at_owner = lax.all_to_all(to_owners, "blk", split_axis=0, concat_axis=0, tiled=True)
    cot, grad_second = call(
        functools.partial(second_gradient, scale, owners, capacity),
        (
            shape((BLOCK, BLOCK * PER_WORKER, FULL), BF16),
            shape((9, HALF, FULL), BF16),
        ),
        [SMEM, VMEM, VMEM, VMEM], counts, (2**30, 2**21), "second_gradient",
    )(routing, incoming, incoming_other, masked)
    grad_second = lax.psum(grad_second, ("blk", "col"))

    saved_tiles = saved_input[0, 0].transpose(1, 2, 0, 3)
    grad_first = call(
        functools.partial(first_gradient, scale),
        shape((9, HALF, FULL), BF16),
        [VMEM] * 6,
        [
            pltpu.VMEM((MIDDLE, MIDDLE, PER_WORKER, FULL), F32),
            pltpu.VMEM((MIDDLE, MIDDLE, PER_WORKER, FULL), BF16),
            pltpu.VMEM((9, FULL, FULL), BF16),
        ],
        (2**31, 2**22), "first_gradient",
    )(cot, masked, masked_other, second_weight, second_other, saved_tiles)
    grad_first = lax.psum(grad_first, ("blk", "col"))

    at_owner_other = swap(at_owner)
    height = TILE_ROWS * BLOCK + 4
    canvas = call(
        functools.partial(owner_canvas, owners, capacity, wide),
        shape((height, WIDE, HALF), F32),
        [SMEM] + [VMEM] * 7,
        tables
        + [
            pltpu.VMEM((BLOCK, FULL, FULL), BF16),
            pltpu.VMEM((MIDDLE, MIDDLE, TILE_BLOCKS, FULL), F32),
            pltpu.VMEM((MIDDLE, MIDDLE, TILE_BLOCKS, FULL), BF16),
            pltpu.VMEM((9, FULL, FULL), BF16),
            pltpu.VMEM((OUTER, OUTER, TILE_BLOCKS, HALF), F32),
        ],
        (2**32, 2**23), "owner_canvas",
    )(routing, tile, tile_other, at_owner, at_owner_other, second_weight, second_other, first_weight)

    up, down = neighbours("blk")
    from_above = lax.ppermute(canvas[height - 2 :].astype(BF16), "blk", up).astype(F32)
    from_below = lax.ppermute(canvas[:2].astype(BF16), "blk", down).astype(F32)
    inner = canvas[2 : height - 2]
    inner = inner.at[:2].add(from_above).at[-2:].add(from_below)
    up, down = neighbours("col")
    from_left = lax.ppermute(inner[:, 32:34].astype(BF16), "col", up).astype(F32)
    from_right = lax.ppermute(inner[:, 34:36].astype(BF16), "col", down).astype(F32)
    inner = inner[:, :32].at[:, :2].add(from_left).at[:, -2:].add(from_right)
    grad_in = (grad_out.astype(F32) + inner).astype(BF16)
    return (grad_in, grad_first.astype(F32), grad_second.astype(F32))


def solution(mesh):
    return jax.shard_map(
        shards,
        mesh=mesh,
        in_specs=(
            P(("groups", "blk"), "col", "ch"),
            P(("groups", "col"), "blk", None, None, None, "ch"),
            P(("groups", "col"), "blk", None, None, None, "ch"),
            P(None, "ch", None),
            P(None, "ch", None),
            P(("groups", "col"), None, None),
        ),
        out_specs=(
            P(("groups", "blk"), "col", "ch"),
            P("groups", "ch", None),
            P("groups", "ch", None),
        ),
        check_vma=False,
    )
```

```python
import functools
import math

import jax
import jax.numpy as jnp
from jax import lax
from jax.experimental import pallas as pl
from jax.experimental.pallas import tpu as pltpu
from jax.sharding import PartitionSpec as P

BLOCK = 8
TILE_ROWS = 8
TILE_COLS = 4
TILE_BLOCKS = 32
PER_WORKER = 16
MIDDLE = 10
OUTER = 12
HALF = 128
FULL = 256
DEAD = -4096
WIDE = 40

BF16 = jnp.bfloat16
F32 = jnp.float32
I32 = jnp.int32

VMEM = pl.BlockSpec(memory_space=pltpu.VMEM)
SMEM = pl.BlockSpec(memory_space=pltpu.SMEM)


def call(body, outs, specs, scratch, cost, name):
    return pl.pallas_call(
        body,
        out_shape=outs,
        in_specs=specs,
        out_specs=jax.tree.map(lambda _: VMEM, outs),
        scratch_shapes=scratch,
        compiler_params=pltpu.CompilerParams(vmem_limit_bytes=48 * 1024 * 1024),
        cost_estimate=pl.CostEstimate(flops=cost[0], bytes_accessed=cost[1], transcendentals=0),
        name=name,
    )


def iota(shape, dim):
    return lax.broadcasted_iota(I32, shape, dim)


def one_hot(hits):
    return jnp.where(hits, 1.0, 0.0).astype(BF16)


def dot(a, b):
    return jnp.dot(a, b, preferred_element_type=F32)


def dot_nt(a, b):
    return lax.dot_general(a, b, (((1,), (1,)), ((), ())), preferred_element_type=F32)


def dot_tn(a, b):
    return lax.dot_general(a, b, (((0,), (0,)), ((), ())), preferred_element_type=F32)


def owner_table(routing, table, owners, capacity):
    me = lax.axis_index("blk")

    def clear(number, carry):
        table[number] = DEAD
        return carry

    lax.fori_loop(0, owners * capacity, clear, 0)

    def worker(number, carry):
        count = jnp.int32(0)
        for slot in range(PER_WORKER):
            code = routing[number, slot]
            hit = (code // TILE_BLOCKS) == me
            table[jnp.where(hit, number * capacity + count, owners * capacity)] = code % TILE_BLOCKS
            count = count + jnp.where(hit, 1, 0)
        return carry

    lax.fori_loop(0, owners, worker, 0)


def worker_codes(routing, counts, owners):
    me = lax.axis_index("blk")

    def clear(number, carry):
        counts[number] = 0
        return carry

    lax.fori_loop(0, owners, clear, 0)
    slots = []
    for slot in range(PER_WORKER):
        code = routing[me, slot]
        owner = code // TILE_BLOCKS
        rank = counts[owner]
        counts[owner] = rank + 1
        slots.append((owner, code % TILE_BLOCKS, rank))
    return slots


def views(refs, count):
    return list(refs) if len(refs) == count else [refs[0].at[k] for k in range(count)]


def partner(axis, step, permuted):
    return step ^ lax.axis_index(axis) if permuted else step


def pack_cotangents(owners, capacity, permuted, routing, tile, *refs):
    outs, table = refs[:-1], refs[-1]
    owner_table(routing, table, owners, capacity)
    rows = BLOCK * capacity
    row, lane = iota((rows, FULL), 0), iota((rows, FULL), 1)
    picks = []
    for step in range(owners):
        worker = partner("blk", step, permuted)
        target = jnp.full((rows, FULL), DEAD, I32)
        for rank in range(capacity):
            place = table[worker * capacity + rank] * BLOCK
            target = jnp.where(row % capacity == rank, place, target)
        picks.append(one_hot(lane == target + row // capacity))
    pick = jnp.concatenate(picks, axis=0)
    for u in range(0, BLOCK, 2):
        pair = [
            jnp.concatenate([tile[r, u + k] for r in range(TILE_ROWS)], axis=0) for k in range(2)
        ]
        moved = dot(pick, jnp.concatenate(pair, axis=1)).astype(BF16)
        for step, out in enumerate(views(outs, owners)):
            part = moved[step * rows : (step + 1) * rows]
            out[u] = part[:, :HALF]
            out[u + 1] = part[:, HALF:]


def pack_saved(owners, columns, capacity, wide, permuted, routing, saved, masked, *refs):
    outs, counts, table = refs[:-2], refs[-2], refs[-1]
    column = lax.axis_index("col")

    def clear(number, carry):
        table[number] = DEAD
        return carry

    lax.fori_loop(0, owners * capacity, clear, 0)
    slots = worker_codes(routing, counts, owners)
    rows = MIDDLE * PER_WORKER
    row = iota((rows, HALF), 0)
    flags = jnp.zeros((rows, HALF), I32)
    for slot, (owner, place, rank) in enumerate(slots):
        table[owner * capacity + rank] = slot
        block_row, block_col = place // TILE_COLS, place % TILE_COLS
        flag = (
            jnp.where((owner == 0) & (block_row == 0), 1, 0)
            + jnp.where((owner == owners - 1) & (block_row == TILE_ROWS - 1), 2, 0)
            + jnp.where((column == 0) & (block_col == 0), 4, 0)
            + jnp.where((column == columns - 1) & (block_col == TILE_COLS - 1), 8, 0)
        )
        flags = jnp.where(row % PER_WORKER == slot, flag, flags)
    across = row // PER_WORKER
    outside = (((flags & 4) != 0) & (across == 0)) | (((flags & 8) != 0) & (across == MIDDLE - 1))
    for m in range(MIDDLE):
        here = outside
        if m == 0:
            here = here | ((flags & 1) != 0)
        if m == MIDDLE - 1:
            here = here | ((flags & 2) != 0)
        masked[m] = jnp.where(here, 0.0, saved[m].astype(F32)).astype(BF16)
    size = wide * capacity
    row, lane = iota((size, FULL), 0), iota((size, FULL), 1)
    picks = []
    for step in range(owners):
        owner = partner("blk", step, permuted)
        target = jnp.full((size, FULL), DEAD, I32)
        for rank in range(capacity):
            target = jnp.where(row % capacity == rank, table[owner * capacity + rank], target)
        at = row // capacity
        picks.append(one_hot((lane == target + at * PER_WORKER) & (at < MIDDLE)))
    pick = jnp.concatenate(picks, axis=0)
    filler = jnp.zeros((FULL - rows, FULL), BF16)
    for m in range(0, MIDDLE, 2):
        pair = jnp.concatenate([masked[m], masked[m + 1]], axis=1)
        moved = dot(pick, jnp.concatenate([pair, filler], axis=0)).astype(BF16)
        for step, out in enumerate(views(outs, owners)):
            part = moved[step * size : (step + 1) * size]
            out[m] = part[:, :HALF]
            out[m + 1] = part[:, HALF:]


def ordered(own, other, axis):
    first = lax.axis_index("ch") == 0
    return jnp.concatenate(
        [jnp.where(first, own, other), jnp.where(first, other, own)], axis=axis
    )


def halves(value, keep, send, tap):
    low, high = value[: HALF // 2], value[HALF // 2 :]
    mine = lax.axis_index("col") == 0
    keep[tap] = jnp.where(mine, low, high)
    send[tap] = jnp.where(mine, high, low).astype(BF16)


def emit(value, outs, tap):
    if len(outs) == 2:
        halves(value, outs[0], outs[1], tap)
    else:
        outs[0][tap] = value


def second_gradient(scale, owners, capacity, permuted, routing, *refs):
    parts = 1 if not permuted else owners
    own, other = views(refs[:parts], owners), views(refs[parts : 2 * parts], owners)
    masked, cot = refs[2 * parts : 2 * parts + 2]
    outs, counts = refs[2 * parts + 2 : -1], refs[-1]
    slots = worker_codes(routing, counts, owners)
    rows, inner = BLOCK * PER_WORKER, owners * BLOCK * capacity
    row, lane = iota((rows, inner), 0), iota((rows, inner), 1)
    target = jnp.full((rows, inner), DEAD, I32)
    for slot, (owner, place, rank) in enumerate(slots):
        step = partner("blk", owner, permuted)
        target = jnp.where(row % PER_WORKER == slot, step * (BLOCK * capacity) + rank, target)
    pick = one_hot(lane == target + (row // PER_WORKER) * capacity)
    for u in range(BLOCK):
        got = jnp.concatenate(
            [ordered(own[o][u], other[o][u], 1) for o in range(owners)], axis=0
        )
        cot[u] = dot(pick, got).astype(BF16)
    grads = cot[...].reshape(BLOCK * rows, FULL)
    for tap in range(9):
        dy, dx = tap // 3, tap % 3
        window = masked[dy : dy + BLOCK, dx : dx + BLOCK].reshape(BLOCK * rows, HALF)
        window = jnp.maximum(window, jnp.zeros_like(window))
        emit(dot_tn(window, grads) * scale, outs, tap)


def first_gradient(
    scale, cot, masked, masked_other, weight, weight_other, saved, *refs
):
    outs, (total, pre, full) = refs[:-3], refs[-3:]
    rows = BLOCK * BLOCK * PER_WORKER
    full[...] = ordered(weight[...], weight_other[...], 1)
    total[...] = jnp.zeros_like(total)
    for tap in range(9):
        dy, dx = tap // 3, tap % 3
        part = dot_nt(cot[...].reshape(rows, FULL), full[tap])
        spot = (slice(dy, dy + BLOCK), slice(dx, dx + BLOCK))
        total[spot] = total[spot] + part.reshape(BLOCK, BLOCK, PER_WORKER, FULL)
    for m in range(MIDDLE):
        live = ordered(masked[m], masked_other[m], 2).astype(F32) > 0
        pre[m] = jnp.where(live, total[m], 0.0).astype(BF16)
    size = MIDDLE * MIDDLE * PER_WORKER
    grads = pre[...].reshape(size, FULL)
    for tap in range(9):
        dy, dx = tap // 3, tap % 3
        window = saved[dy : dy + MIDDLE, dx : dx + MIDDLE].reshape(size, HALF)
        emit(dot_tn(window, grads) * scale, outs, tap)


def owner_spread(tile, tile_other, second, second_other, total, cot, full):
    row, lane = iota((FULL, FULL), 0), iota((FULL, FULL), 1)
    turn = one_hot(lane == (row % TILE_BLOCKS) * BLOCK + row // TILE_BLOCKS)
    for u in range(BLOCK):
        block = jnp.concatenate(
            [ordered(tile[r, u], tile_other[r, u], 1) for r in range(TILE_ROWS)], axis=0
        )
        cot[u] = dot(turn, block).astype(BF16)
    full[...] = ordered(second[...], second_other[...], 1)
    rows = BLOCK * BLOCK * TILE_BLOCKS
    total[...] = jnp.zeros_like(total)
    for tap in range(9):
        dy, dx = tap // 3, tap % 3
        part = dot_nt(cot[...].reshape(rows, FULL), full[tap])
        spot = (slice(dy, dy + BLOCK), slice(dx, dx + BLOCK))
        total[spot] = total[spot] + part.reshape(BLOCK, BLOCK, TILE_BLOCKS, FULL)


def owner_canvas(owners, capacity, wide, permuted, routing, *refs):
    parts = 1 if not permuted else owners
    got, got_other = views(refs[:parts], owners), views(refs[parts : 2 * parts], owners)
    total, first, canvas, table, pre, grown = refs[2 * parts :]
    owner_table(routing, table, owners, capacity)
    size, into = wide * capacity, MIDDLE * TILE_BLOCKS
    row, lane = iota((size, into), 0), iota((size, into), 1)
    picks = []
    for step in range(owners):
        worker = partner("blk", step, permuted)
        target = jnp.full((size, into), DEAD, I32)
        for rank in range(capacity):
            target = jnp.where(row % capacity == rank, table[worker * capacity + rank], target)
        at = row // capacity
        hits = (lane == target + at * TILE_BLOCKS) & (at < MIDDLE)
        picks.append(jnp.where(hits, 1.0, 0.0))
    pick = jnp.concatenate(picks, axis=0).T.astype(BF16)
    for m in range(MIDDLE):
        block = jnp.concatenate(
            [ordered(got[w][m], got_other[w][m], 1) for w in range(owners)], axis=0
        )
        live = dot(pick, block).reshape(MIDDLE, TILE_BLOCKS, FULL) > 0
        pre[m] = jnp.where(live, total[m], 0.0).astype(BF16)
    size = MIDDLE * MIDDLE * TILE_BLOCKS
    grown[...] = jnp.zeros_like(grown)
    for tap in range(9):
        dy, dx = tap // 3, tap % 3
        part = dot_nt(pre[...].reshape(size, FULL), first[tap])
        spot = (slice(dy, dy + MIDDLE), slice(dx, dx + MIDDLE))
        grown[spot] = grown[spot] + part.reshape(MIDDLE, MIDDLE, TILE_BLOCKS, HALF)
    height, depth = TILE_ROWS * WIDE, OUTER * TILE_BLOCKS
    row, lane = iota((height, depth), 0), iota((height, depth), 1)
    at_row, at_col = row // WIDE, row % WIDE
    n, place = lane // TILE_BLOCKS, lane % TILE_BLOCKS
    column = (place % TILE_COLS) * BLOCK + n - 2
    column = jnp.where(column < 0, column + 36, column)
    fold = one_hot((at_row == place // TILE_COLS) & (at_col == column))
    canvas[...] = jnp.zeros_like(canvas)
    for m in range(0, OUTER, 2):
        pair = jnp.concatenate(
            [grown[m + k].reshape(depth, HALF).astype(BF16) for k in range(2)], axis=1
        )
        laid = dot(fold, pair).reshape(TILE_ROWS, WIDE, FULL)
        for r in range(TILE_ROWS):
            for k in range(2):
                canvas[r * BLOCK + m + k] += laid[r, :, k * HALF : (k + 1) * HALF]


def add_columns(columns_of, *refs):
    kept, got, outs, sums = refs[:2], refs[2:4], refs[4:-1], refs[-1]
    for k in range(2):
        sums[k] = kept[k][...] + got[k][...].astype(F32)
    size = HALF // 2 // len(outs)
    for step, out in enumerate(outs):
        at = pl.multiple_of(partner("blk", step, True) * size, size)
        part = sums[:, :, pl.ds(at, size), :]
        out[...] = part if step == 0 else part.astype(BF16)


def add_workers(kept, *refs):
    got, outs = refs[:-2], refs[-2:]
    for k in range(2):
        value = kept[k]
        for part in got:
            value = value + part[k].astype(F32)
        outs[k][...] = value.astype(BF16)


def lay_parts(*refs):
    parts, out = refs[:-1], refs[-1]
    size = HALF // 2 // len(parts)
    for step, part in enumerate(parts):
        at = pl.multiple_of(partner("blk", step, True) * size, size)
        out[:, pl.ds(at, size), :] = part[...]


def lay_halves(own, other, out):
    mine = lax.axis_index("col") == 0
    for tap in range(9):
        out[tap, : HALF // 2] = jnp.where(mine, own[tap], other[tap]).astype(F32)
        out[tap, HALF // 2 :] = jnp.where(mine, other[tap], own[tap]).astype(F32)


def swap(value, axis="ch"):
    return lax.ppermute(value, axis, [(0, 1), (1, 0)])


def flip(value, axis, step):
    size = lax.axis_size(axis)
    return lax.ppermute(value, axis, [(i, i ^ step) for i in range(size)])


def neighbours(axis):
    size = lax.axis_size(axis)
    up = [(i, (i + 1) % size) for i in range(size - 1)]
    return up, [(j, i) for i, j in up]


def shards(grad_out, saved_input, saved_pre, first_weight, second_weight, assignment):
    owners = lax.axis_size("blk")
    columns = lax.axis_size("col")
    capacity = max(2, TILE_BLOCKS // owners)
    wide = MIDDLE if (MIDDLE * capacity) % 16 == 0 else 16
    scale = 1.0 / math.sqrt(owners * columns * PER_WORKER * BLOCK * BLOCK)
    permuted = owners == 4 and columns == 2
    parts = owners if permuted else 1
    routing = assignment[0]
    shape = jax.ShapeDtypeStruct
    tables = [pltpu.SMEM((owners * capacity + 1,), I32)]
    counts = [pltpu.SMEM((owners,), I32)]

    def pieces(*dims):
        return [shape(dims, BF16)] * owners if permuted else [shape((owners,) + dims, BF16)]

    def exchange(values):
        if permuted:
            return [values[0]] + [flip(values[k], "blk", k) for k in range(1, owners)]
        return [lax.all_to_all(values[0], "blk", split_axis=0, concat_axis=0, tiled=True)]

    tile = grad_out.reshape(TILE_ROWS, BLOCK, TILE_COLS * BLOCK, HALF)
    outgoing = call(
        functools.partial(pack_cotangents, owners, capacity, permuted),
        pieces(BLOCK, BLOCK * capacity, HALF),
        [SMEM, VMEM], tables, (2**30, 2**21), "pack_cotangents",
    )(routing, tile)
    incoming = exchange(outgoing)

    saved_slots = saved_pre[0, 0].transpose(1, 2, 0, 3)
    masked, *to_owners = call(
        functools.partial(pack_saved, owners, columns, capacity, wide, permuted),
        [shape((MIDDLE, MIDDLE * PER_WORKER, HALF), BF16)] + pieces(MIDDLE, wide * capacity, HALF),
        [SMEM, VMEM], counts + tables, (2**30, 2**21), "pack_saved",
    )(routing, saved_slots.reshape(MIDDLE, MIDDLE * PER_WORKER, HALF))
    masked = masked.reshape(MIDDLE, MIDDLE, PER_WORKER, HALF)
    second_other = swap(second_weight)
    masked_other = swap(masked)
    tile_other = swap(tile)
    total = call(
        owner_spread,
        shape((MIDDLE, MIDDLE, TILE_BLOCKS, FULL), F32),
        [VMEM] * 4,
        [pltpu.VMEM((BLOCK, FULL, FULL), BF16), pltpu.VMEM((9, FULL, FULL), BF16)],
        (2**32, 2**23), "owner_spread",
    )(tile, tile_other, second_weight, second_other)

    incoming_other = [swap(value) for value in incoming]
    to_owners, incoming = lax.optimization_barrier((to_owners, incoming))
    at_owner = exchange(to_owners)

    if permuted:
        halved = [shape((9, HALF // 2, FULL), F32), shape((9, HALF // 2, FULL), BF16)]
    else:
        halved = [shape((9, HALF, FULL), F32)]
    cot, *second_terms = call(
        functools.partial(second_gradient, scale, owners, capacity, permuted),
        [shape((BLOCK, BLOCK * PER_WORKER, FULL), BF16)] + halved,
        [SMEM] + [VMEM] * (2 * parts + 1), counts, (2**31, 2**21), "second_gradient",
    )(routing, *incoming, *incoming_other, masked)

    saved_tiles = saved_input[0, 0].transpose(1, 2, 0, 3)
    first_terms = call(
        functools.partial(first_gradient, scale),
        halved,
        [VMEM] * 6,
        [
            pltpu.VMEM((MIDDLE, MIDDLE, PER_WORKER, FULL), F32),
            pltpu.VMEM((MIDDLE, MIDDLE, PER_WORKER, FULL), BF16),
            pltpu.VMEM((9, FULL, FULL), BF16),
        ],
        (2**32, 2**22), "first_gradient",
    )(cot, masked, masked_other, second_weight, second_other, saved_tiles)

    if permuted:
        size = HALF // 2 // owners
        part = (2, 9, size, FULL)
        second_got, first_got = swap(second_terms[1], "col"), swap(first_terms[1], "col")
        kept, *sends = call(
            functools.partial(add_columns, columns),
            [shape(part, F32)] + [shape(part, BF16)] * (owners - 1),
            [VMEM] * 4, [pltpu.VMEM((2, 9, HALF // 2, FULL), F32)], (2**28, 2**22), "add_columns",
        )(second_terms[0], first_terms[0], second_got, first_got)
        got = [flip(value, "blk", k + 1) for k, value in enumerate(sends)]
        sums = call(
            add_workers, [shape(part[1:], BF16)] * 2, [VMEM] * owners, [], (2**26, 2**20),
            "add_workers",
        )(kept, *got)
        grads = []
        for value in sums:
            spread = [value] + [flip(value, "blk", k) for k in range(1, owners)]
            half = call(
                lay_parts, shape((9, HALF // 2, FULL), BF16), [VMEM] * owners, [], (2**26, 2**20),
                "lay_parts",
            )(*spread)
            grads.append(
                call(
                    lay_halves, shape((9, HALF, FULL), F32), [VMEM] * 2, [], (2**26, 2**21),
                    "lay_halves",
                )(half, swap(half, "col"))
            )
        grad_second, grad_first = grads
    else:
        grad_first, grad_second = lax.psum((first_terms[0], second_terms[0]), ("blk", "col"))

    at_owner_other = [swap(value) for value in at_owner]
    height = TILE_ROWS * BLOCK + 4
    canvas = call(
        functools.partial(owner_canvas, owners, capacity, wide, permuted),
        shape((height, WIDE, HALF), F32),
        [SMEM] + [VMEM] * (2 * parts + 2),
        tables
        + [
            pltpu.VMEM((MIDDLE, MIDDLE, TILE_BLOCKS, FULL), BF16),
            pltpu.VMEM((OUTER, OUTER, TILE_BLOCKS, HALF), F32),
        ],
        (2**32, 2**23), "owner_canvas",
    )(routing, *at_owner, *at_owner_other, total, first_weight)

    up, down = neighbours("blk")
    from_above = lax.ppermute(canvas[height - 2 :].astype(BF16), "blk", up).astype(F32)
    from_below = lax.ppermute(canvas[:2].astype(BF16), "blk", down).astype(F32)
    inner = canvas[2 : height - 2]
    inner = inner.at[:2].add(from_above).at[-2:].add(from_below)
    up, down = neighbours("col")
    from_left = lax.ppermute(inner[:, 32:34].astype(BF16), "col", up).astype(F32)
    from_right = lax.ppermute(inner[:, 34:36].astype(BF16), "col", down).astype(F32)
    inner = inner[:, :32].at[:, :2].add(from_left).at[:, -2:].add(from_right)
    grad_in = (grad_out.astype(F32) + inner).astype(BF16)
    return (grad_in, grad_first, grad_second)


def solution(mesh):
    return jax.shard_map(
        shards,
        mesh=mesh,
        in_specs=(
            P(("groups", "blk"), "col", "ch"),
            P(("groups", "col"), "blk", None, None, None, "ch"),
            P(("groups", "col"), "blk", None, None, None, "ch"),
            P(None, "ch", None),
            P(None, "ch", None),
            P(("groups", "col"), None, None),
        ),
        out_specs=(
            P(("groups", "blk"), "col", "ch"),
            P("groups", "ch", None),
            P("groups", "ch", None),
        ),
        check_vma=False,
    )
```

```python
import functools
import math

import jax
import jax.numpy as jnp
from jax import lax
from jax.experimental import pallas as pl
from jax.experimental.pallas import tpu as pltpu
from jax.sharding import PartitionSpec as P

BLOCK = 8
TILE_ROWS = 8
TILE_COLS = 4
TILE_BLOCKS = 32
PER_WORKER = 16
MIDDLE = 10
OUTER = 12
HALF = 128
FULL = 256
DEAD = -4096
WIDE = 40

BF16 = jnp.bfloat16
F32 = jnp.float32
I32 = jnp.int32

VMEM = pl.BlockSpec(memory_space=pltpu.VMEM)
SMEM = pl.BlockSpec(memory_space=pltpu.SMEM)


def call(body, outs, specs, scratch, cost, name):
    return pl.pallas_call(
        body,
        out_shape=outs,
        in_specs=specs,
        out_specs=jax.tree.map(lambda _: VMEM, outs),
        scratch_shapes=scratch,
        compiler_params=pltpu.CompilerParams(vmem_limit_bytes=48 * 1024 * 1024),
        cost_estimate=pl.CostEstimate(flops=cost[0], bytes_accessed=cost[1], transcendentals=0),
        name=name,
    )


def iota(shape, dim):
    return lax.broadcasted_iota(I32, shape, dim)


def one_hot(hits):
    return jnp.where(hits, 1.0, 0.0).astype(BF16)


def dot(a, b):
    return jnp.dot(a, b, preferred_element_type=F32)


def dot_nt(a, b):
    return lax.dot_general(a, b, (((1,), (1,)), ((), ())), preferred_element_type=F32)


def dot_tn(a, b):
    return lax.dot_general(a, b, (((0,), (0,)), ((), ())), preferred_element_type=F32)


def owner_table(routing, table, owners, capacity):
    me = lax.axis_index("blk")

    def clear(number, carry):
        table[number] = DEAD
        return carry

    lax.fori_loop(0, owners * capacity, clear, 0)

    def worker(number, carry):
        count = jnp.int32(0)
        for slot in range(PER_WORKER):
            code = routing[number, slot]
            hit = (code // TILE_BLOCKS) == me
            table[jnp.where(hit, number * capacity + count, owners * capacity)] = code % TILE_BLOCKS
            count = count + jnp.where(hit, 1, 0)
        return carry

    lax.fori_loop(0, owners, worker, 0)


def worker_codes(routing, counts, owners):
    me = lax.axis_index("blk")

    def clear(number, carry):
        counts[number] = 0
        return carry

    lax.fori_loop(0, owners, clear, 0)
    slots = []
    for slot in range(PER_WORKER):
        code = routing[me, slot]
        owner = code // TILE_BLOCKS
        rank = counts[owner]
        counts[owner] = rank + 1
        slots.append((owner, code % TILE_BLOCKS, rank))
    return slots


def views(refs, count):
    return list(refs) if len(refs) == count else [refs[0].at[k] for k in range(count)]


def partner(axis, step, permuted):
    return step ^ lax.axis_index(axis) if permuted else step


def pack_cotangents(owners, capacity, permuted, routing, tile, *refs):
    outs, table = refs[:-1], refs[-1]
    owner_table(routing, table, owners, capacity)
    rows = BLOCK * capacity
    row, lane = iota((rows, FULL), 0), iota((rows, FULL), 1)
    picks = []
    for step in range(owners):
        worker = partner("blk", step, permuted)
        target = jnp.full((rows, FULL), DEAD, I32)
        for rank in range(capacity):
            place = table[worker * capacity + rank] * BLOCK
            target = jnp.where(row % capacity == rank, place, target)
        picks.append(one_hot(lane == target + row // capacity))
    pick = jnp.concatenate(picks, axis=0)
    for u in range(0, BLOCK, 2):
        pair = [
            jnp.concatenate([tile[r, u + k] for r in range(TILE_ROWS)], axis=0) for k in range(2)
        ]
        moved = dot(pick, jnp.concatenate(pair, axis=1)).astype(BF16)
        for step, out in enumerate(views(outs, owners)):
            part = moved[step * rows : (step + 1) * rows]
            out[u] = part[:, :HALF]
            out[u + 1] = part[:, HALF:]


def pack_saved(owners, columns, capacity, wide, permuted, routing, saved, masked, *refs):
    outs, counts, table = refs[:-2], refs[-2], refs[-1]
    column = lax.axis_index("col")

    def clear(number, carry):
        table[number] = DEAD
        return carry

    lax.fori_loop(0, owners * capacity, clear, 0)
    slots = worker_codes(routing, counts, owners)
    rows = MIDDLE * PER_WORKER
    row = iota((rows, HALF), 0)
    flags = jnp.zeros((rows, HALF), I32)
    for slot, (owner, place, rank) in enumerate(slots):
        table[owner * capacity + rank] = slot
        block_row, block_col = place // TILE_COLS, place % TILE_COLS
        flag = (
            jnp.where((owner == 0) & (block_row == 0), 1, 0)
            + jnp.where((owner == owners - 1) & (block_row == TILE_ROWS - 1), 2, 0)
            + jnp.where((column == 0) & (block_col == 0), 4, 0)
            + jnp.where((column == columns - 1) & (block_col == TILE_COLS - 1), 8, 0)
        )
        flags = jnp.where(row % PER_WORKER == slot, flag, flags)
    across = row // PER_WORKER
    outside = (((flags & 4) != 0) & (across == 0)) | (((flags & 8) != 0) & (across == MIDDLE - 1))
    for m in range(MIDDLE):
        here = outside
        if m == 0:
            here = here | ((flags & 1) != 0)
        if m == MIDDLE - 1:
            here = here | ((flags & 2) != 0)
        masked[m] = jnp.where(here, 0.0, saved[m].astype(F32)).astype(BF16)
    size = wide * capacity
    row, lane = iota((size, FULL), 0), iota((size, FULL), 1)
    picks = []
    for step in range(owners):
        owner = partner("blk", step, permuted)
        target = jnp.full((size, FULL), DEAD, I32)
        for rank in range(capacity):
            target = jnp.where(row % capacity == rank, table[owner * capacity + rank], target)
        at = row // capacity
        picks.append(one_hot((lane == target + at * PER_WORKER) & (at < MIDDLE)))
    pick = jnp.concatenate(picks, axis=0)
    filler = jnp.zeros((FULL - rows, FULL), BF16)
    for m in range(0, MIDDLE, 2):
        pair = jnp.concatenate([masked[m], masked[m + 1]], axis=1)
        moved = dot(pick, jnp.concatenate([pair, filler], axis=0)).astype(BF16)
        for step, out in enumerate(views(outs, owners)):
            part = moved[step * size : (step + 1) * size]
            out[m] = part[:, :HALF]
            out[m + 1] = part[:, HALF:]


def ordered(own, other, axis):
    first = lax.axis_index("ch") == 0
    return jnp.concatenate(
        [jnp.where(first, own, other), jnp.where(first, other, own)], axis=axis
    )


def halves(value, keep, send, tap):
    low, high = value[: HALF // 2], value[HALF // 2 :]
    mine = lax.axis_index("col") == 0
    keep[tap] = jnp.where(mine, low, high)
    send[tap] = jnp.where(mine, high, low).astype(BF16)


def emit(value, outs, tap):
    if len(outs) == 2:
        halves(value, outs[0], outs[1], tap)
    else:
        outs[0][tap] = value


def second_gradient(scale, owners, capacity, permuted, routing, *refs):
    parts = 1 if not permuted else owners
    own, other = views(refs[:parts], owners), views(refs[parts : 2 * parts], owners)
    masked, cot = refs[2 * parts : 2 * parts + 2]
    outs, counts = refs[2 * parts + 2 : -1], refs[-1]
    slots = worker_codes(routing, counts, owners)
    rows, inner = BLOCK * PER_WORKER, owners * BLOCK * capacity
    row, lane = iota((rows, inner), 0), iota((rows, inner), 1)
    target = jnp.full((rows, inner), DEAD, I32)
    for slot, (owner, place, rank) in enumerate(slots):
        step = partner("blk", owner, permuted)
        target = jnp.where(row % PER_WORKER == slot, step * (BLOCK * capacity) + rank, target)
    pick = one_hot(lane == target + (row // PER_WORKER) * capacity)
    for u in range(BLOCK):
        got = jnp.concatenate(
            [ordered(own[o][u], other[o][u], 1) for o in range(owners)], axis=0
        )
        cot[u] = dot(pick, got).astype(BF16)
    grads = cot[...].reshape(BLOCK * rows, FULL)
    for tap in range(9):
        dy, dx = tap // 3, tap % 3
        window = masked[dy : dy + BLOCK, dx : dx + BLOCK].reshape(BLOCK * rows, HALF)
        window = jnp.maximum(window, jnp.zeros_like(window))
        emit(dot_tn(window, grads) * scale, outs, tap)


def first_gradient(
    scale, cot, masked, masked_other, weight, weight_other, saved, *refs
):
    outs, (total, pre, full) = refs[:-3], refs[-3:]
    rows = BLOCK * BLOCK * PER_WORKER
    full[...] = ordered(weight[...], weight_other[...], 1)
    total[...] = jnp.zeros_like(total)
    for tap in range(9):
        dy, dx = tap // 3, tap % 3
        part = dot_nt(cot[...].reshape(rows, FULL), full[tap])
        spot = (slice(dy, dy + BLOCK), slice(dx, dx + BLOCK))
        total[spot] = total[spot] + part.reshape(BLOCK, BLOCK, PER_WORKER, FULL)
    for m in range(MIDDLE):
        live = ordered(masked[m], masked_other[m], 2).astype(F32) > 0
        pre[m] = jnp.where(live, total[m], 0.0).astype(BF16)
    size = MIDDLE * MIDDLE * PER_WORKER
    grads = pre[...].reshape(size, FULL)
    for tap in range(9):
        dy, dx = tap // 3, tap % 3
        window = saved[dy : dy + MIDDLE, dx : dx + MIDDLE].reshape(size, HALF)
        emit(dot_tn(window, grads) * scale, outs, tap)


def owner_spread(tile, tile_other, second, second_other, total, cot, full):
    row, lane = iota((FULL, FULL), 0), iota((FULL, FULL), 1)
    turn = one_hot(lane == (row % TILE_BLOCKS) * BLOCK + row // TILE_BLOCKS)
    for u in range(BLOCK):
        block = jnp.concatenate(
            [ordered(tile[r, u], tile_other[r, u], 1) for r in range(TILE_ROWS)], axis=0
        )
        cot[u] = dot(turn, block).astype(BF16)
    full[...] = ordered(second[...], second_other[...], 1)
    rows = BLOCK * BLOCK * TILE_BLOCKS
    total[...] = jnp.zeros_like(total)
    for tap in range(9):
        dy, dx = tap // 3, tap % 3
        part = dot_nt(cot[...].reshape(rows, FULL), full[tap])
        spot = (slice(dy, dy + BLOCK), slice(dx, dx + BLOCK))
        total[spot] = total[spot] + part.reshape(BLOCK, BLOCK, TILE_BLOCKS, FULL)


def owner_canvas(owners, capacity, wide, permuted, routing, *refs):
    parts = 1 if not permuted else owners
    got, got_other = views(refs[:parts], owners), views(refs[parts : 2 * parts], owners)
    total, first, canvas, table, pre, grown = refs[2 * parts :]
    owner_table(routing, table, owners, capacity)
    size, into = wide * capacity, MIDDLE * TILE_BLOCKS
    row, lane = iota((size, into), 0), iota((size, into), 1)
    picks = []
    for step in range(owners):
        worker = partner("blk", step, permuted)
        target = jnp.full((size, into), DEAD, I32)
        for rank in range(capacity):
            target = jnp.where(row % capacity == rank, table[worker * capacity + rank], target)
        at = row // capacity
        hits = (lane == target + at * TILE_BLOCKS) & (at < MIDDLE)
        picks.append(jnp.where(hits, 1.0, 0.0))
    pick = jnp.concatenate(picks, axis=0).T.astype(BF16)
    for m in range(MIDDLE):
        block = jnp.concatenate(
            [ordered(got[w][m], got_other[w][m], 1) for w in range(owners)], axis=0
        )
        live = dot(pick, block).reshape(MIDDLE, TILE_BLOCKS, FULL) > 0
        pre[m] = jnp.where(live, total[m], 0.0).astype(BF16)
    size = MIDDLE * MIDDLE * TILE_BLOCKS
    grown[...] = jnp.zeros_like(grown)
    for tap in range(9):
        dy, dx = tap // 3, tap % 3
        part = dot_nt(pre[...].reshape(size, FULL), first[tap])
        spot = (slice(dy, dy + MIDDLE), slice(dx, dx + MIDDLE))
        grown[spot] = grown[spot] + part.reshape(MIDDLE, MIDDLE, TILE_BLOCKS, HALF)
    height, depth = TILE_ROWS * WIDE, OUTER * TILE_BLOCKS
    row, lane = iota((height, depth), 0), iota((height, depth), 1)
    at_row, at_col = row // WIDE, row % WIDE
    n, place = lane // TILE_BLOCKS, lane % TILE_BLOCKS
    column = (place % TILE_COLS) * BLOCK + n - 2
    column = jnp.where(column < 0, column + 36, column)
    fold = one_hot((at_row == place // TILE_COLS) & (at_col == column))
    canvas[...] = jnp.zeros_like(canvas)
    for m in range(0, OUTER, 2):
        pair = jnp.concatenate(
            [grown[m + k].reshape(depth, HALF).astype(BF16) for k in range(2)], axis=1
        )
        laid = dot(fold, pair).reshape(TILE_ROWS, WIDE, FULL)
        for r in range(TILE_ROWS):
            for k in range(2):
                canvas[r * BLOCK + m + k] += laid[r, :, k * HALF : (k + 1) * HALF]


def bit_of(axis, step):
    return (lax.axis_index(axis) // step) % 2


def add_split(step, kept, got, keep, send):
    low_mine = bit_of("blk", step) == 0
    half = kept.shape[1] // 2
    for tap in range(9):
        value = kept[tap] + got[tap].astype(F32)
        low, high = value[:half], value[half:]
        keep[tap] = jnp.where(low_mine, low, high)
        send[tap] = jnp.where(low_mine, high, low).astype(BF16)


def add_last(kept, got, out):
    out[...] = (kept[...] + got[...].astype(F32)).astype(BF16)


def join(step, own, other, out):
    low_mine = bit_of("blk", step) == 0
    half = own.shape[1]
    for tap in range(9):
        out[tap, :half] = jnp.where(low_mine, own[tap], other[tap])
        out[tap, half:] = jnp.where(low_mine, other[tap], own[tap])


def lay(own, beside, across, across_beside, out):
    size = own.shape[1]
    column, side = lax.axis_index("col"), bit_of("blk", 1)
    for value, c, z in (
        (own, column, side),
        (beside, column, 1 - side),
        (across, 1 - column, side),
        (across_beside, 1 - column, 1 - side),
    ):
        at = pl.multiple_of(c * (2 * size) + z * size, size)
        out[:, pl.ds(at, size), :] = value[...].astype(F32)


def swap(value, axis="ch"):
    return lax.ppermute(value, axis, [(0, 1), (1, 0)])


def flip(value, axis, step):
    size = lax.axis_size(axis)
    return lax.ppermute(value, axis, [(i, i ^ step) for i in range(size)])


def neighbours(axis):
    size = lax.axis_size(axis)
    up = [(i, (i + 1) % size) for i in range(size - 1)]
    return up, [(j, i) for i, j in up]


def shards(grad_out, saved_input, saved_pre, first_weight, second_weight, assignment):
    owners = lax.axis_size("blk")
    columns = lax.axis_size("col")
    capacity = max(2, TILE_BLOCKS // owners)
    wide = MIDDLE if (MIDDLE * capacity) % 16 == 0 else 16
    scale = 1.0 / math.sqrt(owners * columns * PER_WORKER * BLOCK * BLOCK)
    permuted = owners == 4 and columns == 2
    parts = owners if permuted else 1
    routing = assignment[0]
    shape = jax.ShapeDtypeStruct
    tables = [pltpu.SMEM((owners * capacity + 1,), I32)]
    counts = [pltpu.SMEM((owners,), I32)]

    def pieces(*dims):
        return [shape(dims, BF16)] * owners if permuted else [shape((owners,) + dims, BF16)]

    def exchange(values):
        if permuted:
            return [values[0]] + [flip(values[k], "blk", k) for k in (1, 2, 3)]
        return [lax.all_to_all(values[0], "blk", split_axis=0, concat_axis=0, tiled=True)]

    tile = grad_out.reshape(TILE_ROWS, BLOCK, TILE_COLS * BLOCK, HALF)
    outgoing = call(
        functools.partial(pack_cotangents, owners, capacity, permuted),
        pieces(BLOCK, BLOCK * capacity, HALF),
        [SMEM, VMEM], tables, (1, 1), "pack_cotangents",
    )(routing, tile)
    tie = lax.optimization_barrier
    saved_slots = saved_pre[0, 0].transpose(1, 2, 0, 3)
    outgoing, saved_slots, second_mine, tile_mine = tie(
        (outgoing, saved_slots, second_weight, tile)
    )
    incoming = exchange(outgoing)
    masked, *to_owners = call(
        functools.partial(pack_saved, owners, columns, capacity, wide, permuted),
        [shape((MIDDLE, MIDDLE * PER_WORKER, HALF), BF16)] + pieces(MIDDLE, wide * capacity, HALF),
        [SMEM, VMEM], counts + tables, (1, 1), "pack_saved",
    )(routing, saved_slots.reshape(MIDDLE, MIDDLE * PER_WORKER, HALF))
    masked = masked.reshape(MIDDLE, MIDDLE, PER_WORKER, HALF)
    second_other = swap(second_mine)
    masked_other = swap(masked)
    tile_other = swap(tile_mine)
    total = call(
        owner_spread,
        shape((MIDDLE, MIDDLE, TILE_BLOCKS, FULL), F32),
        [VMEM] * 4,
        [pltpu.VMEM((BLOCK, FULL, FULL), BF16), pltpu.VMEM((9, FULL, FULL), BF16)],
        (1, 1), "owner_spread",
    )(tile, tile_other, second_weight, second_other)

    incoming, far, total, masked_other = tie((incoming, to_owners[2:], total, masked_other))
    incoming_other = [swap(value) for value in incoming]
    at_owner = exchange(to_owners[:2] + far)

    if permuted:
        halved = [shape((9, HALF // 2, FULL), F32), shape((9, HALF // 2, FULL), BF16)]
    else:
        halved = [shape((9, HALF, FULL), F32)]
    cot, *second_terms = call(
        functools.partial(second_gradient, scale, owners, capacity, permuted),
        [shape((BLOCK, BLOCK * PER_WORKER, FULL), BF16)] + halved,
        [SMEM] + [VMEM] * (2 * parts + 1), counts, (1, 1), "second_gradient",
    )(routing, *incoming, *incoming_other, masked)

    saved_tiles = saved_input[0, 0].transpose(1, 2, 0, 3)
    first_terms = call(
        functools.partial(first_gradient, scale),
        halved,
        [VMEM] * 6,
        [
            pltpu.VMEM((MIDDLE, MIDDLE, PER_WORKER, FULL), F32),
            pltpu.VMEM((MIDDLE, MIDDLE, PER_WORKER, FULL), BF16),
            pltpu.VMEM((9, FULL, FULL), BF16),
        ],
        (1, 1), "first_gradient",
    )(cot, masked, masked_other, second_weight, second_other, saved_tiles)

    if permuted:

        def small(body, rows, kinds, name, *values):
            outs = [shape((9, rows, FULL), kind) for kind in kinds]
            return call(body, outs, [VMEM] * len(values), [], (1, 1), name)(*values)

        def split(step, kept, got):
            rows = kept.shape[1] // 2
            return small(functools.partial(add_split, step), rows, (F32, BF16), "add_split", kept, got)

        def finish(kept, got):
            [own] = small(add_last, kept.shape[1], (BF16,), "add_last", kept, got)
            other = flip(own, "blk", 2)
            [own] = small(functools.partial(join, 2), 2 * own.shape[1], (BF16,), "join", own, other)
            beside = flip(own, "blk", 1)
            across, across_beside = swap(own, "col"), swap(beside, "col")
            return small(lay, HALF, (F32,), "lay", own, beside, across, across_beside)[0]

        second_got = swap(second_terms[1], "col")
        first_send, second_got, at_owner[1], at_owner[3] = tie(
            (first_terms[1], second_got, at_owner[1], at_owner[3])
        )
        first_got = swap(first_send, "col")
        second_kept, second_send = split(1, second_terms[0], second_got)
        second_kept, second_send = split(2, second_kept, flip(second_send, "blk", 1))
        first_kept, first_send = split(1, first_terms[0], first_got)
        first_send, at_owner = tie((first_send, at_owner))
        first_kept, first_send = split(2, first_kept, flip(first_send, "blk", 1))
        grad_second = finish(second_kept, flip(second_send, "blk", 2))
        grad_first = finish(first_kept, flip(first_send, "blk", 2))
    else:
        grad_first, grad_second = lax.psum((first_terms[0], second_terms[0]), ("blk", "col"))

    at_owner_other = [swap(value) for value in at_owner]
    height = TILE_ROWS * BLOCK + 4
    canvas = call(
        functools.partial(owner_canvas, owners, capacity, wide, permuted),
        shape((height, WIDE, HALF), F32),
        [SMEM] + [VMEM] * (2 * parts + 2),
        tables
        + [
            pltpu.VMEM((MIDDLE, MIDDLE, TILE_BLOCKS, FULL), BF16),
            pltpu.VMEM((OUTER, OUTER, TILE_BLOCKS, HALF), F32),
        ],
        (1, 1), "owner_canvas",
    )(routing, *at_owner, *at_owner_other, total, first_weight)

    up, down = neighbours("blk")
    from_above = lax.ppermute(canvas[height - 2 :].astype(BF16), "blk", up).astype(F32)
    from_below = lax.ppermute(canvas[:2].astype(BF16), "blk", down).astype(F32)
    inner = canvas[2 : height - 2]
    inner = inner.at[:2].add(from_above).at[-2:].add(from_below)
    up, down = neighbours("col")
    from_left = lax.ppermute(inner[:, 32:34].astype(BF16), "col", up).astype(F32)
    from_right = lax.ppermute(inner[:, 34:36].astype(BF16), "col", down).astype(F32)
    inner = inner[:, :32].at[:, :2].add(from_left).at[:, -2:].add(from_right)
    grad_in = (grad_out.astype(F32) + inner).astype(BF16)
    return (grad_in, grad_first, grad_second)


def solution(mesh):
    return jax.shard_map(
        shards,
        mesh=mesh,
        in_specs=(
            P(("groups", "blk"), "col", "ch"),
            P(("groups", "col"), "blk", None, None, None, "ch"),
            P(("groups", "col"), "blk", None, None, None, "ch"),
            P(None, "ch", None),
            P(None, "ch", None),
            P(("groups", "col"), None, None),
        ),
        out_specs=(
            P(("groups", "blk"), "col", "ch"),
            P("groups", "ch", None),
            P("groups", "ch", None),
        ),
        check_vma=False,
    )
```

```python
import functools
import math

import jax
import jax.numpy as jnp
from jax import lax
from jax.experimental import pallas as pl
from jax.experimental.pallas import tpu as pltpu
from jax.sharding import PartitionSpec as P

BLOCK = 8
TILE_ROWS = 8
TILE_COLS = 4
TILE_BLOCKS = 32
PER_WORKER = 16
MIDDLE = 10
OUTER = 12
HALF = 128
FULL = 256
DEAD = -4096
WIDE = 40

BF16 = jnp.bfloat16
F32 = jnp.float32
I32 = jnp.int32

VMEM = pl.BlockSpec(memory_space=pltpu.VMEM)
SMEM = pl.BlockSpec(memory_space=pltpu.SMEM)


def call(body, outs, specs, scratch, cost, name):
    return pl.pallas_call(
        body,
        out_shape=outs,
        in_specs=specs,
        out_specs=jax.tree.map(lambda _: VMEM, outs),
        scratch_shapes=scratch,
        compiler_params=pltpu.CompilerParams(vmem_limit_bytes=48 * 1024 * 1024),
        cost_estimate=pl.CostEstimate(flops=cost[0], bytes_accessed=cost[1], transcendentals=0),
        name=name,
    )


def iota(shape, dim):
    return lax.broadcasted_iota(I32, shape, dim)


def one_hot(hits):
    return jnp.where(hits, 1.0, 0.0).astype(BF16)


def dot(a, b):
    return jnp.dot(a, b, preferred_element_type=F32)


def dot_nt(a, b):
    return lax.dot_general(a, b, (((1,), (1,)), ((), ())), preferred_element_type=F32)


def dot_tn(a, b):
    return lax.dot_general(a, b, (((0,), (0,)), ((), ())), preferred_element_type=F32)


def owner_table(routing, table, owners, capacity):
    me = lax.axis_index("blk")

    def clear(number, carry):
        table[number] = DEAD
        return carry

    lax.fori_loop(0, owners * capacity, clear, 0)

    def worker(number, carry):
        count = jnp.int32(0)
        for slot in range(PER_WORKER):
            code = routing[number, slot]
            hit = (code // TILE_BLOCKS) == me
            table[jnp.where(hit, number * capacity + count, owners * capacity)] = code % TILE_BLOCKS
            count = count + jnp.where(hit, 1, 0)
        return carry

    lax.fori_loop(0, owners, worker, 0)


def worker_codes(routing, counts, owners):
    me = lax.axis_index("blk")

    def clear(number, carry):
        counts[number] = 0
        return carry

    lax.fori_loop(0, owners, clear, 0)
    slots = []
    for slot in range(PER_WORKER):
        code = routing[me, slot]
        owner = code // TILE_BLOCKS
        rank = counts[owner]
        counts[owner] = rank + 1
        slots.append((owner, code % TILE_BLOCKS, rank))
    return slots


def views(refs, count):
    return list(refs) if len(refs) == count else [refs[0].at[k] for k in range(count)]


def partner(axis, step, permuted):
    return step ^ lax.axis_index(axis) if permuted else step


def pack_cotangents(owners, capacity, permuted, routing, tile, *refs):
    outs, table = refs[:-1], refs[-1]
    owner_table(routing, table, owners, capacity)
    rows = BLOCK * capacity
    row, lane = iota((rows, FULL), 0), iota((rows, FULL), 1)
    picks = []
    for step in range(owners):
        worker = partner("blk", step, permuted)
        target = jnp.full((rows, FULL), DEAD, I32)
        for rank in range(capacity):
            place = table[worker * capacity + rank] * BLOCK
            target = jnp.where(row % capacity == rank, place, target)
        picks.append(one_hot(lane == target + row // capacity))
    pick = jnp.concatenate(picks, axis=0)
    for u in range(0, BLOCK, 2):
        pair = [
            jnp.concatenate([tile[r, u + k] for r in range(TILE_ROWS)], axis=0) for k in range(2)
        ]
        moved = dot(pick, jnp.concatenate(pair, axis=1)).astype(BF16)
        for step, out in enumerate(views(outs, owners)):
            part = moved[step * rows : (step + 1) * rows]
            out[u] = part[:, :HALF]
            out[u + 1] = part[:, HALF:]


def pack_saved(owners, columns, capacity, wide, permuted, routing, saved, masked, *refs):
    outs, counts, table = refs[:-2], refs[-2], refs[-1]
    column = lax.axis_index("col")

    def clear(number, carry):
        table[number] = DEAD
        return carry

    lax.fori_loop(0, owners * capacity, clear, 0)
    slots = worker_codes(routing, counts, owners)
    rows = MIDDLE * PER_WORKER
    row = iota((rows, HALF), 0)
    flags = jnp.zeros((rows, HALF), I32)
    for slot, (owner, place, rank) in enumerate(slots):
        table[owner * capacity + rank] = slot
        block_row, block_col = place // TILE_COLS, place % TILE_COLS
        flag = (
            jnp.where((owner == 0) & (block_row == 0), 1, 0)
            + jnp.where((owner == owners - 1) & (block_row == TILE_ROWS - 1), 2, 0)
            + jnp.where((column == 0) & (block_col == 0), 4, 0)
            + jnp.where((column == columns - 1) & (block_col == TILE_COLS - 1), 8, 0)
        )
        flags = jnp.where(row % PER_WORKER == slot, flag, flags)
    across = row // PER_WORKER
    outside = (((flags & 4) != 0) & (across == 0)) | (((flags & 8) != 0) & (across == MIDDLE - 1))
    for m in range(MIDDLE):
        here = outside
        if m == 0:
            here = here | ((flags & 1) != 0)
        if m == MIDDLE - 1:
            here = here | ((flags & 2) != 0)
        masked[m] = jnp.where(here, 0.0, saved[m].astype(F32)).astype(BF16)
    size = wide * capacity
    row, lane = iota((size, FULL), 0), iota((size, FULL), 1)
    picks = []
    for step in range(owners):
        owner = partner("blk", step, permuted)
        target = jnp.full((size, FULL), DEAD, I32)
        for rank in range(capacity):
            target = jnp.where(row % capacity == rank, table[owner * capacity + rank], target)
        at = row // capacity
        picks.append(one_hot((lane == target + at * PER_WORKER) & (at < MIDDLE)))
    pick = jnp.concatenate(picks, axis=0)
    filler = jnp.zeros((FULL - rows, FULL), BF16)
    for m in range(0, MIDDLE, 2):
        pair = jnp.concatenate([masked[m], masked[m + 1]], axis=1)
        moved = dot(pick, jnp.concatenate([pair, filler], axis=0)).astype(BF16)
        for step, out in enumerate(views(outs, owners)):
            part = moved[step * size : (step + 1) * size]
            out[m] = part[:, :HALF]
            out[m + 1] = part[:, HALF:]


def ordered(own, other, axis):
    first = lax.axis_index("ch") == 0
    return jnp.concatenate(
        [jnp.where(first, own, other), jnp.where(first, other, own)], axis=axis
    )


def halves(value, keep, send, tap):
    low, high = value[: HALF // 2], value[HALF // 2 :]
    mine = lax.axis_index("col") == 0
    keep[tap] = jnp.where(mine, low, high)
    send[tap] = jnp.where(mine, high, low).astype(BF16)


def emit(value, outs, tap):
    if len(outs) == 2:
        halves(value, outs[0], outs[1], tap)
    else:
        outs[0][tap] = value


def second_gradient(scale, owners, capacity, permuted, routing, *refs):
    parts = 1 if not permuted else owners
    own, other = views(refs[:parts], owners), views(refs[parts : 2 * parts], owners)
    masked, cot = refs[2 * parts : 2 * parts + 2]
    outs, counts = refs[2 * parts + 2 : -1], refs[-1]
    slots = worker_codes(routing, counts, owners)
    rows, inner = BLOCK * PER_WORKER, owners * BLOCK * capacity
    row, lane = iota((rows, inner), 0), iota((rows, inner), 1)
    target = jnp.full((rows, inner), DEAD, I32)
    for slot, (owner, place, rank) in enumerate(slots):
        step = partner("blk", owner, permuted)
        target = jnp.where(row % PER_WORKER == slot, step * (BLOCK * capacity) + rank, target)
    pick = one_hot(lane == target + (row // PER_WORKER) * capacity)
    for u in range(BLOCK):
        got = jnp.concatenate(
            [ordered(own[o][u], other[o][u], 1) for o in range(owners)], axis=0
        )
        cot[u] = dot(pick, got).astype(BF16)
    grads = cot[...].reshape(BLOCK * rows, FULL)
    for tap in range(9):
        dy, dx = tap // 3, tap % 3
        window = masked[dy : dy + BLOCK, dx : dx + BLOCK].reshape(BLOCK * rows, HALF)
        window = jnp.maximum(window, jnp.zeros_like(window))
        emit(dot_tn(window, grads) * scale, outs, tap)


def first_gradient(
    scale, cot, masked, masked_other, weight, weight_other, saved, *refs
):
    outs, (total, pre, full) = refs[:-3], refs[-3:]
    rows = BLOCK * BLOCK * PER_WORKER
    full[...] = ordered(weight[...], weight_other[...], 1)
    total[...] = jnp.zeros_like(total)
    for tap in range(9):
        dy, dx = tap // 3, tap % 3
        part = dot_nt(cot[...].reshape(rows, FULL), full[tap])
        spot = (slice(dy, dy + BLOCK), slice(dx, dx + BLOCK))
        total[spot] = total[spot] + part.reshape(BLOCK, BLOCK, PER_WORKER, FULL)
    for m in range(MIDDLE):
        live = ordered(masked[m], masked_other[m], 2).astype(F32) > 0
        pre[m] = jnp.where(live, total[m], 0.0).astype(BF16)
    size = MIDDLE * MIDDLE * PER_WORKER
    grads = pre[...].reshape(size, FULL)
    for tap in range(9):
        dy, dx = tap // 3, tap % 3
        window = saved[dy : dy + MIDDLE, dx : dx + MIDDLE].reshape(size, HALF)
        emit(dot_tn(window, grads) * scale, outs, tap)


def owner_spread(tile, tile_other, second, second_other, total, cot, full):
    row, lane = iota((FULL, FULL), 0), iota((FULL, FULL), 1)
    turn = one_hot(lane == (row % TILE_BLOCKS) * BLOCK + row // TILE_BLOCKS)
    for u in range(BLOCK):
        block = jnp.concatenate(
            [ordered(tile[r, u], tile_other[r, u], 1) for r in range(TILE_ROWS)], axis=0
        )
        cot[u] = dot(turn, block).astype(BF16)
    full[...] = ordered(second[...], second_other[...], 1)
    rows = BLOCK * BLOCK * TILE_BLOCKS
    total[...] = jnp.zeros_like(total)
    for tap in range(9):
        dy, dx = tap // 3, tap % 3
        part = dot_nt(cot[...].reshape(rows, FULL), full[tap])
        spot = (slice(dy, dy + BLOCK), slice(dx, dx + BLOCK))
        total[spot] = total[spot] + part.reshape(BLOCK, BLOCK, TILE_BLOCKS, FULL)


def prepare(owners, columns, capacity, wide, permuted, routing, saved, *refs):
    (tile, tile_other, second, second_other), refs = refs[:4], refs[4:]
    masked, outs = refs[0], refs[1:-6]
    total, counts, table, spread, cot, full = refs[-6:]
    pack_saved(owners, columns, capacity, wide, permuted, routing, saved, masked, *outs, counts, table)
    owner_spread(tile, tile_other, second, second_other, spread, cot, full)
    total[...] = spread[...].astype(BF16)


def worker(scale, owners, capacity, permuted, routing, *refs):
    parts = 1 if not permuted else owners
    inputs, refs = refs[: 2 * parts], refs[2 * parts :]
    (masked, masked_other, weight, weight_other, saved), refs = refs[:5], refs[5:]
    outs, (counts, cot, total, pre, full) = refs[:-5], refs[-5:]
    pairs = [[out.at[k] for out in outs] for k in range(2)]
    second_gradient(scale, owners, capacity, permuted, routing, *inputs, masked, cot, *pairs[0], counts)
    first_gradient(
        scale, cot, masked, masked_other, weight, weight_other, saved, *pairs[1], total, pre, full
    )


def owner_canvas(owners, capacity, wide, permuted, routing, *refs):
    parts = 1 if not permuted else owners
    got, got_other = views(refs[:parts], owners), views(refs[parts : 2 * parts], owners)
    total, first, canvas, table, pre, grown = refs[2 * parts :]
    owner_table(routing, table, owners, capacity)
    size, into = wide * capacity, MIDDLE * TILE_BLOCKS
    row, lane = iota((size, into), 0), iota((size, into), 1)
    picks = []
    for step in range(owners):
        worker = partner("blk", step, permuted)
        target = jnp.full((size, into), DEAD, I32)
        for rank in range(capacity):
            target = jnp.where(row % capacity == rank, table[worker * capacity + rank], target)
        at = row // capacity
        hits = (lane == target + at * TILE_BLOCKS) & (at < MIDDLE)
        picks.append(jnp.where(hits, 1.0, 0.0))
    pick = jnp.concatenate(picks, axis=0).T.astype(BF16)
    for m in range(MIDDLE):
        block = jnp.concatenate(
            [ordered(got[w][m], got_other[w][m], 1) for w in range(owners)], axis=0
        )
        live = dot(pick, block).reshape(MIDDLE, TILE_BLOCKS, FULL) > 0
        pre[m] = jnp.where(live, total[m].astype(F32), 0.0).astype(BF16)
    size = MIDDLE * MIDDLE * TILE_BLOCKS
    grown[...] = jnp.zeros_like(grown)
    for tap in range(9):
        dy, dx = tap // 3, tap % 3
        part = dot_nt(pre[...].reshape(size, FULL), first[tap])
        spot = (slice(dy, dy + MIDDLE), slice(dx, dx + MIDDLE))
        grown[spot] = grown[spot] + part.reshape(MIDDLE, MIDDLE, TILE_BLOCKS, HALF)
    height, depth = TILE_ROWS * WIDE, OUTER * TILE_BLOCKS
    row, lane = iota((height, depth), 0), iota((height, depth), 1)
    at_row, at_col = row // WIDE, row % WIDE
    n, place = lane // TILE_BLOCKS, lane % TILE_BLOCKS
    column = (place % TILE_COLS) * BLOCK + n - 2
    column = jnp.where(column < 0, column + 36, column)
    fold = one_hot((at_row == place // TILE_COLS) & (at_col == column))
    canvas[...] = jnp.zeros_like(canvas)
    for m in range(0, OUTER, 2):
        pair = jnp.concatenate(
            [grown[m + k].reshape(depth, HALF).astype(BF16) for k in range(2)], axis=1
        )
        laid = dot(fold, pair).reshape(TILE_ROWS, WIDE, FULL)
        for r in range(TILE_ROWS):
            for k in range(2):
                canvas[r * BLOCK + m + k] += laid[r, :, k * HALF : (k + 1) * HALF]


def bit_of(axis, step):
    return (lax.axis_index(axis) // step) % 2


def add_columns(kept, got, *outs):
    size = HALF // 2 // len(outs)
    for step, out in enumerate(outs):
        at = pl.multiple_of(partner("blk", step, True) * size, size)
        part = kept[:, :, pl.ds(at, size), :] + got[:, :, pl.ds(at, size), :].astype(F32)
        out[...] = part if step == 0 else part.astype(BF16)


def add_workers(kept, *refs):
    got, outs = refs[:-2], refs[-2:]
    for k in range(2):
        value = kept[k]
        for part in got:
            value = value + part[k].astype(F32)
        outs[k][...] = value.astype(BF16)


def lay_parts(*refs):
    parts, out = refs[:-1], refs[-1]
    size = HALF // 2 // len(parts)
    for step, part in enumerate(parts):
        at = pl.multiple_of(partner("blk", step, True) * size, size)
        out[:, pl.ds(at, size), :] = part[...]


def lay_halves(own, other, out):
    mine = lax.axis_index("col") == 0
    for tap in range(9):
        out[tap, : HALF // 2] = jnp.where(mine, own[tap], other[tap]).astype(F32)
        out[tap, HALF // 2 :] = jnp.where(mine, other[tap], own[tap]).astype(F32)


def swap(value, axis="ch"):
    return lax.ppermute(value, axis, [(0, 1), (1, 0)])


def flip(value, axis, step):
    size = lax.axis_size(axis)
    return lax.ppermute(value, axis, [(i, i ^ step) for i in range(size)])


def neighbours(axis):
    size = lax.axis_size(axis)
    up = [(i, (i + 1) % size) for i in range(size - 1)]
    return up, [(j, i) for i, j in up]


def shards(grad_out, saved_input, saved_pre, first_weight, second_weight, assignment):
    owners = lax.axis_size("blk")
    columns = lax.axis_size("col")
    capacity = max(2, TILE_BLOCKS // owners)
    wide = MIDDLE if (MIDDLE * capacity) % 16 == 0 else 16
    scale = 1.0 / math.sqrt(owners * columns * PER_WORKER * BLOCK * BLOCK)
    permuted = owners == 4 and columns == 2
    parts = owners if permuted else 1
    routing = assignment[0]
    shape = jax.ShapeDtypeStruct
    tables = [pltpu.SMEM((owners * capacity + 1,), I32)]
    counts = [pltpu.SMEM((owners,), I32)]

    def pieces(*dims):
        return [shape(dims, BF16)] * owners if permuted else [shape((owners,) + dims, BF16)]

    def exchange(values):
        if permuted:
            return [values[0]] + [flip(values[k], "blk", k) for k in (1, 2, 3)]
        return [lax.all_to_all(values[0], "blk", split_axis=0, concat_axis=0, tiled=True)]

    tie = lax.optimization_barrier
    tile = grad_out.reshape(TILE_ROWS, BLOCK, TILE_COLS * BLOCK, HALF)
    second_other, tile_other = swap(second_weight), swap(tile)
    outgoing = call(
        functools.partial(pack_cotangents, owners, capacity, permuted),
        pieces(BLOCK, BLOCK * capacity, HALF),
        [SMEM, VMEM], tables, (1, 1), "pack_cotangents",
    )(routing, tile)
    saved_slots = saved_pre[0, 0].transpose(1, 2, 0, 3)
    outgoing, saved_slots = tie((outgoing, saved_slots))
    incoming = exchange(outgoing)

    masked, *to_owners, total = call(
        functools.partial(prepare, owners, columns, capacity, wide, permuted),
        [shape((MIDDLE, MIDDLE * PER_WORKER, HALF), BF16)]
        + pieces(MIDDLE, wide * capacity, HALF)
        + [shape((MIDDLE, MIDDLE, TILE_BLOCKS, FULL), BF16)],
        [SMEM] + [VMEM] * 5,
        counts
        + tables
        + [
            pltpu.VMEM((MIDDLE, MIDDLE, TILE_BLOCKS, FULL), F32),
            pltpu.VMEM((BLOCK, FULL, FULL), BF16),
            pltpu.VMEM((9, FULL, FULL), BF16),
        ],
        (1, 1), "prepare",
    )(
        routing, saved_slots.reshape(MIDDLE, MIDDLE * PER_WORKER, HALF),
        tile, tile_other, second_weight, second_other,
    )
    masked = masked.reshape(MIDDLE, MIDDLE, PER_WORKER, HALF)
    incoming, to_owners, total, masked = tie((incoming, to_owners, total, masked))
    incoming_other = [swap(value) for value in incoming]
    masked_other = swap(masked)
    at_owner = exchange(to_owners)

    saved_tiles = saved_input[0, 0].transpose(1, 2, 0, 3)
    if permuted:
        halved = (2, 9, HALF // 2, FULL)
        halved = [shape(halved, F32), shape(halved, BF16)]
    else:
        halved = [shape((2, 9, HALF, FULL), F32)]
    terms = call(
        functools.partial(worker, scale, owners, capacity, permuted),
        halved,
        [SMEM] + [VMEM] * (2 * parts + 5),
        counts
        + [
            pltpu.VMEM((BLOCK, BLOCK * PER_WORKER, FULL), BF16),
            pltpu.VMEM((MIDDLE, MIDDLE, PER_WORKER, FULL), F32),
            pltpu.VMEM((MIDDLE, MIDDLE, PER_WORKER, FULL), BF16),
            pltpu.VMEM((9, FULL, FULL), BF16),
        ],
        (1, 1), "worker",
    )(
        routing, *incoming, *incoming_other, masked, masked_other, second_weight, second_other,
        saved_tiles,
    )

    if permuted:
        part = (2, 9, HALF // 2 // owners, FULL)
        send, at_owner[1], at_owner[2] = tie((terms[1], at_owner[1], at_owner[2]))
        got = swap(send, "col")
        kept, *sends = call(
            add_columns, [shape(part, F32)] + [shape(part, BF16)] * (owners - 1),
            [VMEM] * 2, [], (1, 1), "add_columns",
        )(terms[0], got)
        sends, at_owner = tie((sends, at_owner))
        got = [flip(value, "blk", k + 1) for k, value in enumerate(sends)]
        sums = call(
            add_workers, [shape(part[1:], BF16)] * 2, [VMEM] * owners, [], (1, 1), "add_workers",
        )(kept, *got)
        grads = []
        for value in sums:
            spread = [value] + [flip(value, "blk", k) for k in range(1, owners)]
            half = call(
                lay_parts, shape((9, HALF // 2, FULL), BF16), [VMEM] * owners, [], (1, 1),
                "lay_parts",
            )(*spread)
            grads.append(
                call(
                    lay_halves, shape((9, HALF, FULL), F32), [VMEM] * 2, [], (1, 1), "lay_halves",
                )(half, swap(half, "col"))
            )
        grad_second, grad_first = grads
    else:
        grad_first, grad_second = lax.psum((terms[0][1], terms[0][0]), ("blk", "col"))

    at_owner_other = [swap(value) for value in at_owner]
    height = TILE_ROWS * BLOCK + 4
    canvas = call(
        functools.partial(owner_canvas, owners, capacity, wide, permuted),
        shape((height, WIDE, HALF), F32),
        [SMEM] + [VMEM] * (2 * parts + 2),
        tables
        + [
            pltpu.VMEM((MIDDLE, MIDDLE, TILE_BLOCKS, FULL), BF16),
            pltpu.VMEM((OUTER, OUTER, TILE_BLOCKS, HALF), F32),
        ],
        (1, 1), "owner_canvas",
    )(routing, *at_owner, *at_owner_other, total, first_weight)

    up, down = neighbours("blk")
    from_above = lax.ppermute(canvas[height - 2 :].astype(BF16), "blk", up).astype(F32)
    from_below = lax.ppermute(canvas[:2].astype(BF16), "blk", down).astype(F32)
    inner = canvas[2 : height - 2]
    inner = inner.at[:2].add(from_above).at[-2:].add(from_below)
    up, down = neighbours("col")
    from_left = lax.ppermute(inner[:, 32:34].astype(BF16), "col", up).astype(F32)
    from_right = lax.ppermute(inner[:, 34:36].astype(BF16), "col", down).astype(F32)
    inner = inner[:, :32].at[:, :2].add(from_left).at[:, -2:].add(from_right)
    grad_in = (grad_out.astype(F32) + inner).astype(BF16)
    return (grad_in, grad_first, grad_second)


def solution(mesh):
    return jax.shard_map(
        shards,
        mesh=mesh,
        in_specs=(
            P(("groups", "blk"), "col", "ch"),
            P(("groups", "col"), "blk", None, None, None, "ch"),
            P(("groups", "col"), "blk", None, None, None, "ch"),
            P(None, "ch", None),
            P(None, "ch", None),
            P(("groups", "col"), None, None),
        ),
        out_specs=(
            P(("groups", "blk"), "col", "ch"),
            P("groups", "ch", None),
            P("groups", "ch", None),
        ),
        check_vma=False,
    )
```

```python
import functools
import math

import jax
import jax.numpy as jnp
from jax import lax
from jax.experimental import pallas as pl
from jax.experimental.pallas import tpu as pltpu
from jax.sharding import PartitionSpec as P

BLOCK = 8
TILE_ROWS = 8
TILE_COLS = 4
TILE_BLOCKS = 32
PER_WORKER = 16
MIDDLE = 10
OUTER = 12
HALF = 128
FULL = 256
DEAD = -4096
HIGH = 68
RIM = 48
PART = 288
WIDE = 40

BF16 = jnp.bfloat16
F32 = jnp.float32
I32 = jnp.int32

VMEM = pl.BlockSpec(memory_space=pltpu.VMEM)
SMEM = pl.BlockSpec(memory_space=pltpu.SMEM)


def call(body, outs, specs, scratch, cost, name):
    return pl.pallas_call(
        body,
        out_shape=outs,
        in_specs=specs,
        out_specs=jax.tree.map(lambda _: VMEM, outs),
        scratch_shapes=scratch,
        compiler_params=pltpu.CompilerParams(vmem_limit_bytes=48 * 1024 * 1024),
        cost_estimate=pl.CostEstimate(flops=cost[0], bytes_accessed=cost[1], transcendentals=0),
        name=name,
    )


def iota(shape, dim):
    return lax.broadcasted_iota(I32, shape, dim)


def one_hot(hits):
    return jnp.where(hits, 1.0, 0.0).astype(BF16)


def dot(a, b):
    return jnp.dot(a, b, preferred_element_type=F32)


def dot_nt(a, b):
    return lax.dot_general(a, b, (((1,), (1,)), ((), ())), preferred_element_type=F32)


def dot_tn(a, b):
    return lax.dot_general(a, b, (((0,), (0,)), ((), ())), preferred_element_type=F32)


def owner_table(routing, table, owners, capacity):
    me = lax.axis_index("blk")

    def clear(number, carry):
        table[number] = DEAD
        return carry

    lax.fori_loop(0, owners * capacity, clear, 0)

    def worker(number, carry):
        count = jnp.int32(0)
        for slot in range(PER_WORKER):
            code = routing[number, slot]
            hit = (code // TILE_BLOCKS) == me
            table[jnp.where(hit, number * capacity + count, owners * capacity)] = code % TILE_BLOCKS
            count = count + jnp.where(hit, 1, 0)
        return carry

    lax.fori_loop(0, owners, worker, 0)


def worker_codes(routing, counts, owners):
    me = lax.axis_index("blk")

    def clear(number, carry):
        counts[number] = 0
        return carry

    lax.fori_loop(0, owners, clear, 0)
    slots = []
    for slot in range(PER_WORKER):
        code = routing[me, slot]
        owner = code // TILE_BLOCKS
        rank = counts[owner]
        counts[owner] = rank + 1
        slots.append((owner, code % TILE_BLOCKS, rank))
    return slots


def views(refs, count):
    return list(refs) if len(refs) == count else [refs[0].at[k] for k in range(count)]


def partner(axis, step, permuted):
    return step ^ lax.axis_index(axis) if permuted else step


def pack_cotangents(owners, capacity, permuted, routing, tile, *refs):
    outs, table = refs[:-1], refs[-1]
    owner_table(routing, table, owners, capacity)
    rows = BLOCK * capacity
    row, lane = iota((rows, FULL), 0), iota((rows, FULL), 1)
    picks = []
    for step in range(owners):
        worker = partner("blk", step, permuted)
        target = jnp.full((rows, FULL), DEAD, I32)
        for rank in range(capacity):
            place = table[worker * capacity + rank] * BLOCK
            target = jnp.where(row % capacity == rank, place, target)
        picks.append(one_hot(lane == target + row // capacity))
    pick = jnp.concatenate(picks, axis=0)
    for u in range(0, BLOCK, 2):
        pair = [
            jnp.concatenate([tile[r, u + k] for r in range(TILE_ROWS)], axis=0) for k in range(2)
        ]
        moved = dot(pick, jnp.concatenate(pair, axis=1)).astype(BF16)
        for step, out in enumerate(views(outs, owners)):
            part = moved[step * rows : (step + 1) * rows]
            out[u] = part[:, :HALF]
            out[u + 1] = part[:, HALF:]


def pack_saved(owners, columns, capacity, wide, permuted, routing, saved, masked, *refs):
    outs, counts, table = refs[:-2], refs[-2], refs[-1]
    column = lax.axis_index("col")

    def clear(number, carry):
        table[number] = DEAD
        return carry

    lax.fori_loop(0, owners * capacity, clear, 0)
    slots = worker_codes(routing, counts, owners)
    rows = MIDDLE * PER_WORKER
    row = iota((rows, HALF), 0)
    flags = jnp.zeros((rows, HALF), I32)
    for slot, (owner, place, rank) in enumerate(slots):
        table[owner * capacity + rank] = slot
        block_row, block_col = place // TILE_COLS, place % TILE_COLS
        flag = (
            jnp.where((owner == 0) & (block_row == 0), 1, 0)
            + jnp.where((owner == owners - 1) & (block_row == TILE_ROWS - 1), 2, 0)
            + jnp.where((column == 0) & (block_col == 0), 4, 0)
            + jnp.where((column == columns - 1) & (block_col == TILE_COLS - 1), 8, 0)
        )
        flags = jnp.where(row % PER_WORKER == slot, flag, flags)
    across = row // PER_WORKER
    outside = (((flags & 4) != 0) & (across == 0)) | (((flags & 8) != 0) & (across == MIDDLE - 1))
    for m in range(MIDDLE):
        here = outside
        if m == 0:
            here = here | ((flags & 1) != 0)
        if m == MIDDLE - 1:
            here = here | ((flags & 2) != 0)
        masked[m] = jnp.where(here, 0.0, saved[m].astype(F32)).astype(BF16)
    size = wide * capacity
    row, lane = iota((size, FULL), 0), iota((size, FULL), 1)
    picks = []
    for step in range(owners):
        owner = partner("blk", step, permuted)
        target = jnp.full((size, FULL), DEAD, I32)
        for rank in range(capacity):
            target = jnp.where(row % capacity == rank, table[owner * capacity + rank], target)
        at = row // capacity
        picks.append(one_hot((lane == target + at * PER_WORKER) & (at < MIDDLE)))
    pick = jnp.concatenate(picks, axis=0)
    filler = jnp.zeros((FULL - rows, FULL), BF16)
    for m in range(0, MIDDLE, 2):
        pair = jnp.concatenate([masked[m], masked[m + 1]], axis=1)
        moved = dot(pick, jnp.concatenate([pair, filler], axis=0)).astype(BF16)
        for step, out in enumerate(views(outs, owners)):
            part = moved[step * size : (step + 1) * size]
            out[m] = part[:, :HALF]
            out[m + 1] = part[:, HALF:]


def ordered(own, other, axis):
    first = lax.axis_index("ch") == 0
    return jnp.concatenate(
        [jnp.where(first, own, other), jnp.where(first, other, own)], axis=axis
    )


def halves(value, keep, send, tap):
    low, high = value[: HALF // 2], value[HALF // 2 :]
    mine = lax.axis_index("col") == 0
    keep[tap] = jnp.where(mine, low, high)
    send[tap] = jnp.where(mine, high, low).astype(BF16)


def emit(value, outs, tap):
    if len(outs) == 2:
        halves(value, outs[0], outs[1], tap)
    else:
        outs[0][tap] = value


def second_gradient(scale, owners, capacity, permuted, routing, *refs):
    parts = 1 if not permuted else owners
    own, other = views(refs[:parts], owners), views(refs[parts : 2 * parts], owners)
    masked, cot = refs[2 * parts : 2 * parts + 2]
    outs, counts = refs[2 * parts + 2 : -1], refs[-1]
    slots = worker_codes(routing, counts, owners)
    rows, inner = BLOCK * PER_WORKER, owners * BLOCK * capacity
    row, lane = iota((rows, inner), 0), iota((rows, inner), 1)
    target = jnp.full((rows, inner), DEAD, I32)
    for slot, (owner, place, rank) in enumerate(slots):
        step = partner("blk", owner, permuted)
        target = jnp.where(row % PER_WORKER == slot, step * (BLOCK * capacity) + rank, target)
    pick = one_hot(lane == target + (row // PER_WORKER) * capacity)
    for u in range(BLOCK):
        got = jnp.concatenate(
            [ordered(own[o][u], other[o][u], 1) for o in range(owners)], axis=0
        )
        cot[u] = dot(pick, got).astype(BF16)
    grads = cot[...].reshape(BLOCK * rows, FULL)
    for tap in range(9):
        dy, dx = tap // 3, tap % 3
        window = masked[dy : dy + BLOCK, dx : dx + BLOCK].reshape(BLOCK * rows, HALF)
        window = jnp.maximum(window, jnp.zeros_like(window))
        emit(dot_tn(window, grads) * scale, outs, tap)


def first_gradient(
    scale, cot, masked, masked_other, weight, weight_other, saved, *refs
):
    outs, (total, pre, full) = refs[:-3], refs[-3:]
    rows = BLOCK * BLOCK * PER_WORKER
    full[...] = ordered(weight[...], weight_other[...], 1)
    total[...] = jnp.zeros_like(total)
    for tap in range(9):
        dy, dx = tap // 3, tap % 3
        part = dot_nt(cot[...].reshape(rows, FULL), full[tap])
        spot = (slice(dy, dy + BLOCK), slice(dx, dx + BLOCK))
        total[spot] = total[spot] + part.reshape(BLOCK, BLOCK, PER_WORKER, FULL)
    for m in range(MIDDLE):
        live = ordered(masked[m], masked_other[m], 2).astype(F32) > 0
        pre[m] = jnp.where(live, total[m], 0.0).astype(BF16)
    size = MIDDLE * MIDDLE * PER_WORKER
    grads = pre[...].reshape(size, FULL)
    for tap in range(9):
        dy, dx = tap // 3, tap % 3
        window = saved[dy : dy + MIDDLE, dx : dx + MIDDLE].reshape(size, HALF)
        emit(dot_tn(window, grads) * scale, outs, tap)


def owner_spread(tile, tile_other, second, second_other, out, total, cot, full):
    row, lane = iota((FULL, FULL), 0), iota((FULL, FULL), 1)
    turn = one_hot(lane == (row % TILE_BLOCKS) * BLOCK + row // TILE_BLOCKS)
    for u in range(BLOCK):
        block = jnp.concatenate(
            [ordered(tile[r, u], tile_other[r, u], 1) for r in range(TILE_ROWS)], axis=0
        )
        cot[u] = dot(turn, block).astype(BF16)
    full[...] = ordered(second[...], second_other[...], 1)
    rows = BLOCK * BLOCK * TILE_BLOCKS
    total[...] = jnp.zeros_like(total)
    for tap in range(9):
        dy, dx = tap // 3, tap % 3
        part = dot_nt(cot[...].reshape(rows, FULL), full[tap])
        spot = (slice(dy, dy + BLOCK), slice(dx, dx + BLOCK))
        total[spot] = total[spot] + part.reshape(BLOCK, BLOCK, TILE_BLOCKS, FULL)
    out[...] = total[...].astype(BF16)


def worker(scale, owners, capacity, permuted, routing, *refs):
    parts = 1 if not permuted else owners
    inputs, refs = refs[: 2 * parts], refs[2 * parts :]
    (masked, masked_other, weight, weight_other, saved), refs = refs[:5], refs[5:]
    outs, (counts, cot, total, pre, full) = refs[:-5], refs[-5:]
    pairs = [[out.at[k] for out in outs] for k in range(2)]
    second_gradient(scale, owners, capacity, permuted, routing, *inputs, masked, cot, *pairs[0], counts)
    first_gradient(
        scale, cot, masked, masked_other, weight, weight_other, saved, *pairs[1], total, pre, full
    )


def adjacent(step):
    me = lax.axis_index("blk")
    return (me ^ step) == me - 1, (me ^ step) == me + 1


def owner_canvas(owners, capacity, wide, permuted, routing, *refs):
    parts = 1 if not permuted else owners
    got, got_other = views(refs[:parts], owners), views(refs[parts : 2 * parts], owners)
    total, first, canvas = refs[2 * parts : 2 * parts + 3]
    rims, (table, pre, grown) = refs[2 * parts + 3 : -3], refs[-3:]
    owner_table(routing, table, owners, capacity)
    size, into = wide * capacity, MIDDLE * TILE_BLOCKS
    row, lane = iota((size, into), 0), iota((size, into), 1)
    picks = []
    for step in range(owners):
        worker = partner("blk", step, permuted)
        target = jnp.full((size, into), DEAD, I32)
        for rank in range(capacity):
            target = jnp.where(row % capacity == rank, table[worker * capacity + rank], target)
        at = row // capacity
        hits = (lane == target + at * TILE_BLOCKS) & (at < MIDDLE)
        picks.append(jnp.where(hits, 1.0, 0.0))
    pick = jnp.concatenate(picks, axis=0).T.astype(BF16)
    for m in range(MIDDLE):
        block = jnp.concatenate(
            [ordered(got[w][m], got_other[w][m], 1) for w in range(owners)], axis=0
        )
        live = dot(pick, block).reshape(MIDDLE, TILE_BLOCKS, FULL) > 0
        pre[m] = jnp.where(live, total[m].astype(F32), 0.0).astype(BF16)
    size = MIDDLE * MIDDLE * TILE_BLOCKS
    grown[...] = jnp.zeros_like(grown)
    for tap in range(9):
        dy, dx = tap // 3, tap % 3
        part = dot_nt(pre[...].reshape(size, FULL), first[tap])
        spot = (slice(dy, dy + MIDDLE), slice(dx, dx + MIDDLE))
        grown[spot] = grown[spot] + part.reshape(MIDDLE, MIDDLE, TILE_BLOCKS, HALF)
    height, depth = TILE_ROWS * WIDE, OUTER * TILE_BLOCKS
    row, lane = iota((height, depth), 0), iota((height, depth), 1)
    at_row, at_col = row // WIDE, row % WIDE
    n, place = lane // TILE_BLOCKS, lane % TILE_BLOCKS
    column = (place % TILE_COLS) * BLOCK + n - 2
    column = jnp.where(column < 0, column + 36, column)
    fold = one_hot((at_row == place // TILE_COLS) & (at_col == column))
    canvas[...] = jnp.zeros_like(canvas)
    for m in range(0, OUTER, 2):
        pair = jnp.concatenate(
            [grown[m + k].reshape(depth, HALF).astype(BF16) for k in range(2)], axis=1
        )
        laid = dot(fold, pair).reshape(TILE_ROWS, WIDE, FULL)
        for r in range(TILE_ROWS):
            for k in range(2):
                canvas[r * BLOCK + m + k] += laid[r, :, k * HALF : (k + 1) * HALF]
    for k, rim in enumerate(rims):
        above, below = adjacent(2 * k + 1)
        top = jnp.concatenate([canvas[0], canvas[1]], axis=1)
        bottom = jnp.concatenate([canvas[HIGH - 2], canvas[HIGH - 1]], axis=1)
        rim[:WIDE] = jnp.where(below, bottom, jnp.where(above, top, 0.0)).astype(BF16)
        rim[WIDE:] = jnp.zeros((RIM - WIDE, FULL), BF16)


def bit_of(axis, step):
    return (lax.axis_index(axis) // step) % 2


def add_columns(kept, got, *outs):
    size = HALF // 2 // len(outs)
    for step, out in enumerate(outs):
        at = pl.multiple_of(partner("blk", step, True) * size, size)
        part = kept[:, :, pl.ds(at, size), :] + got[:, :, pl.ds(at, size), :].astype(F32)
        out[...] = part if step == 0 else part.astype(BF16)


def add_workers(kept, got_1, got_2, got_3, rim_1, rim_3, out, out_1, out_3):
    value = kept[...]
    for part in (got_1, got_2, got_3):
        value = value + part[...].astype(F32)
    value = value.astype(BF16).reshape(PART, FULL)
    out[...] = value
    for message, rim in ((out_1, rim_1), (out_3, rim_3)):
        message[:PART] = value
        message[PART:] = rim[...]


def column_message(canvas, got_1, got_3, out, rim, strip):
    out[:PART] = got_3[:PART]
    for j in range(2):
        c = 32 + 2 * lax.axis_index("col") + j
        strip[...] = canvas[pl.ds(2 * WIDE + c, 64, stride=WIDE), :]
        for step, got in ((1, got_1), (3, got_3)):
            rim[...] = got[PART:].astype(F32)
            row = rim[pl.ds(c, 1), :]
            above, below = adjacent(step)
            top, bottom = jnp.where(above, row, 0.0), jnp.where(below, row, 0.0)
            strip[0:1] += top[:, :HALF]
            strip[1:2] += top[:, HALF:]
            strip[62:63] += bottom[:, :HALF]
            strip[63:64] += bottom[:, HALF:]
        out[PART:, j * HALF : (j + 1) * HALF] = strip[...].astype(BF16)


def close(tile, canvas, got_1, got_3, across, out, total):
    rows = TILE_ROWS * BLOCK * 32
    inner = canvas[2 : HIGH - 2, :32, :].reshape(rows, HALF)
    total[...] = tile[...].reshape(rows, HALF).astype(F32) + inner
    for step, got in ((1, got_1), (3, got_3)):
        rim = got[PART : PART + 32].astype(F32)
        above, below = adjacent(step)
        top, bottom = jnp.where(above, rim, 0.0), jnp.where(below, rim, 0.0)
        total[0:32] += top[:, :HALF]
        total[32:64] += top[:, HALF:]
        total[rows - 64 : rows - 32] += bottom[:, :HALF]
        total[rows - 32 : rows] += bottom[:, HALF:]
    strip = across[PART:].astype(F32)
    at = jnp.where(lax.axis_index("col") == 0, 30, 0)
    for j in range(2):
        spot = (pl.ds(at + j, 64, stride=32), slice(None))
        total[spot] = total[spot] + strip[:, j * HALF : (j + 1) * HALF]
    out[...] = total[...].astype(BF16).reshape(out.shape)


def lay(*refs):
    outs = refs[-2:]
    size, column = HALF // 8, lax.axis_index("col")
    for k, part in enumerate(refs[:-2]):
        place = (column if k < 4 else 1 - column) * 4 + partner("blk", k % 4, True)
        at = pl.multiple_of(place * size, size)
        value = part[:PART].astype(F32).reshape(2, 9, size, FULL)
        for out, grad in zip(outs, (0, 1)):
            out[:, pl.ds(at, size), :] = value[grad]


def swap(value, axis="ch"):
    return lax.ppermute(value, axis, [(0, 1), (1, 0)])


def flip(value, axis, step):
    size = lax.axis_size(axis)
    return lax.ppermute(value, axis, [(i, i ^ step) for i in range(size)])


def neighbours(axis):
    size = lax.axis_size(axis)
    up = [(i, (i + 1) % size) for i in range(size - 1)]
    return up, [(j, i) for i, j in up]


def shards(grad_out, saved_input, saved_pre, first_weight, second_weight, assignment):
    owners = lax.axis_size("blk")
    columns = lax.axis_size("col")
    capacity = max(2, TILE_BLOCKS // owners)
    wide = MIDDLE if (MIDDLE * capacity) % 16 == 0 else 16
    scale = 1.0 / math.sqrt(owners * columns * PER_WORKER * BLOCK * BLOCK)
    permuted = owners == 4 and columns == 2
    parts = owners if permuted else 1
    routing = assignment[0]
    shape = jax.ShapeDtypeStruct
    tables = [pltpu.SMEM((owners * capacity + 1,), I32)]
    counts = [pltpu.SMEM((owners,), I32)]

    def pieces(*dims):
        return [shape(dims, BF16)] * owners if permuted else [shape((owners,) + dims, BF16)]

    def exchange(values):
        if permuted:
            return [values[0]] + [flip(values[k], "blk", k) for k in (1, 2, 3)]
        return [lax.all_to_all(values[0], "blk", split_axis=0, concat_axis=0, tiled=True)]

    tie = lax.optimization_barrier
    tile = grad_out.reshape(TILE_ROWS, BLOCK, TILE_COLS * BLOCK, HALF)
    second_other, tile_other = swap(second_weight), swap(tile)
    outgoing = call(
        functools.partial(pack_cotangents, owners, capacity, permuted),
        pieces(BLOCK, BLOCK * capacity, HALF),
        [SMEM, VMEM], tables, (1, 1), "pack_cotangents",
    )(routing, tile)
    saved_slots = saved_pre[0, 0].transpose(1, 2, 0, 3)
    outgoing, saved_slots = tie((outgoing, saved_slots))
    incoming = exchange(outgoing)

    masked, *to_owners = call(
        functools.partial(pack_saved, owners, columns, capacity, wide, permuted),
        [shape((MIDDLE, MIDDLE * PER_WORKER, HALF), BF16)] + pieces(MIDDLE, wide * capacity, HALF),
        [SMEM, VMEM], counts + tables, (1, 1), "pack_saved",
    )(routing, saved_slots.reshape(MIDDLE, MIDDLE * PER_WORKER, HALF))
    masked = masked.reshape(MIDDLE, MIDDLE, PER_WORKER, HALF)
    incoming, to_owners, masked = tie((incoming, to_owners, masked))
    incoming_other = [swap(value) for value in incoming]
    masked_other = swap(masked)
    at_owner = exchange(to_owners)

    saved_tiles = saved_input[0, 0].transpose(1, 2, 0, 3)
    if permuted:
        halved = (2, 9, HALF // 2, FULL)
        halved = [shape(halved, F32), shape(halved, BF16)]
    else:
        halved = [shape((2, 9, HALF, FULL), F32)]
    terms = call(
        functools.partial(worker, scale, owners, capacity, permuted),
        halved,
        [SMEM] + [VMEM] * (2 * parts + 5),
        counts
        + [
            pltpu.VMEM((BLOCK, BLOCK * PER_WORKER, FULL), BF16),
            pltpu.VMEM((MIDDLE, MIDDLE, PER_WORKER, FULL), F32),
            pltpu.VMEM((MIDDLE, MIDDLE, PER_WORKER, FULL), BF16),
            pltpu.VMEM((9, FULL, FULL), BF16),
        ],
        (1, 1), "worker",
    )(
        routing, *incoming, *incoming_other, masked, masked_other, second_weight, second_other,
        saved_tiles,
    )

    if permuted:
        terms = list(terms)
        terms[1], at_owner[2] = tie((terms[1], at_owner[2]))
    at_owner, tile_here = tie((at_owner, tile))
    total = call(
        owner_spread,
        shape((MIDDLE, MIDDLE, TILE_BLOCKS, FULL), BF16),
        [VMEM] * 4,
        [
            pltpu.VMEM((MIDDLE, MIDDLE, TILE_BLOCKS, FULL), F32),
            pltpu.VMEM((BLOCK, FULL, FULL), BF16),
            pltpu.VMEM((9, FULL, FULL), BF16),
        ],
        (1, 1), "owner_spread",
    )(tile_here, tile_other, second_weight, second_other)

    def owner(at_owner):
        at_owner_other = [swap(value) for value in at_owner]
        return call(
            functools.partial(owner_canvas, owners, capacity, wide, permuted),
            [shape((HIGH, WIDE, HALF), F32)] + [shape((RIM, FULL), BF16)] * (2 if permuted else 0),
            [SMEM] + [VMEM] * (2 * parts + 2),
            tables
            + [
                pltpu.VMEM((MIDDLE, MIDDLE, TILE_BLOCKS, FULL), BF16),
                pltpu.VMEM((OUTER, OUTER, TILE_BLOCKS, HALF), F32),
            ],
            (1, 1), "owner_canvas",
        )(routing, *at_owner, *at_owner_other, total, first_weight)

    if permuted:
        part = (2, 9, HALF // 2 // owners, FULL)
        got = swap(terms[1], "col")
        total, got = tie((total, got))
        kept, *sends = call(
            add_columns, [shape(part, F32)] + [shape(part, BF16)] * (owners - 1),
            [VMEM] * 2, [], (1, 1), "add_columns",
        )(terms[0], got)
        sends, at_owner = tie((sends, at_owner))
        got = [flip(value, "blk", k + 1) for k, value in enumerate(sends)]
        canvas, *rims = owner(at_owner)
        message = shape((PART, FULL), BF16)
        wider = shape((PART + RIM, FULL), BF16)
        own, *wides = call(
            add_workers, [message, wider, wider], [VMEM] * 6, [], (1, 1), "add_workers",
        )(kept, *got, *rims)
        got = [flip(value, "blk", k) for k, value in ((1, wides[0]), (2, own), (3, wides[1]))]
        last = call(
            column_message, shape((PART + 64, FULL), BF16), [VMEM] * 3,
            [pltpu.VMEM((RIM, FULL), F32), pltpu.VMEM((64, HALF), F32)],
            (1, 1), "column_message",
        )(canvas.reshape(HIGH * WIDE, HALF), got[0], got[2])
        across = [swap(value, "col") for value in (own, got[0][:PART], got[1], last)]
        grad_in = call(
            close, shape(grad_out.shape, BF16), [VMEM] * 5,
            [pltpu.VMEM((TILE_ROWS * BLOCK * 32, HALF), F32)], (1, 1), "close",
        )(grad_out, canvas, got[0], got[2], across[3])
        grad_second, grad_first = call(
            lay, [shape((9, HALF, FULL), F32)] * 2, [VMEM] * 8, [], (1, 1), "lay",
        )(own, *got, *across)
        return (grad_in, grad_first, grad_second)

    grad_first, grad_second = lax.psum((terms[0][1], terms[0][0]), ("blk", "col"))
    [canvas] = owner(at_owner)
    up, down = neighbours("blk")
    from_above = lax.ppermute(canvas[HIGH - 2 :].astype(BF16), "blk", up).astype(F32)
    from_below = lax.ppermute(canvas[:2].astype(BF16), "blk", down).astype(F32)
    inner = canvas[2 : HIGH - 2]
    inner = inner.at[:2].add(from_above).at[-2:].add(from_below)
    up, down = neighbours("col")
    from_left = lax.ppermute(inner[:, 32:34].astype(BF16), "col", up).astype(F32)
    from_right = lax.ppermute(inner[:, 34:36].astype(BF16), "col", down).astype(F32)
    inner = inner[:, :32].at[:, :2].add(from_left).at[:, -2:].add(from_right)
    grad_in = (grad_out.astype(F32) + inner).astype(BF16)
    return (grad_in, grad_first, grad_second)


def solution(mesh):
    return jax.shard_map(
        shards,
        mesh=mesh,
        in_specs=(
            P(("groups", "blk"), "col", "ch"),
            P(("groups", "col"), "blk", None, None, None, "ch"),
            P(("groups", "col"), "blk", None, None, None, "ch"),
            P(None, "ch", None),
            P(None, "ch", None),
            P(("groups", "col"), None, None),
        ),
        out_specs=(
            P(("groups", "blk"), "col", "ch"),
            P("groups", "ch", None),
            P("groups", "ch", None),
        ),
        check_vma=False,
    )
```

```python
import functools
import math

import jax
import jax.numpy as jnp
from jax import lax
from jax.experimental import pallas as pl
from jax.experimental.pallas import tpu as pltpu
from jax.sharding import PartitionSpec as P

BLOCK = 8
TILE_ROWS = 8
TILE_COLS = 4
TILE_BLOCKS = 32
PER_WORKER = 16
MIDDLE = 10
OUTER = 12
HALF = 128
FULL = 256
DEAD = -4096
HIGH = 68
RIM = 48
PART = 288
WIDE = 40

BF16 = jnp.bfloat16
F32 = jnp.float32
I32 = jnp.int32

VMEM = pl.BlockSpec(memory_space=pltpu.VMEM)
HBM = pl.BlockSpec(memory_space=pltpu.HBM)
SMEM = pl.BlockSpec(memory_space=pltpu.SMEM)


def call(body, outs, specs, scratch, cost, name):
    return pl.pallas_call(
        body,
        out_shape=outs,
        in_specs=specs,
        out_specs=jax.tree.map(lambda _: VMEM, outs),
        scratch_shapes=scratch,
        compiler_params=pltpu.CompilerParams(vmem_limit_bytes=48 * 1024 * 1024),
        cost_estimate=pl.CostEstimate(flops=cost[0], bytes_accessed=cost[1], transcendentals=0),
        name=name,
    )


def iota(shape, dim):
    return lax.broadcasted_iota(I32, shape, dim)


def one_hot(hits):
    return jnp.where(hits, 1.0, 0.0).astype(BF16)


def dot(a, b):
    return jnp.dot(a, b, preferred_element_type=F32)


def dot_nt(a, b):
    return lax.dot_general(a, b, (((1,), (1,)), ((), ())), preferred_element_type=F32)


def dot_tn(a, b):
    return lax.dot_general(a, b, (((0,), (0,)), ((), ())), preferred_element_type=F32)


def owner_table(routing, table, owners, capacity):
    me = lax.axis_index("blk")

    def clear(number, carry):
        table[number] = DEAD
        return carry

    lax.fori_loop(0, owners * capacity, clear, 0)

    def worker(number, carry):
        count = jnp.int32(0)
        for slot in range(PER_WORKER):
            code = routing[number, slot]
            hit = (code // TILE_BLOCKS) == me
            table[jnp.where(hit, number * capacity + count, owners * capacity)] = code % TILE_BLOCKS
            count = count + jnp.where(hit, 1, 0)
        return carry

    lax.fori_loop(0, owners, worker, 0)


def worker_codes(routing, counts, owners):
    me = lax.axis_index("blk")

    def clear(number, carry):
        counts[number] = 0
        return carry

    lax.fori_loop(0, owners, clear, 0)
    slots = []
    for slot in range(PER_WORKER):
        code = routing[me, slot]
        owner = code // TILE_BLOCKS
        rank = counts[owner]
        counts[owner] = rank + 1
        slots.append((owner, code % TILE_BLOCKS, rank))
    return slots


def views(refs, count):
    return list(refs) if len(refs) == count else [refs[0].at[k] for k in range(count)]


def partner(axis, step, permuted):
    return step ^ lax.axis_index(axis) if permuted else step


def pack_cotangents(owners, capacity, permuted, routing, source, *refs):
    outs, (table, tile, arrived) = refs[:-3], refs[-3:]
    fetch = pltpu.make_async_copy(source, tile, arrived)
    fetch.start()
    owner_table(routing, table, owners, capacity)
    rows = BLOCK * capacity
    row, lane = iota((rows, FULL), 0), iota((rows, FULL), 1)
    picks = []
    for step in range(owners):
        worker = partner("blk", step, permuted)
        target = jnp.full((rows, FULL), DEAD, I32)
        for rank in range(capacity):
            place = table[worker * capacity + rank] * BLOCK
            target = jnp.where(row % capacity == rank, place, target)
        picks.append(one_hot(lane == target + row // capacity))
    pick = jnp.concatenate(picks, axis=0)
    fetch.wait()
    for u in range(0, BLOCK, 2):
        pair = [
            jnp.concatenate([tile[r, u + k] for r in range(TILE_ROWS)], axis=0) for k in range(2)
        ]
        moved = dot(pick, jnp.concatenate(pair, axis=1)).astype(BF16)
        for step, out in enumerate(views(outs, owners)):
            part = moved[step * rows : (step + 1) * rows]
            out[u] = part[:, :HALF]
            out[u + 1] = part[:, HALF:]


def pack_saved(owners, columns, capacity, wide, permuted, routing, saved, masked, *refs):
    outs, counts, table = refs[:-2], refs[-2], refs[-1]
    column = lax.axis_index("col")

    def clear(number, carry):
        table[number] = DEAD
        return carry

    lax.fori_loop(0, owners * capacity, clear, 0)
    slots = worker_codes(routing, counts, owners)
    rows = MIDDLE * PER_WORKER
    row = iota((rows, HALF), 0)
    flags = jnp.zeros((rows, HALF), I32)
    for slot, (owner, place, rank) in enumerate(slots):
        table[owner * capacity + rank] = slot
        block_row, block_col = place // TILE_COLS, place % TILE_COLS
        flag = (
            jnp.where((owner == 0) & (block_row == 0), 1, 0)
            + jnp.where((owner == owners - 1) & (block_row == TILE_ROWS - 1), 2, 0)
            + jnp.where((column == 0) & (block_col == 0), 4, 0)
            + jnp.where((column == columns - 1) & (block_col == TILE_COLS - 1), 8, 0)
        )
        flags = jnp.where(row % PER_WORKER == slot, flag, flags)
    across = row // PER_WORKER
    outside = (((flags & 4) != 0) & (across == 0)) | (((flags & 8) != 0) & (across == MIDDLE - 1))
    for m in range(MIDDLE):
        here = outside
        if m == 0:
            here = here | ((flags & 1) != 0)
        if m == MIDDLE - 1:
            here = here | ((flags & 2) != 0)
        masked[m] = jnp.where(here, 0.0, saved[m].astype(F32)).astype(BF16)
    size = wide * capacity
    row, lane = iota((size, FULL), 0), iota((size, FULL), 1)
    picks = []
    for step in range(owners):
        owner = partner("blk", step, permuted)
        target = jnp.full((size, FULL), DEAD, I32)
        for rank in range(capacity):
            target = jnp.where(row % capacity == rank, table[owner * capacity + rank], target)
        at = row // capacity
        picks.append(one_hot((lane == target + at * PER_WORKER) & (at < MIDDLE)))
    pick = jnp.concatenate(picks, axis=0)
    filler = jnp.zeros((FULL - rows, FULL), BF16)
    for m in range(0, MIDDLE, 2):
        pair = jnp.concatenate([masked[m], masked[m + 1]], axis=1)
        moved = dot(pick, jnp.concatenate([pair, filler], axis=0)).astype(BF16)
        for step, out in enumerate(views(outs, owners)):
            part = moved[step * size : (step + 1) * size]
            out[m] = part[:, :HALF]
            out[m + 1] = part[:, HALF:]


def ordered(own, other, axis):
    first = lax.axis_index("ch") == 0
    return jnp.concatenate(
        [jnp.where(first, own, other), jnp.where(first, other, own)], axis=axis
    )


def halves(value, keep, send, tap):
    low, high = value[: HALF // 2], value[HALF // 2 :]
    mine = lax.axis_index("col") == 0
    keep[tap] = jnp.where(mine, low, high)
    send[tap] = jnp.where(mine, high, low).astype(BF16)


def emit(value, outs, tap):
    if len(outs) == 2:
        halves(value, outs[0], outs[1], tap)
    else:
        outs[0][tap] = value


def second_gradient(scale, owners, capacity, permuted, routing, *refs):
    parts = 1 if not permuted else owners
    own, other = views(refs[:parts], owners), views(refs[parts : 2 * parts], owners)
    masked, cot = refs[2 * parts : 2 * parts + 2]
    outs, counts = refs[2 * parts + 2 : -1], refs[-1]
    slots = worker_codes(routing, counts, owners)
    rows, inner = BLOCK * PER_WORKER, owners * BLOCK * capacity
    row, lane = iota((rows, inner), 0), iota((rows, inner), 1)
    target = jnp.full((rows, inner), DEAD, I32)
    for slot, (owner, place, rank) in enumerate(slots):
        step = partner("blk", owner, permuted)
        target = jnp.where(row % PER_WORKER == slot, step * (BLOCK * capacity) + rank, target)
    pick = one_hot(lane == target + (row // PER_WORKER) * capacity)
    for u in range(BLOCK):
        got = jnp.concatenate(
            [ordered(own[o][u], other[o][u], 1) for o in range(owners)], axis=0
        )
        cot[u] = dot(pick, got).astype(BF16)
    grads = cot[...].reshape(BLOCK * rows, FULL)
    for tap in range(9):
        dy, dx = tap // 3, tap % 3
        window = masked[dy : dy + BLOCK, dx : dx + BLOCK].reshape(BLOCK * rows, HALF)
        window = jnp.maximum(window, jnp.zeros_like(window))
        emit(dot_tn(window, grads) * scale, outs, tap)


def first_gradient(
    scale, cot, masked, masked_other, weight, weight_other, saved, *refs
):
    outs, (total, pre, full) = refs[:-3], refs[-3:]
    rows = BLOCK * BLOCK * PER_WORKER
    full[...] = ordered(weight[...], weight_other[...], 1)
    total[...] = jnp.zeros_like(total)
    for tap in range(9):
        dy, dx = tap // 3, tap % 3
        part = dot_nt(cot[...].reshape(rows, FULL), full[tap])
        spot = (slice(dy, dy + BLOCK), slice(dx, dx + BLOCK))
        total[spot] = total[spot] + part.reshape(BLOCK, BLOCK, PER_WORKER, FULL)
    for m in range(MIDDLE):
        live = ordered(masked[m], masked_other[m], 2).astype(F32) > 0
        pre[m] = jnp.where(live, total[m], 0.0).astype(BF16)
    size = MIDDLE * MIDDLE * PER_WORKER
    grads = pre[...].reshape(size, FULL)
    for tap in range(9):
        dy, dx = tap // 3, tap % 3
        window = saved[dy : dy + MIDDLE, dx : dx + MIDDLE].reshape(size, HALF)
        emit(dot_tn(window, grads) * scale, outs, tap)


def owner_spread(tile, tile_other, second, second_other, out, total, cot, full):
    row, lane = iota((FULL, FULL), 0), iota((FULL, FULL), 1)
    turn = one_hot(lane == (row % TILE_BLOCKS) * BLOCK + row // TILE_BLOCKS)
    for u in range(BLOCK):
        block = jnp.concatenate(
            [ordered(tile[r, u], tile_other[r, u], 1) for r in range(TILE_ROWS)], axis=0
        )
        cot[u] = dot(turn, block).astype(BF16)
    full[...] = ordered(second[...], second_other[...], 1)
    rows = BLOCK * BLOCK * TILE_BLOCKS
    total[...] = jnp.zeros_like(total)
    for tap in range(9):
        dy, dx = tap // 3, tap % 3
        part = dot_nt(cot[...].reshape(rows, FULL), full[tap])
        spot = (slice(dy, dy + BLOCK), slice(dx, dx + BLOCK))
        total[spot] = total[spot] + part.reshape(BLOCK, BLOCK, TILE_BLOCKS, FULL)
    out[...] = total[...].astype(BF16)


def worker(scale, owners, capacity, permuted, routing, *refs):
    parts = 1 if not permuted else owners
    inputs, refs = refs[: 2 * parts], refs[2 * parts :]
    (masked, masked_other, weight, weight_other, source), refs = refs[:5], refs[5:]
    outs, (counts, cot, total, pre, full, saved, arrived) = refs[:-7], refs[-7:]
    fetch = pltpu.make_async_copy(source, saved, arrived)
    fetch.start()
    pairs = [[out.at[k] for out in outs] for k in range(2)]
    second_gradient(scale, owners, capacity, permuted, routing, *inputs, masked, cot, *pairs[0], counts)
    fetch.wait()
    first_gradient(
        scale, cot, masked, masked_other, weight, weight_other, saved, *pairs[1], total, pre, full
    )


def adjacent(step):
    me = lax.axis_index("blk")
    return (me ^ step) == me - 1, (me ^ step) == me + 1


def owner_canvas(owners, capacity, wide, permuted, routing, *refs):
    parts = 1 if not permuted else owners
    got, got_other = views(refs[:parts], owners), views(refs[parts : 2 * parts], owners)
    total, first, canvas = refs[2 * parts : 2 * parts + 3]
    rims, (table, pre, grown) = refs[2 * parts + 3 : -3], refs[-3:]
    owner_table(routing, table, owners, capacity)
    size, into = wide * capacity, MIDDLE * TILE_BLOCKS
    row, lane = iota((size, into), 0), iota((size, into), 1)
    picks = []
    for step in range(owners):
        worker = partner("blk", step, permuted)
        target = jnp.full((size, into), DEAD, I32)
        for rank in range(capacity):
            target = jnp.where(row % capacity == rank, table[worker * capacity + rank], target)
        at = row // capacity
        hits = (lane == target + at * TILE_BLOCKS) & (at < MIDDLE)
        picks.append(jnp.where(hits, 1.0, 0.0))
    pick = jnp.concatenate(picks, axis=0).T.astype(BF16)
    for m in range(MIDDLE):
        block = jnp.concatenate(
            [ordered(got[w][m], got_other[w][m], 1) for w in range(owners)], axis=0
        )
        live = dot(pick, block).reshape(MIDDLE, TILE_BLOCKS, FULL) > 0
        pre[m] = jnp.where(live, total[m].astype(F32), 0.0).astype(BF16)
    size = MIDDLE * MIDDLE * TILE_BLOCKS
    grown[...] = jnp.zeros_like(grown)
    for tap in range(9):
        dy, dx = tap // 3, tap % 3
        part = dot_nt(pre[...].reshape(size, FULL), first[tap])
        spot = (slice(dy, dy + MIDDLE), slice(dx, dx + MIDDLE))
        grown[spot] = grown[spot] + part.reshape(MIDDLE, MIDDLE, TILE_BLOCKS, HALF)
    height, depth = TILE_ROWS * WIDE, OUTER * TILE_BLOCKS
    row, lane = iota((height, depth), 0), iota((height, depth), 1)
    at_row, at_col = row // WIDE, row % WIDE
    n, place = lane // TILE_BLOCKS, lane % TILE_BLOCKS
    column = (place % TILE_COLS) * BLOCK + n - 2
    column = jnp.where(column < 0, column + 36, column)
    fold = one_hot((at_row == place // TILE_COLS) & (at_col == column))
    canvas[...] = jnp.zeros_like(canvas)
    for m in range(0, OUTER, 2):
        pair = jnp.concatenate(
            [grown[m + k].reshape(depth, HALF).astype(BF16) for k in range(2)], axis=1
        )
        laid = dot(fold, pair).reshape(TILE_ROWS, WIDE, FULL)
        for r in range(TILE_ROWS):
            for k in range(2):
                canvas[r * BLOCK + m + k] += laid[r, :, k * HALF : (k + 1) * HALF]
    for k, rim in enumerate(rims):
        above, below = adjacent(2 * k + 1)
        top = jnp.concatenate([canvas[0], canvas[1]], axis=1)
        bottom = jnp.concatenate([canvas[HIGH - 2], canvas[HIGH - 1]], axis=1)
        rim[:WIDE] = jnp.where(below, bottom, jnp.where(above, top, 0.0)).astype(BF16)
        rim[WIDE:] = jnp.zeros((RIM - WIDE, FULL), BF16)


def bit_of(axis, step):
    return (lax.axis_index(axis) // step) % 2


def add_columns(kept, got, *outs):
    size = HALF // 2 // len(outs)
    for step, out in enumerate(outs):
        at = pl.multiple_of(partner("blk", step, True) * size, size)
        part = kept[:, :, pl.ds(at, size), :] + got[:, :, pl.ds(at, size), :].astype(F32)
        out[...] = part if step == 0 else part.astype(BF16)


def add_workers(kept, got_3, got_2, got_1, rim_1, rim_3, out, out_1, out_3):
    value = kept[...]
    for part in (got_1, got_2, got_3):
        value = value + part[...].astype(F32)
    value = value.astype(BF16).reshape(PART, FULL)
    out[...] = value
    for message, rim in ((out_1, rim_1), (out_3, rim_3)):
        message[:PART] = value
        message[PART:] = rim[...]


def column_message(canvas, got_1, got_3, out, rim, strip):
    out[:PART] = got_3[:PART]
    for j in range(2):
        c = 32 + 2 * lax.axis_index("col") + j
        strip[...] = canvas[pl.ds(2 * WIDE + c, 64, stride=WIDE), :]
        for step, got in ((1, got_1), (3, got_3)):
            rim[...] = got[PART:].astype(F32)
            row = rim[pl.ds(c, 1), :]
            above, below = adjacent(step)
            top, bottom = jnp.where(above, row, 0.0), jnp.where(below, row, 0.0)
            strip[0:1] += top[:, :HALF]
            strip[1:2] += top[:, HALF:]
            strip[62:63] += bottom[:, :HALF]
            strip[63:64] += bottom[:, HALF:]
        out[PART:, j * HALF : (j + 1) * HALF] = strip[...].astype(BF16)


def close(tile, canvas, got_1, got_3, across, out, total):
    rows = TILE_ROWS * BLOCK * 32
    inner = canvas[2 : HIGH - 2, :32, :].reshape(rows, HALF)
    total[...] = tile[...].reshape(rows, HALF).astype(F32) + inner
    for step, got in ((1, got_1), (3, got_3)):
        rim = got[PART : PART + 32].astype(F32)
        above, below = adjacent(step)
        top, bottom = jnp.where(above, rim, 0.0), jnp.where(below, rim, 0.0)
        total[0:32] += top[:, :HALF]
        total[32:64] += top[:, HALF:]
        total[rows - 64 : rows - 32] += bottom[:, :HALF]
        total[rows - 32 : rows] += bottom[:, HALF:]
    strip = across[PART:].astype(F32)
    at = jnp.where(lax.axis_index("col") == 0, 30, 0)
    for j in range(2):
        spot = (pl.ds(at + j, 64, stride=32), slice(None))
        total[spot] = total[spot] + strip[:, j * HALF : (j + 1) * HALF]
    out[...] = total[...].astype(BF16).reshape(out.shape)


def lay(*refs):
    outs = refs[-2:]
    size, column = HALF // 8, lax.axis_index("col")
    for k, part in enumerate(refs[:-2]):
        place = (column if k < 4 else 1 - column) * 4 + partner("blk", k % 4, True)
        at = pl.multiple_of(place * size, size)
        value = part[:PART].astype(F32).reshape(2, 9, size, FULL)
        for out, grad in zip(outs, (0, 1)):
            out[:, pl.ds(at, size), :] = value[grad]


def swap(value, axis="ch"):
    return lax.ppermute(value, axis, [(0, 1), (1, 0)])


def flip(value, axis, step):
    size = lax.axis_size(axis)
    return lax.ppermute(value, axis, [(i, i ^ step) for i in range(size)])


def neighbours(axis):
    size = lax.axis_size(axis)
    up = [(i, (i + 1) % size) for i in range(size - 1)]
    return up, [(j, i) for i, j in up]


def shards(grad_out, saved_input, saved_pre, first_weight, second_weight, assignment):
    owners = lax.axis_size("blk")
    columns = lax.axis_size("col")
    capacity = max(2, TILE_BLOCKS // owners)
    wide = MIDDLE if (MIDDLE * capacity) % 16 == 0 else 16
    scale = 1.0 / math.sqrt(owners * columns * PER_WORKER * BLOCK * BLOCK)
    permuted = owners == 4 and columns == 2
    parts = owners if permuted else 1
    routing = assignment[0]
    shape = jax.ShapeDtypeStruct
    tables = [pltpu.SMEM((owners * capacity + 1,), I32)]
    counts = [pltpu.SMEM((owners,), I32)]

    def pieces(*dims):
        return [shape(dims, BF16)] * owners if permuted else [shape((owners,) + dims, BF16)]

    def exchange(values):
        if permuted:
            return list(values[:1]) + [flip(values[k], "blk", k) for k in (3, 2, 1)][::-1]
        return [lax.all_to_all(values[0], "blk", split_axis=0, concat_axis=0, tiled=True)]

    tie = lax.optimization_barrier
    tile = grad_out.reshape(TILE_ROWS, BLOCK, TILE_COLS * BLOCK, HALF)
    second_other, tile_other = swap(second_weight), swap(tile)
    outgoing = call(
        functools.partial(pack_cotangents, owners, capacity, permuted),
        pieces(BLOCK, BLOCK * capacity, HALF),
        [SMEM, HBM], tables + [pltpu.VMEM(tile.shape, BF16), pltpu.SemaphoreType.DMA],
        (1, 1), "pack_cotangents",
    )(routing, pltpu.with_memory_space_constraint(tile, pltpu.HBM))
    saved_slots = saved_pre[0, 0].transpose(1, 2, 0, 3)
    outgoing, saved_slots = tie((outgoing, saved_slots))
    incoming = exchange(outgoing)

    masked, *to_owners = call(
        functools.partial(pack_saved, owners, columns, capacity, wide, permuted),
        [shape((MIDDLE, MIDDLE * PER_WORKER, HALF), BF16)] + pieces(MIDDLE, wide * capacity, HALF),
        [SMEM, VMEM], counts + tables, (1, 1), "pack_saved",
    )(routing, saved_slots.reshape(MIDDLE, MIDDLE * PER_WORKER, HALF))
    masked = masked.reshape(MIDDLE, MIDDLE, PER_WORKER, HALF)
    incoming, to_owners, masked = tie((incoming[::-1], to_owners[::-1], masked))
    incoming, to_owners = incoming[::-1], to_owners[::-1]
    incoming_other = [swap(value) for value in incoming]
    masked_other = swap(masked)
    at_owner = exchange(to_owners)

    saved_tiles = saved_input[0, 0].transpose(1, 2, 0, 3)
    if permuted:
        halved = (2, 9, HALF // 2, FULL)
        halved = [shape(halved, F32), shape(halved, BF16)]
    else:
        halved = [shape((2, 9, HALF, FULL), F32)]
    terms = call(
        functools.partial(worker, scale, owners, capacity, permuted),
        halved,
        [SMEM] + [VMEM] * (2 * parts + 4) + [HBM],
        counts
        + [
            pltpu.VMEM((BLOCK, BLOCK * PER_WORKER, FULL), BF16),
            pltpu.VMEM((MIDDLE, MIDDLE, PER_WORKER, FULL), F32),
            pltpu.VMEM((MIDDLE, MIDDLE, PER_WORKER, FULL), BF16),
            pltpu.VMEM((9, FULL, FULL), BF16),
            pltpu.VMEM(saved_tiles.shape, BF16),
            pltpu.SemaphoreType.DMA,
        ],
        (1, 1), "worker",
    )(
        routing, *incoming, *incoming_other, masked, masked_other, second_weight, second_other,
        pltpu.with_memory_space_constraint(saved_tiles, pltpu.HBM),
    )

    if permuted:
        terms = list(terms)
        terms[1], at_owner[2] = tie((terms[1], at_owner[2]))
    terms, tile_here = tie((terms, tile))
    total = call(
        owner_spread,
        shape((MIDDLE, MIDDLE, TILE_BLOCKS, FULL), BF16),
        [VMEM] * 4,
        [
            pltpu.VMEM((MIDDLE, MIDDLE, TILE_BLOCKS, FULL), F32),
            pltpu.VMEM((BLOCK, FULL, FULL), BF16),
            pltpu.VMEM((9, FULL, FULL), BF16),
        ],
        (1, 1), "owner_spread",
    )(tile_here, tile_other, second_weight, second_other)

    def owner(at_owner):
        at_owner_other = [swap(value) for value in at_owner]
        return call(
            functools.partial(owner_canvas, owners, capacity, wide, permuted),
            [shape((HIGH, WIDE, HALF), F32)] + [shape((RIM, FULL), BF16)] * (2 if permuted else 0),
            [SMEM] + [VMEM] * (2 * parts + 2),
            tables
            + [
                pltpu.VMEM((MIDDLE, MIDDLE, TILE_BLOCKS, FULL), BF16),
                pltpu.VMEM((OUTER, OUTER, TILE_BLOCKS, HALF), F32),
            ],
            (1, 1), "owner_canvas",
        )(routing, *at_owner, *at_owner_other, total, first_weight)

    if permuted:
        part = (2, 9, HALF // 2 // owners, FULL)
        got = swap(terms[1], "col")
        total, got, at_owner = tie((total, got, at_owner))
        kept, *sends = call(
            add_columns, [shape(part, F32)] + [shape(part, BF16)] * (owners - 1),
            [VMEM] * 2, [], (1, 1), "add_columns",
        )(terms[0], got)
        sends, at_owner = tie((sends, at_owner))
        got = [flip(sends[k - 1], "blk", k) for k in (3, 2, 1)]
        canvas, *rims = owner(at_owner)
        message = shape((PART, FULL), BF16)
        wider = shape((PART + RIM, FULL), BF16)
        own, *wides = call(
            add_workers, [message, wider, wider], [VMEM] * 6, [], (1, 1), "add_workers",
        )(kept, *got, *rims)
        got = [flip(value, "blk", k) for k, value in ((3, wides[1]), (2, own), (1, wides[0]))][::-1]
        across = [swap(own, "col"), swap(got[0][:PART], "col")]
        got, across = tie((got[::-1], across))
        got = got[::-1]
        last = call(
            column_message, shape((PART + 64, FULL), BF16), [VMEM] * 3,
            [pltpu.VMEM((RIM, FULL), F32), pltpu.VMEM((64, HALF), F32)],
            (1, 1), "column_message",
        )(canvas.reshape(HIGH * WIDE, HALF), got[0], got[2])
        across += [swap(got[1], "col"), swap(last, "col")]
        grad_in = call(
            close, shape(grad_out.shape, BF16), [VMEM] * 5,
            [pltpu.VMEM((TILE_ROWS * BLOCK * 32, HALF), F32)], (1, 1), "close",
        )(grad_out, canvas, got[0], got[2], across[3])
        grad_second, grad_first = call(
            lay, [shape((9, HALF, FULL), F32)] * 2, [VMEM] * 8, [], (1, 1), "lay",
        )(own, *got, *across)
        return (grad_in, grad_first, grad_second)

    grad_first, grad_second = lax.psum((terms[0][1], terms[0][0]), ("blk", "col"))
    [canvas] = owner(at_owner)
    up, down = neighbours("blk")
    from_above = lax.ppermute(canvas[HIGH - 2 :].astype(BF16), "blk", up).astype(F32)
    from_below = lax.ppermute(canvas[:2].astype(BF16), "blk", down).astype(F32)
    inner = canvas[2 : HIGH - 2]
    inner = inner.at[:2].add(from_above).at[-2:].add(from_below)
    up, down = neighbours("col")
    from_left = lax.ppermute(inner[:, 32:34].astype(BF16), "col", up).astype(F32)
    from_right = lax.ppermute(inner[:, 34:36].astype(BF16), "col", down).astype(F32)
    inner = inner[:, :32].at[:, :2].add(from_left).at[:, -2:].add(from_right)
    grad_in = (grad_out.astype(F32) + inner).astype(BF16)
    return (grad_in, grad_first, grad_second)


def solution(mesh):
    return jax.shard_map(
        shards,
        mesh=mesh,
        in_specs=(
            P(("groups", "blk"), "col", "ch"),
            P(("groups", "col"), "blk", None, None, None, "ch"),
            P(("groups", "col"), "blk", None, None, None, "ch"),
            P(None, "ch", None),
            P(None, "ch", None),
            P(("groups", "col"), None, None),
        ),
        out_specs=(
            P(("groups", "blk"), "col", "ch"),
            P("groups", "ch", None),
            P("groups", "ch", None),
        ),
        check_vma=False,
    )
```

```python
import functools
import math

import jax
import jax.numpy as jnp
from jax import lax
from jax.experimental import pallas as pl
from jax.experimental.pallas import tpu as pltpu
from jax.sharding import PartitionSpec as P

BLOCK = 8
TILE_ROWS = 8
TILE_COLS = 4
TILE_BLOCKS = 32
PER_WORKER = 16
MIDDLE = 10
OUTER = 12
HALF = 128
FULL = 256
DEAD = -4096
HIGH = 68
RIM = 48
FIRST = 4
ROWS = 16
PART = 288
WIDE = 40

BF16 = jnp.bfloat16
F32 = jnp.float32
I32 = jnp.int32

VMEM = pl.BlockSpec(memory_space=pltpu.VMEM)
HBM = pl.BlockSpec(memory_space=pltpu.HBM)
SMEM = pl.BlockSpec(memory_space=pltpu.SMEM)


def call(body, outs, specs, scratch, cost, name):
    return pl.pallas_call(
        body,
        out_shape=outs,
        in_specs=specs,
        out_specs=jax.tree.map(lambda _: VMEM, outs),
        scratch_shapes=scratch,
        compiler_params=pltpu.CompilerParams(vmem_limit_bytes=48 * 1024 * 1024),
        cost_estimate=pl.CostEstimate(flops=cost[0], bytes_accessed=cost[1], transcendentals=0),
        name=name,
    )


def iota(shape, dim):
    return lax.broadcasted_iota(I32, shape, dim)


def one_hot(hits):
    return jnp.where(hits, 1.0, 0.0).astype(BF16)


def dot(a, b):
    return jnp.dot(a, b, preferred_element_type=F32)


def dot_nt(a, b):
    return lax.dot_general(a, b, (((1,), (1,)), ((), ())), preferred_element_type=F32)


def dot_tn(a, b):
    return lax.dot_general(a, b, (((0,), (0,)), ((), ())), preferred_element_type=F32)


def owner_table(routing, table, owners, capacity):
    me = lax.axis_index("blk")

    def clear(number, carry):
        table[number] = DEAD
        return carry

    lax.fori_loop(0, owners * capacity, clear, 0)

    def worker(number, carry):
        count = jnp.int32(0)
        for slot in range(PER_WORKER):
            code = routing[number, slot]
            hit = (code // TILE_BLOCKS) == me
            table[jnp.where(hit, number * capacity + count, owners * capacity)] = code % TILE_BLOCKS
            count = count + jnp.where(hit, 1, 0)
        return carry

    lax.fori_loop(0, owners, worker, 0)


def worker_codes(routing, counts, owners):
    me = lax.axis_index("blk")

    def clear(number, carry):
        counts[number] = 0
        return carry

    lax.fori_loop(0, owners, clear, 0)
    slots = []
    for slot in range(PER_WORKER):
        code = routing[me, slot]
        owner = code // TILE_BLOCKS
        rank = counts[owner]
        counts[owner] = rank + 1
        slots.append((owner, code % TILE_BLOCKS, rank))
    return slots


def views(refs, count):
    return list(refs) if len(refs) == count else [refs[0].at[k] for k in range(count)]


def rows_of(refs, count):
    if len(refs) == count + 1:
        return [[ref.at[m] for m in range(MIDDLE)] for ref in refs[:-2]] + [
            [ref.at[m] for ref in refs[-2:] for m in range(ref.shape[0])]
        ]
    return [[ref.at[m] for m in range(MIDDLE)] for ref in views(refs, count)]


def partner(axis, step, permuted):
    return step ^ lax.axis_index(axis) if permuted else step


def pack_cotangents(owners, capacity, permuted, routing, source, *refs):
    outs, (table, tile, arrived) = refs[:-3], refs[-3:]
    fetch = pltpu.make_async_copy(source, tile, arrived)
    fetch.start()
    owner_table(routing, table, owners, capacity)
    rows = BLOCK * capacity
    row, lane = iota((rows, FULL), 0), iota((rows, FULL), 1)
    picks = []
    for step in range(owners):
        worker = partner("blk", step, permuted)
        target = jnp.full((rows, FULL), DEAD, I32)
        for rank in range(capacity):
            place = table[worker * capacity + rank] * BLOCK
            target = jnp.where(row % capacity == rank, place, target)
        picks.append(one_hot(lane == target + row // capacity))
    pick = jnp.concatenate(picks, axis=0)
    fetch.wait()
    for u in range(0, BLOCK, 2):
        pair = [
            jnp.concatenate([tile[r, u + k] for r in range(TILE_ROWS)], axis=0) for k in range(2)
        ]
        moved = dot(pick, jnp.concatenate(pair, axis=1)).astype(BF16)
        for step, out in enumerate(views(outs, owners)):
            part = moved[step * rows : (step + 1) * rows]
            out[u] = part[:, :HALF]
            out[u + 1] = part[:, HALF:]


def pack_saved(owners, columns, capacity, wide, permuted, routing, saved, masked, *refs):
    outs, counts, table = refs[:-2], refs[-2], refs[-1]
    column = lax.axis_index("col")

    def clear(number, carry):
        table[number] = DEAD
        return carry

    lax.fori_loop(0, owners * capacity, clear, 0)
    slots = worker_codes(routing, counts, owners)
    rows = MIDDLE * PER_WORKER
    row = iota((rows, HALF), 0)
    flags = jnp.zeros((rows, HALF), I32)
    for slot, (owner, place, rank) in enumerate(slots):
        table[owner * capacity + rank] = slot
        block_row, block_col = place // TILE_COLS, place % TILE_COLS
        flag = (
            jnp.where((owner == 0) & (block_row == 0), 1, 0)
            + jnp.where((owner == owners - 1) & (block_row == TILE_ROWS - 1), 2, 0)
            + jnp.where((column == 0) & (block_col == 0), 4, 0)
            + jnp.where((column == columns - 1) & (block_col == TILE_COLS - 1), 8, 0)
        )
        flags = jnp.where(row % PER_WORKER == slot, flag, flags)
    across = row // PER_WORKER
    outside = (((flags & 4) != 0) & (across == 0)) | (((flags & 8) != 0) & (across == MIDDLE - 1))
    for m in range(MIDDLE):
        here = outside
        if m == 0:
            here = here | ((flags & 1) != 0)
        if m == MIDDLE - 1:
            here = here | ((flags & 2) != 0)
        masked[m] = jnp.where(here, 0.0, saved[m].astype(F32)).astype(BF16)
    size = wide * capacity
    row, lane = iota((size, FULL), 0), iota((size, FULL), 1)
    picks = []
    for step in range(owners):
        owner = partner("blk", step, permuted)
        target = jnp.full((size, FULL), DEAD, I32)
        for rank in range(capacity):
            target = jnp.where(row % capacity == rank, table[owner * capacity + rank], target)
        at = row // capacity
        picks.append(one_hot((lane == target + at * PER_WORKER) & (at < MIDDLE)))
    pick = jnp.concatenate(picks, axis=0)
    filler = jnp.zeros((FULL - rows, FULL), BF16)
    for m in range(0, MIDDLE, 2):
        pair = jnp.concatenate([masked[m], masked[m + 1]], axis=1)
        moved = dot(pick, jnp.concatenate([pair, filler], axis=0)).astype(BF16)
        for step, out in enumerate(rows_of(outs, owners)):
            part = moved[step * size : (step + 1) * size]
            out[m][...] = part[:, :HALF]
            out[m + 1][...] = part[:, HALF:]


def ordered(own, other, axis):
    first = lax.axis_index("ch") == 0
    return jnp.concatenate(
        [jnp.where(first, own, other), jnp.where(first, other, own)], axis=axis
    )


def deal(value, kept, sent, grad, tap):
    low, high = value[: HALF // 2], value[HALF // 2 :]
    mine = lax.axis_index("col") == 0
    keep, send = jnp.where(mine, low, high), jnp.where(mine, high, low).astype(BF16)
    for k in range(4):
        step, rows = partner("blk", k, True), slice(k * ROWS, (k + 1) * ROWS)
        kept[step, grad, tap] = keep[rows]
        sent[step, grad, tap] = send[rows]


def emit(value, outs, grad, tap):
    if len(outs) == 2:
        deal(value, outs[0], outs[1], grad, tap)
    else:
        outs[0][grad, tap] = value


def second_gradient(scale, owners, capacity, permuted, routing, *refs):
    parts = 1 if not permuted else owners
    own, other = views(refs[:parts], owners), views(refs[parts : 2 * parts], owners)
    masked, cot = refs[2 * parts : 2 * parts + 2]
    outs, counts = refs[2 * parts + 2 : -1], refs[-1]
    slots = worker_codes(routing, counts, owners)
    rows, inner = BLOCK * PER_WORKER, owners * BLOCK * capacity
    row, lane = iota((rows, inner), 0), iota((rows, inner), 1)
    target = jnp.full((rows, inner), DEAD, I32)
    for slot, (owner, place, rank) in enumerate(slots):
        step = partner("blk", owner, permuted)
        target = jnp.where(row % PER_WORKER == slot, step * (BLOCK * capacity) + rank, target)
    pick = one_hot(lane == target + (row // PER_WORKER) * capacity)
    for u in range(BLOCK):
        got = jnp.concatenate(
            [ordered(own[o][u], other[o][u], 1) for o in range(owners)], axis=0
        )
        cot[u] = dot(pick, got).astype(BF16)
    grads = cot[...].reshape(BLOCK * rows, FULL)
    for tap in range(9):
        dy, dx = tap // 3, tap % 3
        window = masked[dy : dy + BLOCK, dx : dx + BLOCK].reshape(BLOCK * rows, HALF)
        window = jnp.maximum(window, jnp.zeros_like(window))
        emit(dot_tn(window, grads) * scale, outs, 0, tap)


def first_gradient(
    scale, cot, masked, masked_other, weight, weight_other, saved, *refs
):
    outs, (total, pre, full) = refs[:-3], refs[-3:]
    rows = BLOCK * BLOCK * PER_WORKER
    full[...] = ordered(weight[...], weight_other[...], 1)
    total[...] = jnp.zeros_like(total)
    for tap in range(9):
        dy, dx = tap // 3, tap % 3
        part = dot_nt(cot[...].reshape(rows, FULL), full[tap])
        spot = (slice(dy, dy + BLOCK), slice(dx, dx + BLOCK))
        total[spot] = total[spot] + part.reshape(BLOCK, BLOCK, PER_WORKER, FULL)
    for m in range(MIDDLE):
        live = ordered(masked[m], masked_other[m], 2).astype(F32) > 0
        pre[m] = jnp.where(live, total[m], 0.0).astype(BF16)
    size = MIDDLE * MIDDLE * PER_WORKER
    grads = pre[...].reshape(size, FULL)
    for tap in range(9):
        dy, dx = tap // 3, tap % 3
        window = saved[dy : dy + MIDDLE, dx : dx + MIDDLE].reshape(size, HALF)
        emit(dot_tn(window, grads) * scale, outs, 1, tap)


def owner_spread(tile, tile_other, second, second_other, out, total, cot, full):
    row, lane = iota((FULL, FULL), 0), iota((FULL, FULL), 1)
    turn = one_hot(lane == (row % TILE_BLOCKS) * BLOCK + row // TILE_BLOCKS)
    for u in range(BLOCK):
        block = jnp.concatenate(
            [ordered(tile[r, u], tile_other[r, u], 1) for r in range(TILE_ROWS)], axis=0
        )
        cot[u] = dot(turn, block).astype(BF16)
    full[...] = ordered(second[...], second_other[...], 1)
    rows = BLOCK * BLOCK * TILE_BLOCKS
    total[...] = jnp.zeros_like(total)
    for tap in range(9):
        dy, dx = tap // 3, tap % 3
        part = dot_nt(cot[...].reshape(rows, FULL), full[tap])
        spot = (slice(dy, dy + BLOCK), slice(dx, dx + BLOCK))
        total[spot] = total[spot] + part.reshape(BLOCK, BLOCK, TILE_BLOCKS, FULL)
    out[...] = total[...].astype(BF16)


def worker(scale, owners, capacity, permuted, routing, *refs):
    parts = 1 if not permuted else owners
    inputs, refs = refs[: 2 * parts], refs[2 * parts :]
    (masked, masked_other, weight, weight_other, source), refs = refs[:5], refs[5:]
    if permuted:
        refs, sent = refs[:-1], refs[-1]
    outs, (counts, cot, total, pre, full, saved, arrived) = refs[:-7], refs[-7:]
    if permuted:
        kept, near, far = outs
        outs = (kept, sent)
    fetch = pltpu.make_async_copy(source, saved, arrived)
    fetch.start()
    second_gradient(scale, owners, capacity, permuted, routing, *inputs, masked, cot, *outs, counts)
    fetch.wait()
    first_gradient(
        scale, cot, masked, masked_other, weight, weight_other, saved, *outs, total, pre, full
    )
    if permuted:
        for k in range(2):
            near[k] = sent[2 * k]
            far[k] = sent[2 * k + 1]


def adjacent(step):
    me = lax.axis_index("blk")
    return (me ^ step) == me - 1, (me ^ step) == me + 1


def owner_canvas(owners, capacity, wide, permuted, routing, *refs):
    parts = 1 if not permuted else owners + 1
    got, got_other = rows_of(refs[:parts], owners), rows_of(refs[parts : 2 * parts], owners)
    total, first, canvas = refs[2 * parts : 2 * parts + 3]
    rims, (table, pre, grown) = refs[2 * parts + 3 : -3], refs[-3:]
    owner_table(routing, table, owners, capacity)
    size, into = wide * capacity, MIDDLE * TILE_BLOCKS
    row, lane = iota((size, into), 0), iota((size, into), 1)
    picks = []
    for step in range(owners):
        worker = partner("blk", step, permuted)
        target = jnp.full((size, into), DEAD, I32)
        for rank in range(capacity):
            target = jnp.where(row % capacity == rank, table[worker * capacity + rank], target)
        at = row // capacity
        hits = (lane == target + at * TILE_BLOCKS) & (at < MIDDLE)
        picks.append(jnp.where(hits, 1.0, 0.0))
    pick = jnp.concatenate(picks, axis=0).T.astype(BF16)
    for m in range(MIDDLE):
        block = jnp.concatenate(
            [ordered(got[w][m][...], got_other[w][m][...], 1) for w in range(owners)], axis=0
        )
        live = dot(pick, block).reshape(MIDDLE, TILE_BLOCKS, FULL) > 0
        pre[m] = jnp.where(live, total[m].astype(F32), 0.0).astype(BF16)
    size = MIDDLE * MIDDLE * TILE_BLOCKS
    grown[...] = jnp.zeros_like(grown)
    for tap in range(0, 9, 2):
        taps = range(tap, min(tap + 2, 9))
        weight = jnp.concatenate([first[k] for k in taps], axis=0)
        part = dot_nt(pre[...].reshape(size, FULL), weight)
        for k in taps:
            dy, dx = k // 3, k % 3
            spot = (slice(dy, dy + MIDDLE), slice(dx, dx + MIDDLE))
            here = part[:, (k - tap) * HALF : (k - tap + 1) * HALF]
            grown[spot] = grown[spot] + here.reshape(MIDDLE, MIDDLE, TILE_BLOCKS, HALF)
    height, depth = TILE_ROWS * WIDE, OUTER * TILE_BLOCKS
    row, lane = iota((height, depth), 0), iota((height, depth), 1)
    at_row, at_col = row // WIDE, row % WIDE
    n, place = lane // TILE_BLOCKS, lane % TILE_BLOCKS
    column = (place % TILE_COLS) * BLOCK + n - 2
    column = jnp.where(column < 0, column + 36, column)
    fold = one_hot((at_row == place // TILE_COLS) & (at_col == column))
    canvas[...] = jnp.zeros_like(canvas)
    for m in range(0, OUTER, 2):
        pair = jnp.concatenate(
            [grown[m + k].reshape(depth, HALF).astype(BF16) for k in range(2)], axis=1
        )
        laid = dot(fold, pair).reshape(TILE_ROWS, WIDE, FULL)
        for r in range(TILE_ROWS):
            for k in range(2):
                canvas[r * BLOCK + m + k] += laid[r, :, k * HALF : (k + 1) * HALF]
    for k, rim in enumerate(rims):
        above, below = adjacent(2 * k + 1)
        top = jnp.concatenate([canvas[0], canvas[1]], axis=1)
        bottom = jnp.concatenate([canvas[HIGH - 2], canvas[HIGH - 1]], axis=1)
        rim[:WIDE] = jnp.where(below, bottom, jnp.where(above, top, 0.0)).astype(BF16)
        rim[WIDE:] = jnp.zeros((RIM - WIDE, FULL), BF16)


def add_far(kept, got, out):
    for k in range(2):
        out[k] = (kept[2 * k + 1] + got[k].astype(F32)).astype(BF16)


def add_near(kept, got, passed, keep, send):
    for k, out in enumerate((keep, send)):
        value = kept[2 * k] + got[k].astype(F32) + passed[k].astype(F32)
        out[...] = value.astype(out.dtype)


def add_workers(kept, got, rim_1, rim_3, out, out_1, out_3):
    value = (kept[...] + got[...].astype(F32)).astype(BF16).reshape(PART, FULL)
    out[...] = value
    for message, rim in ((out_1, rim_1), (out_3, rim_3)):
        message[:PART] = value
        message[PART:] = rim[...]


def column_message(canvas, got_1, got_3, out, rim, strip):
    out[:PART] = got_3[:PART]
    for j in range(2):
        c = 32 + 2 * lax.axis_index("col") + j
        strip[...] = canvas[pl.ds(2 * WIDE + c, 64, stride=WIDE), :]
        for step, got in ((1, got_1), (3, got_3)):
            rim[...] = got[PART:].astype(F32)
            row = rim[pl.ds(c, 1), :]
            above, below = adjacent(step)
            top, bottom = jnp.where(above, row, 0.0), jnp.where(below, row, 0.0)
            strip[0:1] += top[:, :HALF]
            strip[1:2] += top[:, HALF:]
            strip[62:63] += bottom[:, :HALF]
            strip[63:64] += bottom[:, HALF:]
        out[PART:, j * HALF : (j + 1) * HALF] = strip[...].astype(BF16)


def close(tile, canvas, got_1, got_3, across, out, total):
    rows = TILE_ROWS * BLOCK * 32
    inner = canvas[2 : HIGH - 2, :32, :].reshape(rows, HALF)
    total[...] = tile[...].reshape(rows, HALF).astype(F32) + inner
    for step, got in ((1, got_1), (3, got_3)):
        rim = got[PART : PART + 32].astype(F32)
        above, below = adjacent(step)
        top, bottom = jnp.where(above, rim, 0.0), jnp.where(below, rim, 0.0)
        total[0:32] += top[:, :HALF]
        total[32:64] += top[:, HALF:]
        total[rows - 64 : rows - 32] += bottom[:, :HALF]
        total[rows - 32 : rows] += bottom[:, HALF:]
    strip = across[PART:].astype(F32)
    at = jnp.where(lax.axis_index("col") == 0, 30, 0)
    for j in range(2):
        spot = (pl.ds(at + j, 64, stride=32), slice(None))
        total[spot] = total[spot] + strip[:, j * HALF : (j + 1) * HALF]
    out[...] = total[...].astype(BF16).reshape(out.shape)


def lay(*refs):
    outs = refs[-2:]
    size, column = HALF // 8, lax.axis_index("col")
    for k, part in enumerate(refs[:-2]):
        place = (column if k < 4 else 1 - column) * 4 + partner("blk", k % 4, True)
        at = pl.multiple_of(place * size, size)
        value = part[:PART].astype(F32).reshape(2, 9, size, FULL)
        for out, grad in zip(outs, (0, 1)):
            out[:, pl.ds(at, size), :] = value[grad]


def swap(value, axis="ch"):
    return lax.ppermute(value, axis, [(0, 1), (1, 0)])


def flip(value, axis, step):
    size = lax.axis_size(axis)
    return lax.ppermute(value, axis, [(i, i ^ step) for i in range(size)])


def neighbours(axis):
    size = lax.axis_size(axis)
    up = [(i, (i + 1) % size) for i in range(size - 1)]
    return up, [(j, i) for i, j in up]


def shards(grad_out, saved_input, saved_pre, first_weight, second_weight, assignment):
    owners = lax.axis_size("blk")
    columns = lax.axis_size("col")
    capacity = max(2, TILE_BLOCKS // owners)
    wide = MIDDLE if (MIDDLE * capacity) % 16 == 0 else 16
    scale = 1.0 / math.sqrt(owners * columns * PER_WORKER * BLOCK * BLOCK)
    permuted = owners == 4 and columns == 2
    parts = owners if permuted else 1
    routing = assignment[0]
    shape = jax.ShapeDtypeStruct
    tables = [pltpu.SMEM((owners * capacity + 1,), I32)]
    counts = [pltpu.SMEM((owners,), I32)]

    def pieces(*dims):
        return [shape(dims, BF16)] * owners if permuted else [shape((owners,) + dims, BF16)]

    def exchange(values):
        if permuted:
            return list(values[:1]) + [flip(values[k], "blk", k) for k in (3, 2, 1)][::-1]
        return [lax.all_to_all(values[0], "blk", split_axis=0, concat_axis=0, tiled=True)]

    tie = lax.optimization_barrier
    tile = grad_out.reshape(TILE_ROWS, BLOCK, TILE_COLS * BLOCK, HALF)
    second_other, tile_other = swap(second_weight), swap(tile)
    outgoing = call(
        functools.partial(pack_cotangents, owners, capacity, permuted),
        pieces(BLOCK, BLOCK * capacity, HALF),
        [SMEM, HBM], tables + [pltpu.VMEM(tile.shape, BF16), pltpu.SemaphoreType.DMA],
        (1, 1), "pack_cotangents",
    )(routing, pltpu.with_memory_space_constraint(tile, pltpu.HBM))
    saved_slots = saved_pre[0, 0].transpose(1, 2, 0, 3)
    outgoing, saved_slots = tie((outgoing, saved_slots))
    incoming = exchange(outgoing)

    saved_pieces = pieces(MIDDLE, wide * capacity, HALF)
    if permuted:
        saved_pieces[3:] = [shape((m, wide * capacity, HALF), BF16) for m in (FIRST, MIDDLE - FIRST)]
    masked, *to_owners = call(
        functools.partial(pack_saved, owners, columns, capacity, wide, permuted),
        [shape((MIDDLE, MIDDLE * PER_WORKER, HALF), BF16)] + saved_pieces,
        [SMEM, VMEM], counts + tables, (1, 1), "pack_saved",
    )(routing, saved_slots.reshape(MIDDLE, MIDDLE * PER_WORKER, HALF))
    masked = masked.reshape(MIDDLE, MIDDLE, PER_WORKER, HALF)
    incoming, to_owners, masked = tie((incoming[::-1], to_owners[::-1], masked))
    incoming, to_owners = incoming[::-1], to_owners[::-1]
    incoming_other = [swap(value) for value in incoming]
    masked_other = swap(masked)
    if permuted:
        at_owner = list(to_owners[:1])
        at_owner += [flip(value, "blk", k) for k, value in zip((1, 2, 3, 3), to_owners[1:])]
    else:
        at_owner = exchange(to_owners)

    saved_tiles = saved_input[0, 0].transpose(1, 2, 0, 3)
    if permuted:
        part = (2, 9, ROWS, FULL)
        halved = [shape((4,) + part, F32)] + [shape((2,) + part, BF16)] * 2
    else:
        halved = [shape((2, 9, HALF, FULL), F32)]
    terms = call(
        functools.partial(worker, scale, owners, capacity, permuted),
        halved,
        [SMEM] + [VMEM] * (2 * parts + 4) + [HBM],
        counts
        + [
            pltpu.VMEM((BLOCK, BLOCK * PER_WORKER, FULL), BF16),
            pltpu.VMEM((MIDDLE, MIDDLE, PER_WORKER, FULL), F32),
            pltpu.VMEM((MIDDLE, MIDDLE, PER_WORKER, FULL), BF16),
            pltpu.VMEM((9, FULL, FULL), BF16),
            pltpu.VMEM(saved_tiles.shape, BF16),
            pltpu.SemaphoreType.DMA,
        ]
        + ([pltpu.VMEM((4,) + part, BF16)] if permuted else []),
        (1, 1), "worker",
    )(
        routing, *incoming, *incoming_other, masked, masked_other, second_weight, second_other,
        pltpu.with_memory_space_constraint(saved_tiles, pltpu.HBM),
    )

    if permuted:
        kept, near, far = terms
        far, at_owner[2] = tie((far, at_owner[2]))
        kept, far, tile_here = tie((kept, far, tile))
    else:
        terms, tile_here = tie((terms, tile))
    total = call(
        owner_spread,
        shape((MIDDLE, MIDDLE, TILE_BLOCKS, FULL), BF16),
        [VMEM] * 4,
        [
            pltpu.VMEM((MIDDLE, MIDDLE, TILE_BLOCKS, FULL), F32),
            pltpu.VMEM((BLOCK, FULL, FULL), BF16),
            pltpu.VMEM((9, FULL, FULL), BF16),
        ],
        (1, 1), "owner_spread",
    )(tile_here, tile_other, second_weight, second_other)

    def owner(at_owner):
        at_owner_other = [swap(value) for value in at_owner]
        return call(
            functools.partial(owner_canvas, owners, capacity, wide, permuted),
            [shape((HIGH, WIDE, HALF), F32)] + [shape((RIM, FULL), BF16)] * (2 if permuted else 0),
            [SMEM] + [VMEM] * (2 * len(at_owner) + 2),
            tables
            + [
                pltpu.VMEM((MIDDLE, MIDDLE, TILE_BLOCKS, FULL), BF16),
                pltpu.VMEM((OUTER, OUTER, TILE_BLOCKS, HALF), F32),
            ],
            (1, 1), "owner_canvas",
        )(routing, *at_owner, *at_owner_other, total, first_weight)

    if permuted:
        far_got = swap(far, "col")
        total, far_got = tie((total, far_got))
        [passed] = call(add_far, [shape((2,) + part, BF16)], [VMEM] * 2, [], (1, 1), "add_far")(
            kept, far_got
        )
        near, at_owner[1], at_owner[3], _ = tie((near, at_owner[1], at_owner[3], passed))
        near_got, passed = swap(near, "col"), flip(passed, "blk", 1)
        keep, send = call(
            add_near, [shape(part, F32), shape(part, BF16)], [VMEM] * 3, [], (1, 1), "add_near",
        )(kept, near_got, passed)
        send, at_owner[4] = tie((send, at_owner[4]))
        got = flip(send, "blk", 2)
        at_owner, _ = tie((at_owner, send))
        canvas, *rims = owner(at_owner)
        message = shape((PART, FULL), BF16)
        wider = shape((PART + RIM, FULL), BF16)
        own, *wides = call(
            add_workers, [message, wider, wider], [VMEM] * 4, [], (1, 1), "add_workers",
        )(keep, got, *rims)
        got_2, got_1 = flip(wides[1], "blk", 2), flip(wides[0], "blk", 1)
        across = [swap(own, "col")]
        got_2, across = tie((got_2, across))
        got = [got_1, got_2, flip(got_2, "blk", 1)]
        across += [swap(got_1, "col"), swap(got_2, "col")]
        got, across = tie((got[::-1], across))
        got = got[::-1]
        last = call(
            column_message, shape((PART + 64, FULL), BF16), [VMEM] * 3,
            [pltpu.VMEM((RIM, FULL), F32), pltpu.VMEM((64, HALF), F32)],
            (1, 1), "column_message",
        )(canvas.reshape(HIGH * WIDE, HALF), got[0], got[2])
        across += [swap(last, "col")]
        grad_in = call(
            close, shape(grad_out.shape, BF16), [VMEM] * 5,
            [pltpu.VMEM((TILE_ROWS * BLOCK * 32, HALF), F32)], (1, 1), "close",
        )(grad_out, canvas, got[0], got[2], across[3])
        grad_second, grad_first = call(
            lay, [shape((9, HALF, FULL), F32)] * 2, [VMEM] * 8, [], (1, 1), "lay",
        )(own, *got, *across)
        return (grad_in, grad_first, grad_second)

    grad_first, grad_second = lax.psum((terms[0][1], terms[0][0]), ("blk", "col"))
    [canvas] = owner(at_owner)
    up, down = neighbours("blk")
    from_above = lax.ppermute(canvas[HIGH - 2 :].astype(BF16), "blk", up).astype(F32)
    from_below = lax.ppermute(canvas[:2].astype(BF16), "blk", down).astype(F32)
    inner = canvas[2 : HIGH - 2]
    inner = inner.at[:2].add(from_above).at[-2:].add(from_below)
    up, down = neighbours("col")
    from_left = lax.ppermute(inner[:, 32:34].astype(BF16), "col", up).astype(F32)
    from_right = lax.ppermute(inner[:, 34:36].astype(BF16), "col", down).astype(F32)
    inner = inner[:, :32].at[:, :2].add(from_left).at[:, -2:].add(from_right)
    grad_in = (grad_out.astype(F32) + inner).astype(BF16)
    return (grad_in, grad_first, grad_second)


def solution(mesh):
    return jax.shard_map(
        shards,
        mesh=mesh,
        in_specs=(
            P(("groups", "blk"), "col", "ch"),
            P(("groups", "col"), "blk", None, None, None, "ch"),
            P(("groups", "col"), "blk", None, None, None, "ch"),
            P(None, "ch", None),
            P(None, "ch", None),
            P(("groups", "col"), None, None),
        ),
        out_specs=(
            P(("groups", "blk"), "col", "ch"),
            P("groups", "ch", None),
            P("groups", "ch", None),
        ),
        check_vma=False,
    )
```

```python
import functools
import math

import jax
import jax.numpy as jnp
from jax import lax
from jax.experimental import pallas as pl
from jax.experimental.pallas import tpu as pltpu
from jax.sharding import PartitionSpec as P

BLOCK = 8
TILE_ROWS = 8
TILE_COLS = 4
TILE_BLOCKS = 32
PER_WORKER = 16
MIDDLE = 10
OUTER = 12
HALF = 128
FULL = 256
DEAD = -4096
HIGH = 68
RIM = 48
ROWS = 16
PART = 288
WIDE = 40

BF16 = jnp.bfloat16
F32 = jnp.float32
I32 = jnp.int32

VMEM = pl.BlockSpec(memory_space=pltpu.VMEM)
HBM = pl.BlockSpec(memory_space=pltpu.HBM)
SMEM = pl.BlockSpec(memory_space=pltpu.SMEM)


def call(body, outs, specs, scratch, cost, name):
    return pl.pallas_call(
        body,
        out_shape=outs,
        in_specs=specs,
        out_specs=jax.tree.map(lambda _: VMEM, outs),
        scratch_shapes=scratch,
        compiler_params=pltpu.CompilerParams(vmem_limit_bytes=48 * 1024 * 1024),
        cost_estimate=pl.CostEstimate(flops=cost[0], bytes_accessed=cost[1], transcendentals=0),
        name=name,
    )


def iota(shape, dim):
    return lax.broadcasted_iota(I32, shape, dim)


def one_hot(hits):
    return jnp.where(hits, 1.0, 0.0).astype(BF16)


def dot(a, b):
    return jnp.dot(a, b, preferred_element_type=F32)


def dot_nt(a, b):
    return lax.dot_general(a, b, (((1,), (1,)), ((), ())), preferred_element_type=F32)


def dot_tn(a, b):
    return lax.dot_general(a, b, (((0,), (0,)), ((), ())), preferred_element_type=F32)


def owner_table(routing, table, owners, capacity):
    me = lax.axis_index("blk")

    def clear(number, carry):
        table[number] = DEAD
        return carry

    lax.fori_loop(0, owners * capacity, clear, 0)

    def worker(number, carry):
        count = jnp.int32(0)
        for slot in range(PER_WORKER):
            code = routing[number, slot]
            hit = (code // TILE_BLOCKS) == me
            table[jnp.where(hit, number * capacity + count, owners * capacity)] = code % TILE_BLOCKS
            count = count + jnp.where(hit, 1, 0)
        return carry

    lax.fori_loop(0, owners, worker, 0)


def worker_codes(routing, counts, owners):
    me = lax.axis_index("blk")

    def clear(number, carry):
        counts[number] = 0
        return carry

    lax.fori_loop(0, owners, clear, 0)
    slots = []
    for slot in range(PER_WORKER):
        code = routing[me, slot]
        owner = code // TILE_BLOCKS
        rank = counts[owner]
        counts[owner] = rank + 1
        slots.append((owner, code % TILE_BLOCKS, rank))
    return slots


def views(refs, count):
    return list(refs) if len(refs) == count else [refs[0].at[k] for k in range(count)]


def partner(axis, step, permuted):
    return step ^ lax.axis_index(axis) if permuted else step


def pack_cotangents(owners, capacity, permuted, routing, source, *refs):
    outs, (table, tile, arrived) = refs[:-3], refs[-3:]
    fetch = pltpu.make_async_copy(source, tile, arrived)
    fetch.start()
    owner_table(routing, table, owners, capacity)
    rows = BLOCK * capacity
    row, lane = iota((rows, FULL), 0), iota((rows, FULL), 1)
    picks = []
    for step in range(owners):
        worker = partner("blk", step, permuted)
        target = jnp.full((rows, FULL), DEAD, I32)
        for rank in range(capacity):
            place = table[worker * capacity + rank] * BLOCK
            target = jnp.where(row % capacity == rank, place, target)
        picks.append(one_hot(lane == target + row // capacity))
    pick = jnp.concatenate(picks, axis=0)
    fetch.wait()
    for u in range(0, BLOCK, 2):
        pair = [
            jnp.concatenate([tile[r, u + k] for r in range(TILE_ROWS)], axis=0) for k in range(2)
        ]
        moved = dot(pick, jnp.concatenate(pair, axis=1)).astype(BF16)
        for step, out in enumerate(views(outs, owners)):
            part = moved[step * rows : (step + 1) * rows]
            out[u] = part[:, :HALF]
            out[u + 1] = part[:, HALF:]


def pack_saved(owners, columns, capacity, wide, permuted, routing, saved, masked, *refs):
    outs, counts, table = refs[:-2], refs[-2], refs[-1]
    column = lax.axis_index("col")

    def clear(number, carry):
        table[number] = DEAD
        return carry

    lax.fori_loop(0, owners * capacity, clear, 0)
    slots = worker_codes(routing, counts, owners)
    rows = MIDDLE * PER_WORKER
    row = iota((rows, HALF), 0)
    flags = jnp.zeros((rows, HALF), I32)
    for slot, (owner, place, rank) in enumerate(slots):
        table[owner * capacity + rank] = slot
        block_row, block_col = place // TILE_COLS, place % TILE_COLS
        flag = (
            jnp.where((owner == 0) & (block_row == 0), 1, 0)
            + jnp.where((owner == owners - 1) & (block_row == TILE_ROWS - 1), 2, 0)
            + jnp.where((column == 0) & (block_col == 0), 4, 0)
            + jnp.where((column == columns - 1) & (block_col == TILE_COLS - 1), 8, 0)
        )
        flags = jnp.where(row % PER_WORKER == slot, flag, flags)
    across = row // PER_WORKER
    outside = (((flags & 4) != 0) & (across == 0)) | (((flags & 8) != 0) & (across == MIDDLE - 1))
    for m in range(MIDDLE):
        here = outside
        if m == 0:
            here = here | ((flags & 1) != 0)
        if m == MIDDLE - 1:
            here = here | ((flags & 2) != 0)
        masked[m] = jnp.where(here, 0.0, saved[m].astype(F32)).astype(BF16)
    size = wide * capacity
    row, lane = iota((size, FULL), 0), iota((size, FULL), 1)
    picks = []
    for step in range(owners):
        owner = partner("blk", step, permuted)
        target = jnp.full((size, FULL), DEAD, I32)
        for rank in range(capacity):
            target = jnp.where(row % capacity == rank, table[owner * capacity + rank], target)
        at = row // capacity
        picks.append(one_hot((lane == target + at * PER_WORKER) & (at < MIDDLE)))
    pick = jnp.concatenate(picks, axis=0)
    filler = jnp.zeros((FULL - rows, FULL), BF16)
    for m in range(0, MIDDLE, 2):
        pair = jnp.concatenate([masked[m], masked[m + 1]], axis=1)
        moved = dot(pick, jnp.concatenate([pair, filler], axis=0)).astype(BF16)
        for step, out in enumerate(views(outs, owners)):
            part = moved[step * size : (step + 1) * size]
            out[m] = part[:, :HALF]
            out[m + 1] = part[:, HALF:]


def ordered(own, other, axis):
    first = lax.axis_index("ch") == 0
    return jnp.concatenate(
        [jnp.where(first, own, other), jnp.where(first, other, own)], axis=axis
    )


def deal(value, kept, sent, grad, tap):
    low, high = value[: HALF // 2], value[HALF // 2 :]
    mine = lax.axis_index("col") == 0
    keep, send = jnp.where(mine, low, high), jnp.where(mine, high, low).astype(BF16)
    for k in range(4):
        step, rows = partner("blk", k, True), slice(k * ROWS, (k + 1) * ROWS)
        kept[step, grad, tap] = keep[rows]
        sent[step, grad, tap] = send[rows]


def emit(value, outs, grad, tap):
    if len(outs) == 2:
        deal(value, outs[0], outs[1], grad, tap)
    else:
        outs[0][grad, tap] = value


def second_gradient(scale, owners, capacity, permuted, routing, *refs):
    parts = 1 if not permuted else owners
    own, other = views(refs[:parts], owners), views(refs[parts : 2 * parts], owners)
    masked, cot = refs[2 * parts : 2 * parts + 2]
    outs, counts = refs[2 * parts + 2 : -1], refs[-1]
    slots = worker_codes(routing, counts, owners)
    rows, inner = BLOCK * PER_WORKER, owners * BLOCK * capacity
    row, lane = iota((rows, inner), 0), iota((rows, inner), 1)
    target = jnp.full((rows, inner), DEAD, I32)
    for slot, (owner, place, rank) in enumerate(slots):
        step = partner("blk", owner, permuted)
        target = jnp.where(row % PER_WORKER == slot, step * (BLOCK * capacity) + rank, target)
    pick = one_hot(lane == target + (row // PER_WORKER) * capacity)
    for u in range(BLOCK):
        got = jnp.concatenate(
            [ordered(own[o][u], other[o][u], 1) for o in range(owners)], axis=0
        )
        cot[u] = dot(pick, got).astype(BF16)
    grads = cot[...].reshape(BLOCK * rows, FULL)
    for tap in range(9):
        dy, dx = tap // 3, tap % 3
        window = masked[dy : dy + BLOCK, dx : dx + BLOCK].reshape(BLOCK * rows, HALF)
        window = jnp.maximum(window, jnp.zeros_like(window))
        emit(dot_tn(window, grads) * scale, outs, 0, tap)


def first_gradient(
    scale, cot, masked, masked_other, weight, weight_other, saved, *refs
):
    outs, (total, pre, full) = refs[:-3], refs[-3:]
    rows = BLOCK * BLOCK * PER_WORKER
    full[...] = ordered(weight[...], weight_other[...], 1)
    total[...] = jnp.zeros_like(total)
    for tap in range(9):
        dy, dx = tap // 3, tap % 3
        part = dot_nt(cot[...].reshape(rows, FULL), full[tap])
        spot = (slice(dy, dy + BLOCK), slice(dx, dx + BLOCK))
        total[spot] = total[spot] + part.reshape(BLOCK, BLOCK, PER_WORKER, FULL)
    for m in range(MIDDLE):
        live = ordered(masked[m], masked_other[m], 2).astype(F32) > 0
        pre[m] = jnp.where(live, total[m], 0.0).astype(BF16)
    size = MIDDLE * MIDDLE * PER_WORKER
    grads = pre[...].reshape(size, FULL)
    for tap in range(9):
        dy, dx = tap // 3, tap % 3
        window = saved[dy : dy + MIDDLE, dx : dx + MIDDLE].reshape(size, HALF)
        emit(dot_tn(window, grads) * scale, outs, 1, tap)


def owner_spread(tile, tile_other, second, second_other, out, total, cot, full):
    row, lane = iota((FULL, FULL), 0), iota((FULL, FULL), 1)
    turn = one_hot(lane == (row % TILE_BLOCKS) * BLOCK + row // TILE_BLOCKS)
    for u in range(BLOCK):
        block = jnp.concatenate(
            [ordered(tile[r, u], tile_other[r, u], 1) for r in range(TILE_ROWS)], axis=0
        )
        cot[u] = dot(turn, block).astype(BF16)
    full[...] = ordered(second[...], second_other[...], 1)
    rows = BLOCK * BLOCK * TILE_BLOCKS
    total[...] = jnp.zeros_like(total)
    for tap in range(9):
        dy, dx = tap // 3, tap % 3
        part = dot_nt(cot[...].reshape(rows, FULL), full[tap])
        spot = (slice(dy, dy + BLOCK), slice(dx, dx + BLOCK))
        total[spot] = total[spot] + part.reshape(BLOCK, BLOCK, TILE_BLOCKS, FULL)
    out[...] = total[...].astype(BF16)


def worker(scale, owners, capacity, permuted, routing, *refs):
    parts = 1 if not permuted else owners
    inputs, refs = refs[: 2 * parts], refs[2 * parts :]
    (masked, masked_other, weight, weight_other, source), refs = refs[:5], refs[5:]
    if permuted:
        refs, sent = refs[:-1], refs[-1]
    outs, (counts, cot, total, pre, full, saved, arrived) = refs[:-7], refs[-7:]
    if permuted:
        kept, near, far = outs
        outs = (kept, sent)
    fetch = pltpu.make_async_copy(source, saved, arrived)
    fetch.start()
    second_gradient(scale, owners, capacity, permuted, routing, *inputs, masked, cot, *outs, counts)
    fetch.wait()
    first_gradient(
        scale, cot, masked, masked_other, weight, weight_other, saved, *outs, total, pre, full
    )
    if permuted:
        near[...] = sent[:2]
        far[...] = sent[2:]


def adjacent(step):
    me = lax.axis_index("blk")
    return (me ^ step) == me - 1, (me ^ step) == me + 1


def owner_canvas(owners, capacity, wide, permuted, routing, *refs):
    parts = 1 if not permuted else owners
    got, got_other = views(refs[:parts], owners), views(refs[parts : 2 * parts], owners)
    total, first, canvas = refs[2 * parts : 2 * parts + 3]
    rims, (table, pre, grown) = refs[2 * parts + 3 : -3], refs[-3:]
    owner_table(routing, table, owners, capacity)
    size, into = wide * capacity, MIDDLE * TILE_BLOCKS
    row, lane = iota((size, into), 0), iota((size, into), 1)
    picks = []
    for step in range(owners):
        worker = partner("blk", step, permuted)
        target = jnp.full((size, into), DEAD, I32)
        for rank in range(capacity):
            target = jnp.where(row % capacity == rank, table[worker * capacity + rank], target)
        at = row // capacity
        hits = (lane == target + at * TILE_BLOCKS) & (at < MIDDLE)
        picks.append(jnp.where(hits, 1.0, 0.0))
    pick = jnp.concatenate(picks, axis=0).T.astype(BF16)
    for m in range(MIDDLE):
        block = jnp.concatenate(
            [ordered(got[w][m], got_other[w][m], 1) for w in range(owners)], axis=0
        )
        live = dot(pick, block).reshape(MIDDLE, TILE_BLOCKS, FULL) > 0
        pre[m] = jnp.where(live, total[m].astype(F32), 0.0).astype(BF16)
    size = MIDDLE * MIDDLE * TILE_BLOCKS
    grown[...] = jnp.zeros_like(grown)
    for tap in range(0, 9, 2):
        taps = range(tap, min(tap + 2, 9))
        weight = jnp.concatenate([first[k] for k in taps], axis=0)
        part = dot_nt(pre[...].reshape(size, FULL), weight)
        for k in taps:
            dy, dx = k // 3, k % 3
            spot = (slice(dy, dy + MIDDLE), slice(dx, dx + MIDDLE))
            here = part[:, (k - tap) * HALF : (k - tap + 1) * HALF]
            grown[spot] = grown[spot] + here.reshape(MIDDLE, MIDDLE, TILE_BLOCKS, HALF)
    height, depth = TILE_ROWS * WIDE, OUTER * TILE_BLOCKS
    row, lane = iota((height, depth), 0), iota((height, depth), 1)
    at_row, at_col = row // WIDE, row % WIDE
    n, place = lane // TILE_BLOCKS, lane % TILE_BLOCKS
    column = (place % TILE_COLS) * BLOCK + n - 2
    column = jnp.where(column < 0, column + 36, column)
    fold = one_hot((at_row == place // TILE_COLS) & (at_col == column))
    canvas[...] = jnp.zeros_like(canvas)
    for m in range(0, OUTER, 2):
        pair = jnp.concatenate(
            [grown[m + k].reshape(depth, HALF).astype(BF16) for k in range(2)], axis=1
        )
        laid = dot(fold, pair).reshape(TILE_ROWS, WIDE, FULL)
        for r in range(TILE_ROWS):
            for k in range(2):
                canvas[r * BLOCK + m + k] += laid[r, :, k * HALF : (k + 1) * HALF]
    for k, rim in enumerate(rims):
        above, below = adjacent(2 * k + 1)
        top = jnp.concatenate([canvas[0], canvas[1]], axis=1)
        bottom = jnp.concatenate([canvas[HIGH - 2], canvas[HIGH - 1]], axis=1)
        rim[:WIDE] = jnp.where(below, bottom, jnp.where(above, top, 0.0)).astype(BF16)
        rim[WIDE:] = jnp.zeros((RIM - WIDE, FULL), BF16)


def add_far(kept, got, *sends):
    for k, out in enumerate(sends):
        out[...] = (kept[2 + k] + got[k].astype(F32)).astype(BF16)


def add_near(kept, got, keep, send):
    keep[...] = kept[0] + got[0].astype(F32)
    send[...] = (kept[1] + got[1].astype(F32)).astype(BF16)


def add_workers(kept, got_3, got_2, got_1, rim_1, rim_3, out, out_1, out_3):
    value = kept[...]
    for part in (got_3, got_2, got_1):
        value = value + part[...].astype(F32)
    value = value.astype(BF16).reshape(PART, FULL)
    out[...] = value
    for message, rim in ((out_1, rim_1), (out_3, rim_3)):
        message[:PART] = value
        message[PART:] = rim[...]


def column_message(canvas, got_1, got_3, out, rim, strip):
    out[:PART] = got_3[:PART]
    for j in range(2):
        c = 32 + 2 * lax.axis_index("col") + j
        strip[...] = canvas[pl.ds(2 * WIDE + c, 64, stride=WIDE), :]
        for step, got in ((1, got_1), (3, got_3)):
            rim[...] = got[PART:].astype(F32)
            row = rim[pl.ds(c, 1), :]
            above, below = adjacent(step)
            top, bottom = jnp.where(above, row, 0.0), jnp.where(below, row, 0.0)
            strip[0:1] += top[:, :HALF]
            strip[1:2] += top[:, HALF:]
            strip[62:63] += bottom[:, :HALF]
            strip[63:64] += bottom[:, HALF:]
        out[PART:, j * HALF : (j + 1) * HALF] = strip[...].astype(BF16)


def close(tile, canvas, got_1, got_3, across, out, total):
    rows = TILE_ROWS * BLOCK * 32
    inner = canvas[2 : HIGH - 2, :32, :].reshape(rows, HALF)
    total[...] = tile[...].reshape(rows, HALF).astype(F32) + inner
    for step, got in ((1, got_1), (3, got_3)):
        rim = got[PART : PART + 32].astype(F32)
        above, below = adjacent(step)
        top, bottom = jnp.where(above, rim, 0.0), jnp.where(below, rim, 0.0)
        total[0:32] += top[:, :HALF]
        total[32:64] += top[:, HALF:]
        total[rows - 64 : rows - 32] += bottom[:, :HALF]
        total[rows - 32 : rows] += bottom[:, HALF:]
    strip = across[PART:].astype(F32)
    at = jnp.where(lax.axis_index("col") == 0, 30, 0)
    for j in range(2):
        spot = (pl.ds(at + j, 64, stride=32), slice(None))
        total[spot] = total[spot] + strip[:, j * HALF : (j + 1) * HALF]
    out[...] = total[...].astype(BF16).reshape(out.shape)


def lay(*refs):
    outs = refs[-2:]
    size, column = HALF // 8, lax.axis_index("col")
    for k, part in enumerate(refs[:-2]):
        place = (column if k < 4 else 1 - column) * 4 + partner("blk", k % 4, True)
        at = pl.multiple_of(place * size, size)
        value = part[:PART].astype(F32).reshape(2, 9, size, FULL)
        for out, grad in zip(outs, (0, 1)):
            out[:, pl.ds(at, size), :] = value[grad]


def swap(value, axis="ch"):
    return lax.ppermute(value, axis, [(0, 1), (1, 0)])


def flip(value, axis, step):
    size = lax.axis_size(axis)
    return lax.ppermute(value, axis, [(i, i ^ step) for i in range(size)])


def neighbours(axis):
    size = lax.axis_size(axis)
    up = [(i, (i + 1) % size) for i in range(size - 1)]
    return up, [(j, i) for i, j in up]


def shards(grad_out, saved_input, saved_pre, first_weight, second_weight, assignment):
    owners = lax.axis_size("blk")
    columns = lax.axis_size("col")
    capacity = max(2, TILE_BLOCKS // owners)
    wide = MIDDLE if (MIDDLE * capacity) % 16 == 0 else 16
    scale = 1.0 / math.sqrt(owners * columns * PER_WORKER * BLOCK * BLOCK)
    permuted = owners == 4 and columns == 2
    parts = owners if permuted else 1
    routing = assignment[0]
    shape = jax.ShapeDtypeStruct
    tables = [pltpu.SMEM((owners * capacity + 1,), I32)]
    counts = [pltpu.SMEM((owners,), I32)]

    def pieces(*dims):
        return [shape(dims, BF16)] * owners if permuted else [shape((owners,) + dims, BF16)]

    def exchange(values):
        if permuted:
            return list(values[:1]) + [flip(values[k], "blk", k) for k in (3, 2, 1)][::-1]
        return [lax.all_to_all(values[0], "blk", split_axis=0, concat_axis=0, tiled=True)]

    tie = lax.optimization_barrier
    tile = grad_out.reshape(TILE_ROWS, BLOCK, TILE_COLS * BLOCK, HALF)
    second_other, tile_other = swap(second_weight), swap(tile)
    outgoing = call(
        functools.partial(pack_cotangents, owners, capacity, permuted),
        pieces(BLOCK, BLOCK * capacity, HALF),
        [SMEM, HBM], tables + [pltpu.VMEM(tile.shape, BF16), pltpu.SemaphoreType.DMA],
        (1, 1), "pack_cotangents",
    )(routing, pltpu.with_memory_space_constraint(tile, pltpu.HBM))
    saved_slots = saved_pre[0, 0].transpose(1, 2, 0, 3)
    outgoing, saved_slots = tie((outgoing, saved_slots))
    incoming = exchange(outgoing)

    masked, *to_owners = call(
        functools.partial(pack_saved, owners, columns, capacity, wide, permuted),
        [shape((MIDDLE, MIDDLE * PER_WORKER, HALF), BF16)] + pieces(MIDDLE, wide * capacity, HALF),
        [SMEM, VMEM], counts + tables, (1, 1), "pack_saved",
    )(routing, saved_slots.reshape(MIDDLE, MIDDLE * PER_WORKER, HALF))
    masked = masked.reshape(MIDDLE, MIDDLE, PER_WORKER, HALF)
    incoming, to_owners, masked = tie((incoming[::-1], to_owners[::-1], masked))
    incoming, to_owners = incoming[::-1], to_owners[::-1]
    incoming_other = [swap(value) for value in incoming]
    masked_other = swap(masked)
    at_owner = exchange(to_owners)

    saved_tiles = saved_input[0, 0].transpose(1, 2, 0, 3)
    if permuted:
        part = (2, 9, ROWS, FULL)
        halved = [shape((4,) + part, F32)] + [shape((2,) + part, BF16)] * 2
    else:
        halved = [shape((2, 9, HALF, FULL), F32)]
    terms = call(
        functools.partial(worker, scale, owners, capacity, permuted),
        halved,
        [SMEM] + [VMEM] * (2 * parts + 4) + [HBM],
        counts
        + [
            pltpu.VMEM((BLOCK, BLOCK * PER_WORKER, FULL), BF16),
            pltpu.VMEM((MIDDLE, MIDDLE, PER_WORKER, FULL), F32),
            pltpu.VMEM((MIDDLE, MIDDLE, PER_WORKER, FULL), BF16),
            pltpu.VMEM((9, FULL, FULL), BF16),
            pltpu.VMEM(saved_tiles.shape, BF16),
            pltpu.SemaphoreType.DMA,
        ]
        + ([pltpu.VMEM((4,) + part, BF16)] if permuted else []),
        (1, 1), "worker",
    )(
        routing, *incoming, *incoming_other, masked, masked_other, second_weight, second_other,
        pltpu.with_memory_space_constraint(saved_tiles, pltpu.HBM),
    )

    if permuted:
        kept, near, far = terms
        far, at_owner[2] = tie((far, at_owner[2]))
        kept, far, tile_here = tie((kept, far, tile))
    else:
        terms, tile_here = tie((terms, tile))
    total = call(
        owner_spread,
        shape((MIDDLE, MIDDLE, TILE_BLOCKS, FULL), BF16),
        [VMEM] * 4,
        [
            pltpu.VMEM((MIDDLE, MIDDLE, TILE_BLOCKS, FULL), F32),
            pltpu.VMEM((BLOCK, FULL, FULL), BF16),
            pltpu.VMEM((9, FULL, FULL), BF16),
        ],
        (1, 1), "owner_spread",
    )(tile_here, tile_other, second_weight, second_other)

    def owner(at_owner):
        at_owner_other = [swap(value) for value in at_owner]
        return call(
            functools.partial(owner_canvas, owners, capacity, wide, permuted),
            [shape((HIGH, WIDE, HALF), F32)] + [shape((RIM, FULL), BF16)] * (2 if permuted else 0),
            [SMEM] + [VMEM] * (2 * len(at_owner) + 2),
            tables
            + [
                pltpu.VMEM((MIDDLE, MIDDLE, TILE_BLOCKS, FULL), BF16),
                pltpu.VMEM((OUTER, OUTER, TILE_BLOCKS, HALF), F32),
            ],
            (1, 1), "owner_canvas",
        )(routing, *at_owner, *at_owner_other, total, first_weight)

    if permuted:
        far_got, near_got = swap(far, "col"), swap(near, "col")
        total, far_got = tie((total, far_got))
        sends = call(add_far, [shape(part, BF16)] * 2, [VMEM] * 2, [], (1, 1), "add_far")(
            kept, far_got
        )
        sends, at_owner[3], at_owner[1] = tie((sends[::-1], at_owner[3], at_owner[1]))
        got = [flip(sends[0], "blk", 3), flip(sends[1], "blk", 2)]
        canvas, *rims = owner(at_owner)
        near_got, canvas = tie((near_got, canvas))
        keep, send = call(
            add_near, [shape(part, F32), shape(part, BF16)], [VMEM] * 2, [], (1, 1), "add_near",
        )(kept, near_got)
        got.append(flip(send, "blk", 1))
        message = shape((PART, FULL), BF16)
        wider = shape((PART + RIM, FULL), BF16)
        own, *wides = call(
            add_workers, [message, wider, wider], [VMEM] * 6, [], (1, 1), "add_workers",
        )(keep, *got, *rims)
        got = [flip(value, "blk", k) for k, value in ((3, wides[1]), (2, own), (1, wides[0]))][::-1]
        across = [swap(own, "col"), swap(got[0][:PART], "col")]
        got, across = tie((got[::-1], across))
        got = got[::-1]
        last = call(
            column_message, shape((PART + 64, FULL), BF16), [VMEM] * 3,
            [pltpu.VMEM((RIM, FULL), F32), pltpu.VMEM((64, HALF), F32)],
            (1, 1), "column_message",
        )(canvas.reshape(HIGH * WIDE, HALF), got[0], got[2])
        across += [swap(got[1], "col"), swap(last, "col")]
        grad_in = call(
            close, shape(grad_out.shape, BF16), [VMEM] * 5,
            [pltpu.VMEM((TILE_ROWS * BLOCK * 32, HALF), F32)], (1, 1), "close",
        )(grad_out, canvas, got[0], got[2], across[3])
        grad_second, grad_first = call(
            lay, [shape((9, HALF, FULL), F32)] * 2, [VMEM] * 8, [], (1, 1), "lay",
        )(own, *got, *across)
        return (grad_in, grad_first, grad_second)

    grad_first, grad_second = lax.psum((terms[0][1], terms[0][0]), ("blk", "col"))
    [canvas] = owner(at_owner)
    up, down = neighbours("blk")
    from_above = lax.ppermute(canvas[HIGH - 2 :].astype(BF16), "blk", up).astype(F32)
    from_below = lax.ppermute(canvas[:2].astype(BF16), "blk", down).astype(F32)
    inner = canvas[2 : HIGH - 2]
    inner = inner.at[:2].add(from_above).at[-2:].add(from_below)
    up, down = neighbours("col")
    from_left = lax.ppermute(inner[:, 32:34].astype(BF16), "col", up).astype(F32)
    from_right = lax.ppermute(inner[:, 34:36].astype(BF16), "col", down).astype(F32)
    inner = inner[:, :32].at[:, :2].add(from_left).at[:, -2:].add(from_right)
    grad_in = (grad_out.astype(F32) + inner).astype(BF16)
    return (grad_in, grad_first, grad_second)


def solution(mesh):
    return jax.shard_map(
        shards,
        mesh=mesh,
        in_specs=(
            P(("groups", "blk"), "col", "ch"),
            P(("groups", "col"), "blk", None, None, None, "ch"),
            P(("groups", "col"), "blk", None, None, None, "ch"),
            P(None, "ch", None),
            P(None, "ch", None),
            P(("groups", "col"), None, None),
        ),
        out_specs=(
            P(("groups", "blk"), "col", "ch"),
            P("groups", "ch", None),
            P("groups", "ch", None),
        ),
        check_vma=False,
    )
```

```python
import functools
import math

import jax
import jax.numpy as jnp
from jax import lax
from jax.experimental import pallas as pl
from jax.experimental.pallas import tpu as pltpu
from jax.sharding import PartitionSpec as P

BLOCK = 8
TILE_ROWS = 8
TILE_COLS = 4
TILE_BLOCKS = 32
PER_WORKER = 16
MIDDLE = 10
OUTER = 12
HALF = 128
FULL = 256
DEAD = -4096
HIGH = 68
RIM = 48
ROWS = 16
PART = 288
WIDE = 40

BF16 = jnp.bfloat16
F32 = jnp.float32
I32 = jnp.int32

VMEM = pl.BlockSpec(memory_space=pltpu.VMEM)
HBM = pl.BlockSpec(memory_space=pltpu.HBM)
SMEM = pl.BlockSpec(memory_space=pltpu.SMEM)


def call(body, outs, specs, scratch, cost, name):
    return pl.pallas_call(
        body,
        out_shape=outs,
        in_specs=specs,
        out_specs=jax.tree.map(lambda _: VMEM, outs),
        scratch_shapes=scratch,
        compiler_params=pltpu.CompilerParams(vmem_limit_bytes=48 * 1024 * 1024),
        cost_estimate=pl.CostEstimate(flops=cost[0], bytes_accessed=cost[1], transcendentals=0),
        name=name,
    )


def iota(shape, dim):
    return lax.broadcasted_iota(I32, shape, dim)


def one_hot(hits):
    return jnp.where(hits, 1.0, 0.0).astype(BF16)


def dot(a, b):
    return jnp.dot(a, b, preferred_element_type=F32)


def dot_nt(a, b):
    return lax.dot_general(a, b, (((1,), (1,)), ((), ())), preferred_element_type=F32)


def dot_tn(a, b):
    return lax.dot_general(a, b, (((0,), (0,)), ((), ())), preferred_element_type=F32)


def owner_table(routing, table, owners, capacity):
    me = lax.axis_index("blk")

    def clear(number, carry):
        table[number] = DEAD
        return carry

    lax.fori_loop(0, owners * capacity, clear, 0)

    def worker(number, carry):
        count = jnp.int32(0)
        for slot in range(PER_WORKER):
            code = routing[number, slot]
            hit = (code // TILE_BLOCKS) == me
            table[jnp.where(hit, number * capacity + count, owners * capacity)] = code % TILE_BLOCKS
            count = count + jnp.where(hit, 1, 0)
        return carry

    lax.fori_loop(0, owners, worker, 0)


def worker_codes(routing, counts, owners):
    me = lax.axis_index("blk")

    def clear(number, carry):
        counts[number] = 0
        return carry

    lax.fori_loop(0, owners, clear, 0)
    slots = []
    for slot in range(PER_WORKER):
        code = routing[me, slot]
        owner = code // TILE_BLOCKS
        rank = counts[owner]
        counts[owner] = rank + 1
        slots.append((owner, code % TILE_BLOCKS, rank))
    return slots


def views(refs, count):
    return list(refs) if len(refs) == count else [refs[0].at[k] for k in range(count)]


def partner(axis, step, permuted):
    return step ^ lax.axis_index(axis) if permuted else step


def pack_cotangents(owners, capacity, permuted, routing, source, *refs):
    outs, (table, tile, arrived) = refs[:-3], refs[-3:]
    fetch = pltpu.make_async_copy(source, tile, arrived)
    fetch.start()
    owner_table(routing, table, owners, capacity)
    rows = BLOCK * capacity
    row, lane = iota((rows, FULL), 0), iota((rows, FULL), 1)
    picks = []
    for step in range(owners):
        worker = partner("blk", step, permuted)
        target = jnp.full((rows, FULL), DEAD, I32)
        for rank in range(capacity):
            place = table[worker * capacity + rank] * BLOCK
            target = jnp.where(row % capacity == rank, place, target)
        picks.append(one_hot(lane == target + row // capacity))
    pick = jnp.concatenate(picks, axis=0)
    fetch.wait()
    for u in range(0, BLOCK, 2):
        pair = [
            jnp.concatenate([tile[r, u + k] for r in range(TILE_ROWS)], axis=0) for k in range(2)
        ]
        moved = dot(pick, jnp.concatenate(pair, axis=1)).astype(BF16)
        for step, out in enumerate(views(outs, owners)):
            part = moved[step * rows : (step + 1) * rows]
            out[u] = part[:, :HALF]
            out[u + 1] = part[:, HALF:]


def outside_image(slots, owners, columns):
    column = lax.axis_index("col")
    row = iota((MIDDLE * PER_WORKER, HALF), 0)
    flags = jnp.zeros_like(row)
    for slot, (owner, place, rank) in enumerate(slots):
        block_row, block_col = place // TILE_COLS, place % TILE_COLS
        flag = (
            jnp.where((owner == 0) & (block_row == 0), 1, 0)
            + jnp.where((owner == owners - 1) & (block_row == TILE_ROWS - 1), 2, 0)
            + jnp.where((column == 0) & (block_col == 0), 4, 0)
            + jnp.where((column == columns - 1) & (block_col == TILE_COLS - 1), 8, 0)
        )
        flags = jnp.where(row % PER_WORKER == slot, flag, flags)
    across = row // PER_WORKER
    sides = (((flags & 4) != 0) & (across == 0)) | (((flags & 8) != 0) & (across == MIDDLE - 1))

    def here(m):
        if m == 0:
            return sides | ((flags & 1) != 0)
        if m == MIDDLE - 1:
            return sides | ((flags & 2) != 0)
        return sides

    return here


def pack_saved(owners, columns, capacity, wide, permuted, routing, saved, masked, *refs):
    outs, counts, table = refs[:-2], refs[-2], refs[-1]

    def clear(number, carry):
        table[number] = DEAD
        return carry

    lax.fori_loop(0, owners * capacity, clear, 0)
    slots = worker_codes(routing, counts, owners)
    rows = MIDDLE * PER_WORKER
    for slot, (owner, place, rank) in enumerate(slots):
        table[owner * capacity + rank] = slot
    outside = outside_image(slots, owners, columns)
    for m in range(MIDDLE):
        masked[m] = jnp.where(outside(m), 0.0, saved[m].astype(F32)).astype(BF16)
    size = wide * capacity
    row, lane = iota((size, FULL), 0), iota((size, FULL), 1)
    picks = []
    for step in range(owners):
        owner = partner("blk", step, permuted)
        target = jnp.full((size, FULL), DEAD, I32)
        for rank in range(capacity):
            target = jnp.where(row % capacity == rank, table[owner * capacity + rank], target)
        at = row // capacity
        picks.append(one_hot((lane == target + at * PER_WORKER) & (at < MIDDLE)))
    pick = jnp.concatenate(picks, axis=0)
    filler = jnp.zeros((FULL - rows, FULL), BF16)
    for m in range(0, MIDDLE, 2):
        pair = jnp.concatenate([masked[m], masked[m + 1]], axis=1)
        moved = dot(pick, jnp.concatenate([pair, filler], axis=0)).astype(BF16)
        for step, out in enumerate(views(outs, owners)):
            part = moved[step * size : (step + 1) * size]
            out[m] = part[:, :HALF]
            out[m + 1] = part[:, HALF:]


def ordered(own, other, axis):
    first = lax.axis_index("ch") == 0
    return jnp.concatenate(
        [jnp.where(first, own, other), jnp.where(first, other, own)], axis=axis
    )


def deal(value, kept, sent, grad, tap):
    low, high = value[: HALF // 2], value[HALF // 2 :]
    mine = lax.axis_index("col") == 0
    keep, send = jnp.where(mine, low, high), jnp.where(mine, high, low).astype(BF16)
    for k in range(4):
        step, rows = partner("blk", k, True), slice(k * ROWS, (k + 1) * ROWS)
        kept[step, grad, tap] = keep[rows]
        sent[step, grad, tap] = send[rows]


def emit(value, outs, grad, tap):
    if len(outs) == 2:
        deal(value, outs[0], outs[1], grad, tap)
    else:
        outs[0][grad, tap] = value


def second_gradient(scale, owners, capacity, permuted, routing, *refs):
    parts = 1 if not permuted else owners
    own, other = views(refs[:parts], owners), views(refs[parts : 2 * parts], owners)
    masked, cot = refs[2 * parts : 2 * parts + 2]
    outs, counts = refs[2 * parts + 2 : -1], refs[-1]
    slots = worker_codes(routing, counts, owners)
    rows, inner = BLOCK * PER_WORKER, owners * BLOCK * capacity
    row, lane = iota((rows, inner), 0), iota((rows, inner), 1)
    target = jnp.full((rows, inner), DEAD, I32)
    for slot, (owner, place, rank) in enumerate(slots):
        step = partner("blk", owner, permuted)
        target = jnp.where(row % PER_WORKER == slot, step * (BLOCK * capacity) + rank, target)
    pick = one_hot(lane == target + (row // PER_WORKER) * capacity)
    for u in range(BLOCK):
        got = jnp.concatenate(
            [ordered(own[o][u], other[o][u], 1) for o in range(owners)], axis=0
        )
        cot[u] = dot(pick, got).astype(BF16)
    grads = cot[...].reshape(BLOCK * rows, FULL)
    for dy in range(3):
        windows = [
            masked[dy : dy + BLOCK, dx * PER_WORKER : (dx + BLOCK) * PER_WORKER] for dx in range(3)
        ]
        window = jnp.concatenate([w.reshape(BLOCK * rows, HALF) for w in windows], axis=1)
        value = dot_tn(jnp.maximum(window, jnp.zeros_like(window)), grads) * scale
        for dx in range(3):
            emit(value[dx * HALF : (dx + 1) * HALF], outs, 0, 3 * dy + dx)
    return slots


def first_gradient(
    scale, outside, cot, masked, saved_other, weight, weight_other, saved, *refs
):
    outs, (total, pre, full) = refs[:-3], refs[-3:]
    rows = BLOCK * BLOCK * PER_WORKER
    full[...] = ordered(weight[...], weight_other[...], 1)
    total[...] = jnp.zeros_like(total)
    for tap in range(9):
        dy, dx = tap // 3, tap % 3
        part = dot_nt(cot[...].reshape(rows, FULL), full[tap])
        spot = (slice(dy, dy + BLOCK), slice(dx, dx + BLOCK))
        total[spot] = total[spot] + part.reshape(BLOCK, BLOCK, PER_WORKER, FULL)
    for m in range(MIDDLE):
        other = jnp.where(outside(m), 0.0, saved_other[m].astype(F32)).astype(BF16)
        live = ordered(masked[m], other, 1).astype(F32) > 0
        value = jnp.where(live, total[m].reshape(MIDDLE * PER_WORKER, FULL), 0.0)
        pre[m] = value.astype(BF16).reshape(MIDDLE, PER_WORKER, FULL)
    size = MIDDLE * MIDDLE * PER_WORKER
    grads = pre[...].reshape(size, FULL)
    for dy in range(3):
        windows = [saved[dy : dy + MIDDLE, dx : dx + MIDDLE] for dx in range(3)]
        window = jnp.concatenate([w.reshape(size, HALF) for w in windows], axis=1)
        value = dot_tn(window, grads) * scale
        for dx in range(3):
            emit(value[dx * HALF : (dx + 1) * HALF], outs, 1, 3 * dy + dx)


def owner_spread(tile, tile_other, second, second_other, out, total, cot, full):
    row, lane = iota((FULL, FULL), 0), iota((FULL, FULL), 1)
    turn = one_hot(lane == (row % TILE_BLOCKS) * BLOCK + row // TILE_BLOCKS)
    for u in range(BLOCK):
        block = jnp.concatenate(
            [ordered(tile[r, u], tile_other[r, u], 1) for r in range(TILE_ROWS)], axis=0
        )
        cot[u] = dot(turn, block).astype(BF16)
    full[...] = ordered(second[...], second_other[...], 1)
    rows = BLOCK * BLOCK * TILE_BLOCKS
    total[...] = jnp.zeros_like(total)
    for tap in range(9):
        dy, dx = tap // 3, tap % 3
        part = dot_nt(cot[...].reshape(rows, FULL), full[tap])
        spot = (slice(dy, dy + BLOCK), slice(dx, dx + BLOCK))
        total[spot] = total[spot] + part.reshape(BLOCK, BLOCK, TILE_BLOCKS, FULL)
    out[...] = total[...].astype(BF16)


def worker(scale, owners, columns, capacity, permuted, routing, *refs):
    parts = 1 if not permuted else owners
    inputs, refs = refs[: 2 * parts], refs[2 * parts :]
    (masked, saved_other, weight, weight_other, source), refs = refs[:5], refs[5:]
    if permuted:
        refs, sent = refs[:-1], refs[-1]
    outs, (counts, cot, total, pre, full, saved, arrived) = refs[:-7], refs[-7:]
    if permuted:
        kept, near, far = outs
        outs = (kept, sent)
    fetch = pltpu.make_async_copy(source, saved, arrived)
    fetch.start()
    slots = second_gradient(
        scale, owners, capacity, permuted, routing, *inputs, masked, cot, *outs, counts
    )
    fetch.wait()
    first_gradient(
        scale, outside_image(slots, owners, columns), cot, masked, saved_other, weight, weight_other,
        saved, *outs, total, pre, full,
    )
    if permuted:
        near[...] = sent[:2]
        far[...] = sent[2:]


def adjacent(step):
    me = lax.axis_index("blk")
    return (me ^ step) == me - 1, (me ^ step) == me + 1


def owner_canvas(owners, capacity, wide, permuted, routing, *refs):
    parts = 1 if not permuted else owners
    got, got_other = views(refs[:parts], owners), views(refs[parts : 2 * parts], owners)
    total, first, canvas = refs[2 * parts : 2 * parts + 3]
    rims, (table, pre, grown) = refs[2 * parts + 3 : -3], refs[-3:]
    owner_table(routing, table, owners, capacity)
    size, into = wide * capacity, MIDDLE * TILE_BLOCKS
    row, lane = iota((size, into), 0), iota((size, into), 1)
    picks = []
    for step in range(owners):
        worker = partner("blk", step, permuted)
        target = jnp.full((size, into), DEAD, I32)
        for rank in range(capacity):
            target = jnp.where(row % capacity == rank, table[worker * capacity + rank], target)
        at = row // capacity
        hits = (lane == target + at * TILE_BLOCKS) & (at < MIDDLE)
        picks.append(jnp.where(hits, 1.0, 0.0))
    pick = jnp.concatenate(picks, axis=0).T.astype(BF16)
    for m in range(MIDDLE):
        block = jnp.concatenate(
            [ordered(got[w][m], got_other[w][m], 1) for w in range(owners)], axis=0
        )
        live = dot(pick, block).reshape(MIDDLE, TILE_BLOCKS, FULL) > 0
        pre[m] = jnp.where(live, total[m].astype(F32), 0.0).astype(BF16)
    size = MIDDLE * MIDDLE * TILE_BLOCKS
    grown[...] = jnp.zeros_like(grown)
    for tap in range(0, 9, 2):
        taps = range(tap, min(tap + 2, 9))
        weight = jnp.concatenate([first[k] for k in taps], axis=0)
        part = dot_nt(pre[...].reshape(size, FULL), weight)
        for k in taps:
            dy, dx = k // 3, k % 3
            spot = (slice(dy, dy + MIDDLE), slice(dx, dx + MIDDLE))
            here = part[:, (k - tap) * HALF : (k - tap + 1) * HALF]
            grown[spot] = grown[spot] + here.reshape(MIDDLE, MIDDLE, TILE_BLOCKS, HALF)
    height, depth = TILE_ROWS * WIDE, OUTER * TILE_BLOCKS
    row, lane = iota((height, depth), 0), iota((height, depth), 1)
    at_row, at_col = row // WIDE, row % WIDE
    n, place = lane // TILE_BLOCKS, lane % TILE_BLOCKS
    column = (place % TILE_COLS) * BLOCK + n - 2
    column = jnp.where(column < 0, column + 36, column)
    fold = one_hot((at_row == place // TILE_COLS) & (at_col == column))
    canvas[...] = jnp.zeros_like(canvas)
    for m in range(0, OUTER, 2):
        pair = jnp.concatenate(
            [grown[m + k].reshape(depth, HALF).astype(BF16) for k in range(2)], axis=1
        )
        laid = dot(fold, pair).reshape(TILE_ROWS, WIDE, FULL)
        for r in range(TILE_ROWS):
            for k in range(2):
                canvas[r * BLOCK + m + k] += laid[r, :, k * HALF : (k + 1) * HALF]
    for k, rim in enumerate(rims):
        above, below = adjacent(2 * k + 1)
        top = jnp.concatenate([canvas[0], canvas[1]], axis=1)
        bottom = jnp.concatenate([canvas[HIGH - 2], canvas[HIGH - 1]], axis=1)
        rim[:WIDE] = jnp.where(below, bottom, jnp.where(above, top, 0.0)).astype(BF16)
        rim[WIDE:] = jnp.zeros((RIM - WIDE, FULL), BF16)


def add_far(kept, got, *sends):
    for k, out in enumerate(sends):
        out[...] = (kept[2 + k] + got[k].astype(F32)).astype(BF16)


def add_near(kept, got, keep, send):
    keep[...] = kept[0] + got[0].astype(F32)
    send[...] = (kept[1] + got[1].astype(F32)).astype(BF16)


def add_workers(kept, got_3, got_2, got_1, rim_1, rim_3, out, out_1, out_3):
    value = kept[...]
    for part in (got_3, got_2, got_1):
        value = value + part[...].astype(F32)
    value = value.astype(BF16).reshape(PART, FULL)
    out[...] = value
    for message, rim in ((out_1, rim_1), (out_3, rim_3)):
        message[:PART] = value
        message[PART:] = rim[...]


def column_message(canvas, got_1, got_3, out, rim, strip):
    out[:PART] = got_3[:PART]
    for j in range(2):
        c = 32 + 2 * lax.axis_index("col") + j
        strip[...] = canvas[pl.ds(2 * WIDE + c, 64, stride=WIDE), :]
        for step, got in ((1, got_1), (3, got_3)):
            rim[...] = got[PART:].astype(F32)
            row = rim[pl.ds(c, 1), :]
            above, below = adjacent(step)
            top, bottom = jnp.where(above, row, 0.0), jnp.where(below, row, 0.0)
            strip[0:1] += top[:, :HALF]
            strip[1:2] += top[:, HALF:]
            strip[62:63] += bottom[:, :HALF]
            strip[63:64] += bottom[:, HALF:]
        out[PART:, j * HALF : (j + 1) * HALF] = strip[...].astype(BF16)


def close(tile, canvas, got_1, got_3, across, out, total):
    rows = TILE_ROWS * BLOCK * 32
    inner = canvas[2 : HIGH - 2, :32, :].reshape(rows, HALF)
    total[...] = tile[...].reshape(rows, HALF).astype(F32) + inner
    for step, got in ((1, got_1), (3, got_3)):
        rim = got[PART : PART + 32].astype(F32)
        above, below = adjacent(step)
        top, bottom = jnp.where(above, rim, 0.0), jnp.where(below, rim, 0.0)
        total[0:32] += top[:, :HALF]
        total[32:64] += top[:, HALF:]
        total[rows - 64 : rows - 32] += bottom[:, :HALF]
        total[rows - 32 : rows] += bottom[:, HALF:]
    strip = across[PART:].astype(F32)
    at = jnp.where(lax.axis_index("col") == 0, 30, 0)
    for j in range(2):
        spot = (pl.ds(at + j, 64, stride=32), slice(None))
        total[spot] = total[spot] + strip[:, j * HALF : (j + 1) * HALF]
    out[...] = total[...].astype(BF16).reshape(out.shape)


def rows_at(number):
    column = lax.axis_index("col")
    place = (column if number < 4 else 1 - column) * 4 + partner("blk", number % 4, True)
    return pl.ds(pl.multiple_of(place * ROWS, ROWS), ROWS)


def lay(*refs):
    for number, part in enumerate(refs[:-2]):
        value = part[:PART].astype(F32).reshape(2, 9, ROWS, FULL)
        for out, grad in zip(refs[-2:], (0, 1)):
            out[:, rows_at(number), :] = value[grad]


def finish(tile, canvas, got_1, got_3, last, late, old_0, old_1, out, out_0, out_1, total, laid, sems):
    copies = []
    for k, (number, part) in enumerate(((6, late), (7, last))):
        laid[k] = part[:PART].astype(F32).reshape(2, 9, ROWS, FULL)
        for grad, dest in enumerate((out_0, out_1)):
            copy = pltpu.make_async_copy(
                laid.at[k, grad], dest.at[:, rows_at(number), :], sems.at[k, grad]
            )
            copy.start()
            copies.append(copy)
    close(tile, canvas, got_1, got_3, last, out, total)
    for copy in copies:
        copy.wait()


def swap(value, axis="ch"):
    return lax.ppermute(value, axis, [(0, 1), (1, 0)])


def flip(value, axis, step):
    size = lax.axis_size(axis)
    return lax.ppermute(value, axis, [(i, i ^ step) for i in range(size)])


def neighbours(axis):
    size = lax.axis_size(axis)
    up = [(i, (i + 1) % size) for i in range(size - 1)]
    return up, [(j, i) for i, j in up]


def shards(grad_out, saved_input, saved_pre, first_weight, second_weight, assignment):
    owners = lax.axis_size("blk")
    columns = lax.axis_size("col")
    capacity = max(2, TILE_BLOCKS // owners)
    wide = MIDDLE if (MIDDLE * capacity) % 16 == 0 else 16
    scale = 1.0 / math.sqrt(owners * columns * PER_WORKER * BLOCK * BLOCK)
    permuted = owners == 4 and columns == 2
    parts = owners if permuted else 1
    routing = assignment[0]
    shape = jax.ShapeDtypeStruct
    tables = [pltpu.SMEM((owners * capacity + 1,), I32)]
    counts = [pltpu.SMEM((owners,), I32)]

    def pieces(*dims):
        return [shape(dims, BF16)] * owners if permuted else [shape((owners,) + dims, BF16)]

    def exchange(values):
        if permuted:
            return list(values[:1]) + [flip(values[k], "blk", k) for k in (3, 2, 1)][::-1]
        return [lax.all_to_all(values[0], "blk", split_axis=0, concat_axis=0, tiled=True)]

    tie = lax.optimization_barrier
    tile = grad_out.reshape(TILE_ROWS, BLOCK, TILE_COLS * BLOCK, HALF)
    second_other, tile_other = swap(second_weight), swap(tile)
    outgoing = call(
        functools.partial(pack_cotangents, owners, capacity, permuted),
        pieces(BLOCK, BLOCK * capacity, HALF),
        [SMEM, HBM], tables + [pltpu.VMEM(tile.shape, BF16), pltpu.SemaphoreType.DMA],
        (1, 1), "pack_cotangents",
    )(routing, pltpu.with_memory_space_constraint(tile, pltpu.HBM))
    saved_slots = saved_pre[0, 0].transpose(1, 2, 0, 3)
    saved_slots = saved_slots.reshape(MIDDLE, MIDDLE * PER_WORKER, HALF)
    outgoing, saved_here = tie((outgoing, saved_slots))
    saved_other = swap(saved_slots)
    incoming = exchange(outgoing)

    masked, *to_owners = call(
        functools.partial(pack_saved, owners, columns, capacity, wide, permuted),
        [shape((MIDDLE, MIDDLE * PER_WORKER, HALF), BF16)] + pieces(MIDDLE, wide * capacity, HALF),
        [SMEM, VMEM], counts + tables, (1, 1), "pack_saved",
    )(routing, saved_here)
    incoming_other = [swap(incoming[0])] if permuted else []
    *rest, to_owners = tie((*incoming[len(incoming_other) :][::-1], to_owners[::-1]))
    incoming = incoming[: len(incoming_other)] + rest[::-1]
    to_owners = to_owners[::-1]
    incoming_other += [swap(value) for value in rest[::-1]]
    at_owner = exchange(to_owners)

    saved_tiles = saved_input[0, 0].transpose(1, 2, 0, 3)
    if permuted:
        part = (2, 9, ROWS, FULL)
        halved = [shape((4,) + part, F32)] + [shape((2,) + part, BF16)] * 2
    else:
        halved = [shape((2, 9, HALF, FULL), F32)]
    terms = call(
        functools.partial(worker, scale, owners, columns, capacity, permuted),
        halved,
        [SMEM] + [VMEM] * (2 * parts + 4) + [HBM],
        counts
        + [
            pltpu.VMEM((BLOCK, BLOCK * PER_WORKER, FULL), BF16),
            pltpu.VMEM((MIDDLE, MIDDLE, PER_WORKER, FULL), F32),
            pltpu.VMEM((MIDDLE, MIDDLE, PER_WORKER, FULL), BF16),
            pltpu.VMEM((9, FULL, FULL), BF16),
            pltpu.VMEM(saved_tiles.shape, BF16),
            pltpu.SemaphoreType.DMA,
        ]
        + ([pltpu.VMEM((4,) + part, BF16)] if permuted else []),
        (1, 1), "worker",
    )(
        routing, *incoming, *incoming_other, masked, saved_other, second_weight, second_other,
        pltpu.with_memory_space_constraint(saved_tiles, pltpu.HBM),
    )

    if permuted:
        kept, near, far = terms
        far, at_owner[2] = tie((far, at_owner[2]))
        kept, far, tile_here = tie((kept, far, tile))
    else:
        terms, tile_here = tie((terms, tile))
    total = call(
        owner_spread,
        shape((MIDDLE, MIDDLE, TILE_BLOCKS, FULL), BF16),
        [VMEM] * 4,
        [
            pltpu.VMEM((MIDDLE, MIDDLE, TILE_BLOCKS, FULL), F32),
            pltpu.VMEM((BLOCK, FULL, FULL), BF16),
            pltpu.VMEM((9, FULL, FULL), BF16),
        ],
        (1, 1), "owner_spread",
    )(tile_here, tile_other, second_weight, second_other)

    def owner(at_owner):
        at_owner_other = [swap(value) for value in at_owner]
        return call(
            functools.partial(owner_canvas, owners, capacity, wide, permuted),
            [shape((HIGH, WIDE, HALF), F32)] + [shape((RIM, FULL), BF16)] * (2 if permuted else 0),
            [SMEM] + [VMEM] * (2 * len(at_owner) + 2),
            tables
            + [
                pltpu.VMEM((MIDDLE, MIDDLE, TILE_BLOCKS, FULL), BF16),
                pltpu.VMEM((OUTER, OUTER, TILE_BLOCKS, HALF), F32),
            ],
            (1, 1), "owner_canvas",
        )(routing, *at_owner, *at_owner_other, total, first_weight)

    if permuted:
        far_got, near_got = swap(far, "col"), swap(near, "col")
        total, far_got = tie((total, far_got))
        sends = call(add_far, [shape(part, BF16)] * 2, [VMEM] * 2, [], (1, 1), "add_far")(
            kept, far_got
        )
        sends, at_owner[3], at_owner[1] = tie((sends[::-1], at_owner[3], at_owner[1]))
        got = [flip(sends[0], "blk", 3), flip(sends[1], "blk", 2)]
        canvas, *rims = owner(at_owner)
        near_got, canvas = tie((near_got, canvas))
        keep, send = call(
            add_near, [shape(part, F32), shape(part, BF16)], [VMEM] * 2, [], (1, 1), "add_near",
        )(kept, near_got)
        got.append(flip(send, "blk", 1))
        message = shape((PART, FULL), BF16)
        wider = shape((PART + RIM, FULL), BF16)
        own, *wides = call(
            add_workers, [message, wider, wider], [VMEM] * 6, [], (1, 1), "add_workers",
        )(keep, *got, *rims)
        got_3, got_2, got_1 = flip(wides[1], "blk", 3), flip(own, "blk", 2), flip(wides[0], "blk", 1)
        across = [swap(own, "col"), swap(got_1[:PART], "col")]
        got_3, got_2, got_1, across = tie((got_3, got_2, got_1, across))
        got = [got_1, got_2, got_3]
        last = call(
            column_message, shape((PART + 64, FULL), BF16), [VMEM] * 3,
            [pltpu.VMEM((RIM, FULL), F32), pltpu.VMEM((64, HALF), F32)],
            (1, 1), "column_message",
        )(canvas.reshape(HIGH * WIDE, HALF), got[0], got[2])
        across += [swap(got[1], "col"), swap(last, "col")]
        early = call(
            lay, [shape((9, HALF, FULL), F32)] * 2, [VMEM] * 6, [], (1, 1), "lay",
        )(own, *got, *across[:2])
        grad_in, grad_second, grad_first = pl.pallas_call(
            finish,
            out_shape=[shape(grad_out.shape, BF16)] + [shape((9, HALF, FULL), F32)] * 2,
            in_specs=[VMEM] * 6 + [HBM] * 2,
            out_specs=[VMEM] + [HBM] * 2,
            scratch_shapes=[
                pltpu.VMEM((TILE_ROWS * BLOCK * 32, HALF), F32),
                pltpu.VMEM((2, 2, 9, ROWS, FULL), F32),
                pltpu.SemaphoreType.DMA((2, 2)),
            ],
            input_output_aliases={6: 1, 7: 2},
            compiler_params=pltpu.CompilerParams(vmem_limit_bytes=48 * 1024 * 1024),
            cost_estimate=pl.CostEstimate(flops=1, bytes_accessed=1, transcendentals=0),
            name="finish",
        )(grad_out, canvas, got[0], got[2], across[3], across[2], *early)
        return (grad_in, grad_first, grad_second)

    grad_first, grad_second = lax.psum((terms[0][1], terms[0][0]), ("blk", "col"))
    [canvas] = owner(at_owner)
    up, down = neighbours("blk")
    from_above = lax.ppermute(canvas[HIGH - 2 :].astype(BF16), "blk", up).astype(F32)
    from_below = lax.ppermute(canvas[:2].astype(BF16), "blk", down).astype(F32)
    inner = canvas[2 : HIGH - 2]
    inner = inner.at[:2].add(from_above).at[-2:].add(from_below)
    up, down = neighbours("col")
    from_left = lax.ppermute(inner[:, 32:34].astype(BF16), "col", up).astype(F32)
    from_right = lax.ppermute(inner[:, 34:36].astype(BF16), "col", down).astype(F32)
    inner = inner[:, :32].at[:, :2].add(from_left).at[:, -2:].add(from_right)
    grad_in = (grad_out.astype(F32) + inner).astype(BF16)
    return (grad_in, grad_first, grad_second)


def solution(mesh):
    return jax.shard_map(
        shards,
        mesh=mesh,
        in_specs=(
            P(("groups", "blk"), "col", "ch"),
            P(("groups", "col"), "blk", None, None, None, "ch"),
            P(("groups", "col"), "blk", None, None, None, "ch"),
            P(None, "ch", None),
            P(None, "ch", None),
            P(("groups", "col"), None, None),
        ),
        out_specs=(
            P(("groups", "blk"), "col", "ch"),
            P("groups", "ch", None),
            P("groups", "ch", None),
        ),
        check_vma=False,
    )
```

```python
import functools
import math

import jax
import jax.numpy as jnp
from jax import lax
from jax.experimental import pallas as pl
from jax.experimental.pallas import tpu as pltpu
from jax.sharding import PartitionSpec as P

BLOCK = 8
TILE_ROWS = 8
TILE_COLS = 4
TILE_BLOCKS = 32
PER_WORKER = 16
MIDDLE = 10
OUTER = 12
HALF = 128
FULL = 256
DEAD = -4096
HIGH = 68
RIM = 48
ROWS = 16
PART = 288
WIDE = 40

BF16 = jnp.bfloat16
F32 = jnp.float32
I32 = jnp.int32

VMEM = pl.BlockSpec(memory_space=pltpu.VMEM)
HBM = pl.BlockSpec(memory_space=pltpu.HBM)
SMEM = pl.BlockSpec(memory_space=pltpu.SMEM)


def call(body, outs, specs, scratch, cost, name):
    return pl.pallas_call(
        body,
        out_shape=outs,
        in_specs=specs,
        out_specs=jax.tree.map(lambda _: VMEM, outs),
        scratch_shapes=scratch,
        compiler_params=pltpu.CompilerParams(vmem_limit_bytes=48 * 1024 * 1024),
        cost_estimate=pl.CostEstimate(flops=cost[0], bytes_accessed=cost[1], transcendentals=0),
        name=name,
    )


def iota(shape, dim):
    return lax.broadcasted_iota(I32, shape, dim)


def one_hot(hits):
    return jnp.where(hits, 1.0, 0.0).astype(BF16)


def dot(a, b):
    return jnp.dot(a, b, preferred_element_type=F32)


def dot_nt(a, b):
    return lax.dot_general(a, b, (((1,), (1,)), ((), ())), preferred_element_type=F32)


def dot_tn(a, b):
    return lax.dot_general(a, b, (((0,), (0,)), ((), ())), preferred_element_type=F32)


def owner_table(routing, table, owners, capacity):
    me = lax.axis_index("blk")

    def clear(number, carry):
        table[number] = DEAD
        return carry

    lax.fori_loop(0, owners * capacity, clear, 0)

    def worker(number, carry):
        count = jnp.int32(0)
        for slot in range(PER_WORKER):
            code = routing[number, slot]
            hit = (code // TILE_BLOCKS) == me
            table[jnp.where(hit, number * capacity + count, owners * capacity)] = code % TILE_BLOCKS
            count = count + jnp.where(hit, 1, 0)
        return carry

    lax.fori_loop(0, owners, worker, 0)


def worker_codes(routing, counts, owners):
    me = lax.axis_index("blk")

    def clear(number, carry):
        counts[number] = 0
        return carry

    lax.fori_loop(0, owners, clear, 0)
    slots = []
    for slot in range(PER_WORKER):
        code = routing[me, slot]
        owner = code // TILE_BLOCKS
        rank = counts[owner]
        counts[owner] = rank + 1
        slots.append((owner, code % TILE_BLOCKS, rank))
    return slots


def views(refs, count):
    return list(refs) if len(refs) == count else [refs[0].at[k] for k in range(count)]


def partner(axis, step, permuted):
    return step ^ lax.axis_index(axis) if permuted else step


def pack_cotangents(owners, capacity, permuted, routing, source, *refs):
    outs, (table, tile, arrived) = refs[:-3], refs[-3:]
    fetch = pltpu.make_async_copy(source, tile, arrived)
    fetch.start()
    owner_table(routing, table, owners, capacity)
    rows = BLOCK * capacity
    row, lane = iota((rows, FULL), 0), iota((rows, FULL), 1)
    picks = []
    for step in range(owners):
        worker = partner("blk", step, permuted)
        target = jnp.full((rows, FULL), DEAD, I32)
        for rank in range(capacity):
            place = table[worker * capacity + rank] * BLOCK
            target = jnp.where(row % capacity == rank, place, target)
        picks.append(one_hot(lane == target + row // capacity))
    pick = jnp.concatenate(picks, axis=0)
    fetch.wait()
    for u in range(0, BLOCK, 2):
        pair = [
            jnp.concatenate([tile[r, u + k] for r in range(TILE_ROWS)], axis=0) for k in range(2)
        ]
        moved = dot(pick, jnp.concatenate(pair, axis=1)).astype(BF16)
        for step, out in enumerate(views(outs, owners)):
            part = moved[step * rows : (step + 1) * rows]
            out[u] = part[:, :HALF]
            out[u + 1] = part[:, HALF:]


def outside_image(slots, owners, columns):
    column = lax.axis_index("col")
    row = iota((MIDDLE * PER_WORKER, HALF), 0)
    flags = jnp.zeros_like(row)
    for slot, (owner, place, rank) in enumerate(slots):
        block_row, block_col = place // TILE_COLS, place % TILE_COLS
        flag = (
            jnp.where((owner == 0) & (block_row == 0), 1, 0)
            + jnp.where((owner == owners - 1) & (block_row == TILE_ROWS - 1), 2, 0)
            + jnp.where((column == 0) & (block_col == 0), 4, 0)
            + jnp.where((column == columns - 1) & (block_col == TILE_COLS - 1), 8, 0)
        )
        flags = jnp.where(row % PER_WORKER == slot, flag, flags)
    across = row // PER_WORKER
    sides = (((flags & 4) != 0) & (across == 0)) | (((flags & 8) != 0) & (across == MIDDLE - 1))

    def here(m):
        if m == 0:
            return sides | ((flags & 1) != 0)
        if m == MIDDLE - 1:
            return sides | ((flags & 2) != 0)
        return sides

    return here


def pack_saved(owners, columns, capacity, wide, permuted, routing, saved, masked, *refs):
    outs, counts, table = refs[:-2], refs[-2], refs[-1]

    def clear(number, carry):
        table[number] = DEAD
        return carry

    lax.fori_loop(0, owners * capacity, clear, 0)
    slots = worker_codes(routing, counts, owners)
    rows = MIDDLE * PER_WORKER
    for slot, (owner, place, rank) in enumerate(slots):
        table[owner * capacity + rank] = slot
    outside = outside_image(slots, owners, columns)
    for m in range(MIDDLE):
        masked[m] = jnp.where(outside(m), 0.0, saved[m].astype(F32)).astype(BF16)
    size = wide * capacity
    row, lane = iota((size, FULL), 0), iota((size, FULL), 1)
    picks = []
    for step in range(owners):
        owner = partner("blk", step, permuted)
        target = jnp.full((size, FULL), DEAD, I32)
        for rank in range(capacity):
            target = jnp.where(row % capacity == rank, table[owner * capacity + rank], target)
        at = row // capacity
        picks.append(one_hot((lane == target + at * PER_WORKER) & (at < MIDDLE)))
    pick = jnp.concatenate(picks, axis=0)
    filler = jnp.zeros((FULL - rows, FULL), BF16)
    for m in range(0, MIDDLE, 2):
        pair = jnp.concatenate([masked[m], masked[m + 1]], axis=1)
        moved = dot(pick, jnp.concatenate([pair, filler], axis=0)).astype(BF16)
        for step, out in enumerate(views(outs, owners)):
            part = moved[step * size : (step + 1) * size]
            out[m] = part[:, :HALF]
            out[m + 1] = part[:, HALF:]


def ordered(own, other, axis):
    first = lax.axis_index("ch") == 0
    return jnp.concatenate(
        [jnp.where(first, own, other), jnp.where(first, other, own)], axis=axis
    )


def deal(value, kept, sent, grad, tap):
    low, high = value[: HALF // 2], value[HALF // 2 :]
    mine = lax.axis_index("col") == 0
    keep, send = jnp.where(mine, low, high), jnp.where(mine, high, low).astype(BF16)
    for k in range(4):
        step, rows = partner("blk", k, True), slice(k * ROWS, (k + 1) * ROWS)
        kept[step, grad, tap] = keep[rows]
        sent[step, grad, tap] = send[rows]


def emit(value, outs, grad, tap):
    if len(outs) == 2:
        deal(value, outs[0], outs[1], grad, tap)
    else:
        outs[0][grad, tap] = value


def spread(padded, weight, total, places):
    height, size = padded.shape[0], total.shape[1]
    for dy in range(3):
        windows, taps = [], []
        for dx in range(3):
            at = (2 - dx) * places
            windows.append(padded[:, at : at + size].reshape(height * size, FULL))
            taps.append(weight[3 * dy + dx])
        part = dot_nt(jnp.concatenate(windows, axis=1), jnp.concatenate(taps, axis=1))
        part = part.reshape(height, size, total.shape[2])
        if dy == 0:
            total[:height] = part
            total[height:] = jnp.zeros((2, size, total.shape[2]), F32)
        else:
            total[dy : dy + height] += part


def pad_sides(padded, places):
    for side in (slice(0, 2 * places), slice(padded.shape[1] - 2 * places, None)):
        padded[:, side] = jnp.zeros((padded.shape[0], 2 * places, FULL), BF16)


def second_gradient(scale, owners, capacity, permuted, routing, *refs):
    parts = 1 if not permuted else owners
    own, other = views(refs[:parts], owners), views(refs[parts : 2 * parts], owners)
    masked, cot = refs[2 * parts : 2 * parts + 2]
    outs, counts = refs[2 * parts + 2 : -1], refs[-1]
    slots = worker_codes(routing, counts, owners)
    rows, inner = BLOCK * PER_WORKER, owners * BLOCK * capacity
    row, lane = iota((rows, inner), 0), iota((rows, inner), 1)
    target = jnp.full((rows, inner), DEAD, I32)
    for slot, (owner, place, rank) in enumerate(slots):
        step = partner("blk", owner, permuted)
        target = jnp.where(row % PER_WORKER == slot, step * (BLOCK * capacity) + rank, target)
    pick = one_hot(lane == target + (row // PER_WORKER) * capacity)
    for u in range(BLOCK):
        got = jnp.concatenate(
            [ordered(own[o][u], other[o][u], 1) for o in range(owners)], axis=0
        )
        cot[u, 2 * PER_WORKER : 2 * PER_WORKER + rows] = dot(pick, got).astype(BF16)
    pad_sides(cot, PER_WORKER)
    grads = cot[:, 2 * PER_WORKER : 2 * PER_WORKER + rows].reshape(BLOCK * rows, FULL)
    for dy in range(3):
        windows = [
            masked[dy : dy + BLOCK, dx * PER_WORKER : (dx + BLOCK) * PER_WORKER] for dx in range(3)
        ]
        window = jnp.concatenate([w.reshape(BLOCK * rows, HALF) for w in windows], axis=1)
        value = dot_tn(jnp.maximum(window, jnp.zeros_like(window)), grads) * scale
        for dx in range(3):
            emit(value[dx * HALF : (dx + 1) * HALF], outs, 0, 3 * dy + dx)
    return slots


def first_gradient(
    scale, outside, cot, masked, saved_other, weight, weight_other, saved, *refs
):
    outs, (total, pre, full) = refs[:-3], refs[-3:]
    full[...] = ordered(weight[...], weight_other[...], 1)
    spread(cot, full, total, PER_WORKER)
    for m in range(MIDDLE):
        other = jnp.where(outside(m), 0.0, saved_other[m].astype(F32)).astype(BF16)
        live = ordered(masked[m], other, 1).astype(F32) > 0
        value = jnp.where(live, total[m], 0.0)
        pre[m] = value.astype(BF16).reshape(MIDDLE, PER_WORKER, FULL)
    size = MIDDLE * MIDDLE * PER_WORKER
    grads = pre[...].reshape(size, FULL)
    for dy in range(3):
        windows = [saved[dy : dy + MIDDLE, dx : dx + MIDDLE] for dx in range(3)]
        window = jnp.concatenate([w.reshape(size, HALF) for w in windows], axis=1)
        value = dot_tn(window, grads) * scale
        for dx in range(3):
            emit(value[dx * HALF : (dx + 1) * HALF], outs, 1, 3 * dy + dx)


def owner_spread(tile, tile_other, second, second_other, out, total, cot, full):
    row, lane = iota((FULL, FULL), 0), iota((FULL, FULL), 1)
    turn = one_hot(lane == (row % TILE_BLOCKS) * BLOCK + row // TILE_BLOCKS)
    for u in range(BLOCK):
        block = jnp.concatenate(
            [ordered(tile[r, u], tile_other[r, u], 1) for r in range(TILE_ROWS)], axis=0
        )
        cot[u, 2 * TILE_BLOCKS : (2 + BLOCK) * TILE_BLOCKS] = dot(turn, block).astype(BF16)
    pad_sides(cot, TILE_BLOCKS)
    full[...] = ordered(second[...], second_other[...], 1)
    spread(cot, full, total, TILE_BLOCKS)
    out[...] = total[...].astype(BF16).reshape(out.shape)


def prepare(owners, columns, capacity, wide, permuted, routing, saved, *refs):
    (tile, tile_other, second, second_other, masked), refs = refs[:5], refs[5:]
    outs, (out, counts, table, total, cot, full) = refs[:-6], refs[-6:]
    pack_saved(owners, columns, capacity, wide, permuted, routing, saved, masked, *outs, counts, table)
    owner_spread(tile, tile_other, second, second_other, out, total, cot, full)


def worker(scale, owners, columns, capacity, permuted, routing, *refs):
    parts = 1 if not permuted else owners
    inputs, refs = refs[: 2 * parts], refs[2 * parts :]
    (masked, saved_other, weight, weight_other, source), refs = refs[:5], refs[5:]
    if permuted:
        refs, sent = refs[:-1], refs[-1]
    outs, (counts, cot, total, pre, full, saved, arrived) = refs[:-7], refs[-7:]
    if permuted:
        kept, near, far = outs
        outs = (kept, sent)
    fetch = pltpu.make_async_copy(source, saved, arrived)
    fetch.start()
    slots = second_gradient(
        scale, owners, capacity, permuted, routing, *inputs, masked, cot, *outs, counts
    )
    fetch.wait()
    first_gradient(
        scale, outside_image(slots, owners, columns), cot, masked, saved_other, weight, weight_other,
        saved, *outs, total, pre, full,
    )
    if permuted:
        near[...] = sent[:2]
        far[...] = sent[2:]


def adjacent(step):
    me = lax.axis_index("blk")
    return (me ^ step) == me - 1, (me ^ step) == me + 1


def owner_canvas(owners, capacity, wide, permuted, routing, *refs):
    parts = 1 if not permuted else owners
    got, got_other = views(refs[:parts], owners), views(refs[parts : 2 * parts], owners)
    total, first, canvas = refs[2 * parts : 2 * parts + 3]
    rims, (table, pre, grown) = refs[2 * parts + 3 : -3], refs[-3:]
    owner_table(routing, table, owners, capacity)
    size, into = wide * capacity, MIDDLE * TILE_BLOCKS
    row, lane = iota((size, into), 0), iota((size, into), 1)
    picks = []
    for step in range(owners):
        worker = partner("blk", step, permuted)
        target = jnp.full((size, into), DEAD, I32)
        for rank in range(capacity):
            target = jnp.where(row % capacity == rank, table[worker * capacity + rank], target)
        at = row // capacity
        hits = (lane == target + at * TILE_BLOCKS) & (at < MIDDLE)
        picks.append(jnp.where(hits, 1.0, 0.0))
    pick = jnp.concatenate(picks, axis=0).T.astype(BF16)
    for m in range(MIDDLE):
        block = jnp.concatenate(
            [ordered(got[w][m], got_other[w][m], 1) for w in range(owners)], axis=0
        )
        value = jnp.where(dot(pick, block) > 0, total[m].reshape(into, FULL).astype(F32), 0.0)
        pre[m, 2 * TILE_BLOCKS : 2 * TILE_BLOCKS + into] = value.astype(BF16)
    pad_sides(pre, TILE_BLOCKS)
    spread(pre, first, grown, TILE_BLOCKS)
    height, depth = TILE_ROWS * WIDE, OUTER * TILE_BLOCKS
    row, lane = iota((height, depth), 0), iota((height, depth), 1)
    at_row, at_col = row // WIDE, row % WIDE
    n, place = lane // TILE_BLOCKS, lane % TILE_BLOCKS
    column = (place % TILE_COLS) * BLOCK + n - 2
    column = jnp.where(column < 0, column + 36, column)
    fold = one_hot((at_row == place // TILE_COLS) & (at_col == column))
    canvas[...] = jnp.zeros_like(canvas)
    for m in range(0, OUTER, 2):
        pair = jnp.concatenate(
            [grown[m + k].astype(BF16) for k in range(2)], axis=1
        )
        laid = dot(fold, pair).reshape(TILE_ROWS, WIDE, FULL)
        for r in range(TILE_ROWS):
            for k in range(2):
                canvas[r * BLOCK + m + k] += laid[r, :, k * HALF : (k + 1) * HALF]
    for k, rim in enumerate(rims):
        above, below = adjacent(2 * k + 1)
        top = jnp.concatenate([canvas[0], canvas[1]], axis=1)
        bottom = jnp.concatenate([canvas[HIGH - 2], canvas[HIGH - 1]], axis=1)
        rim[:WIDE] = jnp.where(below, bottom, jnp.where(above, top, 0.0)).astype(BF16)
        rim[WIDE:] = jnp.zeros((RIM - WIDE, FULL), BF16)


def add_far(kept, got, *sends):
    for k, out in enumerate(sends):
        out[...] = (kept[2 + k] + got[k].astype(F32)).astype(BF16)


def add_near(kept, got, keep, send):
    keep[...] = kept[0] + got[0].astype(F32)
    send[...] = (kept[1] + got[1].astype(F32)).astype(BF16)


def add_workers(kept, got_3, got_2, got_1, rim_1, rim_3, out, out_1, out_3):
    value = kept[...]
    for part in (got_3, got_2, got_1):
        value = value + part[...].astype(F32)
    value = value.astype(BF16).reshape(PART, FULL)
    out[...] = value
    for message, rim in ((out_1, rim_1), (out_3, rim_3)):
        message[:PART] = value
        message[PART:] = rim[...]


def column_message(canvas, got_1, got_3, out, rim, strip):
    out[:PART] = got_3[:PART]
    for j in range(2):
        c = 32 + 2 * lax.axis_index("col") + j
        strip[...] = canvas[pl.ds(2 * WIDE + c, 64, stride=WIDE), :]
        for step, got in ((1, got_1), (3, got_3)):
            rim[...] = got[PART:].astype(F32)
            row = rim[pl.ds(c, 1), :]
            above, below = adjacent(step)
            top, bottom = jnp.where(above, row, 0.0), jnp.where(below, row, 0.0)
            strip[0:1] += top[:, :HALF]
            strip[1:2] += top[:, HALF:]
            strip[62:63] += bottom[:, :HALF]
            strip[63:64] += bottom[:, HALF:]
        out[PART:, j * HALF : (j + 1) * HALF] = strip[...].astype(BF16)


def close(tile, canvas, got_1, got_3, across, out, total):
    rows = TILE_ROWS * BLOCK * 32
    inner = canvas[2 : HIGH - 2, :32, :].reshape(rows, HALF)
    total[...] = tile[...].reshape(rows, HALF).astype(F32) + inner
    for step, got in ((1, got_1), (3, got_3)):
        rim = got[PART : PART + 32].astype(F32)
        above, below = adjacent(step)
        top, bottom = jnp.where(above, rim, 0.0), jnp.where(below, rim, 0.0)
        total[0:32] += top[:, :HALF]
        total[32:64] += top[:, HALF:]
        total[rows - 64 : rows - 32] += bottom[:, :HALF]
        total[rows - 32 : rows] += bottom[:, HALF:]
    strip = across[PART:].astype(F32)
    at = jnp.where(lax.axis_index("col") == 0, 30, 0)
    for j in range(2):
        spot = (pl.ds(at + j, 64, stride=32), slice(None))
        total[spot] = total[spot] + strip[:, j * HALF : (j + 1) * HALF]
    out[...] = total[...].astype(BF16).reshape(out.shape)


def rows_at(number):
    column = lax.axis_index("col")
    place = (column if number < 4 else 1 - column) * 4 + partner("blk", number % 4, True)
    return pl.ds(pl.multiple_of(place * ROWS, ROWS), ROWS)


def lay(*refs):
    for number, part in enumerate(refs[:-2]):
        value = part[:PART].astype(F32).reshape(2, 9, ROWS, FULL)
        for out, grad in zip(refs[-2:], (0, 1)):
            out[:, rows_at(number), :] = value[grad]


def finish(tile, canvas, got_1, got_3, last, late, old_0, old_1, out, out_0, out_1, total, laid, sems):
    copies = []
    for k, (number, part) in enumerate(((6, late), (7, last))):
        laid[k] = part[:PART].astype(F32).reshape(2, 9, ROWS, FULL)
        for grad, dest in enumerate((out_0, out_1)):
            copy = pltpu.make_async_copy(
                laid.at[k, grad], dest.at[:, rows_at(number), :], sems.at[k, grad]
            )
            copy.start()
            copies.append(copy)
    close(tile, canvas, got_1, got_3, last, out, total)
    for copy in copies:
        copy.wait()


def swap(value, axis="ch"):
    return lax.ppermute(value, axis, [(0, 1), (1, 0)])


def flip(value, axis, step):
    size = lax.axis_size(axis)
    return lax.ppermute(value, axis, [(i, i ^ step) for i in range(size)])


def neighbours(axis):
    size = lax.axis_size(axis)
    up = [(i, (i + 1) % size) for i in range(size - 1)]
    return up, [(j, i) for i, j in up]


def shards(grad_out, saved_input, saved_pre, first_weight, second_weight, assignment):
    owners = lax.axis_size("blk")
    columns = lax.axis_size("col")
    capacity = max(2, TILE_BLOCKS // owners)
    wide = MIDDLE if (MIDDLE * capacity) % 16 == 0 else 16
    scale = 1.0 / math.sqrt(owners * columns * PER_WORKER * BLOCK * BLOCK)
    permuted = owners == 4 and columns == 2
    parts = owners if permuted else 1
    routing = assignment[0]
    shape = jax.ShapeDtypeStruct
    tables = [pltpu.SMEM((owners * capacity + 1,), I32)]
    counts = [pltpu.SMEM((owners,), I32)]

    def pieces(*dims):
        return [shape(dims, BF16)] * owners if permuted else [shape((owners,) + dims, BF16)]

    def exchange(values):
        if permuted:
            return list(values[:1]) + [flip(values[k], "blk", k) for k in (3, 2, 1)][::-1]
        return [lax.all_to_all(values[0], "blk", split_axis=0, concat_axis=0, tiled=True)]

    tie = lax.optimization_barrier
    tile = grad_out.reshape(TILE_ROWS, BLOCK, TILE_COLS * BLOCK, HALF)
    second_other, tile_other = swap(second_weight), swap(tile)
    outgoing = call(
        functools.partial(pack_cotangents, owners, capacity, permuted),
        pieces(BLOCK, BLOCK * capacity, HALF),
        [SMEM, HBM], tables + [pltpu.VMEM(tile.shape, BF16), pltpu.SemaphoreType.DMA],
        (1, 1), "pack_cotangents",
    )(routing, pltpu.with_memory_space_constraint(tile, pltpu.HBM))
    saved_slots = saved_pre[0, 0].transpose(1, 2, 0, 3)
    saved_slots = saved_slots.reshape(MIDDLE, MIDDLE * PER_WORKER, HALF)
    outgoing, saved_here = tie((outgoing, saved_slots))
    saved_other = swap(saved_slots)
    incoming = exchange(outgoing)

    masked, *to_owners, total = call(
        functools.partial(prepare, owners, columns, capacity, wide, permuted),
        [shape((MIDDLE, MIDDLE * PER_WORKER, HALF), BF16)]
        + pieces(MIDDLE, wide * capacity, HALF)
        + [shape((MIDDLE, MIDDLE, TILE_BLOCKS, FULL), BF16)],
        [SMEM] + [VMEM] * 5,
        counts
        + tables
        + [
            pltpu.VMEM((MIDDLE, MIDDLE * TILE_BLOCKS, FULL), F32),
            pltpu.VMEM((BLOCK, OUTER * TILE_BLOCKS, FULL), BF16),
            pltpu.VMEM((9, FULL, FULL), BF16),
        ],
        (1, 1), "prepare",
    )(routing, saved_here, tile, tile_other, second_weight, second_other)
    incoming, to_owners, total = tie((incoming[::-1], to_owners[::-1], total))
    incoming, to_owners = incoming[::-1], to_owners[::-1]
    incoming_other = [swap(value) for value in incoming]
    at_owner = exchange(to_owners)

    saved_tiles = saved_input[0, 0].transpose(1, 2, 0, 3)
    if permuted:
        part = (2, 9, ROWS, FULL)
        halved = [shape((4,) + part, F32)] + [shape((2,) + part, BF16)] * 2
    else:
        halved = [shape((2, 9, HALF, FULL), F32)]
    terms = call(
        functools.partial(worker, scale, owners, columns, capacity, permuted),
        halved,
        [SMEM] + [VMEM] * (2 * parts + 4) + [HBM],
        counts
        + [
            pltpu.VMEM((BLOCK, OUTER * PER_WORKER, FULL), BF16),
            pltpu.VMEM((MIDDLE, MIDDLE * PER_WORKER, FULL), F32),
            pltpu.VMEM((MIDDLE, MIDDLE, PER_WORKER, FULL), BF16),
            pltpu.VMEM((9, FULL, FULL), BF16),
            pltpu.VMEM(saved_tiles.shape, BF16),
            pltpu.SemaphoreType.DMA,
        ]
        + ([pltpu.VMEM((4,) + part, BF16)] if permuted else []),
        (1, 1), "worker",
    )(
        routing, *incoming, *incoming_other, masked, saved_other, second_weight, second_other,
        pltpu.with_memory_space_constraint(saved_tiles, pltpu.HBM),
    )

    if permuted:
        kept, near, far = terms
        far, at_owner[2], at_owner[1] = tie((far, at_owner[2], at_owner[1]))

    def owner(at_owner):
        at_owner_other = [swap(value) for value in at_owner]
        return call(
            functools.partial(owner_canvas, owners, capacity, wide, permuted),
            [shape((HIGH, WIDE, HALF), F32)] + [shape((RIM, FULL), BF16)] * (2 if permuted else 0),
            [SMEM] + [VMEM] * (2 * len(at_owner) + 2),
            tables
            + [
                pltpu.VMEM((MIDDLE, (OUTER + 2) * TILE_BLOCKS, FULL), BF16),
                pltpu.VMEM((OUTER, OUTER * TILE_BLOCKS, HALF), F32),
            ],
            (1, 1), "owner_canvas",
        )(routing, *at_owner, *at_owner_other, total, first_weight)

    if permuted:
        far_got, near_got = swap(far, "col"), swap(near, "col")
        sends = call(add_far, [shape(part, BF16)] * 2, [VMEM] * 2, [], (1, 1), "add_far")(
            kept, far_got
        )
        sends, at_owner[3] = tie((sends[::-1], at_owner[3]))
        got = [flip(sends[0], "blk", 3), flip(sends[1], "blk", 2)]
        canvas, *rims = owner(at_owner)
        near_got, canvas = tie((near_got, canvas))
        keep, send = call(
            add_near, [shape(part, F32), shape(part, BF16)], [VMEM] * 2, [], (1, 1), "add_near",
        )(kept, near_got)
        got.append(flip(send, "blk", 1))
        message = shape((PART, FULL), BF16)
        wider = shape((PART + RIM, FULL), BF16)
        own, *wides = call(
            add_workers, [message, wider, wider], [VMEM] * 6, [], (1, 1), "add_workers",
        )(keep, *got, *rims)
        got_2, got_3, got_1 = flip(own, "blk", 2), flip(wides[1], "blk", 3), flip(wides[0], "blk", 1)
        across = [swap(value, "col") for value in (own, got_1[:PART], got_2)]
        got_3, got_2, got_1, across = tie((got_3, got_2, got_1, across))
        got = [got_1, got_2, got_3]
        last = call(
            column_message, shape((PART + 64, FULL), BF16), [VMEM] * 3,
            [pltpu.VMEM((RIM, FULL), F32), pltpu.VMEM((64, HALF), F32)],
            (1, 1), "column_message",
        )(canvas.reshape(HIGH * WIDE, HALF), got[0], got[2])
        across += [swap(last, "col")]
        early = call(
            lay, [shape((9, HALF, FULL), F32)] * 2, [VMEM] * 6, [], (1, 1), "lay",
        )(own, *got, *across[:2])
        grad_in, grad_second, grad_first = pl.pallas_call(
            finish,
            out_shape=[shape(grad_out.shape, BF16)] + [shape((9, HALF, FULL), F32)] * 2,
            in_specs=[VMEM] * 6 + [HBM] * 2,
            out_specs=[VMEM] + [HBM] * 2,
            scratch_shapes=[
                pltpu.VMEM((TILE_ROWS * BLOCK * 32, HALF), F32),
                pltpu.VMEM((2, 2, 9, ROWS, FULL), F32),
                pltpu.SemaphoreType.DMA((2, 2)),
            ],
            input_output_aliases={6: 1, 7: 2},
            compiler_params=pltpu.CompilerParams(vmem_limit_bytes=48 * 1024 * 1024),
            cost_estimate=pl.CostEstimate(flops=1, bytes_accessed=1, transcendentals=0),
            name="finish",
        )(grad_out, canvas, got[0], got[2], across[3], across[2], *early)
        return (grad_in, grad_first, grad_second)

    grad_first, grad_second = lax.psum((terms[0][1], terms[0][0]), ("blk", "col"))
    [canvas] = owner(at_owner)
    up, down = neighbours("blk")
    from_above = lax.ppermute(canvas[HIGH - 2 :].astype(BF16), "blk", up).astype(F32)
    from_below = lax.ppermute(canvas[:2].astype(BF16), "blk", down).astype(F32)
    inner = canvas[2 : HIGH - 2]
    inner = inner.at[:2].add(from_above).at[-2:].add(from_below)
    up, down = neighbours("col")
    from_left = lax.ppermute(inner[:, 32:34].astype(BF16), "col", up).astype(F32)
    from_right = lax.ppermute(inner[:, 34:36].astype(BF16), "col", down).astype(F32)
    inner = inner[:, :32].at[:, :2].add(from_left).at[:, -2:].add(from_right)
    grad_in = (grad_out.astype(F32) + inner).astype(BF16)
    return (grad_in, grad_first, grad_second)


def solution(mesh):
    return jax.shard_map(
        shards,
        mesh=mesh,
        in_specs=(
            P(("groups", "blk"), "col", "ch"),
            P(("groups", "col"), "blk", None, None, None, "ch"),
            P(("groups", "col"), "blk", None, None, None, "ch"),
            P(None, "ch", None),
            P(None, "ch", None),
            P(("groups", "col"), None, None),
        ),
        out_specs=(
            P(("groups", "blk"), "col", "ch"),
            P("groups", "ch", None),
            P("groups", "ch", None),
        ),
        check_vma=False,
    )
```

```python
import functools
import math

import jax
import jax.numpy as jnp
from jax import lax
from jax.experimental import pallas as pl
from jax.experimental.pallas import tpu as pltpu
from jax.sharding import PartitionSpec as P

BLOCK = 8
TILE_ROWS = 8
TILE_COLS = 4
TILE_BLOCKS = 32
PER_WORKER = 16
MIDDLE = 10
OUTER = 12
HALF = 128
FULL = 256
DEAD = -4096
HIGH = 68
RIM = 48
ROWS = 16
PART = 288
WIDE = 40

BF16 = jnp.bfloat16
F32 = jnp.float32
I32 = jnp.int32

VMEM = pl.BlockSpec(memory_space=pltpu.VMEM)
HBM = pl.BlockSpec(memory_space=pltpu.HBM)
SMEM = pl.BlockSpec(memory_space=pltpu.SMEM)


def call(body, outs, specs, scratch, cost, name):
    return pl.pallas_call(
        body,
        out_shape=outs,
        in_specs=specs,
        out_specs=jax.tree.map(lambda _: VMEM, outs),
        scratch_shapes=scratch,
        compiler_params=pltpu.CompilerParams(vmem_limit_bytes=48 * 1024 * 1024),
        cost_estimate=pl.CostEstimate(flops=cost[0], bytes_accessed=cost[1], transcendentals=0),
        name=name,
    )


def iota(shape, dim):
    return lax.broadcasted_iota(I32, shape, dim)


def one_hot(hits):
    return jnp.where(hits, 1.0, 0.0).astype(BF16)


def dot(a, b):
    return jnp.dot(a, b, preferred_element_type=F32)


def dot_nt(a, b):
    return lax.dot_general(a, b, (((1,), (1,)), ((), ())), preferred_element_type=F32)


def dot_tn(a, b):
    return lax.dot_general(a, b, (((0,), (0,)), ((), ())), preferred_element_type=F32)


def owner_table(routing, table, owners, capacity):
    me = lax.axis_index("blk")

    def clear(number, carry):
        table[number] = DEAD
        return carry

    lax.fori_loop(0, owners * capacity, clear, 0)

    def worker(number, carry):
        count = jnp.int32(0)
        for slot in range(PER_WORKER):
            code = routing[number, slot]
            hit = (code // TILE_BLOCKS) == me
            table[jnp.where(hit, number * capacity + count, owners * capacity)] = code % TILE_BLOCKS
            count = count + jnp.where(hit, 1, 0)
        return carry

    lax.fori_loop(0, owners, worker, 0)


def worker_codes(routing, counts, owners):
    me = lax.axis_index("blk")

    def clear(number, carry):
        counts[number] = 0
        return carry

    lax.fori_loop(0, owners, clear, 0)
    slots = []
    for slot in range(PER_WORKER):
        code = routing[me, slot]
        owner = code // TILE_BLOCKS
        rank = counts[owner]
        counts[owner] = rank + 1
        slots.append((owner, code % TILE_BLOCKS, rank))
    return slots


def views(refs, count):
    return list(refs) if len(refs) == count else [refs[0].at[k] for k in range(count)]


def partner(axis, step, permuted):
    return step ^ lax.axis_index(axis) if permuted else step


def pack_cotangents(owners, capacity, permuted, routing, source, *refs):
    outs, (table, tile, arrived) = refs[:-3], refs[-3:]
    fetch = pltpu.make_async_copy(source, tile, arrived)
    fetch.start()
    owner_table(routing, table, owners, capacity)
    rows = BLOCK * capacity
    row, lane = iota((rows, FULL), 0), iota((rows, FULL), 1)
    picks = []
    for step in range(owners):
        worker = partner("blk", step, permuted)
        target = jnp.full((rows, FULL), DEAD, I32)
        for rank in range(capacity):
            place = table[worker * capacity + rank] * BLOCK
            target = jnp.where(row % capacity == rank, place, target)
        picks.append(one_hot(lane == target + row // capacity))
    pick = jnp.concatenate(picks, axis=0)
    fetch.wait()
    for u in range(0, BLOCK, 2):
        pair = [
            jnp.concatenate([tile[r, u + k] for r in range(TILE_ROWS)], axis=0) for k in range(2)
        ]
        moved = dot(pick, jnp.concatenate(pair, axis=1)).astype(BF16)
        for step, out in enumerate(views(outs, owners)):
            part = moved[step * rows : (step + 1) * rows]
            out[u] = part[:, :HALF]
            out[u + 1] = part[:, HALF:]


def outside_image(slots, owners, columns):
    column = lax.axis_index("col")
    row = iota((MIDDLE * PER_WORKER, HALF), 0)
    flags = jnp.zeros_like(row)
    for slot, (owner, place, rank) in enumerate(slots):
        block_row, block_col = place // TILE_COLS, place % TILE_COLS
        flag = (
            jnp.where((owner == 0) & (block_row == 0), 1, 0)
            + jnp.where((owner == owners - 1) & (block_row == TILE_ROWS - 1), 2, 0)
            + jnp.where((column == 0) & (block_col == 0), 4, 0)
            + jnp.where((column == columns - 1) & (block_col == TILE_COLS - 1), 8, 0)
        )
        flags = jnp.where(row % PER_WORKER == slot, flag, flags)
    across = row // PER_WORKER
    sides = (((flags & 4) != 0) & (across == 0)) | (((flags & 8) != 0) & (across == MIDDLE - 1))

    def here(m):
        if m == 0:
            return sides | ((flags & 1) != 0)
        if m == MIDDLE - 1:
            return sides | ((flags & 2) != 0)
        return sides

    return here


def pack_saved(owners, columns, capacity, wide, permuted, routing, saved, masked, *refs):
    outs, counts, table = refs[:-2], refs[-2], refs[-1]

    def clear(number, carry):
        table[number] = DEAD
        return carry

    lax.fori_loop(0, owners * capacity, clear, 0)
    slots = worker_codes(routing, counts, owners)
    rows = MIDDLE * PER_WORKER
    for slot, (owner, place, rank) in enumerate(slots):
        table[owner * capacity + rank] = slot
    outside = outside_image(slots, owners, columns)
    for m in range(MIDDLE):
        masked[m] = jnp.where(outside(m), 0.0, saved[m].astype(F32)).astype(BF16)
    size = wide * capacity
    row, lane = iota((size, FULL), 0), iota((size, FULL), 1)
    picks = []
    for step in range(owners):
        owner = partner("blk", step, permuted)
        target = jnp.full((size, FULL), DEAD, I32)
        for rank in range(capacity):
            target = jnp.where(row % capacity == rank, table[owner * capacity + rank], target)
        at = row // capacity
        picks.append(one_hot((lane == target + at * PER_WORKER) & (at < MIDDLE)))
    pick = jnp.concatenate(picks, axis=0)
    filler = jnp.zeros((FULL - rows, FULL), BF16)
    for m in range(0, MIDDLE, 2):
        pair = jnp.concatenate([masked[m], masked[m + 1]], axis=1)
        moved = dot(pick, jnp.concatenate([pair, filler], axis=0)).astype(BF16)
        for step, out in enumerate(views(outs, owners)):
            part = moved[step * size : (step + 1) * size]
            out[m] = part[:, :HALF]
            out[m + 1] = part[:, HALF:]


def ordered(own, other, axis):
    first = lax.axis_index("ch") == 0
    return jnp.concatenate(
        [jnp.where(first, own, other), jnp.where(first, other, own)], axis=axis
    )


def deal(value, kept, sent, grad, tap):
    low, high = value[: HALF // 2], value[HALF // 2 :]
    mine = lax.axis_index("col") == 0
    keep, send = jnp.where(mine, low, high), jnp.where(mine, high, low).astype(BF16)
    for k in range(4):
        step, rows = partner("blk", k, True), slice(k * ROWS, (k + 1) * ROWS)
        kept[step, grad, tap] = keep[rows]
        sent[step, grad, tap] = send[rows]


def emit(value, outs, grad, tap):
    if len(outs) == 2:
        deal(value, outs[0], outs[1], grad, tap)
    else:
        outs[0][grad, tap] = value


def spread(values, weight, total, places):
    height, extent = values.shape[:2]
    inputs = values[...].reshape(height * extent, FULL)
    width = weight.shape[1]
    group = FULL // width
    total[...] = jnp.zeros_like(total)
    for tap in range(0, 9, group):
        taps = range(tap, min(tap + group, 9))
        part = dot_nt(inputs, jnp.concatenate([weight[k] for k in taps], axis=0))
        for k in taps:
            spot = (slice(k // 3, k // 3 + height), pl.ds(k % 3 * places, extent))
            here = part[:, (k - tap) * width : (k - tap + 1) * width]
            total[spot] = total[spot] + here.reshape(height, extent, width)


def second_gradient(scale, owners, capacity, permuted, routing, *refs):
    parts = 1 if not permuted else owners
    own, other = views(refs[:parts], owners), views(refs[parts : 2 * parts], owners)
    masked, cot = refs[2 * parts : 2 * parts + 2]
    outs, counts = refs[2 * parts + 2 : -1], refs[-1]
    slots = worker_codes(routing, counts, owners)
    rows, inner = BLOCK * PER_WORKER, owners * BLOCK * capacity
    row, lane = iota((rows, inner), 0), iota((rows, inner), 1)
    target = jnp.full((rows, inner), DEAD, I32)
    for slot, (owner, place, rank) in enumerate(slots):
        step = partner("blk", owner, permuted)
        target = jnp.where(row % PER_WORKER == slot, step * (BLOCK * capacity) + rank, target)
    pick = one_hot(lane == target + (row // PER_WORKER) * capacity)
    for u in range(BLOCK):
        got = jnp.concatenate(
            [ordered(own[o][u], other[o][u], 1) for o in range(owners)], axis=0
        )
        cot[u] = dot(pick, got).astype(BF16)
    grads = cot[...].reshape(BLOCK * rows, FULL)
    for dy in range(3):
        windows = [
            masked[dy : dy + BLOCK, dx * PER_WORKER : (dx + BLOCK) * PER_WORKER] for dx in range(3)
        ]
        window = jnp.concatenate([w.reshape(BLOCK * rows, HALF) for w in windows], axis=1)
        value = dot_tn(jnp.maximum(window, jnp.zeros_like(window)), grads) * scale
        for dx in range(3):
            emit(value[dx * HALF : (dx + 1) * HALF], outs, 0, 3 * dy + dx)
    return slots


def first_gradient(
    scale, outside, cot, masked, saved_other, weight, weight_other, saved, *refs
):
    outs, (total, pre, full) = refs[:-3], refs[-3:]
    full[...] = ordered(weight[...], weight_other[...], 1)
    spread(cot, full, total, PER_WORKER)
    for m in range(MIDDLE):
        other = jnp.where(outside(m), 0.0, saved_other[m].astype(F32)).astype(BF16)
        live = ordered(masked[m], other, 1).astype(F32) > 0
        value = jnp.where(live, total[m], 0.0)
        pre[m] = value.astype(BF16).reshape(MIDDLE, PER_WORKER, FULL)
    size = MIDDLE * MIDDLE * PER_WORKER
    grads = pre[...].reshape(size, FULL)
    for dy in range(3):
        windows = [saved[dy : dy + MIDDLE, dx : dx + MIDDLE] for dx in range(3)]
        window = jnp.concatenate([w.reshape(size, HALF) for w in windows], axis=1)
        value = dot_tn(window, grads) * scale
        for dx in range(3):
            emit(value[dx * HALF : (dx + 1) * HALF], outs, 1, 3 * dy + dx)


def owner_spread(tile, tile_other, second, second_other, out, total, cot, full):
    row, lane = iota((FULL, FULL), 0), iota((FULL, FULL), 1)
    turn = one_hot(lane == (row % TILE_BLOCKS) * BLOCK + row // TILE_BLOCKS)
    for u in range(BLOCK):
        block = jnp.concatenate(
            [ordered(tile[r, u], tile_other[r, u], 1) for r in range(TILE_ROWS)], axis=0
        )
        cot[u] = dot(turn, block).astype(BF16)
    full[...] = ordered(second[...], second_other[...], 1)
    spread(cot, full, total, TILE_BLOCKS)
    out[...] = total[...].astype(BF16).reshape(out.shape)


def prepare(owners, columns, capacity, wide, permuted, routing, saved, *refs):
    (tile, tile_other, second, second_other, masked), refs = refs[:5], refs[5:]
    outs, (out, counts, table, total, cot, full) = refs[:-6], refs[-6:]
    pack_saved(owners, columns, capacity, wide, permuted, routing, saved, masked, *outs, counts, table)
    owner_spread(tile, tile_other, second, second_other, out, total, cot, full)


def worker(scale, owners, columns, capacity, permuted, routing, *refs):
    parts = 1 if not permuted else owners
    inputs, refs = refs[: 2 * parts], refs[2 * parts :]
    (masked, saved_other, weight, weight_other, source), refs = refs[:5], refs[5:]
    if permuted:
        refs, sent = refs[:-1], refs[-1]
    outs, (counts, cot, total, pre, full, saved, arrived) = refs[:-7], refs[-7:]
    if permuted:
        kept, near, far = outs
        outs = (kept, sent)
    fetch = pltpu.make_async_copy(source, saved, arrived)
    fetch.start()
    slots = second_gradient(
        scale, owners, capacity, permuted, routing, *inputs, masked, cot, *outs, counts
    )
    fetch.wait()
    first_gradient(
        scale, outside_image(slots, owners, columns), cot, masked, saved_other, weight, weight_other,
        saved, *outs, total, pre, full,
    )
    if permuted:
        near[...] = sent[:2]
        far[...] = sent[2:]


def adjacent(step):
    me = lax.axis_index("blk")
    return (me ^ step) == me - 1, (me ^ step) == me + 1


def owner_canvas(owners, capacity, wide, permuted, routing, *refs):
    parts = 1 if not permuted else owners
    got, got_other = views(refs[:parts], owners), views(refs[parts : 2 * parts], owners)
    total, first, canvas = refs[2 * parts : 2 * parts + 3]
    rims, (table, pre, grown) = refs[2 * parts + 3 : -3], refs[-3:]
    owner_table(routing, table, owners, capacity)
    size, into = wide * capacity, MIDDLE * TILE_BLOCKS
    row, lane = iota((size, into), 0), iota((size, into), 1)
    picks = []
    for step in range(owners):
        worker = partner("blk", step, permuted)
        target = jnp.full((size, into), DEAD, I32)
        for rank in range(capacity):
            target = jnp.where(row % capacity == rank, table[worker * capacity + rank], target)
        at = row // capacity
        hits = (lane == target + at * TILE_BLOCKS) & (at < MIDDLE)
        picks.append(jnp.where(hits, 1.0, 0.0))
    pick = jnp.concatenate(picks, axis=0).T.astype(BF16)
    for m in range(MIDDLE):
        block = jnp.concatenate(
            [ordered(got[w][m], got_other[w][m], 1) for w in range(owners)], axis=0
        )
        value = jnp.where(dot(pick, block) > 0, total[m].reshape(into, FULL).astype(F32), 0.0)
        pre[m] = value.astype(BF16)
    spread(pre, first, grown, TILE_BLOCKS)
    height, depth = TILE_ROWS * WIDE, OUTER * TILE_BLOCKS
    row, lane = iota((height, depth), 0), iota((height, depth), 1)
    at_row, at_col = row // WIDE, row % WIDE
    n, place = lane // TILE_BLOCKS, lane % TILE_BLOCKS
    column = (place % TILE_COLS) * BLOCK + n - 2
    column = jnp.where(column < 0, column + 36, column)
    fold = one_hot((at_row == place // TILE_COLS) & (at_col == column))
    canvas[...] = jnp.zeros_like(canvas)
    for m in range(0, OUTER, 2):
        pair = jnp.concatenate(
            [grown[m + k].astype(BF16) for k in range(2)], axis=1
        )
        laid = dot(fold, pair).reshape(TILE_ROWS, WIDE, FULL)
        for r in range(TILE_ROWS):
            for k in range(2):
                canvas[r * BLOCK + m + k] += laid[r, :, k * HALF : (k + 1) * HALF]
    for k, rim in enumerate(rims):
        above, below = adjacent(2 * k + 1)
        top = jnp.concatenate([canvas[0], canvas[1]], axis=1)
        bottom = jnp.concatenate([canvas[HIGH - 2], canvas[HIGH - 1]], axis=1)
        rim[:WIDE] = jnp.where(below, bottom, jnp.where(above, top, 0.0)).astype(BF16)
        rim[WIDE:] = jnp.zeros((RIM - WIDE, FULL), BF16)


def add_far(kept, got, *sends):
    for k, out in enumerate(sends):
        out[...] = (kept[2 + k] + got[k].astype(F32)).astype(BF16)


def add_near(kept, got, keep, send):
    keep[...] = kept[0] + got[0].astype(F32)
    send[...] = (kept[1] + got[1].astype(F32)).astype(BF16)


def add_workers(kept, got_3, got_2, got_1, rim_1, rim_3, out, out_1, out_3):
    value = kept[...]
    for part in (got_3, got_2, got_1):
        value = value + part[...].astype(F32)
    value = value.astype(BF16).reshape(PART, FULL)
    out[...] = value
    for message, rim in ((out_1, rim_1), (out_3, rim_3)):
        message[:PART] = value
        message[PART:] = rim[...]


def column_message(canvas, got_1, got_3, out, rim, strip):
    out[:PART] = got_3[:PART]
    for j in range(2):
        c = 32 + 2 * lax.axis_index("col") + j
        strip[...] = canvas[pl.ds(2 * WIDE + c, 64, stride=WIDE), :]
        for step, got in ((1, got_1), (3, got_3)):
            rim[...] = got[PART:].astype(F32)
            row = rim[pl.ds(c, 1), :]
            above, below = adjacent(step)
            top, bottom = jnp.where(above, row, 0.0), jnp.where(below, row, 0.0)
            strip[0:1] += top[:, :HALF]
            strip[1:2] += top[:, HALF:]
            strip[62:63] += bottom[:, :HALF]
            strip[63:64] += bottom[:, HALF:]
        out[PART:, j * HALF : (j + 1) * HALF] = strip[...].astype(BF16)


def close(tile, canvas, got_1, got_3, across, out, total):
    rows = TILE_ROWS * BLOCK * 32
    inner = canvas[2 : HIGH - 2, :32, :].reshape(rows, HALF)
    total[...] = tile[...].reshape(rows, HALF).astype(F32) + inner
    for step, got in ((1, got_1), (3, got_3)):
        rim = got[PART : PART + 32].astype(F32)
        above, below = adjacent(step)
        top, bottom = jnp.where(above, rim, 0.0), jnp.where(below, rim, 0.0)
        total[0:32] += top[:, :HALF]
        total[32:64] += top[:, HALF:]
        total[rows - 64 : rows - 32] += bottom[:, :HALF]
        total[rows - 32 : rows] += bottom[:, HALF:]
    strip = across[PART:].astype(F32)
    at = jnp.where(lax.axis_index("col") == 0, 30, 0)
    for j in range(2):
        spot = (pl.ds(at + j, 64, stride=32), slice(None))
        total[spot] = total[spot] + strip[:, j * HALF : (j + 1) * HALF]
    out[...] = total[...].astype(BF16).reshape(out.shape)


def rows_at(number):
    column = lax.axis_index("col")
    place = (column if number < 4 else 1 - column) * 4 + partner("blk", number % 4, True)
    return pl.ds(pl.multiple_of(place * ROWS, ROWS), ROWS)


def lay(*refs):
    for number, part in enumerate(refs[:-2]):
        value = part[:PART].astype(F32).reshape(2, 9, ROWS, FULL)
        for out, grad in zip(refs[-2:], (0, 1)):
            out[:, rows_at(number), :] = value[grad]


def finish(tile, canvas, got_1, got_3, last, late, old_0, old_1, out, out_0, out_1, total, laid, sems):
    copies = []
    for k, (number, part) in enumerate(((6, late), (7, last))):
        laid[k] = part[:PART].astype(F32).reshape(2, 9, ROWS, FULL)
        for grad, dest in enumerate((out_0, out_1)):
            copy = pltpu.make_async_copy(
                laid.at[k, grad], dest.at[:, rows_at(number), :], sems.at[k, grad]
            )
            copy.start()
            copies.append(copy)
    close(tile, canvas, got_1, got_3, last, out, total)
    for copy in copies:
        copy.wait()


def swap(value, axis="ch"):
    return lax.ppermute(value, axis, [(0, 1), (1, 0)])


def flip(value, axis, step):
    size = lax.axis_size(axis)
    return lax.ppermute(value, axis, [(i, i ^ step) for i in range(size)])


def neighbours(axis):
    size = lax.axis_size(axis)
    up = [(i, (i + 1) % size) for i in range(size - 1)]
    return up, [(j, i) for i, j in up]


def shards(grad_out, saved_input, saved_pre, first_weight, second_weight, assignment):
    owners = lax.axis_size("blk")
    columns = lax.axis_size("col")
    capacity = max(2, TILE_BLOCKS // owners)
    wide = MIDDLE if (MIDDLE * capacity) % 16 == 0 else 16
    scale = 1.0 / math.sqrt(owners * columns * PER_WORKER * BLOCK * BLOCK)
    permuted = owners == 4 and columns == 2
    parts = owners if permuted else 1
    routing = assignment[0]
    shape = jax.ShapeDtypeStruct
    tables = [pltpu.SMEM((owners * capacity + 1,), I32)]
    counts = [pltpu.SMEM((owners,), I32)]

    def pieces(*dims):
        return [shape(dims, BF16)] * owners if permuted else [shape((owners,) + dims, BF16)]

    def exchange(values):
        if permuted:
            return list(values[:1]) + [flip(values[k], "blk", k) for k in (3, 2, 1)][::-1]
        return [lax.all_to_all(values[0], "blk", split_axis=0, concat_axis=0, tiled=True)]

    tie = lax.optimization_barrier
    tile = grad_out.reshape(TILE_ROWS, BLOCK, TILE_COLS * BLOCK, HALF)
    second_other, tile_other = swap(second_weight), swap(tile)
    outgoing = call(
        functools.partial(pack_cotangents, owners, capacity, permuted),
        pieces(BLOCK, BLOCK * capacity, HALF),
        [SMEM, HBM], tables + [pltpu.VMEM(tile.shape, BF16), pltpu.SemaphoreType.DMA],
        (1, 1), "pack_cotangents",
    )(routing, pltpu.with_memory_space_constraint(tile, pltpu.HBM))
    saved_slots = saved_pre[0, 0].transpose(1, 2, 0, 3)
    saved_slots = saved_slots.reshape(MIDDLE, MIDDLE * PER_WORKER, HALF)
    outgoing, saved_here = tie((outgoing, saved_slots))
    saved_other = swap(saved_slots)
    incoming = exchange(outgoing)

    masked, *to_owners, total = call(
        functools.partial(prepare, owners, columns, capacity, wide, permuted),
        [shape((MIDDLE, MIDDLE * PER_WORKER, HALF), BF16)]
        + pieces(MIDDLE, wide * capacity, HALF)
        + [shape((MIDDLE, MIDDLE, TILE_BLOCKS, FULL), BF16)],
        [SMEM] + [VMEM] * 5,
        counts
        + tables
        + [
            pltpu.VMEM((MIDDLE, MIDDLE * TILE_BLOCKS, FULL), F32),
            pltpu.VMEM((BLOCK, BLOCK * TILE_BLOCKS, FULL), BF16),
            pltpu.VMEM((9, FULL, FULL), BF16),
        ],
        (1, 1), "prepare",
    )(routing, saved_here, tile, tile_other, second_weight, second_other)
    incoming, to_owners, total = tie((incoming[::-1], to_owners[::-1], total))
    incoming, to_owners = incoming[::-1], to_owners[::-1]
    incoming_other = [swap(value) for value in incoming]
    at_owner = exchange(to_owners)

    saved_tiles = saved_input[0, 0].transpose(1, 2, 0, 3)
    if permuted:
        part = (2, 9, ROWS, FULL)
        halved = [shape((4,) + part, F32)] + [shape((2,) + part, BF16)] * 2
    else:
        halved = [shape((2, 9, HALF, FULL), F32)]
    terms = call(
        functools.partial(worker, scale, owners, columns, capacity, permuted),
        halved,
        [SMEM] + [VMEM] * (2 * parts + 4) + [HBM],
        counts
        + [
            pltpu.VMEM((BLOCK, BLOCK * PER_WORKER, FULL), BF16),
            pltpu.VMEM((MIDDLE, MIDDLE * PER_WORKER, FULL), F32),
            pltpu.VMEM((MIDDLE, MIDDLE, PER_WORKER, FULL), BF16),
            pltpu.VMEM((9, FULL, FULL), BF16),
            pltpu.VMEM(saved_tiles.shape, BF16),
            pltpu.SemaphoreType.DMA,
        ]
        + ([pltpu.VMEM((4,) + part, BF16)] if permuted else []),
        (1, 1), "worker",
    )(
        routing, *incoming, *incoming_other, masked, saved_other, second_weight, second_other,
        pltpu.with_memory_space_constraint(saved_tiles, pltpu.HBM),
    )

    if permuted:
        kept, near, far = terms
        far, at_owner[2], at_owner[1] = tie((far, at_owner[2], at_owner[1]))

    def owner(at_owner):
        at_owner_other = [swap(value) for value in at_owner]
        return call(
            functools.partial(owner_canvas, owners, capacity, wide, permuted),
            [shape((HIGH, WIDE, HALF), F32)] + [shape((RIM, FULL), BF16)] * (2 if permuted else 0),
            [SMEM] + [VMEM] * (2 * len(at_owner) + 2),
            tables
            + [
                pltpu.VMEM((MIDDLE, MIDDLE * TILE_BLOCKS, FULL), BF16),
                pltpu.VMEM((OUTER, OUTER * TILE_BLOCKS, HALF), F32),
            ],
            (1, 1), "owner_canvas",
        )(routing, *at_owner, *at_owner_other, total, first_weight)

    if permuted:
        far_got, near_got = swap(far, "col"), swap(near, "col")
        sends = call(add_far, [shape(part, BF16)] * 2, [VMEM] * 2, [], (1, 1), "add_far")(
            kept, far_got
        )
        sends, at_owner[3] = tie((sends[::-1], at_owner[3]))
        got = [flip(sends[0], "blk", 3), flip(sends[1], "blk", 2)]
        canvas, *rims = owner(at_owner)
        near_got, canvas = tie((near_got, canvas))
        keep, send = call(
            add_near, [shape(part, F32), shape(part, BF16)], [VMEM] * 2, [], (1, 1), "add_near",
        )(kept, near_got)
        got.append(flip(send, "blk", 1))
        message = shape((PART, FULL), BF16)
        wider = shape((PART + RIM, FULL), BF16)
        own, *wides = call(
            add_workers, [message, wider, wider], [VMEM] * 6, [], (1, 1), "add_workers",
        )(keep, *got, *rims)
        got_2, got_3, got_1 = flip(own, "blk", 2), flip(wides[1], "blk", 3), flip(wides[0], "blk", 1)
        across = [swap(value, "col") for value in (own, got_1[:PART])]
        got_3, got_2, got_1, across = tie((got_3, got_2, got_1, across))
        got = [got_1, got_2, got_3]
        last = call(
            column_message, shape((PART + 64, FULL), BF16), [VMEM] * 3,
            [pltpu.VMEM((RIM, FULL), F32), pltpu.VMEM((64, HALF), F32)],
            (1, 1), "column_message",
        )(canvas.reshape(HIGH * WIDE, HALF), got[0], got[2])
        across += [swap(got_2, "col"), swap(last, "col")]
        early = call(
            lay, [shape((9, HALF, FULL), F32)] * 2, [VMEM] * 6, [], (1, 1), "lay",
        )(own, *got, *across[:2])
        grad_in, grad_second, grad_first = pl.pallas_call(
            finish,
            out_shape=[shape(grad_out.shape, BF16)] + [shape((9, HALF, FULL), F32)] * 2,
            in_specs=[VMEM] * 6 + [HBM] * 2,
            out_specs=[VMEM] + [HBM] * 2,
            scratch_shapes=[
                pltpu.VMEM((TILE_ROWS * BLOCK * 32, HALF), F32),
                pltpu.VMEM((2, 2, 9, ROWS, FULL), F32),
                pltpu.SemaphoreType.DMA((2, 2)),
            ],
            input_output_aliases={6: 1, 7: 2},
            compiler_params=pltpu.CompilerParams(vmem_limit_bytes=48 * 1024 * 1024),
            cost_estimate=pl.CostEstimate(flops=1, bytes_accessed=1, transcendentals=0),
            name="finish",
        )(grad_out, canvas, got[0], got[2], across[3], across[2], *early)
        return (grad_in, grad_first, grad_second)

    grad_first, grad_second = lax.psum((terms[0][1], terms[0][0]), ("blk", "col"))
    [canvas] = owner(at_owner)
    up, down = neighbours("blk")
    from_above = lax.ppermute(canvas[HIGH - 2 :].astype(BF16), "blk", up).astype(F32)
    from_below = lax.ppermute(canvas[:2].astype(BF16), "blk", down).astype(F32)
    inner = canvas[2 : HIGH - 2]
    inner = inner.at[:2].add(from_above).at[-2:].add(from_below)
    up, down = neighbours("col")
    from_left = lax.ppermute(inner[:, 32:34].astype(BF16), "col", up).astype(F32)
    from_right = lax.ppermute(inner[:, 34:36].astype(BF16), "col", down).astype(F32)
    inner = inner[:, :32].at[:, :2].add(from_left).at[:, -2:].add(from_right)
    grad_in = (grad_out.astype(F32) + inner).astype(BF16)
    return (grad_in, grad_first, grad_second)


def solution(mesh):
    return jax.shard_map(
        shards,
        mesh=mesh,
        in_specs=(
            P(("groups", "blk"), "col", "ch"),
            P(("groups", "col"), "blk", None, None, None, "ch"),
            P(("groups", "col"), "blk", None, None, None, "ch"),
            P(None, "ch", None),
            P(None, "ch", None),
            P(("groups", "col"), None, None),
        ),
        out_specs=(
            P(("groups", "blk"), "col", "ch"),
            P("groups", "ch", None),
            P("groups", "ch", None),
        ),
        check_vma=False,
    )
```

```python
import functools
import math

import jax
import jax.numpy as jnp
from jax import lax
from jax.experimental import pallas as pl
from jax.experimental.pallas import tpu as pltpu
from jax.sharding import PartitionSpec as P

BLOCK = 8
TILE_ROWS = 8
TILE_COLS = 4
TILE_BLOCKS = 32
PER_WORKER = 16
MIDDLE = 10
OUTER = 12
HALF = 128
FULL = 256
DEAD = -4096
HIGH = 68
RIM = 48
ROWS = 16
PART = 288
WIDE = 40

BF16 = jnp.bfloat16
F32 = jnp.float32
I32 = jnp.int32

VMEM = pl.BlockSpec(memory_space=pltpu.VMEM)
HBM = pl.BlockSpec(memory_space=pltpu.HBM)
SMEM = pl.BlockSpec(memory_space=pltpu.SMEM)


def call(body, outs, specs, scratch, cost, name):
    return pl.pallas_call(
        body,
        out_shape=outs,
        in_specs=specs,
        out_specs=jax.tree.map(lambda _: VMEM, outs),
        scratch_shapes=scratch,
        compiler_params=pltpu.CompilerParams(vmem_limit_bytes=48 * 1024 * 1024),
        cost_estimate=pl.CostEstimate(flops=cost[0], bytes_accessed=cost[1], transcendentals=0),
        name=name,
    )


def iota(shape, dim):
    return lax.broadcasted_iota(I32, shape, dim)


def one_hot(hits):
    return jnp.where(hits, 1.0, 0.0).astype(BF16)


def dot(a, b):
    return jnp.dot(a, b, preferred_element_type=F32)


def dot_nt(a, b):
    return lax.dot_general(a, b, (((1,), (1,)), ((), ())), preferred_element_type=F32)


def dot_tn(a, b):
    return lax.dot_general(a, b, (((0,), (0,)), ((), ())), preferred_element_type=F32)


def owner_table(routing, table, owners, capacity):
    me = lax.axis_index("blk")

    def clear(number, carry):
        table[number] = DEAD
        return carry

    lax.fori_loop(0, owners * capacity, clear, 0)

    def worker(number, carry):
        count = jnp.int32(0)
        for slot in range(PER_WORKER):
            code = routing[number, slot]
            hit = (code // TILE_BLOCKS) == me
            table[jnp.where(hit, number * capacity + count, owners * capacity)] = code % TILE_BLOCKS
            count = count + jnp.where(hit, 1, 0)
        return carry

    lax.fori_loop(0, owners, worker, 0)


def worker_codes(routing, counts, owners):
    me = lax.axis_index("blk")

    def clear(number, carry):
        counts[number] = 0
        return carry

    lax.fori_loop(0, owners, clear, 0)
    slots = []
    for slot in range(PER_WORKER):
        code = routing[me, slot]
        owner = code // TILE_BLOCKS
        rank = counts[owner]
        counts[owner] = rank + 1
        slots.append((owner, code % TILE_BLOCKS, rank))
    return slots


def views(refs, count):
    return list(refs) if len(refs) == count else [refs[0].at[k] for k in range(count)]


def partner(axis, step, permuted):
    return step ^ lax.axis_index(axis) if permuted else step


def pack_cotangents(owners, capacity, permuted, routing, source, *refs):
    outs, (table, tile, arrived) = refs[:-3], refs[-3:]
    fetch = pltpu.make_async_copy(source, tile, arrived)
    fetch.start()
    owner_table(routing, table, owners, capacity)
    rows = BLOCK * capacity
    row, lane = iota((rows, FULL), 0), iota((rows, FULL), 1)
    picks = []
    for step in range(owners):
        worker = partner("blk", step, permuted)
        target = jnp.full((rows, FULL), DEAD, I32)
        for rank in range(capacity):
            place = table[worker * capacity + rank] * BLOCK
            target = jnp.where(row % capacity == rank, place, target)
        picks.append(one_hot(lane == target + row // capacity))
    pick = jnp.concatenate(picks, axis=0)
    fetch.wait()
    for u in range(0, BLOCK, 2):
        pair = [
            jnp.concatenate([tile[r, u + k] for r in range(TILE_ROWS)], axis=0) for k in range(2)
        ]
        moved = dot(pick, jnp.concatenate(pair, axis=1)).astype(BF16)
        for step, out in enumerate(views(outs, owners)):
            part = moved[step * rows : (step + 1) * rows]
            out[u] = part[:, :HALF]
            out[u + 1] = part[:, HALF:]


def outside_image(slots, owners, columns):
    column = lax.axis_index("col")
    row = iota((MIDDLE * PER_WORKER, HALF), 0)
    flags = jnp.zeros_like(row)
    for slot, (owner, place, rank) in enumerate(slots):
        block_row, block_col = place // TILE_COLS, place % TILE_COLS
        flag = (
            jnp.where((owner == 0) & (block_row == 0), 1, 0)
            + jnp.where((owner == owners - 1) & (block_row == TILE_ROWS - 1), 2, 0)
            + jnp.where((column == 0) & (block_col == 0), 4, 0)
            + jnp.where((column == columns - 1) & (block_col == TILE_COLS - 1), 8, 0)
        )
        flags = jnp.where(row % PER_WORKER == slot, flag, flags)
    across = row // PER_WORKER
    sides = (((flags & 4) != 0) & (across == 0)) | (((flags & 8) != 0) & (across == MIDDLE - 1))

    def here(m):
        if m == 0:
            return sides | ((flags & 1) != 0)
        if m == MIDDLE - 1:
            return sides | ((flags & 2) != 0)
        return sides

    return here


def pack_saved(owners, columns, capacity, wide, permuted, routing, saved, masked, *refs):
    outs, counts, table = refs[:-2], refs[-2], refs[-1]

    def clear(number, carry):
        table[number] = DEAD
        return carry

    lax.fori_loop(0, owners * capacity, clear, 0)
    slots = worker_codes(routing, counts, owners)
    rows = MIDDLE * PER_WORKER
    for slot, (owner, place, rank) in enumerate(slots):
        table[owner * capacity + rank] = slot
    outside = outside_image(slots, owners, columns)
    for m in range(MIDDLE):
        masked[m] = jnp.where(outside(m), 0.0, saved[m].astype(F32)).astype(BF16)
    size = wide * capacity
    row, lane = iota((size, FULL), 0), iota((size, FULL), 1)
    picks = []
    for step in range(owners):
        owner = partner("blk", step, permuted)
        target = jnp.full((size, FULL), DEAD, I32)
        for rank in range(capacity):
            target = jnp.where(row % capacity == rank, table[owner * capacity + rank], target)
        at = row // capacity
        picks.append(one_hot((lane == target + at * PER_WORKER) & (at < MIDDLE)))
    pick = jnp.concatenate(picks, axis=0)
    filler = jnp.zeros((FULL - rows, FULL), BF16)
    for m in range(0, MIDDLE, 2):
        pair = jnp.concatenate([masked[m], masked[m + 1]], axis=1)
        moved = dot(pick, jnp.concatenate([pair, filler], axis=0)).astype(BF16)
        for step, out in enumerate(views(outs, owners)):
            part = moved[step * size : (step + 1) * size]
            out[m] = part[:, :HALF]
            out[m + 1] = part[:, HALF:]


def ordered(own, other, axis):
    first = lax.axis_index("ch") == 0
    return jnp.concatenate(
        [jnp.where(first, own, other), jnp.where(first, other, own)], axis=axis
    )


def deal(value, kept, sent, grad, tap):
    low, high = value[: HALF // 2], value[HALF // 2 :]
    mine = lax.axis_index("col") == 0
    keep, send = jnp.where(mine, low, high), jnp.where(mine, high, low).astype(BF16)
    for k in range(4):
        step, rows = partner("blk", k, True), slice(k * ROWS, (k + 1) * ROWS)
        kept[step, grad, tap] = keep[rows]
        sent[step, grad, tap] = send[rows]


def emit(value, outs, grad, tap):
    if len(outs) == 2:
        deal(value, outs[0], outs[1], grad, tap)
    else:
        outs[0][grad, tap] = value


def weight_gradient(window, grads, scale, outs, grad):
    turned = grads.T
    for tap in range(0, 9, 2):
        taps = range(tap, min(tap + 2, 9))
        windows = [window(k) for k in taps]
        value = dot(turned, jnp.concatenate(windows, axis=1)).T * scale
        for k in taps:
            emit(value[(k - tap) * HALF : (k - tap + 1) * HALF], outs, grad, k)


def spread(values, weight, total, places):
    height, extent = values.shape[:2]
    inputs = values[...].reshape(height * extent, FULL)
    width = weight.shape[1]
    group = FULL // width
    total[...] = jnp.zeros_like(total)
    for tap in range(0, 9, group):
        taps = range(tap, min(tap + group, 9))
        part = dot_nt(inputs, jnp.concatenate([weight[k] for k in taps], axis=0))
        for k in taps:
            spot = (slice(k // 3, k // 3 + height), pl.ds(k % 3 * places, extent))
            here = part[:, (k - tap) * width : (k - tap + 1) * width]
            total[spot] = total[spot] + here.reshape(height, extent, width)


def second_gradient(scale, owners, capacity, permuted, routing, *refs):
    parts = 1 if not permuted else owners
    own, other = views(refs[:parts], owners), views(refs[parts : 2 * parts], owners)
    masked, cot = refs[2 * parts : 2 * parts + 2]
    outs, counts = refs[2 * parts + 2 : -1], refs[-1]
    slots = worker_codes(routing, counts, owners)
    rows, inner = BLOCK * PER_WORKER, owners * BLOCK * capacity
    row, lane = iota((rows, inner), 0), iota((rows, inner), 1)
    target = jnp.full((rows, inner), DEAD, I32)
    for slot, (owner, place, rank) in enumerate(slots):
        step = partner("blk", owner, permuted)
        target = jnp.where(row % PER_WORKER == slot, step * (BLOCK * capacity) + rank, target)
    pick = one_hot(lane == target + (row // PER_WORKER) * capacity)
    for u in range(BLOCK):
        got = jnp.concatenate(
            [ordered(own[o][u], other[o][u], 1) for o in range(owners)], axis=0
        )
        cot[u] = dot(pick, got).astype(BF16)
    def window(tap):
        dy, dx = tap // 3, tap % 3
        part = masked[dy : dy + BLOCK, dx * PER_WORKER : (dx + BLOCK) * PER_WORKER]
        return jnp.maximum(part, jnp.zeros_like(part)).reshape(BLOCK * rows, HALF)

    weight_gradient(window, cot[...].reshape(BLOCK * rows, FULL), scale, outs, 0)
    return slots


def first_gradient(
    scale, outside, cot, masked, saved_other, weight, weight_other, saved, *refs
):
    outs, (total, pre, full) = refs[:-3], refs[-3:]
    full[...] = ordered(weight[...], weight_other[...], 1)
    spread(cot, full, total, PER_WORKER)
    for m in range(MIDDLE):
        other = jnp.where(outside(m), 0.0, saved_other[m].astype(F32)).astype(BF16)
        live = ordered(masked[m], other, 1).astype(F32) > 0
        value = jnp.where(live, total[m], 0.0)
        pre[m] = value.astype(BF16).reshape(MIDDLE, PER_WORKER, FULL)
    size = MIDDLE * MIDDLE * PER_WORKER

    def window(tap):
        dy, dx = tap // 3, tap % 3
        return saved[dy : dy + MIDDLE, dx : dx + MIDDLE].reshape(size, HALF)

    weight_gradient(window, pre[...].reshape(size, FULL), scale, outs, 1)


def owner_spread(tile, tile_other, second, second_other, out, total, cot, full):
    row, lane = iota((FULL, FULL), 0), iota((FULL, FULL), 1)
    turn = one_hot(lane == (row % TILE_BLOCKS) * BLOCK + row // TILE_BLOCKS)
    for u in range(BLOCK):
        block = jnp.concatenate(
            [ordered(tile[r, u], tile_other[r, u], 1) for r in range(TILE_ROWS)], axis=0
        )
        cot[u] = dot(turn, block).astype(BF16)
    full[...] = ordered(second[...], second_other[...], 1)
    spread(cot, full, total, TILE_BLOCKS)
    out[...] = total[...].astype(BF16).reshape(out.shape)


def prepare(owners, columns, capacity, wide, permuted, routing, saved, *refs):
    (tile, tile_other, second, second_other, masked), refs = refs[:5], refs[5:]
    outs, (out, counts, table, total, cot, full) = refs[:-6], refs[-6:]
    pack_saved(owners, columns, capacity, wide, permuted, routing, saved, masked, *outs, counts, table)
    owner_spread(tile, tile_other, second, second_other, out, total, cot, full)


def worker(scale, owners, columns, capacity, permuted, routing, *refs):
    parts = 1 if not permuted else owners
    inputs, refs = refs[: 2 * parts], refs[2 * parts :]
    (masked, saved_other, weight, weight_other, source), refs = refs[:5], refs[5:]
    if permuted:
        refs, sent = refs[:-1], refs[-1]
    outs, (counts, cot, total, pre, full, saved, arrived) = refs[:-7], refs[-7:]
    if permuted:
        kept, near, far = outs
        outs = (kept, sent)
    fetch = pltpu.make_async_copy(source, saved, arrived)
    fetch.start()
    slots = second_gradient(
        scale, owners, capacity, permuted, routing, *inputs, masked, cot, *outs, counts
    )
    fetch.wait()
    first_gradient(
        scale, outside_image(slots, owners, columns), cot, masked, saved_other, weight, weight_other,
        saved, *outs, total, pre, full,
    )
    if permuted:
        near[...] = sent[:2]
        far[...] = sent[2:]


def adjacent(step):
    me = lax.axis_index("blk")
    return (me ^ step) == me - 1, (me ^ step) == me + 1


def owner_canvas(owners, capacity, wide, permuted, routing, *refs):
    parts = 1 if not permuted else owners
    got, got_other = views(refs[:parts], owners), views(refs[parts : 2 * parts], owners)
    total, first, canvas = refs[2 * parts : 2 * parts + 3]
    rims, (table, pre, grown) = refs[2 * parts + 3 : -3], refs[-3:]
    owner_table(routing, table, owners, capacity)
    size, into = wide * capacity, MIDDLE * TILE_BLOCKS
    row, lane = iota((size, into), 0), iota((size, into), 1)
    picks = []
    for step in range(owners):
        worker = partner("blk", step, permuted)
        target = jnp.full((size, into), DEAD, I32)
        for rank in range(capacity):
            target = jnp.where(row % capacity == rank, table[worker * capacity + rank], target)
        at = row // capacity
        hits = (lane == target + at * TILE_BLOCKS) & (at < MIDDLE)
        picks.append(jnp.where(hits, 1.0, 0.0))
    pick = jnp.concatenate(picks, axis=0).T.astype(BF16)
    for m in range(MIDDLE):
        block = jnp.concatenate(
            [ordered(got[w][m], got_other[w][m], 1) for w in range(owners)], axis=0
        )
        value = jnp.where(dot(pick, block) > 0, total[m].reshape(into, FULL).astype(F32), 0.0)
        pre[m] = value.astype(BF16)
    spread(pre, first, grown, TILE_BLOCKS)
    height, depth = TILE_ROWS * WIDE, OUTER * TILE_BLOCKS
    row, lane = iota((height, depth), 0), iota((height, depth), 1)
    at_row, at_col = row // WIDE, row % WIDE
    n, place = lane // TILE_BLOCKS, lane % TILE_BLOCKS
    column = (place % TILE_COLS) * BLOCK + n - 2
    column = jnp.where(column < 0, column + 36, column)
    fold = one_hot((at_row == place // TILE_COLS) & (at_col == column))
    canvas[...] = jnp.zeros_like(canvas)
    for m in range(0, OUTER, 2):
        pair = jnp.concatenate(
            [grown[m + k].astype(BF16) for k in range(2)], axis=1
        )
        laid = dot(fold, pair).reshape(TILE_ROWS, WIDE, FULL)
        for r in range(TILE_ROWS):
            for k in range(2):
                canvas[r * BLOCK + m + k] += laid[r, :, k * HALF : (k + 1) * HALF]
    for k, rim in enumerate(rims):
        above, below = adjacent(2 * k + 1)
        top = jnp.concatenate([canvas[0], canvas[1]], axis=1)
        bottom = jnp.concatenate([canvas[HIGH - 2], canvas[HIGH - 1]], axis=1)
        rim[:WIDE] = jnp.where(below, bottom, jnp.where(above, top, 0.0)).astype(BF16)
        rim[WIDE:] = jnp.zeros((RIM - WIDE, FULL), BF16)


def add_far(kept, got, *sends):
    for k, out in enumerate(sends):
        out[...] = (kept[2 + k] + got[k].astype(F32)).astype(BF16)


def add_near(kept, got, keep, send):
    keep[...] = kept[0] + got[0].astype(F32)
    send[...] = (kept[1] + got[1].astype(F32)).astype(BF16)


def add_workers(kept, got_3, got_2, got_1, rim_1, rim_3, out, out_1, out_3):
    value = kept[...]
    for part in (got_3, got_2, got_1):
        value = value + part[...].astype(F32)
    value = value.astype(BF16).reshape(PART, FULL)
    out[...] = value
    for message, rim in ((out_1, rim_1), (out_3, rim_3)):
        message[:PART] = value
        message[PART:] = rim[...]


def column_message(canvas, got_1, got_3, out, rim, strip):
    out[:PART] = got_3[:PART]
    for j in range(2):
        c = 32 + 2 * lax.axis_index("col") + j
        strip[...] = canvas[pl.ds(2 * WIDE + c, 64, stride=WIDE), :]
        for step, got in ((1, got_1), (3, got_3)):
            rim[...] = got[PART:].astype(F32)
            row = rim[pl.ds(c, 1), :]
            above, below = adjacent(step)
            top, bottom = jnp.where(above, row, 0.0), jnp.where(below, row, 0.0)
            strip[0:1] += top[:, :HALF]
            strip[1:2] += top[:, HALF:]
            strip[62:63] += bottom[:, :HALF]
            strip[63:64] += bottom[:, HALF:]
        out[PART:, j * HALF : (j + 1) * HALF] = strip[...].astype(BF16)


def gather_image(tile, canvas, got_1, got_3, total):
    rows = TILE_ROWS * BLOCK * 32
    total[...] = tile[...].astype(F32) + canvas[2 : HIGH - 2, :32, :].reshape(rows, HALF)
    for step, got in ((1, got_1), (3, got_3)):
        rim = got[PART : PART + 32].astype(F32)
        above, below = adjacent(step)
        top, bottom = jnp.where(above, rim, 0.0), jnp.where(below, rim, 0.0)
        total[0:32] += top[:, :HALF]
        total[32:64] += top[:, HALF:]
        total[rows - 64 : rows - 32] += bottom[:, :HALF]
        total[rows - 32 : rows] += bottom[:, HALF:]


def rows_at(number):
    column = lax.axis_index("col")
    place = (column if number < 4 else 1 - column) * 4 + partner("blk", number % 4, True)
    return pl.ds(pl.multiple_of(place * ROWS, ROWS), ROWS)


def lay(tile, canvas, *refs):
    parts, total, outs = refs[:-3], refs[-3], refs[-2:]
    gather_image(tile, canvas, parts[1], parts[3], total)
    for number, part in enumerate(parts):
        value = part[:PART].astype(F32).reshape(2, 9, ROWS, FULL)
        for out, grad in zip(outs, (0, 1)):
            out[:, rows_at(number), :] = value[grad]


def finish(early, last, late, old_0, old_1, out, out_0, out_1, total, laid, sems):
    copies = []
    for k, (number, part) in enumerate(((6, late), (7, last))):
        laid[k] = part[:PART].astype(F32).reshape(2, 9, ROWS, FULL)
        for grad, dest in enumerate((out_0, out_1)):
            copy = pltpu.make_async_copy(
                laid.at[k, grad], dest.at[:, rows_at(number), :], sems.at[k, grad]
            )
            copy.start()
            copies.append(copy)
    total[...] = early[...]
    strip = last[PART:].astype(F32)
    at = jnp.where(lax.axis_index("col") == 0, 30, 0)
    for j in range(2):
        spot = (pl.ds(at + j, 64, stride=32), slice(None))
        total[spot] = total[spot] + strip[:, j * HALF : (j + 1) * HALF]
    out[...] = total[...].astype(BF16)
    for copy in copies:
        copy.wait()


def swap(value, axis="ch"):
    return lax.ppermute(value, axis, [(0, 1), (1, 0)])


def flip(value, axis, step):
    size = lax.axis_size(axis)
    return lax.ppermute(value, axis, [(i, i ^ step) for i in range(size)])


def neighbours(axis):
    size = lax.axis_size(axis)
    up = [(i, (i + 1) % size) for i in range(size - 1)]
    return up, [(j, i) for i, j in up]


def shards(grad_out, saved_input, saved_pre, first_weight, second_weight, assignment):
    owners = lax.axis_size("blk")
    columns = lax.axis_size("col")
    capacity = max(2, TILE_BLOCKS // owners)
    wide = MIDDLE if (MIDDLE * capacity) % 16 == 0 else 16
    scale = 1.0 / math.sqrt(owners * columns * PER_WORKER * BLOCK * BLOCK)
    permuted = owners == 4 and columns == 2
    parts = owners if permuted else 1
    routing = assignment[0]
    shape = jax.ShapeDtypeStruct
    tables = [pltpu.SMEM((owners * capacity + 1,), I32)]
    counts = [pltpu.SMEM((owners,), I32)]

    def pieces(*dims):
        return [shape(dims, BF16)] * owners if permuted else [shape((owners,) + dims, BF16)]

    def exchange(values):
        if permuted:
            return list(values[:1]) + [flip(values[k], "blk", k) for k in (3, 2, 1)][::-1]
        return [lax.all_to_all(values[0], "blk", split_axis=0, concat_axis=0, tiled=True)]

    tie = lax.optimization_barrier
    tile = grad_out.reshape(TILE_ROWS, BLOCK, TILE_COLS * BLOCK, HALF)
    second_other, tile_other = swap(second_weight), swap(tile)
    outgoing = call(
        functools.partial(pack_cotangents, owners, capacity, permuted),
        pieces(BLOCK, BLOCK * capacity, HALF),
        [SMEM, HBM], tables + [pltpu.VMEM(tile.shape, BF16), pltpu.SemaphoreType.DMA],
        (1, 1), "pack_cotangents",
    )(routing, pltpu.with_memory_space_constraint(tile, pltpu.HBM))
    saved_slots = saved_pre[0, 0].transpose(1, 2, 0, 3)
    saved_slots = saved_slots.reshape(MIDDLE, MIDDLE * PER_WORKER, HALF)
    outgoing, saved_here = tie((outgoing, saved_slots))
    saved_other = swap(saved_here)
    incoming = exchange(outgoing)

    masked, *to_owners, total = call(
        functools.partial(prepare, owners, columns, capacity, wide, permuted),
        [shape((MIDDLE, MIDDLE * PER_WORKER, HALF), BF16)]
        + pieces(MIDDLE, wide * capacity, HALF)
        + [shape((MIDDLE, MIDDLE, TILE_BLOCKS, FULL), BF16)],
        [SMEM] + [VMEM] * 5,
        counts
        + tables
        + [
            pltpu.VMEM((MIDDLE, MIDDLE * TILE_BLOCKS, FULL), F32),
            pltpu.VMEM((BLOCK, BLOCK * TILE_BLOCKS, FULL), BF16),
            pltpu.VMEM((9, FULL, FULL), BF16),
        ],
        (1, 1), "prepare",
    )(routing, saved_here, tile, tile_other, second_weight, second_other)
    incoming, to_owners, total = tie((incoming[::-1], to_owners[::-1], total))
    incoming, to_owners = incoming[::-1], to_owners[::-1]
    incoming_other = [swap(value) for value in incoming]
    at_owner = exchange(to_owners)

    saved_tiles = saved_input[0, 0].transpose(1, 2, 0, 3)
    if permuted:
        part = (2, 9, ROWS, FULL)
        halved = [shape((4,) + part, F32)] + [shape((2,) + part, BF16)] * 2
    else:
        halved = [shape((2, 9, HALF, FULL), F32)]
    terms = call(
        functools.partial(worker, scale, owners, columns, capacity, permuted),
        halved,
        [SMEM] + [VMEM] * (2 * parts + 4) + [HBM],
        counts
        + [
            pltpu.VMEM((BLOCK, BLOCK * PER_WORKER, FULL), BF16),
            pltpu.VMEM((MIDDLE, MIDDLE * PER_WORKER, FULL), F32),
            pltpu.VMEM((MIDDLE, MIDDLE, PER_WORKER, FULL), BF16),
            pltpu.VMEM((9, FULL, FULL), BF16),
            pltpu.VMEM(saved_tiles.shape, BF16),
            pltpu.SemaphoreType.DMA,
        ]
        + ([pltpu.VMEM((4,) + part, BF16)] if permuted else []),
        (1, 1), "worker",
    )(
        routing, *incoming, *incoming_other, masked, saved_other, second_weight, second_other,
        pltpu.with_memory_space_constraint(saved_tiles, pltpu.HBM),
    )

    if permuted:
        kept, near, far = terms
        far, at_owner[2], at_owner[1] = tie((far, at_owner[2], at_owner[1]))

    def owner(at_owner, at_owner_other):
        at_owner_other += [swap(value) for value in at_owner[len(at_owner_other) :]]
        return call(
            functools.partial(owner_canvas, owners, capacity, wide, permuted),
            [shape((HIGH, WIDE, HALF), F32)] + [shape((RIM, FULL), BF16)] * (2 if permuted else 0),
            [SMEM] + [VMEM] * (2 * len(at_owner) + 2),
            tables
            + [
                pltpu.VMEM((MIDDLE, MIDDLE * TILE_BLOCKS, FULL), BF16),
                pltpu.VMEM((OUTER, OUTER * TILE_BLOCKS, HALF), F32),
            ],
            (1, 1), "owner_canvas",
        )(routing, *at_owner, *at_owner_other, total, first_weight)

    if permuted:
        others = [swap(value) for value in at_owner[:3]]
        near, others, far_got = tie((near, others, swap(far, "col")))
        near_got = swap(near, "col")
        sends = call(add_far, [shape(part, BF16)] * 2, [VMEM] * 2, [], (1, 1), "add_far")(
            kept, far_got
        )
        sends, at_owner[3] = tie((sends[::-1], at_owner[3]))
        got = [flip(sends[0], "blk", 3), flip(sends[1], "blk", 2)]
        canvas, *rims = owner(at_owner, others)
        near_got, canvas = tie((near_got, canvas))
        keep, send = call(
            add_near, [shape(part, F32), shape(part, BF16)], [VMEM] * 2, [], (1, 1), "add_near",
        )(kept, near_got)
        got.append(flip(send, "blk", 1))
        message = shape((PART, FULL), BF16)
        wider = shape((PART + RIM, FULL), BF16)
        own, *wides = call(
            add_workers, [message, wider, wider], [VMEM] * 6, [], (1, 1), "add_workers",
        )(keep, *got, *rims)
        got_2, got_3, got_1 = flip(own, "blk", 2), flip(wides[1], "blk", 3), flip(wides[0], "blk", 1)
        across = [swap(own, "col")]
        across.append(flip(across[0], "blk", 1))
        got_3, got_2, got_1, across = tie((got_3, got_2, got_1, across))
        got = [got_1, got_2, got_3]
        last = call(
            column_message, shape((PART + 64, FULL), BF16), [VMEM] * 3,
            [pltpu.VMEM((RIM, FULL), F32), pltpu.VMEM((64, HALF), F32)],
            (1, 1), "column_message",
        )(canvas.reshape(HIGH * WIDE, HALF), got[0], got[2])
        across += [swap(got_2, "col"), swap(last, "col")]
        flat = (TILE_ROWS * BLOCK * 32, HALF)
        early = call(
            lay, [shape(flat, F32)] + [shape((9, HALF, FULL), F32)] * 2, [VMEM] * 8, [], (1, 1),
            "lay",
        )(grad_out.reshape(flat), canvas, own, *got, *across[:2])
        grad_in, grad_second, grad_first = pl.pallas_call(
            finish,
            out_shape=[shape(flat, BF16)] + [shape((9, HALF, FULL), F32)] * 2,
            in_specs=[VMEM] * 3 + [HBM] * 2,
            out_specs=[VMEM] + [HBM] * 2,
            scratch_shapes=[
                pltpu.VMEM(flat, F32),
                pltpu.VMEM((2, 2, 9, ROWS, FULL), F32),
                pltpu.SemaphoreType.DMA((2, 2)),
            ],
            input_output_aliases={3: 1, 4: 2},
            compiler_params=pltpu.CompilerParams(vmem_limit_bytes=48 * 1024 * 1024),
            cost_estimate=pl.CostEstimate(flops=1, bytes_accessed=1, transcendentals=0),
            name="finish",
        )(early[0], across[3], across[2], *early[1:])
        grad_in = grad_in.reshape(grad_out.shape)
        return (grad_in, grad_first, grad_second)

    grad_first, grad_second = lax.psum((terms[0][1], terms[0][0]), ("blk", "col"))
    [canvas] = owner(at_owner, [])
    up, down = neighbours("blk")
    from_above = lax.ppermute(canvas[HIGH - 2 :].astype(BF16), "blk", up).astype(F32)
    from_below = lax.ppermute(canvas[:2].astype(BF16), "blk", down).astype(F32)
    inner = canvas[2 : HIGH - 2]
    inner = inner.at[:2].add(from_above).at[-2:].add(from_below)
    up, down = neighbours("col")
    from_left = lax.ppermute(inner[:, 32:34].astype(BF16), "col", up).astype(F32)
    from_right = lax.ppermute(inner[:, 34:36].astype(BF16), "col", down).astype(F32)
    inner = inner[:, :32].at[:, :2].add(from_left).at[:, -2:].add(from_right)
    grad_in = (grad_out.astype(F32) + inner).astype(BF16)
    return (grad_in, grad_first, grad_second)


def solution(mesh):
    return jax.shard_map(
        shards,
        mesh=mesh,
        in_specs=(
            P(("groups", "blk"), "col", "ch"),
            P(("groups", "col"), "blk", None, None, None, "ch"),
            P(("groups", "col"), "blk", None, None, None, "ch"),
            P(None, "ch", None),
            P(None, "ch", None),
            P(("groups", "col"), None, None),
        ),
        out_specs=(
            P(("groups", "blk"), "col", "ch"),
            P("groups", "ch", None),
            P("groups", "ch", None),
        ),
        check_vma=False,
    )
```

```python
import functools
import math

import jax
import jax.numpy as jnp
from jax import lax
from jax.experimental import pallas as pl
from jax.experimental.pallas import tpu as pltpu
from jax.sharding import PartitionSpec as P

BLOCK = 8
TILE_ROWS = 8
TILE_COLS = 4
TILE_BLOCKS = 32
PER_WORKER = 16
MIDDLE = 10
OUTER = 12
HALF = 128
FULL = 256
DEAD = -4096
HIGH = 68
RIM = 48
ROWS = 16
PART = 288
WIDE = 40

BF16 = jnp.bfloat16
F32 = jnp.float32
I32 = jnp.int32

VMEM = pl.BlockSpec(memory_space=pltpu.VMEM)
HBM = pl.BlockSpec(memory_space=pltpu.HBM)
SMEM = pl.BlockSpec(memory_space=pltpu.SMEM)


def call(body, outs, specs, scratch, cost, name):
    return pl.pallas_call(
        body,
        out_shape=outs,
        in_specs=specs,
        out_specs=jax.tree.map(lambda _: VMEM, outs),
        scratch_shapes=scratch,
        compiler_params=pltpu.CompilerParams(vmem_limit_bytes=48 * 1024 * 1024),
        cost_estimate=pl.CostEstimate(flops=cost[0], bytes_accessed=cost[1], transcendentals=0),
        name=name,
    )


def iota(shape, dim):
    return lax.broadcasted_iota(I32, shape, dim)


def one_hot(hits):
    return jnp.where(hits, 1.0, 0.0).astype(BF16)


def dot(a, b):
    return jnp.dot(a, b, preferred_element_type=F32)


def dot_nt(a, b):
    return lax.dot_general(a, b, (((1,), (1,)), ((), ())), preferred_element_type=F32)


def dot_tn(a, b):
    return lax.dot_general(a, b, (((0,), (0,)), ((), ())), preferred_element_type=F32)


def owner_table(routing, table, owners, capacity):
    me = lax.axis_index("blk")

    def clear(number, carry):
        table[number] = DEAD
        return carry

    lax.fori_loop(0, owners * capacity, clear, 0)

    def worker(number, carry):
        count = jnp.int32(0)
        for slot in range(PER_WORKER):
            code = routing[number, slot]
            hit = (code // TILE_BLOCKS) == me
            table[jnp.where(hit, number * capacity + count, owners * capacity)] = code % TILE_BLOCKS
            count = count + jnp.where(hit, 1, 0)
        return carry

    lax.fori_loop(0, owners, worker, 0)


def worker_codes(routing, counts, owners):
    me = lax.axis_index("blk")

    def clear(number, carry):
        counts[number] = 0
        return carry

    lax.fori_loop(0, owners, clear, 0)
    slots = []
    for slot in range(PER_WORKER):
        code = routing[me, slot]
        owner = code // TILE_BLOCKS
        rank = counts[owner]
        counts[owner] = rank + 1
        slots.append((owner, code % TILE_BLOCKS, rank))
    return slots


def views(refs, count):
    return list(refs) if len(refs) == count else [refs[0].at[k] for k in range(count)]


def partner(axis, step, permuted):
    return step ^ lax.axis_index(axis) if permuted else step


def pack_cotangents(owners, capacity, permuted, listed, source, *refs):
    outs, (table, tile, routing, arrived) = refs[:-4], refs[-4:]
    fetch = pltpu.make_async_copy(source, tile, arrived.at[0])
    fetch.start()
    lists = pltpu.make_async_copy(listed, routing, arrived.at[1])
    lists.start()
    lists.wait()
    owner_table(routing, table, owners, capacity)
    rows = BLOCK * capacity
    row, lane = iota((rows, FULL), 0), iota((rows, FULL), 1)
    picks = []
    for step in range(owners):
        worker = partner("blk", step, permuted)
        target = jnp.full((rows, FULL), DEAD, I32)
        for rank in range(capacity):
            place = table[worker * capacity + rank] * BLOCK
            target = jnp.where(row % capacity == rank, place, target)
        picks.append(one_hot(lane == target + row // capacity))
    pick = jnp.concatenate(picks, axis=0)
    fetch.wait()
    for u in range(0, BLOCK, 2):
        pair = [
            jnp.concatenate([tile[r, u + k] for r in range(TILE_ROWS)], axis=0) for k in range(2)
        ]
        moved = dot(pick, jnp.concatenate(pair, axis=1)).astype(BF16)
        for step, out in enumerate(views(outs, owners)):
            part = moved[step * rows : (step + 1) * rows]
            out[u] = part[:, :HALF]
            out[u + 1] = part[:, HALF:]


def outside_image(slots, owners, columns):
    column = lax.axis_index("col")
    row = iota((MIDDLE * PER_WORKER, HALF), 0)
    flags = jnp.zeros_like(row)
    for slot, (owner, place, rank) in enumerate(slots):
        block_row, block_col = place // TILE_COLS, place % TILE_COLS
        flag = (
            jnp.where((owner == 0) & (block_row == 0), 1, 0)
            + jnp.where((owner == owners - 1) & (block_row == TILE_ROWS - 1), 2, 0)
            + jnp.where((column == 0) & (block_col == 0), 4, 0)
            + jnp.where((column == columns - 1) & (block_col == TILE_COLS - 1), 8, 0)
        )
        flags = jnp.where(row % PER_WORKER == slot, flag, flags)
    across = row // PER_WORKER
    sides = (((flags & 4) != 0) & (across == 0)) | (((flags & 8) != 0) & (across == MIDDLE - 1))

    def here(m):
        if m == 0:
            return sides | ((flags & 1) != 0)
        if m == MIDDLE - 1:
            return sides | ((flags & 2) != 0)
        return sides

    return here


def pack_saved(owners, columns, capacity, wide, permuted, routing, saved, masked, *refs):
    outs, counts, table = refs[:-2], refs[-2], refs[-1]

    def clear(number, carry):
        table[number] = DEAD
        return carry

    lax.fori_loop(0, owners * capacity, clear, 0)
    slots = worker_codes(routing, counts, owners)
    rows = MIDDLE * PER_WORKER
    for slot, (owner, place, rank) in enumerate(slots):
        table[owner * capacity + rank] = slot
    outside = outside_image(slots, owners, columns)
    for m in range(MIDDLE):
        masked[m] = jnp.where(outside(m), 0.0, saved[m].astype(F32)).astype(BF16)
    size = wide * capacity
    row, lane = iota((size, FULL), 0), iota((size, FULL), 1)
    picks = []
    for step in range(owners):
        owner = partner("blk", step, permuted)
        target = jnp.full((size, FULL), DEAD, I32)
        for rank in range(capacity):
            target = jnp.where(row % capacity == rank, table[owner * capacity + rank], target)
        at = row // capacity
        picks.append(one_hot((lane == target + at * PER_WORKER) & (at < MIDDLE)))
    pick = jnp.concatenate(picks, axis=0)
    filler = jnp.zeros((FULL - rows, FULL), BF16)
    for m in range(0, MIDDLE, 2):
        pair = jnp.concatenate([masked[m], masked[m + 1]], axis=1)
        moved = dot(pick, jnp.concatenate([pair, filler], axis=0)).astype(BF16)
        for step, out in enumerate(views(outs, owners)):
            part = moved[step * size : (step + 1) * size]
            out[m] = part[:, :HALF]
            out[m + 1] = part[:, HALF:]


def ordered(own, other, axis):
    first = lax.axis_index("ch") == 0
    return jnp.concatenate(
        [jnp.where(first, own, other), jnp.where(first, other, own)], axis=axis
    )


def deal(value, kept, sent, grad, tap):
    low, high = value[: HALF // 2], value[HALF // 2 :]
    mine = lax.axis_index("col") == 0
    keep, send = jnp.where(mine, low, high), jnp.where(mine, high, low).astype(BF16)
    for k in range(4):
        step, rows = partner("blk", k, True), slice(k * ROWS, (k + 1) * ROWS)
        kept[step, grad, tap] = keep[rows]
        sent[step, grad, tap] = send[rows]


def emit(value, outs, grad, tap):
    if len(outs) == 2:
        deal(value, outs[0], outs[1], grad, tap)
    else:
        outs[0][grad, tap] = value


def spread(values, weight, total, places):
    height, extent = values.shape[:2]
    inputs = values[...].reshape(height * extent, FULL)
    width, step = weight.shape[1], places
    for dy in range(3):
        taps = jnp.concatenate([weight[3 * dy + dx] for dx in range(3)], axis=0)
        part = dot_nt(inputs, taps).reshape(height, extent, 3 * width)
        p, q, r = [part[:, :, dx * width : (dx + 1) * width] for dx in range(3)]
        sums = [
            p[:, :step],
            p[:, step : 2 * step] + q[:, :step],
            p[:, 2 * step :] + q[:, step : extent - step] + r[:, : extent - 2 * step],
            q[:, extent - step :] + r[:, extent - 2 * step : extent - step],
            r[:, extent - step :],
        ]
        at = 0
        for value in sums:
            size = value.shape[1]
            here = slice(at, at + size)
            if dy == 0:
                total[:height, here] = value
            else:
                total[dy : dy + height - 1, here] += value[:-1]
                total[dy + height - 1, here] = value[height - 1]
            at += size


def second_gradient(scale, owners, capacity, permuted, routing, *refs):
    parts = 1 if not permuted else owners
    own, other = views(refs[:parts], owners), views(refs[parts : 2 * parts], owners)
    masked, cot = refs[2 * parts : 2 * parts + 2]
    outs, counts = refs[2 * parts + 2 : -1], refs[-1]
    slots = worker_codes(routing, counts, owners)
    rows, inner = BLOCK * PER_WORKER, owners * BLOCK * capacity
    row, lane = iota((rows, inner), 0), iota((rows, inner), 1)
    target = jnp.full((rows, inner), DEAD, I32)
    for slot, (owner, place, rank) in enumerate(slots):
        step = partner("blk", owner, permuted)
        target = jnp.where(row % PER_WORKER == slot, step * (BLOCK * capacity) + rank, target)
    pick = one_hot(lane == target + (row // PER_WORKER) * capacity)
    for u in range(BLOCK):
        got = jnp.concatenate(
            [ordered(own[o][u], other[o][u], 1) for o in range(owners)], axis=0
        )
        cot[u] = dot(pick, got).astype(BF16)
    grads = cot[...].reshape(BLOCK * rows, FULL)
    for dy in range(3):
        windows = [
            masked[dy : dy + BLOCK, dx * PER_WORKER : (dx + BLOCK) * PER_WORKER] for dx in range(3)
        ]
        window = jnp.concatenate([w.reshape(BLOCK * rows, HALF) for w in windows], axis=1)
        value = dot_tn(jnp.maximum(window, jnp.zeros_like(window)), grads) * scale
        for dx in range(3):
            emit(value[dx * HALF : (dx + 1) * HALF], outs, 0, 3 * dy + dx)
    return slots


def first_gradient(
    scale, outside, cot, masked, saved_other, weight, weight_other, saved, *refs
):
    outs, (total, pre, full) = refs[:-3], refs[-3:]
    full[...] = ordered(weight[...], weight_other[...], 1)
    spread(cot, full, total, PER_WORKER)
    for m in range(MIDDLE):
        other = jnp.where(outside(m), 0.0, saved_other[m].astype(F32)).astype(BF16)
        live = ordered(masked[m], other, 1).astype(F32) > 0
        value = jnp.where(live, total[m], 0.0)
        pre[m] = value.astype(BF16).reshape(MIDDLE, PER_WORKER, FULL)
    size = MIDDLE * MIDDLE * PER_WORKER
    grads = pre[...].reshape(size, FULL)
    for dy in range(3):
        windows = [saved[dy : dy + MIDDLE, dx : dx + MIDDLE] for dx in range(3)]
        window = jnp.concatenate([w.reshape(size, HALF) for w in windows], axis=1)
        value = dot_tn(window, grads) * scale
        for dx in range(3):
            emit(value[dx * HALF : (dx + 1) * HALF], outs, 1, 3 * dy + dx)


def owner_spread(tile, tile_other, second, second_other, out, total, cot, full):
    row, lane = iota((FULL, FULL), 0), iota((FULL, FULL), 1)
    turn = one_hot(lane == (row % TILE_BLOCKS) * BLOCK + row // TILE_BLOCKS)
    for u in range(BLOCK):
        block = jnp.concatenate(
            [ordered(tile[r, u], tile_other[r, u], 1) for r in range(TILE_ROWS)], axis=0
        )
        cot[u] = dot(turn, block).astype(BF16)
    full[...] = ordered(second[...], second_other[...], 1)
    spread(cot, full, total, TILE_BLOCKS)
    out[...] = total[...].astype(BF16).reshape(out.shape)


def prepare(owners, columns, capacity, wide, permuted, routing, saved, *refs):
    (tile, tile_other, second, second_other, masked), refs = refs[:5], refs[5:]
    outs, (out, counts, table, total, cot, full) = refs[:-6], refs[-6:]
    pack_saved(owners, columns, capacity, wide, permuted, routing, saved, masked, *outs, counts, table)
    owner_spread(tile, tile_other, second, second_other, out, total, cot, full)


def worker(scale, owners, columns, capacity, permuted, routing, *refs):
    parts = 1 if not permuted else owners
    inputs, refs = refs[: 2 * parts], refs[2 * parts :]
    (masked, saved_other, weight, weight_other, source), refs = refs[:5], refs[5:]
    if permuted:
        refs, sent = refs[:-1], refs[-1]
    outs, (counts, cot, total, pre, full, saved, arrived) = refs[:-7], refs[-7:]
    if permuted:
        kept, near, far = outs
        outs = (kept, sent)
    fetch = pltpu.make_async_copy(source, saved, arrived)
    fetch.start()
    slots = second_gradient(
        scale, owners, capacity, permuted, routing, *inputs, masked, cot, *outs, counts
    )
    fetch.wait()
    first_gradient(
        scale, outside_image(slots, owners, columns), cot, masked, saved_other, weight, weight_other,
        saved, *outs, total, pre, full,
    )
    if permuted:
        near[...] = sent[:2]
        far[...] = sent[2:]


def adjacent(step):
    me = lax.axis_index("blk")
    return (me ^ step) == me - 1, (me ^ step) == me + 1


def owner_canvas(owners, capacity, wide, permuted, routing, *refs):
    parts = 1 if not permuted else owners
    got, got_other = views(refs[:parts], owners), views(refs[parts : 2 * parts], owners)
    total, first, canvas = refs[2 * parts : 2 * parts + 3]
    rims, (table, pre, grown) = refs[2 * parts + 3 : -3], refs[-3:]
    owner_table(routing, table, owners, capacity)
    size, into = wide * capacity, MIDDLE * TILE_BLOCKS
    row, lane = iota((size, into), 0), iota((size, into), 1)
    picks = []
    for step in range(owners):
        worker = partner("blk", step, permuted)
        target = jnp.full((size, into), DEAD, I32)
        for rank in range(capacity):
            target = jnp.where(row % capacity == rank, table[worker * capacity + rank], target)
        at = row // capacity
        hits = (lane == target + at * TILE_BLOCKS) & (at < MIDDLE)
        picks.append(jnp.where(hits, 1.0, 0.0))
    pick = jnp.concatenate(picks, axis=0).T.astype(BF16)
    for m in range(MIDDLE):
        block = jnp.concatenate(
            [ordered(got[w][m], got_other[w][m], 1) for w in range(owners)], axis=0
        )
        value = jnp.where(dot(pick, block) > 0, total[m].reshape(into, FULL).astype(F32), 0.0)
        pre[m] = value.astype(BF16)
    spread(pre, first, grown, TILE_BLOCKS)
    height, depth = TILE_ROWS * WIDE, OUTER * TILE_BLOCKS
    row, lane = iota((height, depth), 0), iota((height, depth), 1)
    at_row, at_col = row // WIDE, row % WIDE
    n, place = lane // TILE_BLOCKS, lane % TILE_BLOCKS
    column = (place % TILE_COLS) * BLOCK + n - 2
    column = jnp.where(column < 0, column + 36, column)
    fold = one_hot((at_row == place // TILE_COLS) & (at_col == column))
    canvas[...] = jnp.zeros_like(canvas)
    for m in range(0, OUTER, 2):
        pair = jnp.concatenate(
            [grown[m + k].astype(BF16) for k in range(2)], axis=1
        )
        laid = dot(fold, pair).reshape(TILE_ROWS, WIDE, FULL)
        for r in range(TILE_ROWS):
            for k in range(2):
                canvas[r * BLOCK + m + k] += laid[r, :, k * HALF : (k + 1) * HALF]
    for k, rim in enumerate(rims):
        above, below = adjacent(2 * k + 1)
        top = jnp.concatenate([canvas[0], canvas[1]], axis=1)
        bottom = jnp.concatenate([canvas[HIGH - 2], canvas[HIGH - 1]], axis=1)
        rim[:WIDE] = jnp.where(below, bottom, jnp.where(above, top, 0.0)).astype(BF16)
        rim[WIDE:] = jnp.zeros((RIM - WIDE, FULL), BF16)


def add_far(kept, got, *sends):
    for k, out in enumerate(sends):
        out[...] = (kept[2 + k] + got[k].astype(F32)).astype(BF16)


def add_near(kept, got, keep, send):
    keep[...] = kept[0] + got[0].astype(F32)
    send[...] = (kept[1] + got[1].astype(F32)).astype(BF16)


def add_workers(kept, got_3, got_2, got_1, rim_1, rim_3, out, out_1, out_3):
    value = kept[...]
    for part in (got_3, got_2, got_1):
        value = value + part[...].astype(F32)
    value = value.astype(BF16).reshape(PART, FULL)
    out[...] = value
    for message, rim in ((out_1, rim_1), (out_3, rim_3)):
        message[:PART] = value
        message[PART:] = rim[...]


def column_message(canvas, got_1, got_3, out, rim, strip):
    out[:PART] = got_3[:PART]
    for j in range(2):
        c = 32 + 2 * lax.axis_index("col") + j
        strip[...] = canvas[pl.ds(2 * WIDE + c, 64, stride=WIDE), :]
        for step, got in ((1, got_1), (3, got_3)):
            rim[...] = got[PART:].astype(F32)
            row = rim[pl.ds(c, 1), :]
            above, below = adjacent(step)
            top, bottom = jnp.where(above, row, 0.0), jnp.where(below, row, 0.0)
            strip[0:1] += top[:, :HALF]
            strip[1:2] += top[:, HALF:]
            strip[62:63] += bottom[:, :HALF]
            strip[63:64] += bottom[:, HALF:]
        out[PART:, j * HALF : (j + 1) * HALF] = strip[...].astype(BF16)


def close(tile, canvas, got_1, got_3, across, out, total):
    rows = TILE_ROWS * BLOCK * 32
    inner = canvas[2 : HIGH - 2, :32, :].reshape(rows, HALF)
    total[...] = tile[...].reshape(rows, HALF).astype(F32) + inner
    for step, got in ((1, got_1), (3, got_3)):
        rim = got[PART : PART + 32].astype(F32)
        above, below = adjacent(step)
        top, bottom = jnp.where(above, rim, 0.0), jnp.where(below, rim, 0.0)
        total[0:32] += top[:, :HALF]
        total[32:64] += top[:, HALF:]
        total[rows - 64 : rows - 32] += bottom[:, :HALF]
        total[rows - 32 : rows] += bottom[:, HALF:]
    strip = across[PART:].astype(F32)
    at = jnp.where(lax.axis_index("col") == 0, 30, 0)
    for j in range(2):
        spot = (pl.ds(at + j, 64, stride=32), slice(None))
        total[spot] = total[spot] + strip[:, j * HALF : (j + 1) * HALF]
    out[...] = total[...].astype(BF16).reshape(out.shape)


def rows_at(number):
    column = lax.axis_index("col")
    place = (column if number < 4 else 1 - column) * 4 + partner("blk", number % 4, True)
    return pl.ds(pl.multiple_of(place * ROWS, ROWS), ROWS)


def lay(*refs):
    for number, part in enumerate(refs[:-2]):
        value = part[:PART].astype(F32).reshape(2, 9, ROWS, FULL)
        for out, grad in zip(refs[-2:], (0, 1)):
            out[:, rows_at(number), :] = value[grad]


def finish(tile, canvas, got_1, got_3, last, late, old_0, old_1, out, out_0, out_1, total, laid, sems):
    copies = []
    for k, (number, part) in enumerate(((6, late), (7, last))):
        laid[k] = part[:PART].astype(F32).reshape(2, 9, ROWS, FULL)
        for grad, dest in enumerate((out_0, out_1)):
            copy = pltpu.make_async_copy(
                laid.at[k, grad], dest.at[:, rows_at(number), :], sems.at[k, grad]
            )
            copy.start()
            copies.append(copy)
    close(tile, canvas, got_1, got_3, last, out, total)
    for copy in copies:
        copy.wait()


def swap(value, axis="ch"):
    return lax.ppermute(value, axis, [(0, 1), (1, 0)])


def flip(value, axis, step):
    size = lax.axis_size(axis)
    return lax.ppermute(value, axis, [(i, i ^ step) for i in range(size)])


def neighbours(axis):
    size = lax.axis_size(axis)
    up = [(i, (i + 1) % size) for i in range(size - 1)]
    return up, [(j, i) for i, j in up]


def shards(grad_out, saved_input, saved_pre, first_weight, second_weight, assignment):
    owners = lax.axis_size("blk")
    columns = lax.axis_size("col")
    capacity = max(2, TILE_BLOCKS // owners)
    wide = MIDDLE if (MIDDLE * capacity) % 16 == 0 else 16
    scale = 1.0 / math.sqrt(owners * columns * PER_WORKER * BLOCK * BLOCK)
    permuted = owners == 4 and columns == 2
    parts = owners if permuted else 1
    routing = assignment[0]
    shape = jax.ShapeDtypeStruct
    tables = [pltpu.SMEM((owners * capacity + 1,), I32)]
    counts = [pltpu.SMEM((owners,), I32)]

    def pieces(*dims):
        return [shape(dims, BF16)] * owners if permuted else [shape((owners,) + dims, BF16)]

    def exchange(values):
        if permuted:
            return list(values[:1]) + [flip(values[k], "blk", k) for k in (3, 2, 1)][::-1]
        return [lax.all_to_all(values[0], "blk", split_axis=0, concat_axis=0, tiled=True)]

    tie = lax.optimization_barrier
    tile = grad_out.reshape(TILE_ROWS, BLOCK, TILE_COLS * BLOCK, HALF)
    second_other, tile_other = swap(second_weight), swap(tile)
    outgoing = call(
        functools.partial(pack_cotangents, owners, capacity, permuted),
        pieces(BLOCK, BLOCK * capacity, HALF),
        [HBM, HBM],
        tables
        + [
            pltpu.VMEM(tile.shape, BF16),
            pltpu.SMEM(routing.shape, I32),
            pltpu.SemaphoreType.DMA((2,)),
        ],
        (1, 1), "pack_cotangents",
    )(*[pltpu.with_memory_space_constraint(value, pltpu.HBM) for value in (routing, tile)])
    saved_slots = saved_pre[0, 0].transpose(1, 2, 0, 3)
    saved_slots = saved_slots.reshape(MIDDLE, MIDDLE * PER_WORKER, HALF)
    outgoing, saved_here = tie((outgoing, saved_slots))
    saved_other = swap(saved_slots)
    incoming = exchange(outgoing)

    masked, *to_owners, total = call(
        functools.partial(prepare, owners, columns, capacity, wide, permuted),
        [shape((MIDDLE, MIDDLE * PER_WORKER, HALF), BF16)]
        + pieces(MIDDLE, wide * capacity, HALF)
        + [shape((MIDDLE, MIDDLE, TILE_BLOCKS, FULL), BF16)],
        [SMEM] + [VMEM] * 5,
        counts
        + tables
        + [
            pltpu.VMEM((MIDDLE, MIDDLE * TILE_BLOCKS, FULL), F32),
            pltpu.VMEM((BLOCK, BLOCK * TILE_BLOCKS, FULL), BF16),
            pltpu.VMEM((9, FULL, FULL), BF16),
        ],
        (1, 1), "prepare",
    )(routing, saved_here, tile, tile_other, second_weight, second_other)
    incoming, to_owners, total = tie((incoming[::-1], to_owners[::-1], total))
    incoming, to_owners = incoming[::-1], to_owners[::-1]
    incoming_other = [swap(value) for value in incoming]
    at_owner = exchange(to_owners)

    saved_tiles = saved_input[0, 0].transpose(1, 2, 0, 3)
    if permuted:
        part = (2, 9, ROWS, FULL)
        halved = [shape((4,) + part, F32)] + [shape((2,) + part, BF16)] * 2
    else:
        halved = [shape((2, 9, HALF, FULL), F32)]
    terms = call(
        functools.partial(worker, scale, owners, columns, capacity, permuted),
        halved,
        [SMEM] + [VMEM] * (2 * parts + 4) + [HBM],
        counts
        + [
            pltpu.VMEM((BLOCK, BLOCK * PER_WORKER, FULL), BF16),
            pltpu.VMEM((MIDDLE, MIDDLE * PER_WORKER, FULL), F32),
            pltpu.VMEM((MIDDLE, MIDDLE, PER_WORKER, FULL), BF16),
            pltpu.VMEM((9, FULL, FULL), BF16),
            pltpu.VMEM(saved_tiles.shape, BF16),
            pltpu.SemaphoreType.DMA,
        ]
        + ([pltpu.VMEM((4,) + part, BF16)] if permuted else []),
        (1, 1), "worker",
    )(
        routing, *incoming, *incoming_other, masked, saved_other, second_weight, second_other,
        pltpu.with_memory_space_constraint(saved_tiles, pltpu.HBM),
    )

    if permuted:
        kept, near, far = terms
        far, at_owner[2], at_owner[1] = tie((far, at_owner[2], at_owner[1]))

    def owner(at_owner):
        at_owner_other = [swap(value) for value in at_owner]
        return call(
            functools.partial(owner_canvas, owners, capacity, wide, permuted),
            [shape((HIGH, WIDE, HALF), F32)] + [shape((RIM, FULL), BF16)] * (2 if permuted else 0),
            [SMEM] + [VMEM] * (2 * len(at_owner) + 2),
            tables
            + [
                pltpu.VMEM((MIDDLE, MIDDLE * TILE_BLOCKS, FULL), BF16),
                pltpu.VMEM((OUTER, OUTER * TILE_BLOCKS, HALF), F32),
            ],
            (1, 1), "owner_canvas",
        )(routing, *at_owner, *at_owner_other, total, first_weight)

    if permuted:
        far_got, near_got = swap(far, "col"), swap(near, "col")
        sends = call(add_far, [shape(part, BF16)] * 2, [VMEM] * 2, [], (1, 1), "add_far")(
            kept, far_got
        )
        sends, at_owner[3] = tie((sends[::-1], at_owner[3]))
        got = [flip(sends[0], "blk", 3), flip(sends[1], "blk", 2)]
        canvas, *rims = owner(at_owner)
        near_got, canvas = tie((near_got, canvas))
        keep, send = call(
            add_near, [shape(part, F32), shape(part, BF16)], [VMEM] * 2, [], (1, 1), "add_near",
        )(kept, near_got)
        got.append(flip(send, "blk", 1))
        message = shape((PART, FULL), BF16)
        wider = shape((PART + RIM, FULL), BF16)
        own, *wides = call(
            add_workers, [message, wider, wider], [VMEM] * 6, [], (1, 1), "add_workers",
        )(keep, *got, *rims)
        got_2, got_3, got_1 = flip(own, "blk", 2), flip(wides[1], "blk", 3), flip(wides[0], "blk", 1)
        across = [swap(value, "col") for value in (own, got_1[:PART])]
        got_3, got_2, got_1, across = tie((got_3, got_2, got_1, across))
        got = [got_1, got_2, got_3]
        last = call(
            column_message, shape((PART + 64, FULL), BF16), [VMEM] * 3,
            [pltpu.VMEM((RIM, FULL), F32), pltpu.VMEM((64, HALF), F32)],
            (1, 1), "column_message",
        )(canvas.reshape(HIGH * WIDE, HALF), got[0], got[2])
        across += [swap(got_2, "col"), swap(last, "col")]
        early = call(
            lay, [shape((9, HALF, FULL), F32)] * 2, [VMEM] * 6, [], (1, 1), "lay",
        )(own, *got, *across[:2])
        grad_in, grad_second, grad_first = pl.pallas_call(
            finish,
            out_shape=[shape(grad_out.shape, BF16)] + [shape((9, HALF, FULL), F32)] * 2,
            in_specs=[VMEM] * 6 + [HBM] * 2,
            out_specs=[VMEM] + [HBM] * 2,
            scratch_shapes=[
                pltpu.VMEM((TILE_ROWS * BLOCK * 32, HALF), F32),
                pltpu.VMEM((2, 2, 9, ROWS, FULL), F32),
                pltpu.SemaphoreType.DMA((2, 2)),
            ],
            input_output_aliases={6: 1, 7: 2},
            compiler_params=pltpu.CompilerParams(vmem_limit_bytes=48 * 1024 * 1024),
            cost_estimate=pl.CostEstimate(flops=1, bytes_accessed=1, transcendentals=0),
            name="finish",
        )(grad_out, canvas, got[0], got[2], across[3], across[2], *early)
        return (grad_in, grad_first, grad_second)

    grad_first, grad_second = lax.psum((terms[0][1], terms[0][0]), ("blk", "col"))
    [canvas] = owner(at_owner)
    up, down = neighbours("blk")
    from_above = lax.ppermute(canvas[HIGH - 2 :].astype(BF16), "blk", up).astype(F32)
    from_below = lax.ppermute(canvas[:2].astype(BF16), "blk", down).astype(F32)
    inner = canvas[2 : HIGH - 2]
    inner = inner.at[:2].add(from_above).at[-2:].add(from_below)
    up, down = neighbours("col")
    from_left = lax.ppermute(inner[:, 32:34].astype(BF16), "col", up).astype(F32)
    from_right = lax.ppermute(inner[:, 34:36].astype(BF16), "col", down).astype(F32)
    inner = inner[:, :32].at[:, :2].add(from_left).at[:, -2:].add(from_right)
    grad_in = (grad_out.astype(F32) + inner).astype(BF16)
    return (grad_in, grad_first, grad_second)


def solution(mesh):
    return jax.shard_map(
        shards,
        mesh=mesh,
        in_specs=(
            P(("groups", "blk"), "col", "ch"),
            P(("groups", "col"), "blk", None, None, None, "ch"),
            P(("groups", "col"), "blk", None, None, None, "ch"),
            P(None, "ch", None),
            P(None, "ch", None),
            P(("groups", "col"), None, None),
        ),
        out_specs=(
            P(("groups", "blk"), "col", "ch"),
            P("groups", "ch", None),
            P("groups", "ch", None),
        ),
        check_vma=False,
    )
```

```python
import functools
import math

import jax
import jax.numpy as jnp
from jax import lax
from jax.experimental import pallas as pl
from jax.experimental.pallas import tpu as pltpu
from jax.sharding import PartitionSpec as P

BLOCK = 8
TILE_ROWS = 8
TILE_COLS = 4
TILE_BLOCKS = 32
PER_WORKER = 16
MIDDLE = 10
OUTER = 12
HALF = 128
FULL = 256
DEAD = -4096
HIGH = 68
RIM = 48
ROWS = 16
SOLE = 144
PART = 2 * SOLE
WIDE = 40

BF16 = jnp.bfloat16
F32 = jnp.float32
I32 = jnp.int32

VMEM = pl.BlockSpec(memory_space=pltpu.VMEM)
HBM = pl.BlockSpec(memory_space=pltpu.HBM)
SMEM = pl.BlockSpec(memory_space=pltpu.SMEM)


def call(body, outs, specs, scratch, cost, name):
    return pl.pallas_call(
        body,
        out_shape=outs,
        in_specs=specs,
        out_specs=jax.tree.map(lambda _: VMEM, outs),
        scratch_shapes=scratch,
        compiler_params=pltpu.CompilerParams(vmem_limit_bytes=48 * 1024 * 1024),
        cost_estimate=pl.CostEstimate(flops=cost[0], bytes_accessed=cost[1], transcendentals=0),
        name=name,
    )


def iota(shape, dim):
    return lax.broadcasted_iota(I32, shape, dim)


def one_hot(hits):
    return jnp.where(hits, 1.0, 0.0).astype(BF16)


def dot(a, b):
    return jnp.dot(a, b, preferred_element_type=F32)


def dot_nt(a, b):
    return lax.dot_general(a, b, (((1,), (1,)), ((), ())), preferred_element_type=F32)


def dot_tn(a, b):
    return lax.dot_general(a, b, (((0,), (0,)), ((), ())), preferred_element_type=F32)


def owner_table(routing, table, owners, capacity):
    me = lax.axis_index("blk")

    def clear(number, carry):
        table[number] = DEAD
        return carry

    lax.fori_loop(0, owners * capacity, clear, 0)

    def worker(number, carry):
        count = jnp.int32(0)
        for slot in range(PER_WORKER):
            code = routing[number, slot]
            hit = (code // TILE_BLOCKS) == me
            table[jnp.where(hit, number * capacity + count, owners * capacity)] = code % TILE_BLOCKS
            count = count + jnp.where(hit, 1, 0)
        return carry

    lax.fori_loop(0, owners, worker, 0)


def worker_codes(routing, counts, owners):
    me = lax.axis_index("blk")

    def clear(number, carry):
        counts[number] = 0
        return carry

    lax.fori_loop(0, owners, clear, 0)
    slots = []
    for slot in range(PER_WORKER):
        code = routing[me, slot]
        owner = code // TILE_BLOCKS
        rank = counts[owner]
        counts[owner] = rank + 1
        slots.append((owner, code % TILE_BLOCKS, rank))
    return slots


def views(refs, count):
    return list(refs) if len(refs) == count else [refs[0].at[k] for k in range(count)]


def partner(axis, step, permuted):
    return step ^ lax.axis_index(axis) if permuted else step


def pack_cotangents(owners, capacity, permuted, listed, source, *refs):
    outs, (table, tile, routing, arrived) = refs[:-4], refs[-4:]
    fetch = pltpu.make_async_copy(source, tile, arrived.at[0])
    fetch.start()
    lists = pltpu.make_async_copy(listed, routing, arrived.at[1])
    lists.start()
    lists.wait()
    owner_table(routing, table, owners, capacity)
    rows = BLOCK * capacity
    row, lane = iota((rows, FULL), 0), iota((rows, FULL), 1)
    picks = []
    for step in range(owners):
        worker = partner("blk", step, permuted)
        target = jnp.full((rows, FULL), DEAD, I32)
        for rank in range(capacity):
            place = table[worker * capacity + rank] * BLOCK
            target = jnp.where(row % capacity == rank, place, target)
        picks.append(one_hot(lane == target + row // capacity))
    pick = jnp.concatenate(picks, axis=0)
    fetch.wait()
    for u in range(0, BLOCK, 2):
        pair = [
            jnp.concatenate([tile[r, u + k] for r in range(TILE_ROWS)], axis=0) for k in range(2)
        ]
        moved = dot(pick, jnp.concatenate(pair, axis=1)).astype(BF16)
        for step, out in enumerate(views(outs, owners)):
            part = moved[step * rows : (step + 1) * rows]
            out[u] = part[:, :HALF]
            out[u + 1] = part[:, HALF:]


def outside_image(slots, owners, columns):
    column = lax.axis_index("col")
    row = iota((MIDDLE * PER_WORKER, HALF), 0)
    flags = jnp.zeros_like(row)
    for slot, (owner, place, rank) in enumerate(slots):
        block_row, block_col = place // TILE_COLS, place % TILE_COLS
        flag = (
            jnp.where((owner == 0) & (block_row == 0), 1, 0)
            + jnp.where((owner == owners - 1) & (block_row == TILE_ROWS - 1), 2, 0)
            + jnp.where((column == 0) & (block_col == 0), 4, 0)
            + jnp.where((column == columns - 1) & (block_col == TILE_COLS - 1), 8, 0)
        )
        flags = jnp.where(row % PER_WORKER == slot, flag, flags)
    across = row // PER_WORKER
    sides = (((flags & 4) != 0) & (across == 0)) | (((flags & 8) != 0) & (across == MIDDLE - 1))

    def here(m):
        if m == 0:
            return sides | ((flags & 1) != 0)
        if m == MIDDLE - 1:
            return sides | ((flags & 2) != 0)
        return sides

    return here


def pack_saved(owners, columns, capacity, wide, permuted, routing, saved, masked, *refs):
    outs, counts, table = refs[:-2], refs[-2], refs[-1]

    def clear(number, carry):
        table[number] = DEAD
        return carry

    lax.fori_loop(0, owners * capacity, clear, 0)
    slots = worker_codes(routing, counts, owners)
    rows = MIDDLE * PER_WORKER
    for slot, (owner, place, rank) in enumerate(slots):
        table[owner * capacity + rank] = slot
    outside = outside_image(slots, owners, columns)
    for m in range(MIDDLE):
        masked[m] = jnp.where(outside(m), 0.0, saved[m].astype(F32)).astype(BF16)
    size = wide * capacity
    row, lane = iota((size, FULL), 0), iota((size, FULL), 1)
    picks = []
    for step in range(owners):
        owner = partner("blk", step, permuted)
        target = jnp.full((size, FULL), DEAD, I32)
        for rank in range(capacity):
            target = jnp.where(row % capacity == rank, table[owner * capacity + rank], target)
        at = row // capacity
        picks.append(one_hot((lane == target + at * PER_WORKER) & (at < MIDDLE)))
    pick = jnp.concatenate(picks, axis=0)
    filler = jnp.zeros((FULL - rows, FULL), BF16)
    for m in range(0, MIDDLE, 2):
        pair = jnp.concatenate([masked[m], masked[m + 1]], axis=1)
        moved = dot(pick, jnp.concatenate([pair, filler], axis=0)).astype(BF16)
        for step, out in enumerate(views(outs, owners)):
            part = moved[step * size : (step + 1) * size]
            out[m] = part[:, :HALF]
            out[m + 1] = part[:, HALF:]


def ordered(own, other, axis):
    first = lax.axis_index("ch") == 0
    return jnp.concatenate(
        [jnp.where(first, own, other), jnp.where(first, other, own)], axis=axis
    )


def deal(value, kept, sent, grad, tap):
    low, high = value[: HALF // 2], value[HALF // 2 :]
    mine = lax.axis_index("col") == 0
    keep, send = jnp.where(mine, low, high), jnp.where(mine, high, low).astype(BF16)
    for k in range(4):
        step, rows = partner("blk", k, True), slice(k * ROWS, (k + 1) * ROWS)
        kept[step, grad, tap] = keep[rows]
        sent[step, grad, tap] = send[rows]


def emit(value, outs, grad, tap):
    if len(outs) == 2:
        deal(value, outs[0], outs[1], grad, tap)
    else:
        outs[0][grad, tap] = value


def spread(values, weight, total, places):
    height, extent = values.shape[:2]
    inputs = values[...].reshape(height * extent, FULL)
    width, step = weight.shape[1], places
    for dy in range(3):
        taps = jnp.concatenate([weight[3 * dy + dx] for dx in range(3)], axis=0)
        part = dot_nt(inputs, taps).reshape(height, extent, 3 * width)
        p, q, r = [part[:, :, dx * width : (dx + 1) * width] for dx in range(3)]
        sums = [
            p[:, :step],
            p[:, step : 2 * step] + q[:, :step],
            p[:, 2 * step :] + q[:, step : extent - step] + r[:, : extent - 2 * step],
            q[:, extent - step :] + r[:, extent - 2 * step : extent - step],
            r[:, extent - step :],
        ]
        at = 0
        for value in sums:
            size = value.shape[1]
            here = slice(at, at + size)
            if dy == 0:
                total[:height, here] = value
            else:
                total[dy : dy + height - 1, here] += value[:-1]
                total[dy + height - 1, here] = value[height - 1]
            at += size


def second_gradient(scale, owners, capacity, permuted, routing, *refs):
    parts = 1 if not permuted else owners
    own, other = views(refs[:parts], owners), views(refs[parts : 2 * parts], owners)
    masked, cot = refs[2 * parts : 2 * parts + 2]
    outs, counts = refs[2 * parts + 2 : -1], refs[-1]
    slots = worker_codes(routing, counts, owners)
    rows, inner = BLOCK * PER_WORKER, owners * BLOCK * capacity
    row, lane = iota((rows, inner), 0), iota((rows, inner), 1)
    target = jnp.full((rows, inner), DEAD, I32)
    for slot, (owner, place, rank) in enumerate(slots):
        step = partner("blk", owner, permuted)
        target = jnp.where(row % PER_WORKER == slot, step * (BLOCK * capacity) + rank, target)
    pick = one_hot(lane == target + (row // PER_WORKER) * capacity)
    for u in range(BLOCK):
        got = jnp.concatenate(
            [ordered(own[o][u], other[o][u], 1) for o in range(owners)], axis=0
        )
        cot[u] = dot(pick, got).astype(BF16)
    grads = cot[...].reshape(BLOCK * rows, FULL)
    for dy in range(3):
        windows = [
            masked[dy : dy + BLOCK, dx * PER_WORKER : (dx + BLOCK) * PER_WORKER] for dx in range(3)
        ]
        window = jnp.concatenate([w.reshape(BLOCK * rows, HALF) for w in windows], axis=1)
        value = dot_tn(jnp.maximum(window, jnp.zeros_like(window)), grads) * scale
        for dx in range(3):
            emit(value[dx * HALF : (dx + 1) * HALF], outs, 0, 3 * dy + dx)
    return slots


def first_gradient(
    scale, outside, cot, masked, saved_other, weight, weight_other, saved, *refs
):
    outs, (total, pre, full) = refs[:-3], refs[-3:]
    full[...] = ordered(weight[...], weight_other[...], 1)
    spread(cot, full, total, PER_WORKER)
    for m in range(MIDDLE):
        other = jnp.where(outside(m), 0.0, saved_other[m].astype(F32)).astype(BF16)
        live = ordered(masked[m], other, 1).astype(F32) > 0
        value = jnp.where(live, total[m], 0.0)
        pre[m] = value.astype(BF16).reshape(MIDDLE, PER_WORKER, FULL)
    size = MIDDLE * MIDDLE * PER_WORKER
    grads = pre[...].reshape(size, FULL)
    for dy in range(3):
        windows = [saved[dy : dy + MIDDLE, dx : dx + MIDDLE] for dx in range(3)]
        window = jnp.concatenate([w.reshape(size, HALF) for w in windows], axis=1)
        value = dot_tn(window, grads) * scale
        for dx in range(3):
            emit(value[dx * HALF : (dx + 1) * HALF], outs, 1, 3 * dy + dx)


def owner_spread(tile, tile_other, second, second_other, out, total, cot, full):
    row, lane = iota((FULL, FULL), 0), iota((FULL, FULL), 1)
    turn = one_hot(lane == (row % TILE_BLOCKS) * BLOCK + row // TILE_BLOCKS)
    for u in range(BLOCK):
        block = jnp.concatenate(
            [ordered(tile[r, u], tile_other[r, u], 1) for r in range(TILE_ROWS)], axis=0
        )
        cot[u] = dot(turn, block).astype(BF16)
    full[...] = ordered(second[...], second_other[...], 1)
    spread(cot, full, total, TILE_BLOCKS)
    out[...] = total[...].astype(BF16).reshape(out.shape)


def prepare(owners, columns, capacity, wide, permuted, routing, saved, *refs):
    (tile, tile_other, second, second_other, masked), refs = refs[:5], refs[5:]
    outs, (out, counts, table, total, cot, full) = refs[:-6], refs[-6:]
    pack_saved(owners, columns, capacity, wide, permuted, routing, saved, masked, *outs, counts, table)
    owner_spread(tile, tile_other, second, second_other, out, total, cot, full)


def worker(scale, owners, columns, capacity, permuted, routing, *refs):
    parts = 1 if not permuted else owners
    inputs, refs = refs[: 2 * parts], refs[2 * parts :]
    (masked, saved_other, weight, weight_other, source), refs = refs[:5], refs[5:]
    if permuted:
        refs, sent = refs[:-1], refs[-1]
    outs, (counts, cot, total, pre, full, saved, arrived) = refs[:-7], refs[-7:]
    if permuted:
        kept, near, far = outs
        outs = (kept, sent)
    fetch = pltpu.make_async_copy(source, saved, arrived)
    fetch.start()
    slots = second_gradient(
        scale, owners, capacity, permuted, routing, *inputs, masked, cot, *outs, counts
    )
    fetch.wait()
    first_gradient(
        scale, outside_image(slots, owners, columns), cot, masked, saved_other, weight, weight_other,
        saved, *outs, total, pre, full,
    )
    if permuted:
        near[...] = sent[:2]
        far[...] = sent[2:]


def adjacent(step):
    me = lax.axis_index("blk")
    return (me ^ step) == me - 1, (me ^ step) == me + 1


def owner_canvas(owners, capacity, wide, permuted, routing, *refs):
    parts = 1 if not permuted else owners
    got, got_other = views(refs[:parts], owners), views(refs[parts : 2 * parts], owners)
    total, first, canvas = refs[2 * parts : 2 * parts + 3]
    rims, (table, pre, grown) = refs[2 * parts + 3 : -3], refs[-3:]
    owner_table(routing, table, owners, capacity)
    size, into = wide * capacity, MIDDLE * TILE_BLOCKS
    row, lane = iota((size, into), 0), iota((size, into), 1)
    picks = []
    for step in range(owners):
        worker = partner("blk", step, permuted)
        target = jnp.full((size, into), DEAD, I32)
        for rank in range(capacity):
            target = jnp.where(row % capacity == rank, table[worker * capacity + rank], target)
        at = row // capacity
        hits = (lane == target + at * TILE_BLOCKS) & (at < MIDDLE)
        picks.append(jnp.where(hits, 1.0, 0.0))
    pick = jnp.concatenate(picks, axis=0).T.astype(BF16)
    for m in range(MIDDLE):
        block = jnp.concatenate(
            [ordered(got[w][m], got_other[w][m], 1) for w in range(owners)], axis=0
        )
        value = jnp.where(dot(pick, block) > 0, total[m].reshape(into, FULL).astype(F32), 0.0)
        pre[m] = value.astype(BF16)
    spread(pre, first, grown, TILE_BLOCKS)
    height, depth = TILE_ROWS * WIDE, OUTER * TILE_BLOCKS
    row, lane = iota((height, depth), 0), iota((height, depth), 1)
    at_row, at_col = row // WIDE, row % WIDE
    n, place = lane // TILE_BLOCKS, lane % TILE_BLOCKS
    column = (place % TILE_COLS) * BLOCK + n - 2
    column = jnp.where(column < 0, column + 36, column)
    fold = one_hot((at_row == place // TILE_COLS) & (at_col == column))
    canvas[...] = jnp.zeros_like(canvas)
    for m in range(0, OUTER, 2):
        pair = jnp.concatenate(
            [grown[m + k].astype(BF16) for k in range(2)], axis=1
        )
        laid = dot(fold, pair).reshape(TILE_ROWS, WIDE, FULL)
        for r in range(TILE_ROWS):
            for k in range(2):
                canvas[r * BLOCK + m + k] += laid[r, :, k * HALF : (k + 1) * HALF]
    for k, rim in enumerate(rims):
        above, below = adjacent(2 * k + 1)
        top = jnp.concatenate([canvas[0], canvas[1]], axis=1)
        bottom = jnp.concatenate([canvas[HIGH - 2], canvas[HIGH - 1]], axis=1)
        rim[:WIDE] = jnp.where(below, bottom, jnp.where(above, top, 0.0)).astype(BF16)
        rim[WIDE:] = jnp.zeros((RIM - WIDE, FULL), BF16)


def add_far(kept, got, *sends):
    for k, out in enumerate(sends):
        out[...] = (kept[2 + k] + got[k].astype(F32)).astype(BF16)


def add_near(kept, got, keep, send):
    keep[...] = kept[0] + got[0].astype(F32)
    send[...] = (kept[1] + got[1].astype(F32)).astype(BF16)


def add_workers(kept, got_3, got_2, got_1, rim_1, rim_3, out, out_1, out_second, out_3):
    value = kept[...]
    for part in (got_3, got_2, got_1):
        value = value + part[...].astype(F32)
    value = value.astype(BF16).reshape(PART, FULL)
    out[...] = value
    out_second[...] = value[:SOLE]
    out_1[:PART] = value
    out_1[PART:] = rim_1[...]
    out_3[:SOLE] = value[SOLE:]
    out_3[SOLE:] = rim_3[...]


def row_rim(message, step):
    rim = message[message.shape[0] - RIM :].astype(F32)
    above, below = adjacent(step)
    return jnp.where(above, rim, 0.0), jnp.where(below, rim, 0.0)


def column_message(canvas, got_1, got_3, out, rims, strip):
    out[:SOLE] = got_3[:SOLE]
    rims[0], rims[1] = row_rim(got_1, 1)
    rims[2], rims[3] = row_rim(got_3, 3)
    for j in range(2):
        c = 32 + 2 * lax.axis_index("col") + j
        strip[...] = canvas[pl.ds(2 * WIDE + c, 64, stride=WIDE), :]
        for k in range(4):
            row, at = rims[k, pl.ds(c, 1), :], 62 * (k % 2)
            strip[at : at + 1] += row[:, :HALF]
            strip[at + 1 : at + 2] += row[:, HALF:]
        out[SOLE:, j * HALF : (j + 1) * HALF] = strip[...].astype(BF16)


def sum_image(tile, canvas, total):
    total[...] = tile[...].astype(F32) + canvas[2 : HIGH - 2, :32, :].reshape(total.shape)


def add_row_rims(got_1, got_3, total):
    rows = total.shape[0]
    for step, got in ((1, got_1), (3, got_3)):
        top, bottom = [rim[:32] for rim in row_rim(got, step)]
        total[0:32] += top[:, :HALF]
        total[32:64] += top[:, HALF:]
        total[rows - 64 : rows - 32] += bottom[:, :HALF]
        total[rows - 32 : rows] += bottom[:, HALF:]


def rows_at(number):
    column = lax.axis_index("col")
    place = (column if number < 4 else 1 - column) * 4 + partner("blk", number % 4, True)
    return pl.ds(pl.multiple_of(place * ROWS, ROWS), ROWS)


def lay(*refs):
    parts, outs = refs[:-2], refs[-2:]
    own, got_1, got_2, second_3, first_3, across, across_2, across_1, across_3 = parts
    for number, part in (
        (0, own), (1, got_1), (2, got_2), (4, across), (5, across_1), (6, across_2)
    ):
        value = part[:PART].astype(F32).reshape(2, 9, ROWS, FULL)
        for out, grad in zip(outs, (0, 1)):
            out[:, rows_at(number), :] = value[grad]
    for number, grad, part in ((3, 0, second_3), (7, 0, across_3), (3, 1, first_3)):
        outs[grad][:, rows_at(number), :] = part[:SOLE].astype(F32).reshape(9, ROWS, FULL)


def finish(early, got_1, got_3, last, old, out, dest, total, laid, sem):
    laid[...] = last[:SOLE].astype(F32).reshape(9, ROWS, FULL)
    copy = pltpu.make_async_copy(laid, dest.at[:, rows_at(7), :], sem)
    copy.start()
    total[...] = early[...]
    add_row_rims(got_1, got_3, total)
    strip = last[SOLE:].astype(F32)
    at = jnp.where(lax.axis_index("col") == 0, 30, 0)
    for j in range(2):
        spot = (pl.ds(at + j, 64, stride=32), slice(None))
        total[spot] = total[spot] + strip[:, j * HALF : (j + 1) * HALF]
    out[...] = total[...].astype(BF16)
    copy.wait()


def swap(value, axis="ch"):
    return lax.ppermute(value, axis, [(0, 1), (1, 0)])


def flip(value, axis, step):
    size = lax.axis_size(axis)
    return lax.ppermute(value, axis, [(i, i ^ step) for i in range(size)])


def neighbours(axis):
    size = lax.axis_size(axis)
    up = [(i, (i + 1) % size) for i in range(size - 1)]
    return up, [(j, i) for i, j in up]


def shards(grad_out, saved_input, saved_pre, first_weight, second_weight, assignment):
    owners = lax.axis_size("blk")
    columns = lax.axis_size("col")
    capacity = max(2, TILE_BLOCKS // owners)
    wide = MIDDLE if (MIDDLE * capacity) % 16 == 0 else 16
    scale = 1.0 / math.sqrt(owners * columns * PER_WORKER * BLOCK * BLOCK)
    permuted = owners == 4 and columns == 2
    parts = owners if permuted else 1
    routing = assignment[0]
    shape = jax.ShapeDtypeStruct
    tables = [pltpu.SMEM((owners * capacity + 1,), I32)]
    counts = [pltpu.SMEM((owners,), I32)]

    def pieces(*dims):
        return [shape(dims, BF16)] * owners if permuted else [shape((owners,) + dims, BF16)]

    def exchange(values):
        if permuted:
            return list(values[:1]) + [flip(values[k], "blk", k) for k in (3, 2, 1)][::-1]
        return [lax.all_to_all(values[0], "blk", split_axis=0, concat_axis=0, tiled=True)]

    tie = lax.optimization_barrier
    tile = grad_out.reshape(TILE_ROWS, BLOCK, TILE_COLS * BLOCK, HALF)
    second_other, tile_other = swap(second_weight), swap(tile)
    outgoing = call(
        functools.partial(pack_cotangents, owners, capacity, permuted),
        pieces(BLOCK, BLOCK * capacity, HALF),
        [HBM, HBM],
        tables
        + [
            pltpu.VMEM(tile.shape, BF16),
            pltpu.SMEM(routing.shape, I32),
            pltpu.SemaphoreType.DMA((2,)),
        ],
        (1, 1), "pack_cotangents",
    )(*[pltpu.with_memory_space_constraint(value, pltpu.HBM) for value in (routing, tile)])
    saved_slots = saved_pre[0, 0].transpose(1, 2, 0, 3)
    saved_slots = saved_slots.reshape(MIDDLE, MIDDLE * PER_WORKER, HALF)
    outgoing, saved_here = tie((outgoing, saved_slots))
    saved_other = swap(saved_slots)
    incoming = exchange(outgoing)

    masked, *to_owners, total = call(
        functools.partial(prepare, owners, columns, capacity, wide, permuted),
        [shape((MIDDLE, MIDDLE * PER_WORKER, HALF), BF16)]
        + pieces(MIDDLE, wide * capacity, HALF)
        + [shape((MIDDLE, MIDDLE, TILE_BLOCKS, FULL), BF16)],
        [SMEM] + [VMEM] * 5,
        counts
        + tables
        + [
            pltpu.VMEM((MIDDLE, MIDDLE * TILE_BLOCKS, FULL), F32),
            pltpu.VMEM((BLOCK, BLOCK * TILE_BLOCKS, FULL), BF16),
            pltpu.VMEM((9, FULL, FULL), BF16),
        ],
        (1, 1), "prepare",
    )(routing, saved_here, tile, tile_other, second_weight, second_other)
    incoming, to_owners, total = tie((incoming[::-1], to_owners[::-1], total))
    incoming, to_owners = incoming[::-1], to_owners[::-1]
    incoming_other = [swap(value) for value in incoming]
    at_owner = exchange(to_owners)

    saved_tiles = saved_input[0, 0].transpose(1, 2, 0, 3)
    if permuted:
        part = (2, 9, ROWS, FULL)
        halved = [shape((4,) + part, F32)] + [shape((2,) + part, BF16)] * 2
    else:
        halved = [shape((2, 9, HALF, FULL), F32)]
    terms = call(
        functools.partial(worker, scale, owners, columns, capacity, permuted),
        halved,
        [SMEM] + [VMEM] * (2 * parts + 4) + [HBM],
        counts
        + [
            pltpu.VMEM((BLOCK, BLOCK * PER_WORKER, FULL), BF16),
            pltpu.VMEM((MIDDLE, MIDDLE * PER_WORKER, FULL), F32),
            pltpu.VMEM((MIDDLE, MIDDLE, PER_WORKER, FULL), BF16),
            pltpu.VMEM((9, FULL, FULL), BF16),
            pltpu.VMEM(saved_tiles.shape, BF16),
            pltpu.SemaphoreType.DMA,
        ]
        + ([pltpu.VMEM((4,) + part, BF16)] if permuted else []),
        (1, 1), "worker",
    )(
        routing, *incoming, *incoming_other, masked, saved_other, second_weight, second_other,
        pltpu.with_memory_space_constraint(saved_tiles, pltpu.HBM),
    )

    if permuted:
        kept, near, far = terms
        far, at_owner[2], at_owner[1] = tie((far, at_owner[2], at_owner[1]))

    def owner(at_owner):
        at_owner_other = [swap(value) for value in at_owner]
        return call(
            functools.partial(owner_canvas, owners, capacity, wide, permuted),
            [shape((HIGH, WIDE, HALF), F32)] + [shape((RIM, FULL), BF16)] * (2 if permuted else 0),
            [SMEM] + [VMEM] * (2 * len(at_owner) + 2),
            tables
            + [
                pltpu.VMEM((MIDDLE, MIDDLE * TILE_BLOCKS, FULL), BF16),
                pltpu.VMEM((OUTER, OUTER * TILE_BLOCKS, HALF), F32),
            ],
            (1, 1), "owner_canvas",
        )(routing, *at_owner, *at_owner_other, total, first_weight)

    if permuted:
        far_got, near_got = swap(far, "col"), swap(near, "col")
        sends = call(add_far, [shape(part, BF16)] * 2, [VMEM] * 2, [], (1, 1), "add_far")(
            kept, far_got
        )
        sends, at_owner[3] = tie((sends[::-1], at_owner[3]))
        got = [flip(sends[0], "blk", 3), flip(sends[1], "blk", 2)]
        canvas, *rims = owner(at_owner)
        near_got, canvas = tie((near_got, canvas))
        keep, send = call(
            add_near, [shape(part, F32), shape(part, BF16)], [VMEM] * 2, [], (1, 1), "add_near",
        )(kept, near_got)
        got.append(flip(send, "blk", 1))
        messages = [shape((n, FULL), BF16) for n in (PART, PART + RIM, SOLE, SOLE + RIM)]
        own, wide_1, second, wide_3 = call(
            add_workers, messages, [VMEM] * 6, [], (1, 1), "add_workers",
        )(keep, *got, *rims)
        second_3, got_2, first_3 = flip(second, "blk", 3), flip(own, "blk", 2), flip(wide_3, "blk", 3)
        got_1 = flip(wide_1, "blk", 1)
        flat = (TILE_ROWS * BLOCK * 32, HALF)
        canvas, _ = tie((canvas, own))
        image = call(sum_image, shape(flat, F32), [VMEM] * 2, [], (1, 1), "sum_image")(
            grad_out.reshape(flat), canvas
        )
        across = [
            swap(tie((value, image))[0], "col") for value in (own, got_2, got_1, second_3)
        ]
        first_3, got_1, across = tie((first_3, got_1, across))
        last = call(
            column_message, shape((SOLE + 64, FULL), BF16), [VMEM] * 3,
            [pltpu.VMEM((4, RIM, FULL), F32), pltpu.VMEM((64, HALF), F32)],
            (1, 1), "column_message",
        )(canvas.reshape(HIGH * WIDE, HALF), got_1, first_3)
        last = swap(last, "col")
        grad_second, grad_first = call(
            lay, [shape((9, HALF, FULL), F32)] * 2, [VMEM] * 9, [], (1, 1), "lay",
        )(own, got_1, got_2, second_3, first_3, *across)
        grad_in, grad_first = pl.pallas_call(
            finish,
            out_shape=[shape(flat, BF16), shape((9, HALF, FULL), F32)],
            in_specs=[VMEM] * 4 + [HBM],
            out_specs=[VMEM, HBM],
            scratch_shapes=[
                pltpu.VMEM(flat, F32),
                pltpu.VMEM((9, ROWS, FULL), F32),
                pltpu.SemaphoreType.DMA,
            ],
            input_output_aliases={4: 1},
            compiler_params=pltpu.CompilerParams(vmem_limit_bytes=48 * 1024 * 1024),
            cost_estimate=pl.CostEstimate(flops=1, bytes_accessed=1, transcendentals=0),
            name="finish",
        )(image, got_1, first_3, last, grad_first)
        grad_in = grad_in.reshape(grad_out.shape)
        return (grad_in, grad_first, grad_second)

    grad_first, grad_second = lax.psum((terms[0][1], terms[0][0]), ("blk", "col"))
    [canvas] = owner(at_owner)
    up, down = neighbours("blk")
    from_above = lax.ppermute(canvas[HIGH - 2 :].astype(BF16), "blk", up).astype(F32)
    from_below = lax.ppermute(canvas[:2].astype(BF16), "blk", down).astype(F32)
    inner = canvas[2 : HIGH - 2]
    inner = inner.at[:2].add(from_above).at[-2:].add(from_below)
    up, down = neighbours("col")
    from_left = lax.ppermute(inner[:, 32:34].astype(BF16), "col", up).astype(F32)
    from_right = lax.ppermute(inner[:, 34:36].astype(BF16), "col", down).astype(F32)
    inner = inner[:, :32].at[:, :2].add(from_left).at[:, -2:].add(from_right)
    grad_in = (grad_out.astype(F32) + inner).astype(BF16)
    return (grad_in, grad_first, grad_second)


def solution(mesh):
    return jax.shard_map(
        shards,
        mesh=mesh,
        in_specs=(
            P(("groups", "blk"), "col", "ch"),
            P(("groups", "col"), "blk", None, None, None, "ch"),
            P(("groups", "col"), "blk", None, None, None, "ch"),
            P(None, "ch", None),
            P(None, "ch", None),
            P(("groups", "col"), None, None),
        ),
        out_specs=(
            P(("groups", "blk"), "col", "ch"),
            P("groups", "ch", None),
            P("groups", "ch", None),
        ),
        check_vma=False,
    )
```

```python
import functools
import math

import jax
import jax.numpy as jnp
from jax import lax
from jax.experimental import pallas as pl
from jax.experimental.pallas import tpu as pltpu
from jax.sharding import PartitionSpec as P

BLOCK = 8
TILE_ROWS = 8
TILE_COLS = 4
TILE_BLOCKS = 32
PER_WORKER = 16
MIDDLE = 10
OUTER = 12
HALF = 128
FULL = 256
DEAD = -4096
HIGH = 68
RIM = 48
ROWS = 16
PART = 288
WIDE = 40

BF16 = jnp.bfloat16
F32 = jnp.float32
I32 = jnp.int32

VMEM = pl.BlockSpec(memory_space=pltpu.VMEM)
HBM = pl.BlockSpec(memory_space=pltpu.HBM)
SMEM = pl.BlockSpec(memory_space=pltpu.SMEM)


def call(body, outs, specs, scratch, cost, name):
    return pl.pallas_call(
        body,
        out_shape=outs,
        in_specs=specs,
        out_specs=jax.tree.map(lambda _: VMEM, outs),
        scratch_shapes=scratch,
        compiler_params=pltpu.CompilerParams(vmem_limit_bytes=48 * 1024 * 1024),
        cost_estimate=pl.CostEstimate(flops=cost[0], bytes_accessed=cost[1], transcendentals=0),
        name=name,
    )


def iota(shape, dim):
    return lax.broadcasted_iota(I32, shape, dim)


def one_hot(hits):
    return jnp.where(hits, 1.0, 0.0).astype(BF16)


def dot(a, b):
    return jnp.dot(a, b, preferred_element_type=F32)


def dot_nt(a, b):
    return lax.dot_general(a, b, (((1,), (1,)), ((), ())), preferred_element_type=F32)


def dot_tn(a, b):
    return lax.dot_general(a, b, (((0,), (0,)), ((), ())), preferred_element_type=F32)


def owner_table(routing, table, owners, capacity):
    me = lax.axis_index("blk")

    def clear(number, carry):
        table[number] = DEAD
        return carry

    lax.fori_loop(0, owners * capacity, clear, 0)

    def worker(number, carry):
        count = jnp.int32(0)
        for slot in range(PER_WORKER):
            code = routing[number, slot]
            hit = (code // TILE_BLOCKS) == me
            table[jnp.where(hit, number * capacity + count, owners * capacity)] = code % TILE_BLOCKS
            count = count + jnp.where(hit, 1, 0)
        return carry

    lax.fori_loop(0, owners, worker, 0)


def worker_codes(routing, counts, owners):
    me = lax.axis_index("blk")

    def clear(number, carry):
        counts[number] = 0
        return carry

    lax.fori_loop(0, owners, clear, 0)
    slots = []
    for slot in range(PER_WORKER):
        code = routing[me, slot]
        owner = code // TILE_BLOCKS
        rank = counts[owner]
        counts[owner] = rank + 1
        slots.append((owner, code % TILE_BLOCKS, rank))
    return slots


def views(refs, count):
    return list(refs) if len(refs) == count else [refs[0].at[k] for k in range(count)]


def partner(axis, step, permuted):
    return step ^ lax.axis_index(axis) if permuted else step


def pack_cotangents(owners, capacity, permuted, listed, source, *refs):
    outs, (places, tile, codes, arrived) = refs[:-4], refs[-4:]
    fetch = pltpu.make_async_copy(source, tile, arrived.at[0])
    fetch.start()
    lists = pltpu.make_async_copy(listed, codes, arrived.at[1])
    lists.start()
    lists.wait()
    hit = (codes[...] // TILE_BLOCKS) == lax.axis_index("blk")
    places[0] = jnp.where(hit, codes[...] % TILE_BLOCKS + 1, 0)
    before = (iota((PER_WORKER, PER_WORKER), 0) < iota((PER_WORKER, PER_WORKER), 1))
    places[1] = dot(one_hot(hit), one_hot(before)).astype(I32)
    rows = BLOCK * capacity
    row, lane = iota((rows, FULL), 0), iota((rows, FULL), 1)
    picks = []
    for step in range(owners):
        at = pl.ds(partner("blk", step, permuted), 1)
        same = places[1, at, :] == iota((rows, PER_WORKER), 0) % capacity
        place = jnp.sum(jnp.where(same, places[0, at, :], 0).astype(F32), axis=1, keepdims=True)
        target = (place.astype(I32) - 1) * BLOCK
        picks.append(one_hot(lane == target + row // capacity))
    pick = jnp.concatenate(picks, axis=0)
    fetch.wait()
    for u in range(0, BLOCK, 2):
        pair = [
            jnp.concatenate([tile[r, u + k] for r in range(TILE_ROWS)], axis=0) for k in range(2)
        ]
        moved = dot(pick, jnp.concatenate(pair, axis=1)).astype(BF16)
        for step, out in enumerate(views(outs, owners)):
            part = moved[step * rows : (step + 1) * rows]
            out[u] = part[:, :HALF]
            out[u + 1] = part[:, HALF:]


def outside_image(slots, owners, columns):
    column = lax.axis_index("col")
    row = iota((MIDDLE * PER_WORKER, HALF), 0)
    flags = jnp.zeros_like(row)
    for slot, (owner, place, rank) in enumerate(slots):
        block_row, block_col = place // TILE_COLS, place % TILE_COLS
        flag = (
            jnp.where((owner == 0) & (block_row == 0), 1, 0)
            + jnp.where((owner == owners - 1) & (block_row == TILE_ROWS - 1), 2, 0)
            + jnp.where((column == 0) & (block_col == 0), 4, 0)
            + jnp.where((column == columns - 1) & (block_col == TILE_COLS - 1), 8, 0)
        )
        flags = jnp.where(row % PER_WORKER == slot, flag, flags)
    across = row // PER_WORKER
    sides = (((flags & 4) != 0) & (across == 0)) | (((flags & 8) != 0) & (across == MIDDLE - 1))

    def here(m):
        if m == 0:
            return sides | ((flags & 1) != 0)
        if m == MIDDLE - 1:
            return sides | ((flags & 2) != 0)
        return sides

    return here


def pack_saved(owners, columns, capacity, wide, permuted, routing, saved, masked, *refs):
    outs, counts, table = refs[:-2], refs[-2], refs[-1]

    def clear(number, carry):
        table[number] = DEAD
        return carry

    lax.fori_loop(0, owners * capacity, clear, 0)
    slots = worker_codes(routing, counts, owners)
    rows = MIDDLE * PER_WORKER
    for slot, (owner, place, rank) in enumerate(slots):
        table[owner * capacity + rank] = slot
    outside = outside_image(slots, owners, columns)
    for m in range(MIDDLE):
        masked[m] = jnp.where(outside(m), 0.0, saved[m].astype(F32)).astype(BF16)
    size = wide * capacity
    row, lane = iota((size, FULL), 0), iota((size, FULL), 1)
    picks = []
    for step in range(owners):
        owner = partner("blk", step, permuted)
        target = jnp.full((size, FULL), DEAD, I32)
        for rank in range(capacity):
            target = jnp.where(row % capacity == rank, table[owner * capacity + rank], target)
        at = row // capacity
        picks.append(one_hot((lane == target + at * PER_WORKER) & (at < MIDDLE)))
    pick = jnp.concatenate(picks, axis=0)
    filler = jnp.zeros((FULL - rows, FULL), BF16)
    for m in range(0, MIDDLE, 2):
        pair = jnp.concatenate([masked[m], masked[m + 1]], axis=1)
        moved = dot(pick, jnp.concatenate([pair, filler], axis=0)).astype(BF16)
        for step, out in enumerate(views(outs, owners)):
            part = moved[step * size : (step + 1) * size]
            out[m] = part[:, :HALF]
            out[m + 1] = part[:, HALF:]


def ordered(own, other, axis):
    first = lax.axis_index("ch") == 0
    return jnp.concatenate(
        [jnp.where(first, own, other), jnp.where(first, other, own)], axis=axis
    )


def deal(value, kept, sent, grad, tap):
    low, high = value[: HALF // 2], value[HALF // 2 :]
    mine = lax.axis_index("col") == 0
    keep, send = jnp.where(mine, low, high), jnp.where(mine, high, low).astype(BF16)
    for k in range(4):
        step, rows = partner("blk", k, True), slice(k * ROWS, (k + 1) * ROWS)
        kept[step, grad, tap] = keep[rows]
        sent[step, grad, tap] = send[rows]


def emit(value, outs, grad, tap):
    if len(outs) == 2:
        deal(value, outs[0], outs[1], grad, tap)
    else:
        outs[0][grad, tap] = value


def spread(values, weight, total, places):
    height, extent = values.shape[:2]
    inputs = values[...].reshape(height * extent, FULL)
    width, step = weight.shape[1], places
    for dy in range(3):
        taps = jnp.concatenate([weight[3 * dy + dx] for dx in range(3)], axis=0)
        part = dot_nt(inputs, taps).reshape(height, extent, 3 * width)
        p, q, r = [part[:, :, dx * width : (dx + 1) * width] for dx in range(3)]
        sums = [
            p[:, :step],
            p[:, step : 2 * step] + q[:, :step],
            p[:, 2 * step :] + q[:, step : extent - step] + r[:, : extent - 2 * step],
            q[:, extent - step :] + r[:, extent - 2 * step : extent - step],
            r[:, extent - step :],
        ]
        at = 0
        for value in sums:
            size = value.shape[1]
            here = slice(at, at + size)
            if dy == 0:
                total[:height, here] = value
            else:
                total[dy : dy + height - 1, here] += value[:-1]
                total[dy + height - 1, here] = value[height - 1]
            at += size


def second_gradient(scale, owners, capacity, permuted, routing, *refs):
    parts = 1 if not permuted else owners
    own, other = views(refs[:parts], owners), views(refs[parts : 2 * parts], owners)
    masked, cot = refs[2 * parts : 2 * parts + 2]
    outs, counts = refs[2 * parts + 2 : -1], refs[-1]
    slots = worker_codes(routing, counts, owners)
    rows, inner = BLOCK * PER_WORKER, owners * BLOCK * capacity
    row, lane = iota((rows, inner), 0), iota((rows, inner), 1)
    target = jnp.full((rows, inner), DEAD, I32)
    for slot, (owner, place, rank) in enumerate(slots):
        step = partner("blk", owner, permuted)
        target = jnp.where(row % PER_WORKER == slot, step * (BLOCK * capacity) + rank, target)
    pick = one_hot(lane == target + (row // PER_WORKER) * capacity)
    for u in range(BLOCK):
        got = jnp.concatenate(
            [ordered(own[o][u], other[o][u], 1) for o in range(owners)], axis=0
        )
        cot[u] = dot(pick, got).astype(BF16)
    grads = cot[...].reshape(BLOCK * rows, FULL)
    for dy in range(3):
        windows = [
            masked[dy : dy + BLOCK, dx * PER_WORKER : (dx + BLOCK) * PER_WORKER] for dx in range(3)
        ]
        window = jnp.concatenate([w.reshape(BLOCK * rows, HALF) for w in windows], axis=1)
        value = dot_tn(jnp.maximum(window, jnp.zeros_like(window)), grads) * scale
        for dx in range(3):
            emit(value[dx * HALF : (dx + 1) * HALF], outs, 0, 3 * dy + dx)
    return slots


def first_gradient(
    scale, outside, cot, masked, saved_other, weight, weight_other, saved, *refs
):
    outs, (total, pre, full) = refs[:-3], refs[-3:]
    full[...] = ordered(weight[...], weight_other[...], 1)
    spread(cot, full, total, PER_WORKER)
    for m in range(MIDDLE):
        other = jnp.where(outside(m), 0.0, saved_other[m].astype(F32)).astype(BF16)
        live = ordered(masked[m], other, 1).astype(F32) > 0
        value = jnp.where(live, total[m], 0.0)
        pre[m] = value.astype(BF16).reshape(MIDDLE, PER_WORKER, FULL)
    size = MIDDLE * MIDDLE * PER_WORKER
    grads = pre[...].reshape(size, FULL)
    for dy in range(3):
        windows = [saved[dy : dy + MIDDLE, dx : dx + MIDDLE] for dx in range(3)]
        window = jnp.concatenate([w.reshape(size, HALF) for w in windows], axis=1)
        value = dot_tn(window, grads) * scale
        for dx in range(3):
            emit(value[dx * HALF : (dx + 1) * HALF], outs, 1, 3 * dy + dx)


def owner_spread(tile, tile_other, second, second_other, out, total, cot, full):
    row, lane = iota((FULL, FULL), 0), iota((FULL, FULL), 1)
    turn = one_hot(lane == (row % TILE_BLOCKS) * BLOCK + row // TILE_BLOCKS)
    for u in range(BLOCK):
        block = jnp.concatenate(
            [ordered(tile[r, u], tile_other[r, u], 1) for r in range(TILE_ROWS)], axis=0
        )
        cot[u] = dot(turn, block).astype(BF16)
    full[...] = ordered(second[...], second_other[...], 1)
    spread(cot, full, total, TILE_BLOCKS)
    out[...] = total[...].astype(BF16).reshape(out.shape)


def worker(scale, owners, columns, capacity, permuted, routing, *refs):
    parts = 1 if not permuted else owners
    inputs, refs = refs[: 2 * parts], refs[2 * parts :]
    (masked, saved_other, weight, weight_other, source), refs = refs[:5], refs[5:]
    if permuted:
        refs, sent = refs[:-1], refs[-1]
    outs, (counts, cot, total, pre, full, saved, arrived) = refs[:-7], refs[-7:]
    if permuted:
        kept, near, far = outs
        outs = (kept, sent)
    fetch = pltpu.make_async_copy(source, saved, arrived)
    fetch.start()
    slots = second_gradient(
        scale, owners, capacity, permuted, routing, *inputs, masked, cot, *outs, counts
    )
    fetch.wait()
    first_gradient(
        scale, outside_image(slots, owners, columns), cot, masked, saved_other, weight, weight_other,
        saved, *outs, total, pre, full,
    )
    if permuted:
        near[...] = sent[:2]
        far[...] = sent[2:]


def adjacent(step):
    me = lax.axis_index("blk")
    return (me ^ step) == me - 1, (me ^ step) == me + 1


def owner_canvas(owners, capacity, wide, permuted, routing, *refs):
    parts = 1 if not permuted else owners
    got, got_other = views(refs[:parts], owners), views(refs[parts : 2 * parts], owners)
    total, first, canvas = refs[2 * parts : 2 * parts + 3]
    rims, (table, pre, grown) = refs[2 * parts + 3 : -3], refs[-3:]
    owner_table(routing, table, owners, capacity)
    size, into = wide * capacity, MIDDLE * TILE_BLOCKS
    row, lane = iota((size, into), 0), iota((size, into), 1)
    picks = []
    for step in range(owners):
        worker = partner("blk", step, permuted)
        target = jnp.full((size, into), DEAD, I32)
        for rank in range(capacity):
            target = jnp.where(row % capacity == rank, table[worker * capacity + rank], target)
        at = row // capacity
        hits = (lane == target + at * TILE_BLOCKS) & (at < MIDDLE)
        picks.append(jnp.where(hits, 1.0, 0.0))
    pick = jnp.concatenate(picks, axis=0).T.astype(BF16)
    for m in range(MIDDLE):
        block = jnp.concatenate(
            [ordered(got[w][m], got_other[w][m], 1) for w in range(owners)], axis=0
        )
        value = jnp.where(dot(pick, block) > 0, total[m].reshape(into, FULL).astype(F32), 0.0)
        pre[m] = value.astype(BF16)
    spread(pre, first, grown, TILE_BLOCKS)
    height, depth = TILE_ROWS * WIDE, OUTER * TILE_BLOCKS
    row, lane = iota((height, depth), 0), iota((height, depth), 1)
    at_row, at_col = row // WIDE, row % WIDE
    n, place = lane // TILE_BLOCKS, lane % TILE_BLOCKS
    column = (place % TILE_COLS) * BLOCK + n - 2
    column = jnp.where(column < 0, column + 36, column)
    fold = one_hot((at_row == place // TILE_COLS) & (at_col == column))
    canvas[...] = jnp.zeros_like(canvas)
    for m in range(0, OUTER, 2):
        pair = jnp.concatenate(
            [grown[m + k].astype(BF16) for k in range(2)], axis=1
        )
        laid = dot(fold, pair).reshape(TILE_ROWS, WIDE, FULL)
        for r in range(TILE_ROWS):
            for k in range(2):
                canvas[r * BLOCK + m + k] += laid[r, :, k * HALF : (k + 1) * HALF]
    for k, rim in enumerate(rims):
        above, below = adjacent(2 * k + 1)
        top = jnp.concatenate([canvas[0], canvas[1]], axis=1)
        bottom = jnp.concatenate([canvas[HIGH - 2], canvas[HIGH - 1]], axis=1)
        rim[:WIDE] = jnp.where(below, bottom, jnp.where(above, top, 0.0)).astype(BF16)
        rim[WIDE:] = jnp.zeros((RIM - WIDE, FULL), BF16)


def add_far(kept, got, *sends):
    for k, out in enumerate(sends):
        out[...] = (kept[2 + k] + got[k].astype(F32)).astype(BF16)


def add_near(kept, got, keep, send):
    keep[...] = kept[0] + got[0].astype(F32)
    send[...] = (kept[1] + got[1].astype(F32)).astype(BF16)


def add_workers(kept, got_3, got_2, got_1, rim_1, rim_3, out, out_1, out_3):
    value = kept[...]
    for part in (got_3, got_2, got_1):
        value = value + part[...].astype(F32)
    value = value.astype(BF16).reshape(PART, FULL)
    out[...] = value
    for message, rim in ((out_1, rim_1), (out_3, rim_3)):
        message[:PART] = value
        message[PART:] = rim[...]


def column_message(canvas, got_1, got_3, out, rim, strip):
    out[:PART] = got_3[:PART]
    for j in range(2):
        c = 32 + 2 * lax.axis_index("col") + j
        strip[...] = canvas[pl.ds(2 * WIDE + c, 64, stride=WIDE), :]
        for step, got in ((1, got_1), (3, got_3)):
            rim[...] = got[PART:].astype(F32)
            row = rim[pl.ds(c, 1), :]
            above, below = adjacent(step)
            top, bottom = jnp.where(above, row, 0.0), jnp.where(below, row, 0.0)
            strip[0:1] += top[:, :HALF]
            strip[1:2] += top[:, HALF:]
            strip[62:63] += bottom[:, :HALF]
            strip[63:64] += bottom[:, HALF:]
        out[PART:, j * HALF : (j + 1) * HALF] = strip[...].astype(BF16)


def gather_image(tile, canvas, got_1, got_3, total):
    rows = TILE_ROWS * BLOCK * 32
    total[...] = tile[...].reshape(rows, HALF).astype(F32) + canvas[
        2 : HIGH - 2, :32, :
    ].reshape(rows, HALF)
    for step, got in ((1, got_1), (3, got_3)):
        rim = got[PART : PART + 32].astype(F32)
        above, below = adjacent(step)
        top, bottom = jnp.where(above, rim, 0.0), jnp.where(below, rim, 0.0)
        total[0:32] += top[:, :HALF]
        total[32:64] += top[:, HALF:]
        total[rows - 64 : rows - 32] += bottom[:, :HALF]
        total[rows - 32 : rows] += bottom[:, HALF:]


def rows_at(number):
    column = lax.axis_index("col")
    place = (column if number < 4 else 1 - column) * 4 + partner("blk", number % 4, True)
    return pl.ds(pl.multiple_of(place * ROWS, ROWS), ROWS)


def lay(tile, canvas, *refs):
    parts, (image, slab), outs, total = refs[:-5], refs[-5:-3], refs[-3:-1], refs[-1]
    gather_image(tile, canvas, parts[1], parts[3], total)
    whole = total[...].reshape(image.shape)
    image[...] = whole.astype(BF16)
    slab[...] = jnp.where(lax.axis_index("col") == 0, whole[:, 16:], whole[:, :16])
    for number, part in enumerate(parts):
        value = part[:PART].astype(F32).reshape(2, 9, ROWS, FULL)
        for out, grad in zip(outs, (0, 1)):
            out[:, rows_at(number), :] = value[grad]


def finish(slab, last, late, old, old_0, old_1, image, out_0, out_1, total, side, laid, sems):
    copies = []
    for k, (number, part) in enumerate(((6, late), (7, last))):
        laid[k] = part[:PART].astype(F32).reshape(2, 9, ROWS, FULL)
        for grad, dest in enumerate((out_0, out_1)):
            copies.append(
                pltpu.make_async_copy(
                    laid.at[k, grad], dest.at[:, rows_at(number), :], sems.at[k, grad]
                )
            )
            copies[-1].start()
    total[...] = slab[...].reshape(total.shape)
    strip = last[PART:].astype(F32)
    left = lax.axis_index("col") == 0
    at = jnp.where(left, 14, 0)
    for j in range(2):
        spot = (pl.ds(at + j, 64, stride=16), slice(None))
        total[spot] = total[spot] + strip[:, j * HALF : (j + 1) * HALF]
    side[...] = total[...].astype(BF16).reshape(side.shape)
    columns = pl.ds(pl.multiple_of(jnp.where(left, 16, 0), 16), 16)
    copies.append(pltpu.make_async_copy(side, image.at[:, columns, :], sems.at[2, 0]))
    copies[-1].start()
    for copy in copies:
        copy.wait()


def swap(value, axis="ch"):
    return lax.ppermute(value, axis, [(0, 1), (1, 0)])


def flip(value, axis, step):
    size = lax.axis_size(axis)
    return lax.ppermute(value, axis, [(i, i ^ step) for i in range(size)])


def neighbours(axis):
    size = lax.axis_size(axis)
    up = [(i, (i + 1) % size) for i in range(size - 1)]
    return up, [(j, i) for i, j in up]


def shards(grad_out, saved_input, saved_pre, first_weight, second_weight, assignment):
    owners = lax.axis_size("blk")
    columns = lax.axis_size("col")
    capacity = max(2, TILE_BLOCKS // owners)
    wide = MIDDLE if (MIDDLE * capacity) % 16 == 0 else 16
    scale = 1.0 / math.sqrt(owners * columns * PER_WORKER * BLOCK * BLOCK)
    permuted = owners == 4 and columns == 2
    parts = owners if permuted else 1
    routing = assignment[0]
    shape = jax.ShapeDtypeStruct
    tables = [pltpu.SMEM((owners * capacity + 1,), I32)]
    counts = [pltpu.SMEM((owners,), I32)]

    def pieces(*dims):
        return [shape(dims, BF16)] * owners if permuted else [shape((owners,) + dims, BF16)]

    def exchange(values):
        if permuted:
            return list(values[:1]) + [flip(values[k], "blk", k) for k in (3, 2, 1)][::-1]
        return [lax.all_to_all(values[0], "blk", split_axis=0, concat_axis=0, tiled=True)]

    tie = lax.optimization_barrier
    tile = grad_out.reshape(TILE_ROWS, BLOCK, TILE_COLS * BLOCK, HALF)
    outgoing = call(
        functools.partial(pack_cotangents, owners, capacity, permuted),
        pieces(BLOCK, BLOCK * capacity, HALF),
        [HBM, HBM],
        [
            pltpu.VMEM((2,) + routing.shape, I32),
            pltpu.VMEM(tile.shape, BF16),
            pltpu.VMEM(routing.shape, I32),
            pltpu.SemaphoreType.DMA((2,)),
        ],
        (1, 1), "pack_cotangents",
    )(*[pltpu.with_memory_space_constraint(value, pltpu.HBM) for value in (routing, tile)])
    saved_slots = saved_pre[0, 0].transpose(1, 2, 0, 3)
    saved_slots = saved_slots.reshape(MIDDLE, MIDDLE * PER_WORKER, HALF)
    outgoing, saved_here = tie((outgoing, saved_slots))
    incoming = exchange(outgoing)

    masked, *to_owners = call(
        functools.partial(pack_saved, owners, columns, capacity, wide, permuted),
        [shape((MIDDLE, MIDDLE * PER_WORKER, HALF), BF16)] + pieces(MIDDLE, wide * capacity, HALF),
        [SMEM, VMEM], counts + tables, (1, 1), "pack_saved",
    )(routing, saved_here)
    second_other, saved_other = swap(second_weight), swap(saved_slots)

    incoming, to_owners = tie((incoming[::-1], to_owners[::-1]))
    incoming, to_owners = incoming[::-1], to_owners[::-1]
    incoming_other = [swap(value) for value in incoming]
    at_owner = exchange(to_owners)

    saved_tiles = saved_input[0, 0].transpose(1, 2, 0, 3)
    if permuted:
        part = (2, 9, ROWS, FULL)
        halved = [shape((4,) + part, F32)] + [shape((2,) + part, BF16)] * 2
    else:
        halved = [shape((2, 9, HALF, FULL), F32)]
    terms = call(
        functools.partial(worker, scale, owners, columns, capacity, permuted),
        halved,
        [SMEM] + [VMEM] * (2 * parts + 4) + [HBM],
        counts
        + [
            pltpu.VMEM((BLOCK, BLOCK * PER_WORKER, FULL), BF16),
            pltpu.VMEM((MIDDLE, MIDDLE * PER_WORKER, FULL), F32),
            pltpu.VMEM((MIDDLE, MIDDLE, PER_WORKER, FULL), BF16),
            pltpu.VMEM((9, FULL, FULL), BF16),
            pltpu.VMEM(saved_tiles.shape, BF16),
            pltpu.SemaphoreType.DMA,
        ]
        + ([pltpu.VMEM((4,) + part, BF16)] if permuted else []),
        (1, 1), "worker",
    )(
        routing, *incoming, *incoming_other, masked, saved_other, second_weight, second_other,
        pltpu.with_memory_space_constraint(saved_tiles, pltpu.HBM),
    )

    if permuted:
        kept, near, far = terms
        far, at_owner[2], at_owner[1] = tie((far, at_owner[2], at_owner[1]))
        far, tile_mine, tile_here = tie((far, tile, tile))
    else:
        terms, tile_mine, tile_here = tie((terms, tile, tile))
    total = call(
        owner_spread,
        shape((MIDDLE, MIDDLE, TILE_BLOCKS, FULL), BF16),
        [VMEM] * 4,
        [
            pltpu.VMEM((MIDDLE, MIDDLE * TILE_BLOCKS, FULL), F32),
            pltpu.VMEM((BLOCK, BLOCK * TILE_BLOCKS, FULL), BF16),
            pltpu.VMEM((9, FULL, FULL), BF16),
        ],
        (1, 1), "owner_spread",
    )(tile_here, swap(tile_mine), second_weight, second_other)

    def owner(at_owner):
        at_owner_other = [swap(value) for value in at_owner]
        return call(
            functools.partial(owner_canvas, owners, capacity, wide, permuted),
            [shape((HIGH, WIDE, HALF), F32)] + [shape((RIM, FULL), BF16)] * (2 if permuted else 0),
            [SMEM] + [VMEM] * (2 * len(at_owner) + 2),
            tables
            + [
                pltpu.VMEM((MIDDLE, MIDDLE * TILE_BLOCKS, FULL), BF16),
                pltpu.VMEM((OUTER, OUTER * TILE_BLOCKS, HALF), F32),
            ],
            (1, 1), "owner_canvas",
        )(routing, *at_owner, *at_owner_other, total, first_weight)

    if permuted:
        far_got, near_got = swap(far, "col"), swap(near, "col")
        total, far_got = tie((total, far_got))
        sends = call(add_far, [shape(part, BF16)] * 2, [VMEM] * 2, [], (1, 1), "add_far")(
            kept, far_got
        )
        sends, at_owner[3] = tie((sends[::-1], at_owner[3]))
        got = [flip(sends[0], "blk", 3), flip(sends[1], "blk", 2)]
        canvas, *rims = owner(at_owner)
        near_got, canvas = tie((near_got, canvas))
        keep, send = call(
            add_near, [shape(part, F32), shape(part, BF16)], [VMEM] * 2, [], (1, 1), "add_near",
        )(kept, near_got)
        got.append(flip(send, "blk", 1))
        message = shape((PART, FULL), BF16)
        wider = shape((PART + RIM, FULL), BF16)
        own, *wides = call(
            add_workers, [message, wider, wider], [VMEM] * 6, [], (1, 1), "add_workers",
        )(keep, *got, *rims)
        got_2, got_3, got_1 = flip(own, "blk", 2), flip(wides[1], "blk", 3), flip(wides[0], "blk", 1)
        across = [swap(value, "col") for value in (own, got_1[:PART])]
        got_3, got_2, got_1, across = tie((got_3, got_2, got_1, across))
        got = [got_1, got_2, got_3]
        last = call(
            column_message, shape((PART + 64, FULL), BF16), [VMEM] * 3,
            [pltpu.VMEM((RIM, FULL), F32), pltpu.VMEM((64, HALF), F32)],
            (1, 1), "column_message",
        )(canvas.reshape(HIGH * WIDE, HALF), got[0], got[2])
        across += [swap(got_2, "col"), swap(last, "col")]
        slab = (TILE_ROWS * BLOCK, 16, HALF)
        weights = [shape((9, HALF, FULL), F32)] * 2
        early, *outs = call(
            lay, [shape(grad_out.shape, BF16), shape(slab, F32)] + weights, [VMEM] * 8,
            [pltpu.VMEM((TILE_ROWS * BLOCK * 32, HALF), F32)], (1, 1), "lay",
        )(grad_out, canvas, own, *got, *across[:2])
        grad_in, grad_second, grad_first = pl.pallas_call(
            finish,
            out_shape=[shape(grad_out.shape, BF16)] + weights,
            in_specs=[VMEM] * 3 + [HBM] * 3,
            out_specs=[HBM] * 3,
            scratch_shapes=[
                pltpu.VMEM((TILE_ROWS * BLOCK * 16, HALF), F32),
                pltpu.VMEM(slab, BF16),
                pltpu.VMEM((2, 2, 9, ROWS, FULL), F32),
                pltpu.SemaphoreType.DMA((3, 2)),
            ],
            input_output_aliases={3: 0, 4: 1, 5: 2},
            compiler_params=pltpu.CompilerParams(vmem_limit_bytes=48 * 1024 * 1024),
            cost_estimate=pl.CostEstimate(flops=1, bytes_accessed=1, transcendentals=0),
            name="finish",
        )(outs[0], across[3], across[2], early, *outs[1:])
        return (grad_in, grad_first, grad_second)

    grad_first, grad_second = lax.psum((terms[0][1], terms[0][0]), ("blk", "col"))
    [canvas] = owner(at_owner)
    up, down = neighbours("blk")
    from_above = lax.ppermute(canvas[HIGH - 2 :].astype(BF16), "blk", up).astype(F32)
    from_below = lax.ppermute(canvas[:2].astype(BF16), "blk", down).astype(F32)
    inner = canvas[2 : HIGH - 2]
    inner = inner.at[:2].add(from_above).at[-2:].add(from_below)
    up, down = neighbours("col")
    from_left = lax.ppermute(inner[:, 32:34].astype(BF16), "col", up).astype(F32)
    from_right = lax.ppermute(inner[:, 34:36].astype(BF16), "col", down).astype(F32)
    inner = inner[:, :32].at[:, :2].add(from_left).at[:, -2:].add(from_right)
    grad_in = (grad_out.astype(F32) + inner).astype(BF16)
    return (grad_in, grad_first, grad_second)


def solution(mesh):
    return jax.shard_map(
        shards,
        mesh=mesh,
        in_specs=(
            P(("groups", "blk"), "col", "ch"),
            P(("groups", "col"), "blk", None, None, None, "ch"),
            P(("groups", "col"), "blk", None, None, None, "ch"),
            P(None, "ch", None),
            P(None, "ch", None),
            P(("groups", "col"), None, None),
        ),
        out_specs=(
            P(("groups", "blk"), "col", "ch"),
            P("groups", "ch", None),
            P("groups", "ch", None),
        ),
        check_vma=False,
    )
```

```python
import functools
import math

import jax
import jax.numpy as jnp
from jax import lax
from jax.experimental import pallas as pl
from jax.experimental.pallas import tpu as pltpu
from jax.sharding import PartitionSpec as P

BLOCK = 8
TILE_ROWS = 8
TILE_COLS = 4
TILE_BLOCKS = 32
PER_WORKER = 16
MIDDLE = 10
OUTER = 12
HALF = 128
FULL = 256
DEAD = -4096
HIGH = 68
RIM = 48
ROWS = 16
PART = 288
WIDE = 40

BF16 = jnp.bfloat16
F32 = jnp.float32
I32 = jnp.int32

VMEM = pl.BlockSpec(memory_space=pltpu.VMEM)
HBM = pl.BlockSpec(memory_space=pltpu.HBM)
SMEM = pl.BlockSpec(memory_space=pltpu.SMEM)


def call(body, outs, specs, scratch, cost, name):
    return pl.pallas_call(
        body,
        out_shape=outs,
        in_specs=specs,
        out_specs=jax.tree.map(lambda _: VMEM, outs),
        scratch_shapes=scratch,
        compiler_params=pltpu.CompilerParams(vmem_limit_bytes=48 * 1024 * 1024),
        cost_estimate=pl.CostEstimate(flops=cost[0], bytes_accessed=cost[1], transcendentals=0),
        name=name,
    )


def iota(shape, dim):
    return lax.broadcasted_iota(I32, shape, dim)


def one_hot(hits):
    return jnp.where(hits, 1.0, 0.0).astype(BF16)


def dot(a, b):
    return jnp.dot(a, b, preferred_element_type=F32)


def dot_nt(a, b):
    return lax.dot_general(a, b, (((1,), (1,)), ((), ())), preferred_element_type=F32)


def dot_tn(a, b):
    return lax.dot_general(a, b, (((0,), (0,)), ((), ())), preferred_element_type=F32)


def owner_table(routing, table, owners, capacity):
    me = lax.axis_index("blk")

    def clear(number, carry):
        table[number] = DEAD
        return carry

    lax.fori_loop(0, owners * capacity, clear, 0)

    def worker(number, carry):
        count = jnp.int32(0)
        for slot in range(PER_WORKER):
            code = routing[number, slot]
            hit = (code // TILE_BLOCKS) == me
            table[jnp.where(hit, number * capacity + count, owners * capacity)] = code % TILE_BLOCKS
            count = count + jnp.where(hit, 1, 0)
        return carry

    lax.fori_loop(0, owners, worker, 0)


def worker_codes(routing, counts, owners):
    me = lax.axis_index("blk")

    def clear(number, carry):
        counts[number] = 0
        return carry

    lax.fori_loop(0, owners, clear, 0)
    slots = []
    for slot in range(PER_WORKER):
        code = routing[me, slot]
        owner = code // TILE_BLOCKS
        rank = counts[owner]
        counts[owner] = rank + 1
        slots.append((owner, code % TILE_BLOCKS, rank))
    return slots


def views(refs, count):
    return list(refs) if len(refs) == count else [refs[0].at[k] for k in range(count)]


def partner(axis, step, permuted):
    return step ^ lax.axis_index(axis) if permuted else step


def pack_cotangents(owners, capacity, permuted, listed, source, *refs):
    outs, (places, tile, codes, arrived) = refs[:-4], refs[-4:]
    fetch = pltpu.make_async_copy(source, tile, arrived.at[0])
    fetch.start()
    lists = pltpu.make_async_copy(listed, codes, arrived.at[1])
    lists.start()
    lists.wait()
    hit = (codes[...] // TILE_BLOCKS) == lax.axis_index("blk")
    places[0] = jnp.where(hit, codes[...] % TILE_BLOCKS + 1, 0)
    before = (iota((PER_WORKER, PER_WORKER), 0) < iota((PER_WORKER, PER_WORKER), 1))
    places[1] = dot(one_hot(hit), one_hot(before)).astype(I32)
    rows = BLOCK * capacity
    row, lane = iota((rows, FULL), 0), iota((rows, FULL), 1)
    picks = []
    for step in range(owners):
        at = pl.ds(partner("blk", step, permuted), 1)
        same = places[1, at, :] == iota((rows, PER_WORKER), 0) % capacity
        place = jnp.sum(jnp.where(same, places[0, at, :], 0).astype(F32), axis=1, keepdims=True)
        target = (place.astype(I32) - 1) * BLOCK
        picks.append(one_hot(lane == target + row // capacity))
    pick = jnp.concatenate(picks, axis=0)
    fetch.wait()
    for u in range(0, BLOCK, 2):
        pair = [
            jnp.concatenate([tile[r, u + k] for r in range(TILE_ROWS)], axis=0) for k in range(2)
        ]
        moved = dot(pick, jnp.concatenate(pair, axis=1)).astype(BF16)
        for step, out in enumerate(views(outs, owners)):
            part = moved[step * rows : (step + 1) * rows]
            out[u] = part[:, :HALF]
            out[u + 1] = part[:, HALF:]


def outside_image(slots, owners, columns):
    column = lax.axis_index("col")
    row = iota((MIDDLE * PER_WORKER, HALF), 0)
    flags = jnp.zeros_like(row)
    for slot, (owner, place, rank) in enumerate(slots):
        block_row, block_col = place // TILE_COLS, place % TILE_COLS
        flag = (
            jnp.where((owner == 0) & (block_row == 0), 1, 0)
            + jnp.where((owner == owners - 1) & (block_row == TILE_ROWS - 1), 2, 0)
            + jnp.where((column == 0) & (block_col == 0), 4, 0)
            + jnp.where((column == columns - 1) & (block_col == TILE_COLS - 1), 8, 0)
        )
        flags = jnp.where(row % PER_WORKER == slot, flag, flags)
    across = row // PER_WORKER
    sides = (((flags & 4) != 0) & (across == 0)) | (((flags & 8) != 0) & (across == MIDDLE - 1))

    def here(m):
        if m == 0:
            return sides | ((flags & 1) != 0)
        if m == MIDDLE - 1:
            return sides | ((flags & 2) != 0)
        return sides

    return here


def pack_saved(owners, columns, capacity, wide, permuted, routing, saved, masked, *refs):
    outs, counts, table = refs[:-2], refs[-2], refs[-1]

    def clear(number, carry):
        table[number] = DEAD
        return carry

    lax.fori_loop(0, owners * capacity, clear, 0)
    slots = worker_codes(routing, counts, owners)
    rows = MIDDLE * PER_WORKER
    for slot, (owner, place, rank) in enumerate(slots):
        table[owner * capacity + rank] = slot
    outside = outside_image(slots, owners, columns)
    for m in range(MIDDLE):
        masked[m] = jnp.where(outside(m), 0.0, saved[m].astype(F32)).astype(BF16)
    size = wide * capacity
    row, lane = iota((size, FULL), 0), iota((size, FULL), 1)
    picks = []
    for step in range(owners):
        owner = partner("blk", step, permuted)
        target = jnp.full((size, FULL), DEAD, I32)
        for rank in range(capacity):
            target = jnp.where(row % capacity == rank, table[owner * capacity + rank], target)
        at = row // capacity
        picks.append(one_hot((lane == target + at * PER_WORKER) & (at < MIDDLE)))
    pick = jnp.concatenate(picks, axis=0)
    filler = jnp.zeros((FULL - rows, FULL), BF16)
    for m in range(0, MIDDLE, 2):
        pair = jnp.concatenate([masked[m], masked[m + 1]], axis=1)
        moved = dot(pick, jnp.concatenate([pair, filler], axis=0)).astype(BF16)
        for step, out in enumerate(views(outs, owners)):
            part = moved[step * size : (step + 1) * size]
            out[m] = part[:, :HALF]
            out[m + 1] = part[:, HALF:]


def ordered(own, other, axis):
    first = lax.axis_index("ch") == 0
    return jnp.concatenate(
        [jnp.where(first, own, other), jnp.where(first, other, own)], axis=axis
    )


def deal(value, kept, sent, grad, tap):
    low, high = value[: HALF // 2], value[HALF // 2 :]
    mine = lax.axis_index("col") == 0
    keep, send = jnp.where(mine, low, high), jnp.where(mine, high, low).astype(BF16)
    for k in range(4):
        step, rows = partner("blk", k, True), slice(k * ROWS, (k + 1) * ROWS)
        kept[step, grad, tap] = keep[rows]
        sent[step, grad, tap] = send[rows]


def emit(value, outs, grad, tap):
    if len(outs) == 2:
        deal(value, outs[0], outs[1], grad, tap)
    else:
        outs[0][grad, tap] = value


def spread(values, weight, total, places):
    height, extent = values.shape[:2]
    inputs = values[...].reshape(height * extent, FULL)
    width, step = weight.shape[1], places
    for dy in range(3):
        taps = jnp.concatenate([weight[3 * dy + dx] for dx in range(3)], axis=0)
        part = dot_nt(inputs, taps).reshape(height, extent, 3 * width)
        p, q, r = [part[:, :, dx * width : (dx + 1) * width] for dx in range(3)]
        sums = [
            p[:, :step],
            p[:, step : 2 * step] + q[:, :step],
            p[:, 2 * step :] + q[:, step : extent - step] + r[:, : extent - 2 * step],
            q[:, extent - step :] + r[:, extent - 2 * step : extent - step],
            r[:, extent - step :],
        ]
        at = 0
        for value in sums:
            size = value.shape[1]
            here = slice(at, at + size)
            if dy == 0:
                total[:height, here] = value
            else:
                total[dy : dy + height - 1, here] += value[:-1]
                total[dy + height - 1, here] = value[height - 1]
            at += size


def second_gradient(scale, owners, capacity, permuted, routing, *refs):
    parts = 1 if not permuted else owners
    own, other = views(refs[:parts], owners), views(refs[parts : 2 * parts], owners)
    masked, cot = refs[2 * parts : 2 * parts + 2]
    outs, counts = refs[2 * parts + 2 : -1], refs[-1]
    slots = worker_codes(routing, counts, owners)
    rows, inner = BLOCK * PER_WORKER, owners * BLOCK * capacity
    row, lane = iota((rows, inner), 0), iota((rows, inner), 1)
    target = jnp.full((rows, inner), DEAD, I32)
    for slot, (owner, place, rank) in enumerate(slots):
        step = partner("blk", owner, permuted)
        target = jnp.where(row % PER_WORKER == slot, step * (BLOCK * capacity) + rank, target)
    pick = one_hot(lane == target + (row // PER_WORKER) * capacity)
    for u in range(BLOCK):
        got = jnp.concatenate(
            [ordered(own[o][u], other[o][u], 1) for o in range(owners)], axis=0
        )
        cot[u] = dot(pick, got).astype(BF16)
    grads = cot[...].reshape(BLOCK * rows, FULL)
    turned = []
    for dx in range(3):
        window = masked[:, dx * PER_WORKER : (dx + BLOCK) * PER_WORKER].reshape(MIDDLE * rows, HALF)
        turned.append(jnp.maximum(window, jnp.zeros_like(window)).T)
    turned = jnp.concatenate(turned, axis=0)
    for dy in range(3):
        value = dot(turned[:, dy * rows : (dy + BLOCK) * rows], grads) * scale
        for dx in range(3):
            emit(value[dx * HALF : (dx + 1) * HALF], outs, 0, 3 * dy + dx)
    return slots


def first_gradient(
    scale, outside, cot, masked, saved_other, weight, weight_other, saved, *refs
):
    outs, (total, pre, full) = refs[:-3], refs[-3:]
    full[...] = ordered(weight[...], weight_other[...], 1)
    spread(cot, full, total, PER_WORKER)
    for m in range(MIDDLE):
        other = jnp.where(outside(m), 0.0, saved_other[m].astype(F32)).astype(BF16)
        live = ordered(masked[m], other, 1).astype(F32) > 0
        value = jnp.where(live, total[m], 0.0)
        pre[m] = value.astype(BF16).reshape(MIDDLE, PER_WORKER, FULL)
    size = MIDDLE * MIDDLE * PER_WORKER
    grads = pre[...].reshape(size, FULL)
    for dy in range(3):
        windows = [saved[dy : dy + MIDDLE, dx : dx + MIDDLE] for dx in range(3)]
        window = jnp.concatenate([w.reshape(size, HALF) for w in windows], axis=1)
        value = dot_tn(window, grads) * scale
        for dx in range(3):
            emit(value[dx * HALF : (dx + 1) * HALF], outs, 1, 3 * dy + dx)


def owner_spread(tile, tile_other, second, second_other, out, total, cot, full):
    row, lane = iota((FULL, FULL), 0), iota((FULL, FULL), 1)
    turn = one_hot(lane == (row % TILE_BLOCKS) * BLOCK + row // TILE_BLOCKS)
    for u in range(BLOCK):
        block = jnp.concatenate(
            [ordered(tile[r, u], tile_other[r, u], 1) for r in range(TILE_ROWS)], axis=0
        )
        cot[u] = dot(turn, block).astype(BF16)
    full[...] = ordered(second[...], second_other[...], 1)
    spread(cot, full, total, TILE_BLOCKS)
    out[...] = total[...].astype(BF16).reshape(out.shape)


def worker(scale, owners, columns, capacity, permuted, routing, *refs):
    parts = 1 if not permuted else owners
    inputs, refs = refs[: 2 * parts], refs[2 * parts :]
    (masked, saved_other, weight, weight_other, source), refs = refs[:5], refs[5:]
    if permuted:
        refs, sent = refs[:-1], refs[-1]
    outs, (counts, cot, total, pre, full, saved, arrived) = refs[:-7], refs[-7:]
    if permuted:
        kept, near, far = outs
        outs = (kept, sent)
    fetch = pltpu.make_async_copy(source, saved, arrived)
    fetch.start()
    slots = second_gradient(
        scale, owners, capacity, permuted, routing, *inputs, masked, cot, *outs, counts
    )
    fetch.wait()
    first_gradient(
        scale, outside_image(slots, owners, columns), cot, masked, saved_other, weight, weight_other,
        saved, *outs, total, pre, full,
    )
    if permuted:
        near[...] = sent[:2]
        far[...] = sent[2:]


def adjacent(step):
    me = lax.axis_index("blk")
    return (me ^ step) == me - 1, (me ^ step) == me + 1


def owner_canvas(owners, capacity, wide, permuted, routing, *refs):
    parts = 1 if not permuted else owners
    got, got_other = views(refs[:parts], owners), views(refs[parts : 2 * parts], owners)
    total, first, canvas = refs[2 * parts : 2 * parts + 3]
    rims, (table, pre, grown) = refs[2 * parts + 3 : -3], refs[-3:]
    owner_table(routing, table, owners, capacity)
    size, into = wide * capacity, MIDDLE * TILE_BLOCKS
    row, lane = iota((size, into), 0), iota((size, into), 1)
    picks = []
    for step in range(owners):
        worker = partner("blk", step, permuted)
        target = jnp.full((size, into), DEAD, I32)
        for rank in range(capacity):
            target = jnp.where(row % capacity == rank, table[worker * capacity + rank], target)
        at = row // capacity
        hits = (lane == target + at * TILE_BLOCKS) & (at < MIDDLE)
        picks.append(jnp.where(hits, 1.0, 0.0))
    pick = jnp.concatenate(picks, axis=0).T.astype(BF16)
    for m in range(MIDDLE):
        block = jnp.concatenate(
            [ordered(got[w][m], got_other[w][m], 1) for w in range(owners)], axis=0
        )
        value = jnp.where(dot(pick, block) > 0, total[m].reshape(into, FULL).astype(F32), 0.0)
        pre[m] = value.astype(BF16)
    spread(pre, first, grown, TILE_BLOCKS)
    height, depth = TILE_ROWS * WIDE, OUTER * TILE_BLOCKS
    row, lane = iota((height, depth), 0), iota((height, depth), 1)
    at_row, at_col = row // WIDE, row % WIDE
    n, place = lane // TILE_BLOCKS, lane % TILE_BLOCKS
    column = (place % TILE_COLS) * BLOCK + n - 2
    column = jnp.where(column < 0, column + 36, column)
    fold = one_hot((at_row == place // TILE_COLS) & (at_col == column))
    canvas[...] = jnp.zeros_like(canvas)
    for m in range(0, OUTER, 2):
        pair = jnp.concatenate(
            [grown[m + k].astype(BF16) for k in range(2)], axis=1
        )
        laid = dot(fold, pair).reshape(TILE_ROWS, WIDE, FULL)
        for r in range(TILE_ROWS):
            for k in range(2):
                canvas[r * BLOCK + m + k] += laid[r, :, k * HALF : (k + 1) * HALF]
    for k, rim in enumerate(rims):
        above, below = adjacent(2 * k + 1)
        top = jnp.concatenate([canvas[0], canvas[1]], axis=1)
        bottom = jnp.concatenate([canvas[HIGH - 2], canvas[HIGH - 1]], axis=1)
        here = jnp.where(below, bottom, jnp.where(above, top, 0.0))
        rim[...] = jnp.concatenate([here, jnp.zeros((RIM - WIDE, FULL), F32)], axis=0).astype(BF16)


def add_far(kept, got, *sends):
    for k, out in enumerate(sends):
        out[...] = (kept[2 + k] + got[k].astype(F32)).astype(BF16)


def add_near(kept, got, keep, send):
    keep[...] = kept[0] + got[0].astype(F32)
    send[...] = (kept[1] + got[1].astype(F32)).astype(BF16)


def add_workers(kept, got_3, got_2, got_1, rim_1, rim_3, out, out_1, out_3):
    value = kept[...]
    for part in (got_3, got_2, got_1):
        value = value + part[...].astype(F32)
    value = value.astype(BF16).reshape(PART, FULL)
    out[...] = value
    for message, rim in ((out_1, rim_1), (out_3, rim_3)):
        message[:PART] = value
        message[PART:] = rim[...]


def column_message(canvas, got_1, got_3, out, rim, strip):
    out[:PART] = got_3[:PART]
    for j in range(2):
        c = 32 + 2 * lax.axis_index("col") + j
        strip[...] = canvas[pl.ds(2 * WIDE + c, 64, stride=WIDE), :]
        for step, got in ((1, got_1), (3, got_3)):
            rim[...] = got[PART:].astype(F32)
            row = rim[pl.ds(c, 1), :]
            above, below = adjacent(step)
            top, bottom = jnp.where(above, row, 0.0), jnp.where(below, row, 0.0)
            strip[0:1] += top[:, :HALF]
            strip[1:2] += top[:, HALF:]
            strip[62:63] += bottom[:, :HALF]
            strip[63:64] += bottom[:, HALF:]
        out[PART:, j * HALF : (j + 1) * HALF] = strip[...].astype(BF16)


def gather_image(tile, canvas, got_1, got_3, total):
    rows = TILE_ROWS * BLOCK * 32
    total[...] = tile[...].reshape(rows, HALF).astype(F32) + canvas[
        2 : HIGH - 2, :32, :
    ].reshape(rows, HALF)
    for step, got in ((1, got_1), (3, got_3)):
        rim = got[PART : PART + 32].astype(F32)
        above, below = adjacent(step)
        top, bottom = jnp.where(above, rim, 0.0), jnp.where(below, rim, 0.0)
        total[0:32] += top[:, :HALF]
        total[32:64] += top[:, HALF:]
        total[rows - 64 : rows - 32] += bottom[:, :HALF]
        total[rows - 32 : rows] += bottom[:, HALF:]


def rows_at(number):
    column = lax.axis_index("col")
    place = (column if number < 4 else 1 - column) * 4 + partner("blk", number % 4, True)
    return pl.ds(pl.multiple_of(place * ROWS, ROWS), ROWS)


def lay(tile, canvas, *refs):
    parts, (image, slab), outs, total = refs[:-5], refs[-5:-3], refs[-3:-1], refs[-1]
    gather_image(tile, canvas, parts[1], parts[3], total)
    whole = total[...].reshape(image.shape)
    image[...] = whole.astype(BF16)
    slab[...] = jnp.where(lax.axis_index("col") == 0, whole[:, 16:], whole[:, :16])
    for number, part in enumerate(parts):
        value = part[:PART].astype(F32).reshape(2, 9, ROWS, FULL)
        for out, grad in zip(outs, (0, 1)):
            out[:, rows_at(number), :] = value[grad]


def finish(slab, last, late, old, old_0, old_1, image, out_0, out_1, total, side, laid, sems):
    copies = []
    for k, (number, part) in enumerate(((6, late), (7, last))):
        laid[k] = part[:PART].astype(F32).reshape(2, 9, ROWS, FULL)
        for grad, dest in enumerate((out_0, out_1)):
            copies.append(
                pltpu.make_async_copy(
                    laid.at[k, grad], dest.at[:, rows_at(number), :], sems.at[k, grad]
                )
            )
            copies[-1].start()
    rows = TILE_ROWS * BLOCK * 16
    total[:rows] = slab[...].reshape(rows, HALF)
    strip = last[PART:].astype(F32)
    left = lax.axis_index("col") == 0
    at = jnp.where(left, 14, 0)
    for j in range(2):
        spot = (pl.ds(at + j, 64, stride=16), slice(None))
        total[spot] = total[spot] + strip[:, j * HALF : (j + 1) * HALF]
    side[...] = total[:rows].astype(BF16).reshape(side.shape)
    columns = pl.ds(pl.multiple_of(jnp.where(left, 16, 0), 16), 16)
    copies.append(pltpu.make_async_copy(side, image.at[:, columns, :], sems.at[2, 0]))
    copies[-1].start()
    for copy in copies:
        copy.wait()


def swap(value, axis="ch"):
    return lax.ppermute(value, axis, [(0, 1), (1, 0)])


def flip(value, axis, step):
    size = lax.axis_size(axis)
    return lax.ppermute(value, axis, [(i, i ^ step) for i in range(size)])


def neighbours(axis):
    size = lax.axis_size(axis)
    up = [(i, (i + 1) % size) for i in range(size - 1)]
    return up, [(j, i) for i, j in up]


def shards(grad_out, saved_input, saved_pre, first_weight, second_weight, assignment):
    owners = lax.axis_size("blk")
    columns = lax.axis_size("col")
    capacity = max(2, TILE_BLOCKS // owners)
    wide = MIDDLE if (MIDDLE * capacity) % 16 == 0 else 16
    scale = 1.0 / math.sqrt(owners * columns * PER_WORKER * BLOCK * BLOCK)
    permuted = owners == 4 and columns == 2
    parts = owners if permuted else 1
    routing = assignment[0]
    shape = jax.ShapeDtypeStruct
    tables = [pltpu.SMEM((owners * capacity + 1,), I32)]
    counts = [pltpu.SMEM((owners,), I32)]

    def pieces(*dims):
        return [shape(dims, BF16)] * owners if permuted else [shape((owners,) + dims, BF16)]

    def exchange(values):
        if permuted:
            return list(values[:1]) + [flip(values[k], "blk", k) for k in (3, 2, 1)][::-1]
        return [lax.all_to_all(values[0], "blk", split_axis=0, concat_axis=0, tiled=True)]

    tie = lax.optimization_barrier
    tile = grad_out.reshape(TILE_ROWS, BLOCK, TILE_COLS * BLOCK, HALF)
    outgoing = call(
        functools.partial(pack_cotangents, owners, capacity, permuted),
        pieces(BLOCK, BLOCK * capacity, HALF),
        [HBM, HBM],
        [
            pltpu.VMEM((2,) + routing.shape, I32),
            pltpu.VMEM(tile.shape, BF16),
            pltpu.VMEM(routing.shape, I32),
            pltpu.SemaphoreType.DMA((2,)),
        ],
        (1, 1), "pack_cotangents",
    )(*[pltpu.with_memory_space_constraint(value, pltpu.HBM) for value in (routing, tile)])
    saved_slots = saved_pre[0, 0].transpose(1, 2, 0, 3)
    saved_slots = saved_slots.reshape(MIDDLE, MIDDLE * PER_WORKER, HALF)
    outgoing, saved_here = tie((outgoing, saved_slots))
    incoming = exchange(outgoing)

    masked, *to_owners = call(
        functools.partial(pack_saved, owners, columns, capacity, wide, permuted),
        [shape((MIDDLE, MIDDLE * PER_WORKER, HALF), BF16)] + pieces(MIDDLE, wide * capacity, HALF),
        [SMEM, VMEM], counts + tables, (1, 1), "pack_saved",
    )(routing, saved_here)
    second_other, saved_other = swap(second_weight), swap(saved_slots)

    incoming, to_owners = tie((incoming[::-1], to_owners[::-1]))
    incoming, to_owners = incoming[::-1], to_owners[::-1]
    incoming_other = [swap(value) for value in incoming]
    at_owner = exchange(to_owners)

    saved_tiles = saved_input[0, 0].transpose(1, 2, 0, 3)
    if permuted:
        part = (2, 9, ROWS, FULL)
        halved = [shape((4,) + part, F32)] + [shape((2,) + part, BF16)] * 2
    else:
        halved = [shape((2, 9, HALF, FULL), F32)]
    terms = call(
        functools.partial(worker, scale, owners, columns, capacity, permuted),
        halved,
        [SMEM] + [VMEM] * (2 * parts + 4) + [HBM],
        counts
        + [
            pltpu.VMEM((BLOCK, BLOCK * PER_WORKER, FULL), BF16),
            pltpu.VMEM((MIDDLE, MIDDLE * PER_WORKER, FULL), F32),
            pltpu.VMEM((MIDDLE, MIDDLE, PER_WORKER, FULL), BF16),
            pltpu.VMEM((9, FULL, FULL), BF16),
            pltpu.VMEM(saved_tiles.shape, BF16),
            pltpu.SemaphoreType.DMA,
        ]
        + ([pltpu.VMEM((4,) + part, BF16)] if permuted else []),
        (1, 1), "worker",
    )(
        routing, *incoming, *incoming_other, masked, saved_other, second_weight, second_other,
        pltpu.with_memory_space_constraint(saved_tiles, pltpu.HBM),
    )

    if permuted:
        kept, near, far = terms
        far, at_owner[2], at_owner[1] = tie((far, at_owner[2], at_owner[1]))
        far, tile_mine, tile_here = tie((far, tile, tile))
    else:
        terms, tile_mine, tile_here = tie((terms, tile, tile))
    total = call(
        owner_spread,
        shape((MIDDLE, MIDDLE, TILE_BLOCKS, FULL), BF16),
        [VMEM] * 4,
        [
            pltpu.VMEM((MIDDLE, MIDDLE * TILE_BLOCKS, FULL), F32),
            pltpu.VMEM((BLOCK, BLOCK * TILE_BLOCKS, FULL), BF16),
            pltpu.VMEM((9, FULL, FULL), BF16),
        ],
        (1, 1), "owner_spread",
    )(tile_here, swap(tile_mine), second_weight, second_other)

    def owner(at_owner):
        at_owner_other = [swap(value) for value in at_owner]
        return call(
            functools.partial(owner_canvas, owners, capacity, wide, permuted),
            [shape((HIGH, WIDE, HALF), F32)] + [shape((RIM, FULL), BF16)] * (2 if permuted else 0),
            [SMEM] + [VMEM] * (2 * len(at_owner) + 2),
            tables
            + [
                pltpu.VMEM((MIDDLE, MIDDLE * TILE_BLOCKS, FULL), BF16),
                pltpu.VMEM((OUTER, OUTER * TILE_BLOCKS, HALF), F32),
            ],
            (1, 1), "owner_canvas",
        )(routing, *at_owner, *at_owner_other, total, first_weight)

    if permuted:
        far_got, near_got = swap(far, "col"), swap(near, "col")
        total, far_got = tie((total, far_got))
        sends = call(add_far, [shape(part, BF16)] * 2, [VMEM] * 2, [], (1, 1), "add_far")(
            kept, far_got
        )
        sends, at_owner[3] = tie((sends[::-1], at_owner[3]))
        got = [flip(sends[0], "blk", 3), flip(sends[1], "blk", 2)]
        canvas, *rims = owner(at_owner)
        near_got, canvas = tie((near_got, canvas))
        keep, send = call(
            add_near, [shape(part, F32), shape(part, BF16)], [VMEM] * 2, [], (1, 1), "add_near",
        )(kept, near_got)
        got.append(flip(send, "blk", 1))
        message = shape((PART, FULL), BF16)
        wider = shape((PART + RIM, FULL), BF16)
        own, *wides = call(
            add_workers, [message, wider, wider], [VMEM] * 6, [], (1, 1), "add_workers",
        )(keep, *got, *rims)
        got_2, got_3, got_1 = flip(own, "blk", 2), flip(wides[1], "blk", 3), flip(wides[0], "blk", 1)
        across = [swap(value, "col") for value in (own, got_1[:PART])]
        got_3, got_2, got_1, across = tie((got_3, got_2, got_1, across))
        got = [got_1, got_2, got_3]
        last = call(
            column_message, shape((PART + 64, FULL), BF16), [VMEM] * 3,
            [pltpu.VMEM((RIM, FULL), F32), pltpu.VMEM((64, HALF), F32)],
            (1, 1), "column_message",
        )(canvas.reshape(HIGH * WIDE, HALF), got[0], got[2])
        across += [swap(got_2, "col"), swap(last, "col")]
        slab = (TILE_ROWS * BLOCK, 16, HALF)
        weights = [shape((9, HALF, FULL), F32)] * 2
        early, *outs = call(
            lay, [shape(grad_out.shape, BF16), shape(slab, F32)] + weights, [VMEM] * 8,
            [pltpu.VMEM((TILE_ROWS * BLOCK * 32, HALF), F32)], (1, 1), "lay",
        )(grad_out, canvas, own, *got, *across[:2])
        grad_in, grad_second, grad_first = pl.pallas_call(
            finish,
            out_shape=[shape(grad_out.shape, BF16)] + weights,
            in_specs=[VMEM] * 3 + [HBM] * 3,
            out_specs=[HBM] * 3,
            scratch_shapes=[
                pltpu.VMEM((TILE_ROWS * BLOCK * 16 + 16, HALF), F32),
                pltpu.VMEM(slab, BF16),
                pltpu.VMEM((2, 2, 9, ROWS, FULL), F32),
                pltpu.SemaphoreType.DMA((3, 2)),
            ],
            input_output_aliases={3: 0, 4: 1, 5: 2},
            compiler_params=pltpu.CompilerParams(vmem_limit_bytes=48 * 1024 * 1024),
            cost_estimate=pl.CostEstimate(flops=1, bytes_accessed=1, transcendentals=0),
            name="finish",
        )(outs[0], across[3], across[2], early, *outs[1:])
        return (grad_in, grad_first, grad_second)

    grad_first, grad_second = lax.psum((terms[0][1], terms[0][0]), ("blk", "col"))
    [canvas] = owner(at_owner)
    up, down = neighbours("blk")
    from_above = lax.ppermute(canvas[HIGH - 2 :].astype(BF16), "blk", up).astype(F32)
    from_below = lax.ppermute(canvas[:2].astype(BF16), "blk", down).astype(F32)
    inner = canvas[2 : HIGH - 2]
    inner = inner.at[:2].add(from_above).at[-2:].add(from_below)
    up, down = neighbours("col")
    from_left = lax.ppermute(inner[:, 32:34].astype(BF16), "col", up).astype(F32)
    from_right = lax.ppermute(inner[:, 34:36].astype(BF16), "col", down).astype(F32)
    inner = inner[:, :32].at[:, :2].add(from_left).at[:, -2:].add(from_right)
    grad_in = (grad_out.astype(F32) + inner).astype(BF16)
    return (grad_in, grad_first, grad_second)


def solution(mesh):
    return jax.shard_map(
        shards,
        mesh=mesh,
        in_specs=(
            P(("groups", "blk"), "col", "ch"),
            P(("groups", "col"), "blk", None, None, None, "ch"),
            P(("groups", "col"), "blk", None, None, None, "ch"),
            P(None, "ch", None),
            P(None, "ch", None),
            P(("groups", "col"), None, None),
        ),
        out_specs=(
            P(("groups", "blk"), "col", "ch"),
            P("groups", "ch", None),
            P("groups", "ch", None),
        ),
        check_vma=False,
    )
```

```python
import functools
import math

import jax
import jax.numpy as jnp
from jax import lax
from jax.experimental import pallas as pl
from jax.experimental.pallas import tpu as pltpu
from jax.sharding import PartitionSpec as P

BLOCK = 8
TILE_ROWS = 8
TILE_COLS = 4
TILE_BLOCKS = 32
PER_WORKER = 16
MIDDLE = 10
OUTER = 12
HALF = 128
FULL = 256
DEAD = -4096
HIGH = 68
RIM = 48
ROWS = 16
PART = 288
WIDE = 40

BF16 = jnp.bfloat16
F32 = jnp.float32
I32 = jnp.int32

VMEM = pl.BlockSpec(memory_space=pltpu.VMEM)
HBM = pl.BlockSpec(memory_space=pltpu.HBM)
SMEM = pl.BlockSpec(memory_space=pltpu.SMEM)


def call(body, outs, specs, scratch, cost, name):
    return pl.pallas_call(
        body,
        out_shape=outs,
        in_specs=specs,
        out_specs=jax.tree.map(lambda _: VMEM, outs),
        scratch_shapes=scratch,
        compiler_params=pltpu.CompilerParams(vmem_limit_bytes=48 * 1024 * 1024),
        cost_estimate=pl.CostEstimate(flops=cost[0], bytes_accessed=cost[1], transcendentals=0),
        name=name,
    )


def iota(shape, dim):
    return lax.broadcasted_iota(I32, shape, dim)


def one_hot(hits):
    return jnp.where(hits, 1.0, 0.0).astype(BF16)


def dot(a, b):
    return jnp.dot(a, b, preferred_element_type=F32)


def dot_nt(a, b):
    return lax.dot_general(a, b, (((1,), (1,)), ((), ())), preferred_element_type=F32)


def dot_tn(a, b):
    return lax.dot_general(a, b, (((0,), (0,)), ((), ())), preferred_element_type=F32)


def owner_table(routing, table, owners, capacity):
    me = lax.axis_index("blk")

    def clear(number, carry):
        table[number] = DEAD
        return carry

    lax.fori_loop(0, owners * capacity, clear, 0)

    def worker(number, carry):
        count = jnp.int32(0)
        for slot in range(PER_WORKER):
            code = routing[number, slot]
            hit = (code // TILE_BLOCKS) == me
            table[jnp.where(hit, number * capacity + count, owners * capacity)] = code % TILE_BLOCKS
            count = count + jnp.where(hit, 1, 0)
        return carry

    lax.fori_loop(0, owners, worker, 0)


def worker_codes(routing, counts, owners):
    me = lax.axis_index("blk")

    def clear(number, carry):
        counts[number] = 0
        return carry

    lax.fori_loop(0, owners, clear, 0)
    slots = []
    for slot in range(PER_WORKER):
        code = routing[me, slot]
        owner = code // TILE_BLOCKS
        rank = counts[owner]
        counts[owner] = rank + 1
        slots.append((owner, code % TILE_BLOCKS, rank))
    return slots


def views(refs, count):
    return list(refs) if len(refs) == count else [refs[0].at[k] for k in range(count)]


def partner(axis, step, permuted):
    return step ^ lax.axis_index(axis) if permuted else step


def pack_cotangents(owners, capacity, permuted, listed, source, *refs):
    outs, (places, tile, codes, arrived) = refs[:-4], refs[-4:]
    fetch = pltpu.make_async_copy(source, tile, arrived.at[0])
    fetch.start()
    lists = pltpu.make_async_copy(listed, codes, arrived.at[1])
    lists.start()
    lists.wait()
    hit = (codes[...] // TILE_BLOCKS) == lax.axis_index("blk")
    places[0] = jnp.where(hit, codes[...] % TILE_BLOCKS + 1, 0)
    before = (iota((PER_WORKER, PER_WORKER), 0) < iota((PER_WORKER, PER_WORKER), 1))
    places[1] = dot(one_hot(hit), one_hot(before)).astype(I32)
    rows = BLOCK * capacity
    row, lane = iota((rows, FULL), 0), iota((rows, FULL), 1)
    picks = []
    for step in range(owners):
        at = pl.ds(partner("blk", step, permuted), 1)
        same = places[1, at, :] == iota((rows, PER_WORKER), 0) % capacity
        place = jnp.sum(jnp.where(same, places[0, at, :], 0).astype(F32), axis=1, keepdims=True)
        target = (place.astype(I32) - 1) * BLOCK
        picks.append(one_hot(lane == target + row // capacity))
    pick = jnp.concatenate(picks, axis=0)
    fetch.wait()
    for u in range(0, BLOCK, 2):
        pair = [
            jnp.concatenate([tile[r, u + k] for r in range(TILE_ROWS)], axis=0) for k in range(2)
        ]
        moved = dot(pick, jnp.concatenate(pair, axis=1)).astype(BF16)
        for step, out in enumerate(views(outs, owners)):
            part = moved[step * rows : (step + 1) * rows]
            out[u] = part[:, :HALF]
            out[u + 1] = part[:, HALF:]


def outside_image(slots, owners, columns):
    column = lax.axis_index("col")
    row = iota((MIDDLE * PER_WORKER, HALF), 0)
    flags = jnp.zeros_like(row)
    for slot, (owner, place, rank) in enumerate(slots):
        block_row, block_col = place // TILE_COLS, place % TILE_COLS
        flag = (
            jnp.where((owner == 0) & (block_row == 0), 1, 0)
            + jnp.where((owner == owners - 1) & (block_row == TILE_ROWS - 1), 2, 0)
            + jnp.where((column == 0) & (block_col == 0), 4, 0)
            + jnp.where((column == columns - 1) & (block_col == TILE_COLS - 1), 8, 0)
        )
        flags = jnp.where(row % PER_WORKER == slot, flag, flags)
    across = row // PER_WORKER
    sides = (((flags & 4) != 0) & (across == 0)) | (((flags & 8) != 0) & (across == MIDDLE - 1))

    def here(m):
        if m == 0:
            return sides | ((flags & 1) != 0)
        if m == MIDDLE - 1:
            return sides | ((flags & 2) != 0)
        return sides

    return here


def pack_saved(owners, columns, capacity, wide, permuted, routing, saved, masked, *refs):
    outs, counts, table = refs[:-2], refs[-2], refs[-1]

    def clear(number, carry):
        table[number] = DEAD
        return carry

    lax.fori_loop(0, owners * capacity, clear, 0)
    slots = worker_codes(routing, counts, owners)
    rows = MIDDLE * PER_WORKER
    for slot, (owner, place, rank) in enumerate(slots):
        table[owner * capacity + rank] = slot
    outside = outside_image(slots, owners, columns)
    for m in range(MIDDLE):
        masked[m] = jnp.where(outside(m), 0.0, saved[m].astype(F32)).astype(BF16)
    size = wide * capacity
    row, lane = iota((size, FULL), 0), iota((size, FULL), 1)
    picks = []
    for step in range(owners):
        owner = partner("blk", step, permuted)
        target = jnp.full((size, FULL), DEAD, I32)
        for rank in range(capacity):
            target = jnp.where(row % capacity == rank, table[owner * capacity + rank], target)
        at = row // capacity
        picks.append(one_hot((lane == target + at * PER_WORKER) & (at < MIDDLE)))
    pick = jnp.concatenate(picks, axis=0)
    filler = jnp.zeros((FULL - rows, FULL), BF16)
    for m in range(0, MIDDLE, 2):
        pair = jnp.concatenate([masked[m], masked[m + 1]], axis=1)
        moved = dot(pick, jnp.concatenate([pair, filler], axis=0)).astype(BF16)
        for step, out in enumerate(views(outs, owners)):
            part = moved[step * size : (step + 1) * size]
            out[m] = part[:, :HALF]
            out[m + 1] = part[:, HALF:]


def ordered(own, other, axis):
    first = lax.axis_index("ch") == 0
    return jnp.concatenate(
        [jnp.where(first, own, other), jnp.where(first, other, own)], axis=axis
    )


def deal(value, kept, sent, grad, tap):
    low, high = value[: HALF // 2], value[HALF // 2 :]
    mine = lax.axis_index("col") == 0
    keep, send = jnp.where(mine, low, high), jnp.where(mine, high, low).astype(BF16)
    for k in range(4):
        step, rows = partner("blk", k, True), slice(k * ROWS, (k + 1) * ROWS)
        kept[step, grad, tap] = keep[rows]
        sent[step, grad, tap] = send[rows]


def emit(value, outs, grad, tap):
    if len(outs) == 2:
        deal(value, outs[0], outs[1], grad, tap)
    else:
        outs[0][grad, tap] = value


def spread(values, weight, total, places):
    height, extent = values.shape[:2]
    inputs = values[...].reshape(height * extent, FULL)
    width, step = weight.shape[1], places
    for dy in range(3):
        taps = jnp.concatenate([weight[3 * dy + dx] for dx in range(3)], axis=0)
        part = dot_nt(inputs, taps).reshape(height, extent, 3 * width)
        p, q, r = [part[:, :, dx * width : (dx + 1) * width] for dx in range(3)]
        sums = [
            p[:, :step],
            p[:, step : 2 * step] + q[:, :step],
            p[:, 2 * step :] + q[:, step : extent - step] + r[:, : extent - 2 * step],
            q[:, extent - step :] + r[:, extent - 2 * step : extent - step],
            r[:, extent - step :],
        ]
        at = 0
        for value in sums:
            size = value.shape[1]
            here = slice(at, at + size)
            if dy == 0:
                total[:height, here] = value
            else:
                total[dy : dy + height - 1, here] += value[:-1]
                total[dy + height - 1, here] = value[height - 1]
            at += size


def second_gradient(scale, owners, capacity, permuted, routing, *refs):
    parts = 1 if not permuted else owners
    own, other = views(refs[:parts], owners), views(refs[parts : 2 * parts], owners)
    masked, cot = refs[2 * parts : 2 * parts + 2]
    outs, counts = refs[2 * parts + 2 : -1], refs[-1]
    slots = worker_codes(routing, counts, owners)
    rows, inner = BLOCK * PER_WORKER, owners * BLOCK * capacity
    row, lane = iota((rows, inner), 0), iota((rows, inner), 1)
    target = jnp.full((rows, inner), DEAD, I32)
    for slot, (owner, place, rank) in enumerate(slots):
        step = partner("blk", owner, permuted)
        target = jnp.where(row % PER_WORKER == slot, step * (BLOCK * capacity) + rank, target)
    pick = one_hot(lane == target + (row // PER_WORKER) * capacity)
    for u in range(BLOCK):
        got = jnp.concatenate(
            [ordered(own[o][u], other[o][u], 1) for o in range(owners)], axis=0
        )
        cot[u] = dot(pick, got).astype(BF16)
    grads = cot[...].reshape(BLOCK * rows, FULL)
    turned = []
    for dx in range(3):
        window = masked[:, dx * PER_WORKER : (dx + BLOCK) * PER_WORKER].reshape(MIDDLE * rows, HALF)
        turned.append(jnp.maximum(window, jnp.zeros_like(window)).T)
    turned = jnp.concatenate(turned, axis=0)
    for dy in range(3):
        value = dot(turned[:, dy * rows : (dy + BLOCK) * rows], grads) * scale
        for dx in range(3):
            emit(value[dx * HALF : (dx + 1) * HALF], outs, 0, 3 * dy + dx)
    return slots


def first_gradient(
    scale, outside, cot, masked, saved_other, weight, weight_other, saved, *refs
):
    outs, (total, pre, full) = refs[:-3], refs[-3:]
    full[...] = ordered(weight[...], weight_other[...], 1)
    spread(cot, full, total, PER_WORKER)
    for m in range(MIDDLE):
        other = jnp.where(outside(m), 0.0, saved_other[m].astype(F32)).astype(BF16)
        live = ordered(masked[m], other, 1).astype(F32) > 0
        value = jnp.where(live, total[m], 0.0)
        pre[m] = value.astype(BF16).reshape(MIDDLE, PER_WORKER, FULL)
    size = MIDDLE * MIDDLE * PER_WORKER
    grads = pre[...].reshape(size, FULL)
    for dy in range(3):
        windows = [saved[dy : dy + MIDDLE, dx : dx + MIDDLE] for dx in range(3)]
        window = jnp.concatenate([w.reshape(size, HALF) for w in windows], axis=1)
        value = dot_tn(window, grads) * scale
        for dx in range(3):
            emit(value[dx * HALF : (dx + 1) * HALF], outs, 1, 3 * dy + dx)


def owner_spread(tile, tile_other, second, second_other, out, total, cot, full):
    row, lane = iota((FULL, FULL), 0), iota((FULL, FULL), 1)
    turn = one_hot(lane == (row % TILE_BLOCKS) * BLOCK + row // TILE_BLOCKS)
    for u in range(BLOCK):
        block = jnp.concatenate(
            [ordered(tile[r, u], tile_other[r, u], 1) for r in range(TILE_ROWS)], axis=0
        )
        cot[u] = dot(turn, block).astype(BF16)
    full[...] = ordered(second[...], second_other[...], 1)
    spread(cot, full, total, TILE_BLOCKS)
    out[...] = total[...].astype(BF16).reshape(out.shape)


def worker(scale, owners, columns, capacity, permuted, routing, *refs):
    parts = 1 if not permuted else owners
    inputs, refs = refs[: 2 * parts], refs[2 * parts :]
    (masked, saved_other, weight, weight_other, source), refs = refs[:5], refs[5:]
    if permuted:
        refs, sent = refs[:-1], refs[-1]
    outs, (counts, cot, total, pre, full, saved, arrived) = refs[:-7], refs[-7:]
    if permuted:
        kept, near, far = outs
        outs = (kept, sent)
    fetch = pltpu.make_async_copy(source, saved, arrived)
    fetch.start()
    slots = second_gradient(
        scale, owners, capacity, permuted, routing, *inputs, masked, cot, *outs, counts
    )
    fetch.wait()
    first_gradient(
        scale, outside_image(slots, owners, columns), cot, masked, saved_other, weight, weight_other,
        saved, *outs, total, pre, full,
    )
    if permuted:
        near[...] = sent[:2]
        far[...] = sent[2:]


def adjacent(step):
    me = lax.axis_index("blk")
    return (me ^ step) == me - 1, (me ^ step) == me + 1


def owner_canvas(owners, capacity, wide, permuted, routing, *refs):
    parts = 1 if not permuted else owners
    got, got_other = views(refs[:parts], owners), views(refs[parts : 2 * parts], owners)
    total, first, canvas = refs[2 * parts : 2 * parts + 3]
    rims, (table, pre, grown) = refs[2 * parts + 3 : -3], refs[-3:]
    owner_table(routing, table, owners, capacity)
    size, into = wide * capacity, MIDDLE * TILE_BLOCKS
    row, lane = iota((size, into), 0), iota((size, into), 1)
    picks = []
    for step in range(owners):
        worker = partner("blk", step, permuted)
        target = jnp.full((size, into), DEAD, I32)
        for rank in range(capacity):
            target = jnp.where(row % capacity == rank, table[worker * capacity + rank], target)
        at = row // capacity
        hits = (lane == target + at * TILE_BLOCKS) & (at < MIDDLE)
        picks.append(jnp.where(hits, 1.0, 0.0))
    pick = jnp.concatenate(picks, axis=0).T.astype(BF16)
    for m in range(MIDDLE):
        block = jnp.concatenate(
            [ordered(got[w][m], got_other[w][m], 1) for w in range(owners)], axis=0
        )
        value = jnp.where(dot(pick, block) > 0, total[m].reshape(into, FULL).astype(F32), 0.0)
        pre[m] = value.astype(BF16)
    spread(pre, first, grown, TILE_BLOCKS)
    height, depth = TILE_ROWS * WIDE, OUTER * TILE_BLOCKS
    row, lane = iota((height, depth), 0), iota((height, depth), 1)
    at_row, at_col = row // WIDE, row % WIDE
    n, place = lane // TILE_BLOCKS, lane % TILE_BLOCKS
    column = (place % TILE_COLS) * BLOCK + n - 2
    column = jnp.where(column < 0, column + 36, column)
    fold = one_hot((at_row == place // TILE_COLS) & (at_col == column))
    canvas[...] = jnp.zeros_like(canvas)
    for m in range(0, OUTER, 2):
        pair = jnp.concatenate(
            [grown[m + k].astype(BF16) for k in range(2)], axis=1
        )
        laid = dot(fold, pair).reshape(TILE_ROWS, WIDE, FULL)
        for r in range(TILE_ROWS):
            for k in range(2):
                canvas[r * BLOCK + m + k] += laid[r, :, k * HALF : (k + 1) * HALF]
    for k, rim in enumerate(rims):
        above, below = adjacent(2 * k + 1)
        top = jnp.concatenate([canvas[0], canvas[1]], axis=1)
        bottom = jnp.concatenate([canvas[HIGH - 2], canvas[HIGH - 1]], axis=1)
        here = jnp.where(below, bottom, jnp.where(above, top, 0.0))
        rim[...] = jnp.concatenate([here, jnp.zeros((RIM - WIDE, FULL), F32)], axis=0).astype(BF16)


def add_far(kept, got, *sends):
    for k, out in enumerate(sends):
        out[...] = (kept[2 + k] + got[k].astype(F32)).astype(BF16)


def add_near(kept, got, keep, send):
    keep[...] = kept[0] + got[0].astype(F32)
    send[...] = (kept[1] + got[1].astype(F32)).astype(BF16)


def add_workers(kept, got_3, got_2, got_1, rim_1, rim_3, out, out_1, out_3):
    value = kept[...]
    for part in (got_3, got_2, got_1):
        value = value + part[...].astype(F32)
    value = value.astype(BF16).reshape(PART, FULL)
    out[...] = value
    for message, rim in ((out_1, rim_1), (out_3, rim_3)):
        message[:PART] = value
        message[PART:] = rim[...]


def column_message(canvas, got_1, got_3, out, rim, strip):
    out[:PART] = got_3[:PART]
    for j in range(2):
        c = 32 + 2 * lax.axis_index("col") + j
        strip[...] = canvas[pl.ds(2 * WIDE + c, 64, stride=WIDE), :]
        for step, got in ((1, got_1), (3, got_3)):
            rim[...] = got[PART:].astype(F32)
            row = rim[pl.ds(c, 1), :]
            above, below = adjacent(step)
            top, bottom = jnp.where(above, row, 0.0), jnp.where(below, row, 0.0)
            strip[0:1] += top[:, :HALF]
            strip[1:2] += top[:, HALF:]
            strip[62:63] += bottom[:, :HALF]
            strip[63:64] += bottom[:, HALF:]
        out[PART:, j * HALF : (j + 1) * HALF] = strip[...].astype(BF16)


def gather_image(tile, canvas, got_1, got_3, total):
    rows = TILE_ROWS * BLOCK * 32
    total[...] = tile[...].reshape(rows, HALF).astype(F32) + canvas[
        2 : HIGH - 2, :32, :
    ].reshape(rows, HALF)
    for step, got in ((1, got_1), (3, got_3)):
        rim = got[PART : PART + 32].astype(F32)
        above, below = adjacent(step)
        top, bottom = jnp.where(above, rim, 0.0), jnp.where(below, rim, 0.0)
        total[0:32] += top[:, :HALF]
        total[32:64] += top[:, HALF:]
        total[rows - 64 : rows - 32] += bottom[:, :HALF]
        total[rows - 32 : rows] += bottom[:, HALF:]


def rows_at(number):
    column = lax.axis_index("col")
    place = (column if number < 4 else 1 - column) * 4 + partner("blk", number % 4, True)
    return pl.ds(pl.multiple_of(place * ROWS, ROWS), ROWS)


def lay(tile, canvas, *refs):
    parts, (image, slab), outs, total = refs[:-5], refs[-5:-3], refs[-3:-1], refs[-1]
    gather_image(tile, canvas, parts[1], parts[3], total)
    whole = total[...].reshape(image.shape)
    image[...] = whole.astype(BF16)
    slab[...] = jnp.where(lax.axis_index("col") == 0, whole[:, 16:], whole[:, :16])
    for number, part in zip((0, 1, 2, 3, 4, 5, 6), parts):
        value = part[:PART].astype(F32).reshape(2, 9, ROWS, FULL)
        for out, grad in zip(outs, (0, 1)):
            out[:, rows_at(number), :] = value[grad]


def finish(slab, last, old, old_0, old_1, image, out_0, out_1, total, side, laid, sems):
    copies = []
    laid[...] = last[:PART].astype(F32).reshape(2, 9, ROWS, FULL)
    for grad, dest in enumerate((out_0, out_1)):
        copies.append(
            pltpu.make_async_copy(laid.at[grad], dest.at[:, rows_at(7), :], sems.at[grad])
        )
        copies[-1].start()
    rows = TILE_ROWS * BLOCK * 16
    total[:rows] = slab[...].reshape(rows, HALF)
    strip = last[PART:].astype(F32)
    left = lax.axis_index("col") == 0
    at = jnp.where(left, 14, 0)
    for j in range(2):
        spot = (pl.ds(at + j, 64, stride=16), slice(None))
        total[spot] = total[spot] + strip[:, j * HALF : (j + 1) * HALF]
    side[...] = total[:rows].astype(BF16).reshape(side.shape)
    columns = pl.ds(pl.multiple_of(jnp.where(left, 16, 0), 16), 16)
    copies.append(pltpu.make_async_copy(side, image.at[:, columns, :], sems.at[2]))
    copies[-1].start()
    for copy in copies:
        copy.wait()


def swap(value, axis="ch"):
    return lax.ppermute(value, axis, [(0, 1), (1, 0)])


def flip(value, axis, step):
    size = lax.axis_size(axis)
    return lax.ppermute(value, axis, [(i, i ^ step) for i in range(size)])


def neighbours(axis):
    size = lax.axis_size(axis)
    up = [(i, (i + 1) % size) for i in range(size - 1)]
    return up, [(j, i) for i, j in up]


def shards(grad_out, saved_input, saved_pre, first_weight, second_weight, assignment):
    owners = lax.axis_size("blk")
    columns = lax.axis_size("col")
    capacity = max(2, TILE_BLOCKS // owners)
    wide = MIDDLE if (MIDDLE * capacity) % 16 == 0 else 16
    scale = 1.0 / math.sqrt(owners * columns * PER_WORKER * BLOCK * BLOCK)
    permuted = owners == 4 and columns == 2
    parts = owners if permuted else 1
    routing = assignment[0]
    shape = jax.ShapeDtypeStruct
    tables = [pltpu.SMEM((owners * capacity + 1,), I32)]
    counts = [pltpu.SMEM((owners,), I32)]

    def pieces(*dims):
        return [shape(dims, BF16)] * owners if permuted else [shape((owners,) + dims, BF16)]

    def exchange(values):
        if permuted:
            return list(values[:1]) + [flip(values[k], "blk", k) for k in (3, 2, 1)][::-1]
        return [lax.all_to_all(values[0], "blk", split_axis=0, concat_axis=0, tiled=True)]

    tie = lax.optimization_barrier
    tile = grad_out.reshape(TILE_ROWS, BLOCK, TILE_COLS * BLOCK, HALF)
    outgoing = call(
        functools.partial(pack_cotangents, owners, capacity, permuted),
        pieces(BLOCK, BLOCK * capacity, HALF),
        [HBM, HBM],
        [
            pltpu.VMEM((2,) + routing.shape, I32),
            pltpu.VMEM(tile.shape, BF16),
            pltpu.VMEM(routing.shape, I32),
            pltpu.SemaphoreType.DMA((2,)),
        ],
        (1, 1), "pack_cotangents",
    )(*[pltpu.with_memory_space_constraint(value, pltpu.HBM) for value in (routing, tile)])
    saved_slots = saved_pre[0, 0].transpose(1, 2, 0, 3)
    saved_slots = saved_slots.reshape(MIDDLE, MIDDLE * PER_WORKER, HALF)
    outgoing, saved_here = tie((outgoing, saved_slots))
    incoming = exchange(outgoing)

    masked, *to_owners = call(
        functools.partial(pack_saved, owners, columns, capacity, wide, permuted),
        [shape((MIDDLE, MIDDLE * PER_WORKER, HALF), BF16)] + pieces(MIDDLE, wide * capacity, HALF),
        [SMEM, VMEM], counts + tables, (1, 1), "pack_saved",
    )(routing, saved_here)
    second_other, saved_other = swap(second_weight), swap(saved_slots)

    incoming, to_owners = tie((incoming[::-1], to_owners[::-1]))
    incoming, to_owners = incoming[::-1], to_owners[::-1]
    incoming_other = [swap(value) for value in incoming]
    at_owner = exchange(to_owners)

    saved_tiles = saved_input[0, 0].transpose(1, 2, 0, 3)
    if permuted:
        part = (2, 9, ROWS, FULL)
        halved = [shape((4,) + part, F32)] + [shape((2,) + part, BF16)] * 2
    else:
        halved = [shape((2, 9, HALF, FULL), F32)]
    terms = call(
        functools.partial(worker, scale, owners, columns, capacity, permuted),
        halved,
        [SMEM] + [VMEM] * (2 * parts + 4) + [HBM],
        counts
        + [
            pltpu.VMEM((BLOCK, BLOCK * PER_WORKER, FULL), BF16),
            pltpu.VMEM((MIDDLE, MIDDLE * PER_WORKER, FULL), F32),
            pltpu.VMEM((MIDDLE, MIDDLE, PER_WORKER, FULL), BF16),
            pltpu.VMEM((9, FULL, FULL), BF16),
            pltpu.VMEM(saved_tiles.shape, BF16),
            pltpu.SemaphoreType.DMA,
        ]
        + ([pltpu.VMEM((4,) + part, BF16)] if permuted else []),
        (1, 1), "worker",
    )(
        routing, *incoming, *incoming_other, masked, saved_other, second_weight, second_other,
        pltpu.with_memory_space_constraint(saved_tiles, pltpu.HBM),
    )

    if permuted:
        kept, near, far = terms
        far, at_owner[2], at_owner[1] = tie((far, at_owner[2], at_owner[1]))
        far, tile_mine, tile_here = tie((far, tile, tile))
    else:
        terms, tile_mine, tile_here = tie((terms, tile, tile))
    total = call(
        owner_spread,
        shape((MIDDLE, MIDDLE, TILE_BLOCKS, FULL), BF16),
        [VMEM] * 4,
        [
            pltpu.VMEM((MIDDLE, MIDDLE * TILE_BLOCKS, FULL), F32),
            pltpu.VMEM((BLOCK, BLOCK * TILE_BLOCKS, FULL), BF16),
            pltpu.VMEM((9, FULL, FULL), BF16),
        ],
        (1, 1), "owner_spread",
    )(tile_here, swap(tile_mine), second_weight, second_other)

    def owner(at_owner):
        at_owner_other = [swap(value) for value in at_owner]
        return call(
            functools.partial(owner_canvas, owners, capacity, wide, permuted),
            [shape((HIGH, WIDE, HALF), F32)] + [shape((RIM, FULL), BF16)] * (2 if permuted else 0),
            [SMEM] + [VMEM] * (2 * len(at_owner) + 2),
            tables
            + [
                pltpu.VMEM((MIDDLE, MIDDLE * TILE_BLOCKS, FULL), BF16),
                pltpu.VMEM((OUTER, OUTER * TILE_BLOCKS, HALF), F32),
            ],
            (1, 1), "owner_canvas",
        )(routing, *at_owner, *at_owner_other, total, first_weight)

    if permuted:
        far_got, near_got = swap(far, "col"), swap(near, "col")
        total, far_got = tie((total, far_got))
        sends = call(add_far, [shape(part, BF16)] * 2, [VMEM] * 2, [], (1, 1), "add_far")(
            kept, far_got
        )
        sends, at_owner[3] = tie((sends[::-1], at_owner[3]))
        got = [flip(sends[0], "blk", 3), flip(sends[1], "blk", 2)]
        canvas, *rims = owner(at_owner)
        near_got, canvas = tie((near_got, canvas))
        keep, send = call(
            add_near, [shape(part, F32), shape(part, BF16)], [VMEM] * 2, [], (1, 1), "add_near",
        )(kept, near_got)
        got.append(flip(send, "blk", 1))
        message = shape((PART, FULL), BF16)
        wider = shape((PART + RIM, FULL), BF16)
        own, *wides = call(
            add_workers, [message, wider, wider], [VMEM] * 6, [], (1, 1), "add_workers",
        )(keep, *got, *rims)
        got_2, got_1 = flip(own, "blk", 2), flip(wides[0], "blk", 1)
        wide_3, got_2, across = tie((wides[1], got_2, swap(own, "col")))
        got_3 = flip(wide_3, "blk", 3)
        across = [across] + [swap(value, "col") for value in (got_1[:PART], got_2)]
        got_3, got_1, across = tie((got_3, got_1, across))
        got = [got_1, got_2, got_3]
        last = call(
            column_message, shape((PART + 64, FULL), BF16), [VMEM] * 3,
            [pltpu.VMEM((RIM, FULL), F32), pltpu.VMEM((64, HALF), F32)],
            (1, 1), "column_message",
        )(canvas.reshape(HIGH * WIDE, HALF), got[0], got[2])
        last = swap(last, "col")
        slab = (TILE_ROWS * BLOCK, 16, HALF)
        weights = [shape((9, HALF, FULL), F32)] * 2
        early, *outs = call(
            lay, [shape(grad_out.shape, BF16), shape(slab, F32)] + weights, [VMEM] * 9,
            [pltpu.VMEM((TILE_ROWS * BLOCK * 32, HALF), F32)], (1, 1), "lay",
        )(grad_out, canvas, own, *got, *across)
        grad_in, grad_second, grad_first = pl.pallas_call(
            finish,
            out_shape=[shape(grad_out.shape, BF16)] + weights,
            in_specs=[VMEM] * 2 + [HBM] * 3,
            out_specs=[HBM] * 3,
            scratch_shapes=[
                pltpu.VMEM((TILE_ROWS * BLOCK * 16 + 16, HALF), F32),
                pltpu.VMEM(slab, BF16),
                pltpu.VMEM((2, 9, ROWS, FULL), F32),
                pltpu.SemaphoreType.DMA((3,)),
            ],
            input_output_aliases={2: 0, 3: 1, 4: 2},
            compiler_params=pltpu.CompilerParams(vmem_limit_bytes=48 * 1024 * 1024),
            cost_estimate=pl.CostEstimate(flops=1, bytes_accessed=1, transcendentals=0),
            name="finish",
        )(outs[0], last, early, *outs[1:])
        return (grad_in, grad_first, grad_second)

    grad_first, grad_second = lax.psum((terms[0][1], terms[0][0]), ("blk", "col"))
    [canvas] = owner(at_owner)
    up, down = neighbours("blk")
    from_above = lax.ppermute(canvas[HIGH - 2 :].astype(BF16), "blk", up).astype(F32)
    from_below = lax.ppermute(canvas[:2].astype(BF16), "blk", down).astype(F32)
    inner = canvas[2 : HIGH - 2]
    inner = inner.at[:2].add(from_above).at[-2:].add(from_below)
    up, down = neighbours("col")
    from_left = lax.ppermute(inner[:, 32:34].astype(BF16), "col", up).astype(F32)
    from_right = lax.ppermute(inner[:, 34:36].astype(BF16), "col", down).astype(F32)
    inner = inner[:, :32].at[:, :2].add(from_left).at[:, -2:].add(from_right)
    grad_in = (grad_out.astype(F32) + inner).astype(BF16)
    return (grad_in, grad_first, grad_second)


def solution(mesh):
    return jax.shard_map(
        shards,
        mesh=mesh,
        in_specs=(
            P(("groups", "blk"), "col", "ch"),
            P(("groups", "col"), "blk", None, None, None, "ch"),
            P(("groups", "col"), "blk", None, None, None, "ch"),
            P(None, "ch", None),
            P(None, "ch", None),
            P(("groups", "col"), None, None),
        ),
        out_specs=(
            P(("groups", "blk"), "col", "ch"),
            P("groups", "ch", None),
            P("groups", "ch", None),
        ),
        check_vma=False,
    )
```

```python
import functools
import math

import jax
import jax.numpy as jnp
from jax import lax
from jax.experimental import pallas as pl
from jax.experimental.pallas import tpu as pltpu
from jax.sharding import PartitionSpec as P

BLOCK = 8
TILE_ROWS = 8
TILE_COLS = 4
TILE_BLOCKS = 32
PER_WORKER = 16
MIDDLE = 10
OUTER = 12
HALF = 128
FULL = 256
DEAD = -4096
HIGH = 68
RIM = 48
ROWS = 16
PART = 288
WIDE = 40

BF16 = jnp.bfloat16
F32 = jnp.float32
I32 = jnp.int32

VMEM = pl.BlockSpec(memory_space=pltpu.VMEM)
HBM = pl.BlockSpec(memory_space=pltpu.HBM)
SMEM = pl.BlockSpec(memory_space=pltpu.SMEM)


def call(body, outs, specs, scratch, cost, name):
    return pl.pallas_call(
        body,
        out_shape=outs,
        in_specs=specs,
        out_specs=jax.tree.map(lambda _: VMEM, outs),
        scratch_shapes=scratch,
        compiler_params=pltpu.CompilerParams(vmem_limit_bytes=48 * 1024 * 1024),
        cost_estimate=pl.CostEstimate(flops=cost[0], bytes_accessed=cost[1], transcendentals=0),
        name=name,
    )


def iota(shape, dim):
    return lax.broadcasted_iota(I32, shape, dim)


def one_hot(hits):
    return jnp.where(hits, 1.0, 0.0).astype(BF16)


def dot(a, b):
    return jnp.dot(a, b, preferred_element_type=F32)


def dot_nt(a, b):
    return lax.dot_general(a, b, (((1,), (1,)), ((), ())), preferred_element_type=F32)


def dot_tn(a, b):
    return lax.dot_general(a, b, (((0,), (0,)), ((), ())), preferred_element_type=F32)


def owner_table(routing, table, owners, capacity):
    me = lax.axis_index("blk")

    def clear(number, carry):
        table[number] = DEAD
        return carry

    lax.fori_loop(0, owners * capacity, clear, 0)

    def worker(number, carry):
        count = jnp.int32(0)
        for slot in range(PER_WORKER):
            code = routing[number, slot]
            hit = (code // TILE_BLOCKS) == me
            table[jnp.where(hit, number * capacity + count, owners * capacity)] = code % TILE_BLOCKS
            count = count + jnp.where(hit, 1, 0)
        return carry

    lax.fori_loop(0, owners, worker, 0)


def worker_codes(routing, counts, owners):
    me = lax.axis_index("blk")

    def clear(number, carry):
        counts[number] = 0
        return carry

    lax.fori_loop(0, owners, clear, 0)
    slots = []
    for slot in range(PER_WORKER):
        code = routing[me, slot]
        owner = code // TILE_BLOCKS
        rank = counts[owner]
        counts[owner] = rank + 1
        slots.append((owner, code % TILE_BLOCKS, rank))
    return slots


def views(refs, count):
    return list(refs) if len(refs) == count else [refs[0].at[k] for k in range(count)]


def partner(axis, step, permuted):
    return step ^ lax.axis_index(axis) if permuted else step


def pack_cotangents(owners, capacity, permuted, listed, source, *refs):
    outs, (places, tile, codes, arrived) = refs[:-4], refs[-4:]
    fetch = pltpu.make_async_copy(source, tile, arrived.at[0])
    fetch.start()
    lists = pltpu.make_async_copy(listed, codes, arrived.at[1])
    lists.start()
    lists.wait()
    hit = (codes[...] // TILE_BLOCKS) == lax.axis_index("blk")
    places[0] = jnp.where(hit, codes[...] % TILE_BLOCKS + 1, 0)
    before = (iota((PER_WORKER, PER_WORKER), 0) < iota((PER_WORKER, PER_WORKER), 1))
    places[1] = dot(one_hot(hit), one_hot(before)).astype(I32)
    rows = BLOCK * capacity
    row, lane = iota((rows, FULL), 0), iota((rows, FULL), 1)
    picks = []
    for step in range(owners):
        at = pl.ds(partner("blk", step, permuted), 1)
        same = places[1, at, :] == iota((rows, PER_WORKER), 0) % capacity
        place = jnp.sum(jnp.where(same, places[0, at, :], 0).astype(F32), axis=1, keepdims=True)
        target = (place.astype(I32) - 1) * BLOCK
        picks.append(one_hot(lane == target + row // capacity))
    pick = jnp.concatenate(picks, axis=0)
    fetch.wait()
    for u in range(0, BLOCK, 2):
        pair = [
            jnp.concatenate([tile[r, u + k] for r in range(TILE_ROWS)], axis=0) for k in range(2)
        ]
        moved = dot(pick, jnp.concatenate(pair, axis=1)).astype(BF16)
        for step, out in enumerate(views(outs, owners)):
            part = moved[step * rows : (step + 1) * rows]
            out[u] = part[:, :HALF]
            out[u + 1] = part[:, HALF:]


def outside_image(slots, owners, columns):
    column = lax.axis_index("col")
    row = iota((MIDDLE * PER_WORKER, HALF), 0)
    flags = jnp.zeros_like(row)
    for slot, (owner, place, rank) in enumerate(slots):
        block_row, block_col = place // TILE_COLS, place % TILE_COLS
        flag = (
            jnp.where((owner == 0) & (block_row == 0), 1, 0)
            + jnp.where((owner == owners - 1) & (block_row == TILE_ROWS - 1), 2, 0)
            + jnp.where((column == 0) & (block_col == 0), 4, 0)
            + jnp.where((column == columns - 1) & (block_col == TILE_COLS - 1), 8, 0)
        )
        flags = jnp.where(row % PER_WORKER == slot, flag, flags)
    across = row // PER_WORKER
    sides = (((flags & 4) != 0) & (across == 0)) | (((flags & 8) != 0) & (across == MIDDLE - 1))

    def here(m):
        if m == 0:
            return sides | ((flags & 1) != 0)
        if m == MIDDLE - 1:
            return sides | ((flags & 2) != 0)
        return sides

    return here


def pack_saved(owners, columns, capacity, wide, permuted, routing, saved, masked, *refs):
    outs, counts, table = refs[:-2], refs[-2], refs[-1]

    def clear(number, carry):
        table[number] = DEAD
        return carry

    lax.fori_loop(0, owners * capacity, clear, 0)
    slots = worker_codes(routing, counts, owners)
    rows = MIDDLE * PER_WORKER
    for slot, (owner, place, rank) in enumerate(slots):
        table[owner * capacity + rank] = slot
    outside = outside_image(slots, owners, columns)
    for m in range(MIDDLE):
        masked[m] = jnp.where(outside(m), 0.0, saved[m].astype(F32)).astype(BF16)
    size = wide * capacity
    row, lane = iota((size, FULL), 0), iota((size, FULL), 1)
    picks = []
    for step in range(owners):
        owner = partner("blk", step, permuted)
        target = jnp.full((size, FULL), DEAD, I32)
        for rank in range(capacity):
            target = jnp.where(row % capacity == rank, table[owner * capacity + rank], target)
        at = row // capacity
        picks.append(one_hot((lane == target + at * PER_WORKER) & (at < MIDDLE)))
    pick = jnp.concatenate(picks, axis=0)
    filler = jnp.zeros((FULL - rows, FULL), BF16)
    for m in range(0, MIDDLE, 2):
        pair = jnp.concatenate([masked[m], masked[m + 1]], axis=1)
        moved = dot(pick, jnp.concatenate([pair, filler], axis=0)).astype(BF16)
        for step, out in enumerate(views(outs, owners)):
            part = moved[step * size : (step + 1) * size]
            out[m] = part[:, :HALF]
            out[m + 1] = part[:, HALF:]


def ordered(own, other, axis):
    first = lax.axis_index("ch") == 0
    return jnp.concatenate(
        [jnp.where(first, own, other), jnp.where(first, other, own)], axis=axis
    )


def deal(value, kept, sent, grad, tap):
    low, high = value[: HALF // 2], value[HALF // 2 :]
    mine = lax.axis_index("col") == 0
    keep, send = jnp.where(mine, low, high), jnp.where(mine, high, low).astype(BF16)
    for k in range(4):
        step, rows = partner("blk", k, True), slice(k * ROWS, (k + 1) * ROWS)
        kept[step, grad, tap] = keep[rows]
        sent[step, grad, tap] = send[rows]


def emit(value, outs, grad, tap):
    if len(outs) == 2:
        deal(value, outs[0], outs[1], grad, tap)
    else:
        outs[0][grad, tap] = value


def spread(values, weight, total, places):
    height, extent = values.shape[:2]
    inputs = values[...].reshape(height * extent, FULL)
    width, step = weight.shape[1], places
    for dy in range(3):
        taps = jnp.concatenate([weight[3 * dy + dx] for dx in range(3)], axis=0)
        part = dot_nt(inputs, taps).reshape(height, extent, 3 * width)
        p, q, r = [part[:, :, dx * width : (dx + 1) * width] for dx in range(3)]
        sums = [
            p[:, :step],
            p[:, step : 2 * step] + q[:, :step],
            p[:, 2 * step :] + q[:, step : extent - step] + r[:, : extent - 2 * step],
            q[:, extent - step :] + r[:, extent - 2 * step : extent - step],
            r[:, extent - step :],
        ]
        at = 0
        for value in sums:
            size = value.shape[1]
            here = slice(at, at + size)
            if dy == 0:
                total[:height, here] = value
            else:
                total[dy : dy + height - 1, here] += value[:-1]
                total[dy + height - 1, here] = value[height - 1]
            at += size


def second_gradient(scale, owners, capacity, permuted, routing, *refs):
    parts = 1 if not permuted else owners
    own, other = views(refs[:parts], owners), views(refs[parts : 2 * parts], owners)
    masked, cot = refs[2 * parts : 2 * parts + 2]
    outs, counts = refs[2 * parts + 2 : -1], refs[-1]
    slots = worker_codes(routing, counts, owners)
    rows, inner = BLOCK * PER_WORKER, owners * BLOCK * capacity
    row, lane = iota((rows, inner), 0), iota((rows, inner), 1)
    target = jnp.full((rows, inner), DEAD, I32)
    for slot, (owner, place, rank) in enumerate(slots):
        step = partner("blk", owner, permuted)
        target = jnp.where(row % PER_WORKER == slot, step * (BLOCK * capacity) + rank, target)
    pick = one_hot(lane == target + (row // PER_WORKER) * capacity)
    for u in range(BLOCK):
        got = jnp.concatenate(
            [ordered(own[o][u], other[o][u], 1) for o in range(owners)], axis=0
        )
        cot[u] = dot(pick, got).astype(BF16)
    grads = cot[...].reshape(BLOCK * rows, FULL)
    turned = []
    for dx in range(3):
        window = masked[:, dx * PER_WORKER : (dx + BLOCK) * PER_WORKER].reshape(MIDDLE * rows, HALF)
        turned.append(jnp.maximum(window, jnp.zeros_like(window)).T)
    turned = jnp.concatenate(turned, axis=0)
    for dy in range(3):
        value = dot(turned[:, dy * rows : (dy + BLOCK) * rows], grads) * scale
        for dx in range(3):
            emit(value[dx * HALF : (dx + 1) * HALF], outs, 0, 3 * dy + dx)
    return slots


def first_gradient(
    scale, outside, cot, masked, saved_other, weight, weight_other, saved, *refs
):
    outs, (total, pre, full) = refs[:-3], refs[-3:]
    full[...] = ordered(weight[...], weight_other[...], 1)
    spread(cot, full, total, PER_WORKER)
    for m in range(MIDDLE):
        other = jnp.where(outside(m), 0.0, saved_other[m].astype(F32)).astype(BF16)
        live = ordered(masked[m], other, 1).astype(F32) > 0
        value = jnp.where(live, total[m], 0.0)
        pre[m] = value.astype(BF16).reshape(MIDDLE, PER_WORKER, FULL)
    size = MIDDLE * MIDDLE * PER_WORKER
    grads = pre[...].reshape(size, FULL)
    for dy in range(3):
        windows = [saved[dy : dy + MIDDLE, dx : dx + MIDDLE] for dx in range(3)]
        window = jnp.concatenate([w.reshape(size, HALF) for w in windows], axis=1)
        value = dot_tn(window, grads) * scale
        for dx in range(3):
            emit(value[dx * HALF : (dx + 1) * HALF], outs, 1, 3 * dy + dx)


def owner_spread(tile, tile_other, second, second_other, out, total, cot, full):
    row, lane = iota((FULL, FULL), 0), iota((FULL, FULL), 1)
    turn = one_hot(lane == (row % TILE_BLOCKS) * BLOCK + row // TILE_BLOCKS)
    for u in range(BLOCK):
        block = jnp.concatenate(
            [ordered(tile[r, u], tile_other[r, u], 1) for r in range(TILE_ROWS)], axis=0
        )
        cot[u] = dot(turn, block).astype(BF16)
    full[...] = ordered(second[...], second_other[...], 1)
    spread(cot, full, total, TILE_BLOCKS)
    out[...] = total[...].astype(BF16).reshape(out.shape)


def worker(scale, owners, columns, capacity, permuted, routing, *refs):
    parts = 1 if not permuted else owners
    inputs, refs = refs[: 2 * parts], refs[2 * parts :]
    (masked, saved_other, weight, weight_other, source), refs = refs[:5], refs[5:]
    if permuted:
        refs, sent = refs[:-1], refs[-1]
    outs, (counts, cot, total, pre, full, saved, arrived) = refs[:-7], refs[-7:]
    if permuted:
        kept, near, far = outs
        outs = (kept, sent)
    fetch = pltpu.make_async_copy(source, saved, arrived)
    fetch.start()
    slots = second_gradient(
        scale, owners, capacity, permuted, routing, *inputs, masked, cot, *outs, counts
    )
    fetch.wait()
    first_gradient(
        scale, outside_image(slots, owners, columns), cot, masked, saved_other, weight, weight_other,
        saved, *outs, total, pre, full,
    )
    if permuted:
        near[...] = sent[:2]
        far[...] = sent[2:]


def adjacent(step):
    me = lax.axis_index("blk")
    return (me ^ step) == me - 1, (me ^ step) == me + 1


def owner_canvas(owners, capacity, wide, permuted, routing, *refs):
    parts = 1 if not permuted else owners
    got, got_other = views(refs[:parts], owners), views(refs[parts : 2 * parts], owners)
    total, first, canvas = refs[2 * parts : 2 * parts + 3]
    rims, (table, pre, grown) = refs[2 * parts + 3 : -3], refs[-3:]
    owner_table(routing, table, owners, capacity)
    size, into = wide * capacity, MIDDLE * TILE_BLOCKS
    row, lane = iota((size, into), 0), iota((size, into), 1)
    picks = []
    for step in range(owners):
        worker = partner("blk", step, permuted)
        target = jnp.full((size, into), DEAD, I32)
        for rank in range(capacity):
            target = jnp.where(row % capacity == rank, table[worker * capacity + rank], target)
        at = row // capacity
        hits = (lane == target + at * TILE_BLOCKS) & (at < MIDDLE)
        picks.append(jnp.where(hits, 1.0, 0.0))
    pick = jnp.concatenate(picks, axis=0).T.astype(BF16)
    for m in range(MIDDLE):
        block = jnp.concatenate(
            [ordered(got[w][m], got_other[w][m], 1) for w in range(owners)], axis=0
        )
        value = jnp.where(dot(pick, block) > 0, total[m].reshape(into, FULL).astype(F32), 0.0)
        pre[m] = value.astype(BF16)
    spread(pre, first, grown, TILE_BLOCKS)
    height, depth = TILE_ROWS * WIDE, OUTER * TILE_BLOCKS
    row, lane = iota((height, depth), 0), iota((height, depth), 1)
    at_row, at_col = row // WIDE, row % WIDE
    n, place = lane // TILE_BLOCKS, lane % TILE_BLOCKS
    column = (place % TILE_COLS) * BLOCK + n - 2
    column = jnp.where(column < 0, column + 36, column)
    fold = one_hot((at_row == place // TILE_COLS) & (at_col == column))
    canvas[...] = jnp.zeros_like(canvas)
    for m in range(0, OUTER, 2):
        pair = jnp.concatenate(
            [grown[m + k].astype(BF16) for k in range(2)], axis=1
        )
        laid = dot(fold, pair).reshape(TILE_ROWS, WIDE, FULL)
        for r in range(TILE_ROWS):
            for k in range(2):
                canvas[r * BLOCK + m + k] += laid[r, :, k * HALF : (k + 1) * HALF]
    for k, rim in enumerate(rims):
        above, below = adjacent(2 * k + 1)
        top = jnp.concatenate([canvas[0], canvas[1]], axis=1)
        bottom = jnp.concatenate([canvas[HIGH - 2], canvas[HIGH - 1]], axis=1)
        here = jnp.where(below, bottom, jnp.where(above, top, 0.0))
        rim[...] = jnp.concatenate([here, jnp.zeros((RIM - WIDE, FULL), F32)], axis=0).astype(BF16)


def add_far(kept, got, *sends):
    for k, out in enumerate(sends):
        out[...] = (kept[2 + k] + got[k].astype(F32)).astype(BF16)


def add_near(kept, got, keep, send):
    keep[...] = kept[0] + got[0].astype(F32)
    send[...] = (kept[1] + got[1].astype(F32)).astype(BF16)


def add_workers(kept, got_3, got_2, got_1, rim_1, rim_3, out, out_1, out_3):
    value = kept[...]
    for part in (got_3, got_2, got_1):
        value = value + part[...].astype(F32)
    value = value.astype(BF16).reshape(PART, FULL)
    out[...] = value
    for message, rim in ((out_1, rim_1), (out_3, rim_3)):
        message[:PART] = value
        message[PART:] = rim[...]


def column_message(canvas, got_1, got_3, out, rim, strip):
    out[:PART] = got_3[:PART]
    for j in range(2):
        c = 32 + 2 * lax.axis_index("col") + j
        strip[...] = canvas[pl.ds(2 * WIDE + c, 64, stride=WIDE), :]
        for step, got in ((1, got_1), (3, got_3)):
            rim[...] = got[PART:].astype(F32)
            row = rim[pl.ds(c, 1), :]
            above, below = adjacent(step)
            top, bottom = jnp.where(above, row, 0.0), jnp.where(below, row, 0.0)
            strip[0:1] += top[:, :HALF]
            strip[1:2] += top[:, HALF:]
            strip[62:63] += bottom[:, :HALF]
            strip[63:64] += bottom[:, HALF:]
        out[PART:, j * HALF : (j + 1) * HALF] = strip[...].astype(BF16)


def gather_image(tile, canvas, got_1, got_3, total):
    rows = TILE_ROWS * BLOCK * 32
    total[...] = tile[...].reshape(rows, HALF).astype(F32) + canvas[
        2 : HIGH - 2, :32, :
    ].reshape(rows, HALF)
    for step, got in ((1, got_1), (3, got_3)):
        rim = got[PART : PART + 32].astype(F32)
        above, below = adjacent(step)
        top, bottom = jnp.where(above, rim, 0.0), jnp.where(below, rim, 0.0)
        total[0:32] += top[:, :HALF]
        total[32:64] += top[:, HALF:]
        total[rows - 64 : rows - 32] += bottom[:, :HALF]
        total[rows - 32 : rows] += bottom[:, HALF:]


def rows_at(number):
    column = lax.axis_index("col")
    place = (column if number < 4 else 1 - column) * 4 + partner("blk", number % 4, True)
    return pl.ds(pl.multiple_of(place * ROWS, ROWS), ROWS)


def lay(tile, canvas, *refs):
    parts, (image, slab), outs, total = refs[:-5], refs[-5:-3], refs[-3:-1], refs[-1]
    gather_image(tile, canvas, parts[1], parts[3], total)
    whole = total[...].reshape(image.shape)
    image[...] = whole.astype(BF16)
    slab[...] = jnp.where(lax.axis_index("col") == 0, whole[:, 16:], whole[:, :16])
    for number, part in zip((0, 1, 2, 3, 4, 5, 6), parts):
        value = part[:PART].astype(F32).reshape(2, 9, ROWS, FULL)
        for out, grad in zip(outs, (0, 1)):
            out[:, rows_at(number), :] = value[grad]


def finish(slab, last, old, old_0, old_1, image, out_0, out_1, total, side, laid, sems):
    copies = []
    laid[...] = last[:PART].astype(F32).reshape(2, 9, ROWS, FULL)
    for grad, dest in enumerate((out_0, out_1)):
        copies.append(
            pltpu.make_async_copy(laid.at[grad], dest.at[:, rows_at(7), :], sems.at[grad])
        )
        copies[-1].start()
    rows = TILE_ROWS * BLOCK * 16
    total[:rows] = slab[...].reshape(rows, HALF)
    strip = last[PART:].astype(F32)
    left = lax.axis_index("col") == 0
    at = jnp.where(left, 14, 0)
    for j in range(2):
        spot = (pl.ds(at + j, 64, stride=16), slice(None))
        total[spot] = total[spot] + strip[:, j * HALF : (j + 1) * HALF]
    side[...] = total[:rows].astype(BF16).reshape(side.shape)
    columns = pl.ds(pl.multiple_of(jnp.where(left, 16, 0), 16), 16)
    copies.append(pltpu.make_async_copy(side, image.at[:, columns, :], sems.at[2]))
    copies[-1].start()
    for copy in copies:
        copy.wait()


def swap(value, axis="ch"):
    return lax.ppermute(value, axis, [(0, 1), (1, 0)])


def flip(value, axis, step):
    size = lax.axis_size(axis)
    return lax.ppermute(value, axis, [(i, i ^ step) for i in range(size)])


def neighbours(axis):
    size = lax.axis_size(axis)
    up = [(i, (i + 1) % size) for i in range(size - 1)]
    return up, [(j, i) for i, j in up]


def shards(grad_out, saved_input, saved_pre, first_weight, second_weight, assignment):
    owners = lax.axis_size("blk")
    columns = lax.axis_size("col")
    capacity = max(2, TILE_BLOCKS // owners)
    wide = MIDDLE if (MIDDLE * capacity) % 16 == 0 else 16
    scale = 1.0 / math.sqrt(owners * columns * PER_WORKER * BLOCK * BLOCK)
    permuted = owners == 4 and columns == 2
    parts = owners if permuted else 1
    routing = assignment[0]
    shape = jax.ShapeDtypeStruct
    tables = [pltpu.SMEM((owners * capacity + 1,), I32)]
    counts = [pltpu.SMEM((owners,), I32)]

    def pieces(*dims):
        return [shape(dims, BF16)] * owners if permuted else [shape((owners,) + dims, BF16)]

    def exchange(values):
        if permuted:
            return list(values[:1]) + [flip(values[k], "blk", k) for k in (3, 2, 1)][::-1]
        return [lax.all_to_all(values[0], "blk", split_axis=0, concat_axis=0, tiled=True)]

    tie = lax.optimization_barrier
    tile = grad_out.reshape(TILE_ROWS, BLOCK, TILE_COLS * BLOCK, HALF)
    outgoing = call(
        functools.partial(pack_cotangents, owners, capacity, permuted),
        pieces(BLOCK, BLOCK * capacity, HALF),
        [HBM, HBM],
        [
            pltpu.VMEM((2,) + routing.shape, I32),
            pltpu.VMEM(tile.shape, BF16),
            pltpu.VMEM(routing.shape, I32),
            pltpu.SemaphoreType.DMA((2,)),
        ],
        (1, 1), "pack_cotangents",
    )(*[pltpu.with_memory_space_constraint(value, pltpu.HBM) for value in (routing, tile)])
    saved_slots = saved_pre[0, 0].transpose(1, 2, 0, 3)
    saved_slots = saved_slots.reshape(MIDDLE, MIDDLE * PER_WORKER, HALF)
    second_other, saved_other = swap(second_weight), swap(saved_slots)
    outgoing, saved_here = tie((outgoing, saved_slots))
    incoming = exchange(outgoing)

    second_other, saved_here = tie((second_other, saved_here))
    masked, *to_owners = call(
        functools.partial(pack_saved, owners, columns, capacity, wide, permuted),
        [shape((MIDDLE, MIDDLE * PER_WORKER, HALF), BF16)] + pieces(MIDDLE, wide * capacity, HALF),
        [SMEM, VMEM], counts + tables, (1, 1), "pack_saved",
    )(routing, saved_here)
    incoming_other = [swap(incoming[0])] if permuted else []
    incoming, to_owners, incoming_other = tie((incoming[::-1], to_owners[::-1], incoming_other))
    incoming, to_owners = incoming[::-1], to_owners[::-1]
    incoming_other += [swap(value) for value in incoming[len(incoming_other) :]]
    at_owner = exchange(to_owners)

    saved_tiles = saved_input[0, 0].transpose(1, 2, 0, 3)
    if permuted:
        part = (2, 9, ROWS, FULL)
        halved = [shape((4,) + part, F32)] + [shape((2,) + part, BF16)] * 2
    else:
        halved = [shape((2, 9, HALF, FULL), F32)]
    terms = call(
        functools.partial(worker, scale, owners, columns, capacity, permuted),
        halved,
        [SMEM] + [VMEM] * (2 * parts + 4) + [HBM],
        counts
        + [
            pltpu.VMEM((BLOCK, BLOCK * PER_WORKER, FULL), BF16),
            pltpu.VMEM((MIDDLE, MIDDLE * PER_WORKER, FULL), F32),
            pltpu.VMEM((MIDDLE, MIDDLE, PER_WORKER, FULL), BF16),
            pltpu.VMEM((9, FULL, FULL), BF16),
            pltpu.VMEM(saved_tiles.shape, BF16),
            pltpu.SemaphoreType.DMA,
        ]
        + ([pltpu.VMEM((4,) + part, BF16)] if permuted else []),
        (1, 1), "worker",
    )(
        routing, *incoming, *incoming_other, masked, saved_other, second_weight, second_other,
        pltpu.with_memory_space_constraint(saved_tiles, pltpu.HBM),
    )

    if permuted:
        kept, near, far = terms
        far, at_owner[2], at_owner[1] = tie((far, at_owner[2], at_owner[1]))
        far, tile_mine, tile_here = tie((far, tile, tile))
    else:
        terms, tile_mine, tile_here = tie((terms, tile, tile))
    total = call(
        owner_spread,
        shape((MIDDLE, MIDDLE, TILE_BLOCKS, FULL), BF16),
        [VMEM] * 4,
        [
            pltpu.VMEM((MIDDLE, MIDDLE * TILE_BLOCKS, FULL), F32),
            pltpu.VMEM((BLOCK, BLOCK * TILE_BLOCKS, FULL), BF16),
            pltpu.VMEM((9, FULL, FULL), BF16),
        ],
        (1, 1), "owner_spread",
    )(tile_here, swap(tile_mine), second_weight, second_other)

    def owner(at_owner):
        at_owner_other = [swap(value) for value in at_owner]
        return call(
            functools.partial(owner_canvas, owners, capacity, wide, permuted),
            [shape((HIGH, WIDE, HALF), F32)] + [shape((RIM, FULL), BF16)] * (2 if permuted else 0),
            [SMEM] + [VMEM] * (2 * len(at_owner) + 2),
            tables
            + [
                pltpu.VMEM((MIDDLE, MIDDLE * TILE_BLOCKS, FULL), BF16),
                pltpu.VMEM((OUTER, OUTER * TILE_BLOCKS, HALF), F32),
            ],
            (1, 1), "owner_canvas",
        )(routing, *at_owner, *at_owner_other, total, first_weight)

    if permuted:
        far_got, near_got = swap(far, "col"), swap(near, "col")
        total, far_got = tie((total, far_got))
        sends = call(add_far, [shape(part, BF16)] * 2, [VMEM] * 2, [], (1, 1), "add_far")(
            kept, far_got
        )
        sends, at_owner[3] = tie((sends[::-1], at_owner[3]))
        got = [flip(sends[0], "blk", 3), flip(sends[1], "blk", 2)]
        canvas, *rims = owner(at_owner)
        near_got, canvas = tie((near_got, canvas))
        keep, send = call(
            add_near, [shape(part, F32), shape(part, BF16)], [VMEM] * 2, [], (1, 1), "add_near",
        )(kept, near_got)
        got.append(flip(send, "blk", 1))
        message = shape((PART, FULL), BF16)
        wider = shape((PART + RIM, FULL), BF16)
        own, *wides = call(
            add_workers, [message, wider, wider], [VMEM] * 6, [], (1, 1), "add_workers",
        )(keep, *got, *rims)
        got_2, got_1 = flip(own, "blk", 2), flip(wides[0], "blk", 1)
        wide_3, got_2, across = tie((wides[1], got_2, swap(own, "col")))
        got_3 = flip(wide_3, "blk", 3)
        across = [across] + [swap(value, "col") for value in (got_1[:PART], got_2)]
        got_3, got_1, across = tie((got_3, got_1, across))
        got = [got_1, got_2, got_3]
        last = call(
            column_message, shape((PART + 64, FULL), BF16), [VMEM] * 3,
            [pltpu.VMEM((RIM, FULL), F32), pltpu.VMEM((64, HALF), F32)],
            (1, 1), "column_message",
        )(canvas.reshape(HIGH * WIDE, HALF), got[0], got[2])
        last = swap(last, "col")
        slab = (TILE_ROWS * BLOCK, 16, HALF)
        weights = [shape((9, HALF, FULL), F32)] * 2
        early, *outs = call(
            lay, [shape(grad_out.shape, BF16), shape(slab, F32)] + weights, [VMEM] * 9,
            [pltpu.VMEM((TILE_ROWS * BLOCK * 32, HALF), F32)], (1, 1), "lay",
        )(grad_out, canvas, own, *got, *across)
        grad_in, grad_second, grad_first = pl.pallas_call(
            finish,
            out_shape=[shape(grad_out.shape, BF16)] + weights,
            in_specs=[VMEM] * 2 + [HBM] * 3,
            out_specs=[HBM] * 3,
            scratch_shapes=[
                pltpu.VMEM((TILE_ROWS * BLOCK * 16 + 16, HALF), F32),
                pltpu.VMEM(slab, BF16),
                pltpu.VMEM((2, 9, ROWS, FULL), F32),
                pltpu.SemaphoreType.DMA((3,)),
            ],
            input_output_aliases={2: 0, 3: 1, 4: 2},
            compiler_params=pltpu.CompilerParams(vmem_limit_bytes=48 * 1024 * 1024),
            cost_estimate=pl.CostEstimate(flops=1, bytes_accessed=1, transcendentals=0),
            name="finish",
        )(outs[0], last, early, *outs[1:])
        return (grad_in, grad_first, grad_second)

    grad_first, grad_second = lax.psum((terms[0][1], terms[0][0]), ("blk", "col"))
    [canvas] = owner(at_owner)
    up, down = neighbours("blk")
    from_above = lax.ppermute(canvas[HIGH - 2 :].astype(BF16), "blk", up).astype(F32)
    from_below = lax.ppermute(canvas[:2].astype(BF16), "blk", down).astype(F32)
    inner = canvas[2 : HIGH - 2]
    inner = inner.at[:2].add(from_above).at[-2:].add(from_below)
    up, down = neighbours("col")
    from_left = lax.ppermute(inner[:, 32:34].astype(BF16), "col", up).astype(F32)
    from_right = lax.ppermute(inner[:, 34:36].astype(BF16), "col", down).astype(F32)
    inner = inner[:, :32].at[:, :2].add(from_left).at[:, -2:].add(from_right)
    grad_in = (grad_out.astype(F32) + inner).astype(BF16)
    return (grad_in, grad_first, grad_second)


def solution(mesh):
    return jax.shard_map(
        shards,
        mesh=mesh,
        in_specs=(
            P(("groups", "blk"), "col", "ch"),
            P(("groups", "col"), "blk", None, None, None, "ch"),
            P(("groups", "col"), "blk", None, None, None, "ch"),
            P(None, "ch", None),
            P(None, "ch", None),
            P(("groups", "col"), None, None),
        ),
        out_specs=(
            P(("groups", "blk"), "col", "ch"),
            P("groups", "ch", None),
            P("groups", "ch", None),
        ),
        check_vma=False,
    )
```

```python
import functools
import math

import jax
import jax.numpy as jnp
from jax import lax
from jax.experimental import pallas as pl
from jax.experimental.pallas import tpu as pltpu
from jax.sharding import PartitionSpec as P

BLOCK = 8
TILE_ROWS = 8
TILE_COLS = 4
TILE_BLOCKS = 32
PER_WORKER = 16
MIDDLE = 10
OUTER = 12
HALF = 128
FULL = 256
DEAD = -4096
HIGH = 68
RIM = 48
ROWS = 16
PART = 288
WIDE = 40

BF16 = jnp.bfloat16
F32 = jnp.float32
I32 = jnp.int32

VMEM = pl.BlockSpec(memory_space=pltpu.VMEM)
HBM = pl.BlockSpec(memory_space=pltpu.HBM)
SMEM = pl.BlockSpec(memory_space=pltpu.SMEM)


def call(body, outs, specs, scratch, cost, name):
    return pl.pallas_call(
        body,
        out_shape=outs,
        in_specs=specs,
        out_specs=jax.tree.map(lambda _: VMEM, outs),
        scratch_shapes=scratch,
        compiler_params=pltpu.CompilerParams(vmem_limit_bytes=48 * 1024 * 1024),
        cost_estimate=pl.CostEstimate(flops=cost[0], bytes_accessed=cost[1], transcendentals=0),
        name=name,
    )


def iota(shape, dim):
    return lax.broadcasted_iota(I32, shape, dim)


def one_hot(hits):
    return jnp.where(hits, 1.0, 0.0).astype(BF16)


def dot(a, b):
    return jnp.dot(a, b, preferred_element_type=F32)


def dot_nt(a, b):
    return lax.dot_general(a, b, (((1,), (1,)), ((), ())), preferred_element_type=F32)


def dot_tn(a, b):
    return lax.dot_general(a, b, (((0,), (0,)), ((), ())), preferred_element_type=F32)


def owner_table(routing, table, owners, capacity):
    me = lax.axis_index("blk")

    def clear(number, carry):
        table[number] = DEAD
        return carry

    lax.fori_loop(0, owners * capacity, clear, 0)

    def worker(number, carry):
        count = jnp.int32(0)
        for slot in range(PER_WORKER):
            code = routing[number, slot]
            hit = (code // TILE_BLOCKS) == me
            table[jnp.where(hit, number * capacity + count, owners * capacity)] = code % TILE_BLOCKS
            count = count + jnp.where(hit, 1, 0)
        return carry

    lax.fori_loop(0, owners, worker, 0)


def worker_codes(routing, counts, owners):
    me = lax.axis_index("blk")

    def clear(number, carry):
        counts[number] = 0
        return carry

    lax.fori_loop(0, owners, clear, 0)
    slots = []
    for slot in range(PER_WORKER):
        code = routing[me, slot]
        owner = code // TILE_BLOCKS
        rank = counts[owner]
        counts[owner] = rank + 1
        slots.append((owner, code % TILE_BLOCKS, rank))
    return slots


def views(refs, count):
    return list(refs) if len(refs) == count else [refs[0].at[k] for k in range(count)]


def partner(axis, step, permuted):
    return step ^ lax.axis_index(axis) if permuted else step


def pack_cotangents(owners, capacity, permuted, listed, source, *refs):
    outs, (places, tile, codes, arrived) = refs[:-4], refs[-4:]
    fetch = pltpu.make_async_copy(source, tile, arrived.at[0])
    fetch.start()
    lists = pltpu.make_async_copy(listed, codes, arrived.at[1])
    lists.start()
    lists.wait()
    hit = (codes[...] // TILE_BLOCKS) == lax.axis_index("blk")
    places[0] = jnp.where(hit, codes[...] % TILE_BLOCKS + 1, 0)
    before = (iota((PER_WORKER, PER_WORKER), 0) < iota((PER_WORKER, PER_WORKER), 1))
    places[1] = dot(one_hot(hit), one_hot(before)).astype(I32)
    rows = BLOCK * capacity
    row, lane = iota((rows, FULL), 0), iota((rows, FULL), 1)
    picks = []
    for step in range(owners):
        at = pl.ds(partner("blk", step, permuted), 1)
        same = places[1, at, :] == iota((rows, PER_WORKER), 0) % capacity
        place = jnp.sum(jnp.where(same, places[0, at, :], 0).astype(F32), axis=1, keepdims=True)
        target = (place.astype(I32) - 1) * BLOCK
        picks.append(one_hot(lane == target + row // capacity))
    pick = jnp.concatenate(picks, axis=0)
    fetch.wait()
    for u in range(0, BLOCK, 2):
        pair = [
            jnp.concatenate([tile[r, u + k] for r in range(TILE_ROWS)], axis=0) for k in range(2)
        ]
        moved = dot(pick, jnp.concatenate(pair, axis=1)).astype(BF16)
        for step, out in enumerate(views(outs, owners)):
            part = moved[step * rows : (step + 1) * rows]
            out[u] = part[:, :HALF]
            out[u + 1] = part[:, HALF:]


def outside_image(slots, owners, columns):
    column = lax.axis_index("col")
    row = iota((MIDDLE * PER_WORKER, HALF), 0)
    flags = jnp.zeros_like(row)
    for slot, (owner, place, rank) in enumerate(slots):
        block_row, block_col = place // TILE_COLS, place % TILE_COLS
        flag = (
            jnp.where((owner == 0) & (block_row == 0), 1, 0)
            + jnp.where((owner == owners - 1) & (block_row == TILE_ROWS - 1), 2, 0)
            + jnp.where((column == 0) & (block_col == 0), 4, 0)
            + jnp.where((column == columns - 1) & (block_col == TILE_COLS - 1), 8, 0)
        )
        flags = jnp.where(row % PER_WORKER == slot, flag, flags)
    across = row // PER_WORKER
    sides = (((flags & 4) != 0) & (across == 0)) | (((flags & 8) != 0) & (across == MIDDLE - 1))

    def here(m):
        if m == 0:
            return sides | ((flags & 1) != 0)
        if m == MIDDLE - 1:
            return sides | ((flags & 2) != 0)
        return sides

    return here


def pack_saved(owners, columns, capacity, wide, permuted, routing, saved, saved_other, *refs):
    (weight, weight_other, masked, whole, full, pick_slots), refs = refs[:6], refs[6:]
    outs, counts, table = refs[:-2], refs[-2], refs[-1]
    full[...] = ordered(weight[...], weight_other[...], 1)

    def clear(number, carry):
        table[number] = DEAD
        return carry

    lax.fori_loop(0, owners * capacity, clear, 0)
    slots = worker_codes(routing, counts, owners)
    rows = MIDDLE * PER_WORKER
    for slot, (owner, place, rank) in enumerate(slots):
        table[owner * capacity + rank] = slot
    outside = outside_image(slots, owners, columns)
    for m in range(MIDDLE):
        here = outside(m)
        masked[m] = jnp.where(here, 0.0, saved[m].astype(F32)).astype(BF16)
        other = jnp.where(here, 0.0, saved_other[m].astype(F32)).astype(BF16)
        whole[m] = ordered(masked[m], other, 1)
    pick_slots[...] = slot_selection(slots, owners, capacity, permuted)
    size = wide * capacity
    row, lane = iota((size, FULL), 0), iota((size, FULL), 1)
    picks = []
    for step in range(owners):
        owner = partner("blk", step, permuted)
        target = jnp.full((size, FULL), DEAD, I32)
        for rank in range(capacity):
            target = jnp.where(row % capacity == rank, table[owner * capacity + rank], target)
        at = row // capacity
        picks.append(one_hot((lane == target + at * PER_WORKER) & (at < MIDDLE)))
    pick = jnp.concatenate(picks, axis=0)
    filler = jnp.zeros((FULL - rows, FULL), BF16)
    for m in range(0, MIDDLE, 2):
        pair = jnp.concatenate([masked[m], masked[m + 1]], axis=1)
        moved = dot(pick, jnp.concatenate([pair, filler], axis=0)).astype(BF16)
        for step, out in enumerate(views(outs, owners)):
            part = moved[step * size : (step + 1) * size]
            out[m] = part[:, :HALF]
            out[m + 1] = part[:, HALF:]


def ordered(own, other, axis):
    first = lax.axis_index("ch") == 0
    return jnp.concatenate(
        [jnp.where(first, own, other), jnp.where(first, other, own)], axis=axis
    )


def deal(value, kept, sent, grad, tap):
    low, high = value[: HALF // 2], value[HALF // 2 :]
    mine = lax.axis_index("col") == 0
    keep, send = jnp.where(mine, low, high), jnp.where(mine, high, low).astype(BF16)
    for k in range(4):
        step, rows = partner("blk", k, True), slice(k * ROWS, (k + 1) * ROWS)
        kept[step, grad, tap] = keep[rows]
        sent[step, grad, tap] = send[rows]


def emit(value, outs, grad, tap):
    if len(outs) == 2:
        deal(value, outs[0], outs[1], grad, tap)
    else:
        outs[0][grad, tap] = value


def spread(values, weight, total, places):
    height, extent = values.shape[:2]
    inputs = values[...].reshape(height * extent, FULL)
    width, step = weight.shape[1], places
    for dy in range(3):
        taps = jnp.concatenate([weight[3 * dy + dx] for dx in range(3)], axis=0)
        part = dot_nt(inputs, taps).reshape(height, extent, 3 * width)
        p, q, r = [part[:, :, dx * width : (dx + 1) * width] for dx in range(3)]
        sums = [
            p[:, :step],
            p[:, step : 2 * step] + q[:, :step],
            p[:, 2 * step :] + q[:, step : extent - step] + r[:, : extent - 2 * step],
            q[:, extent - step :] + r[:, extent - 2 * step : extent - step],
            r[:, extent - step :],
        ]
        at = 0
        for value in sums:
            size = value.shape[1]
            here = slice(at, at + size)
            if dy == 0:
                total[:height, here] = value
            else:
                total[dy : dy + height - 1, here] += value[:-1]
                total[dy + height - 1, here] = value[height - 1]
            at += size


def slot_selection(slots, owners, capacity, permuted):
    rows, inner = BLOCK * PER_WORKER, owners * BLOCK * capacity
    row, lane = iota((rows, inner), 0), iota((rows, inner), 1)
    target = jnp.full((rows, inner), DEAD, I32)
    for slot, (owner, place, rank) in enumerate(slots):
        step = partner("blk", owner, permuted)
        target = jnp.where(row % PER_WORKER == slot, step * (BLOCK * capacity) + rank, target)
    return one_hot(lane == target + (row // PER_WORKER) * capacity)


def second_gradient(scale, owners, capacity, permuted, *refs):
    parts = 1 if not permuted else owners
    own, other = views(refs[:parts], owners), views(refs[parts : 2 * parts], owners)
    pick, masked, cot = refs[2 * parts : 2 * parts + 3]
    outs = refs[2 * parts + 3 :]
    rows = BLOCK * PER_WORKER
    for u in range(BLOCK):
        got = jnp.concatenate(
            [ordered(own[o][u], other[o][u], 1) for o in range(owners)], axis=0
        )
        cot[u] = dot(pick[...], got).astype(BF16)
    grads = cot[...].reshape(BLOCK * rows, FULL)
    turned = []
    for dx in range(3):
        window = masked[:, dx * PER_WORKER : (dx + BLOCK) * PER_WORKER].reshape(MIDDLE * rows, HALF)
        turned.append(jnp.maximum(window, jnp.zeros_like(window)).T)
    turned = jnp.concatenate(turned, axis=0)
    for dy in range(3):
        value = dot(turned[:, dy * rows : (dy + BLOCK) * rows], grads) * scale
        for dx in range(3):
            emit(value[dx * HALF : (dx + 1) * HALF], outs, 0, 3 * dy + dx)


def first_gradient(
    scale, cot, whole, full, saved, *refs
):
    outs, (total, pre) = refs[:-2], refs[-2:]
    spread(cot, full, total, PER_WORKER)
    for m in range(MIDDLE):
        live = whole[m].astype(F32) > 0
        value = jnp.where(live, total[m], 0.0)
        pre[m] = value.astype(BF16).reshape(MIDDLE, PER_WORKER, FULL)
    size = MIDDLE * MIDDLE * PER_WORKER
    grads = pre[...].reshape(size, FULL)
    for dy in range(3):
        windows = [saved[dy : dy + MIDDLE, dx : dx + MIDDLE] for dx in range(3)]
        window = jnp.concatenate([w.reshape(size, HALF) for w in windows], axis=1)
        value = dot_tn(window, grads) * scale
        for dx in range(3):
            emit(value[dx * HALF : (dx + 1) * HALF], outs, 1, 3 * dy + dx)


def owner_spread(tile, tile_other, full, out, total, cot):
    row, lane = iota((FULL, FULL), 0), iota((FULL, FULL), 1)
    turn = one_hot(lane == (row % TILE_BLOCKS) * BLOCK + row // TILE_BLOCKS)
    for u in range(BLOCK):
        block = jnp.concatenate(
            [ordered(tile[r, u], tile_other[r, u], 1) for r in range(TILE_ROWS)], axis=0
        )
        cot[u] = dot(turn, block).astype(BF16)
    spread(cot, full, total, TILE_BLOCKS)
    out[...] = total[...].astype(BF16).reshape(out.shape)


def worker(scale, owners, capacity, permuted, *refs):
    parts = 1 if not permuted else owners
    inputs, refs = refs[: 2 * parts], refs[2 * parts :]
    (pick, masked, whole, full, source), refs = refs[:5], refs[5:]
    if permuted:
        refs, sent = refs[:-1], refs[-1]
    outs, (cot, total, pre, saved, arrived) = refs[:-5], refs[-5:]
    if permuted:
        kept, near, far = outs
        outs = (kept, sent)
    fetch = pltpu.make_async_copy(source, saved, arrived)
    fetch.start()
    second_gradient(scale, owners, capacity, permuted, *inputs, pick, masked, cot, *outs)
    fetch.wait()
    first_gradient(scale, cot, whole, full, saved, *outs, total, pre)
    if permuted:
        near[...] = sent[:2]
        far[...] = sent[2:]


def adjacent(step):
    me = lax.axis_index("blk")
    return (me ^ step) == me - 1, (me ^ step) == me + 1


def owner_canvas(owners, capacity, wide, permuted, routing, *refs):
    parts = 1 if not permuted else owners
    got, got_other = views(refs[:parts], owners), views(refs[parts : 2 * parts], owners)
    total, first, canvas = refs[2 * parts : 2 * parts + 3]
    rims, (table, pre, grown) = refs[2 * parts + 3 : -3], refs[-3:]
    owner_table(routing, table, owners, capacity)
    size, into = wide * capacity, MIDDLE * TILE_BLOCKS
    row, lane = iota((size, into), 0), iota((size, into), 1)
    picks = []
    for step in range(owners):
        worker = partner("blk", step, permuted)
        target = jnp.full((size, into), DEAD, I32)
        for rank in range(capacity):
            target = jnp.where(row % capacity == rank, table[worker * capacity + rank], target)
        at = row // capacity
        hits = (lane == target + at * TILE_BLOCKS) & (at < MIDDLE)
        picks.append(jnp.where(hits, 1.0, 0.0))
    pick = jnp.concatenate(picks, axis=0).T.astype(BF16)
    for m in range(MIDDLE):
        block = jnp.concatenate(
            [ordered(got[w][m], got_other[w][m], 1) for w in range(owners)], axis=0
        )
        value = jnp.where(dot(pick, block) > 0, total[m].reshape(into, FULL).astype(F32), 0.0)
        pre[m] = value.astype(BF16)
    spread(pre, first, grown, TILE_BLOCKS)
    height, depth = TILE_ROWS * WIDE, OUTER * TILE_BLOCKS
    row, lane = iota((height, depth), 0), iota((height, depth), 1)
    at_row, at_col = row // WIDE, row % WIDE
    n, place = lane // TILE_BLOCKS, lane % TILE_BLOCKS
    column = (place % TILE_COLS) * BLOCK + n - 2
    column = jnp.where(column < 0, column + 36, column)
    fold = one_hot((at_row == place // TILE_COLS) & (at_col == column))
    canvas[...] = jnp.zeros_like(canvas)
    for m in range(0, OUTER, 2):
        pair = jnp.concatenate(
            [grown[m + k].astype(BF16) for k in range(2)], axis=1
        )
        laid = dot(fold, pair).reshape(TILE_ROWS, WIDE, FULL)
        for r in range(TILE_ROWS):
            for k in range(2):
                canvas[r * BLOCK + m + k] += laid[r, :, k * HALF : (k + 1) * HALF]
    for k, rim in enumerate(rims):
        above, below = adjacent(2 * k + 1)
        top = jnp.concatenate([canvas[0], canvas[1]], axis=1)
        bottom = jnp.concatenate([canvas[HIGH - 2], canvas[HIGH - 1]], axis=1)
        here = jnp.where(below, bottom, jnp.where(above, top, 0.0))
        rim[...] = jnp.concatenate([here, jnp.zeros((RIM - WIDE, FULL), F32)], axis=0).astype(BF16)


def add_far(kept, got, *sends):
    for k, out in enumerate(sends):
        out[...] = (kept[2 + k] + got[k].astype(F32)).astype(BF16)


def add_near(kept, got, keep, send):
    keep[...] = kept[0] + got[0].astype(F32)
    send[...] = (kept[1] + got[1].astype(F32)).astype(BF16)


def add_workers(kept, got_3, got_2, got_1, rim_1, rim_3, out, out_1, out_3):
    value = kept[...]
    for part in (got_3, got_2, got_1):
        value = value + part[...].astype(F32)
    value = value.astype(BF16).reshape(PART, FULL)
    out[...] = value
    for message, rim in ((out_1, rim_1), (out_3, rim_3)):
        message[:PART] = value
        message[PART:] = rim[...]


def column_message(canvas, got_1, got_3, out, rim, strip):
    out[:PART] = got_3[:PART]
    for j in range(2):
        c = 32 + 2 * lax.axis_index("col") + j
        strip[...] = canvas[pl.ds(2 * WIDE + c, 64, stride=WIDE), :]
        for step, got in ((1, got_1), (3, got_3)):
            rim[...] = got[PART:].astype(F32)
            row = rim[pl.ds(c, 1), :]
            above, below = adjacent(step)
            top, bottom = jnp.where(above, row, 0.0), jnp.where(below, row, 0.0)
            strip[0:1] += top[:, :HALF]
            strip[1:2] += top[:, HALF:]
            strip[62:63] += bottom[:, :HALF]
            strip[63:64] += bottom[:, HALF:]
        out[PART:, j * HALF : (j + 1) * HALF] = strip[...].astype(BF16)


def gather_image(tile, canvas, got_1, got_3, total):
    rows = TILE_ROWS * BLOCK * 32
    total[...] = tile[...].reshape(rows, HALF).astype(F32) + canvas[
        2 : HIGH - 2, :32, :
    ].reshape(rows, HALF)
    for step, got in ((1, got_1), (3, got_3)):
        rim = got[PART : PART + 32].astype(F32)
        above, below = adjacent(step)
        top, bottom = jnp.where(above, rim, 0.0), jnp.where(below, rim, 0.0)
        total[0:32] += top[:, :HALF]
        total[32:64] += top[:, HALF:]
        total[rows - 64 : rows - 32] += bottom[:, :HALF]
        total[rows - 32 : rows] += bottom[:, HALF:]


def rows_at(number):
    column = lax.axis_index("col")
    place = (column if number < 4 else 1 - column) * 4 + partner("blk", number % 4, True)
    return pl.ds(pl.multiple_of(place * ROWS, ROWS), ROWS)


def lay(tile, canvas, *refs):
    parts, (image, slab), outs, total = refs[:-5], refs[-5:-3], refs[-3:-1], refs[-1]
    gather_image(tile, canvas, parts[1], parts[3], total)
    whole = total[...].reshape(image.shape)
    image[...] = whole.astype(BF16)
    slab[...] = jnp.where(lax.axis_index("col") == 0, whole[:, 16:], whole[:, :16])
    for number, part in zip((0, 1, 2, 3, 4, 5, 6), parts):
        value = part[:PART].astype(F32).reshape(2, 9, ROWS, FULL)
        for out, grad in zip(outs, (0, 1)):
            out[:, rows_at(number), :] = value[grad]


def finish(slab, last, old, old_0, old_1, image, out_0, out_1, total, side, laid, sems):
    copies = []
    laid[...] = last[:PART].astype(F32).reshape(2, 9, ROWS, FULL)
    for grad, dest in enumerate((out_0, out_1)):
        copies.append(
            pltpu.make_async_copy(laid.at[grad], dest.at[:, rows_at(7), :], sems.at[grad])
        )
        copies[-1].start()
    rows = TILE_ROWS * BLOCK * 16
    total[:rows] = slab[...].reshape(rows, HALF)
    strip = last[PART:].astype(F32)
    left = lax.axis_index("col") == 0
    at = jnp.where(left, 14, 0)
    for j in range(2):
        spot = (pl.ds(at + j, 64, stride=16), slice(None))
        total[spot] = total[spot] + strip[:, j * HALF : (j + 1) * HALF]
    side[...] = total[:rows].astype(BF16).reshape(side.shape)
    columns = pl.ds(pl.multiple_of(jnp.where(left, 16, 0), 16), 16)
    copies.append(pltpu.make_async_copy(side, image.at[:, columns, :], sems.at[2]))
    copies[-1].start()
    for copy in copies:
        copy.wait()


def swap(value, axis="ch"):
    return lax.ppermute(value, axis, [(0, 1), (1, 0)])


def flip(value, axis, step):
    size = lax.axis_size(axis)
    return lax.ppermute(value, axis, [(i, i ^ step) for i in range(size)])


def neighbours(axis):
    size = lax.axis_size(axis)
    up = [(i, (i + 1) % size) for i in range(size - 1)]
    return up, [(j, i) for i, j in up]


def shards(grad_out, saved_input, saved_pre, first_weight, second_weight, assignment):
    owners = lax.axis_size("blk")
    columns = lax.axis_size("col")
    capacity = max(2, TILE_BLOCKS // owners)
    wide = MIDDLE if (MIDDLE * capacity) % 16 == 0 else 16
    scale = 1.0 / math.sqrt(owners * columns * PER_WORKER * BLOCK * BLOCK)
    permuted = owners == 4 and columns == 2
    parts = owners if permuted else 1
    routing = assignment[0]
    shape = jax.ShapeDtypeStruct
    tables = [pltpu.SMEM((owners * capacity + 1,), I32)]
    counts = [pltpu.SMEM((owners,), I32)]

    def pieces(*dims):
        return [shape(dims, BF16)] * owners if permuted else [shape((owners,) + dims, BF16)]

    def exchange(values):
        if permuted:
            return list(values[:1]) + [flip(values[k], "blk", k) for k in (3, 2, 1)][::-1]
        return [lax.all_to_all(values[0], "blk", split_axis=0, concat_axis=0, tiled=True)]

    tie = lax.optimization_barrier
    tile = grad_out.reshape(TILE_ROWS, BLOCK, TILE_COLS * BLOCK, HALF)
    outgoing = call(
        functools.partial(pack_cotangents, owners, capacity, permuted),
        pieces(BLOCK, BLOCK * capacity, HALF),
        [HBM, HBM],
        [
            pltpu.VMEM((2,) + routing.shape, I32),
            pltpu.VMEM(tile.shape, BF16),
            pltpu.VMEM(routing.shape, I32),
            pltpu.SemaphoreType.DMA((2,)),
        ],
        (1, 1), "pack_cotangents",
    )(*[pltpu.with_memory_space_constraint(value, pltpu.HBM) for value in (routing, tile)])
    saved_slots = saved_pre[0, 0].transpose(1, 2, 0, 3)
    saved_slots = saved_slots.reshape(MIDDLE, MIDDLE * PER_WORKER, HALF)
    second_other, saved_other = swap(second_weight), swap(saved_slots)
    outgoing, saved_here = tie((outgoing, saved_slots))
    incoming = exchange(outgoing)

    second_other, saved_other, saved_here = tie((second_other, saved_other, saved_here))
    masked, whole, full, pick, *to_owners = call(
        functools.partial(pack_saved, owners, columns, capacity, wide, permuted),
        [
            shape((MIDDLE, MIDDLE * PER_WORKER, HALF), BF16),
            shape((MIDDLE, MIDDLE * PER_WORKER, FULL), BF16),
            shape((9, FULL, FULL), BF16),
            shape((BLOCK * PER_WORKER, owners * BLOCK * capacity), BF16),
        ]
        + pieces(MIDDLE, wide * capacity, HALF),
        [SMEM] + [VMEM] * 4, counts + tables, (1, 1), "pack_saved",
    )(routing, saved_here, saved_other, second_weight, second_other)

    incoming_other = [swap(incoming[0])] if permuted else []
    incoming, to_owners, incoming_other = tie((incoming[::-1], to_owners[::-1], incoming_other))
    incoming, to_owners = incoming[::-1], to_owners[::-1]
    incoming_other += [swap(value) for value in incoming[len(incoming_other) :]]
    at_owner = exchange(to_owners)

    saved_tiles = saved_input[0, 0].transpose(1, 2, 0, 3)
    if permuted:
        part = (2, 9, ROWS, FULL)
        halved = [shape((4,) + part, F32)] + [shape((2,) + part, BF16)] * 2
    else:
        halved = [shape((2, 9, HALF, FULL), F32)]
    terms = call(
        functools.partial(worker, scale, owners, capacity, permuted),
        halved,
        [VMEM] * (2 * parts + 4) + [HBM],
        [
            pltpu.VMEM((BLOCK, BLOCK * PER_WORKER, FULL), BF16),
            pltpu.VMEM((MIDDLE, MIDDLE * PER_WORKER, FULL), F32),
            pltpu.VMEM((MIDDLE, MIDDLE, PER_WORKER, FULL), BF16),
            pltpu.VMEM(saved_tiles.shape, BF16),
            pltpu.SemaphoreType.DMA,
        ]
        + ([pltpu.VMEM((4,) + part, BF16)] if permuted else []),
        (1, 1), "worker",
    )(
        *incoming, *incoming_other, pick, masked, whole, full,
        pltpu.with_memory_space_constraint(saved_tiles, pltpu.HBM),
    )

    if permuted:
        kept, near, far = terms
        far, at_owner[2], at_owner[1] = tie((far, at_owner[2], at_owner[1]))
        far, tile_mine, tile_here = tie((far, tile, tile))
    else:
        terms, tile_mine, tile_here = tie((terms, tile, tile))
    total = call(
        owner_spread,
        shape((MIDDLE, MIDDLE, TILE_BLOCKS, FULL), BF16),
        [VMEM] * 3,
        [
            pltpu.VMEM((MIDDLE, MIDDLE * TILE_BLOCKS, FULL), F32),
            pltpu.VMEM((BLOCK, BLOCK * TILE_BLOCKS, FULL), BF16),
        ],
        (1, 1), "owner_spread",
    )(tile_here, swap(tile_mine), full)

    def owner(at_owner):
        at_owner_other = [swap(value) for value in at_owner]
        return call(
            functools.partial(owner_canvas, owners, capacity, wide, permuted),
            [shape((HIGH, WIDE, HALF), F32)] + [shape((RIM, FULL), BF16)] * (2 if permuted else 0),
            [SMEM] + [VMEM] * (2 * len(at_owner) + 2),
            tables
            + [
                pltpu.VMEM((MIDDLE, MIDDLE * TILE_BLOCKS, FULL), BF16),
                pltpu.VMEM((OUTER, OUTER * TILE_BLOCKS, HALF), F32),
            ],
            (1, 1), "owner_canvas",
        )(routing, *at_owner, *at_owner_other, total, first_weight)

    if permuted:
        far_got, near_got = swap(far, "col"), swap(near, "col")
        total, far_got = tie((total, far_got))
        sends = call(add_far, [shape(part, BF16)] * 2, [VMEM] * 2, [], (1, 1), "add_far")(
            kept, far_got
        )
        sends, at_owner[3] = tie((sends[::-1], at_owner[3]))
        got = [flip(sends[0], "blk", 3), flip(sends[1], "blk", 2)]
        canvas, *rims = owner(at_owner)
        near_got, canvas = tie((near_got, canvas))
        keep, send = call(
            add_near, [shape(part, F32), shape(part, BF16)], [VMEM] * 2, [], (1, 1), "add_near",
        )(kept, near_got)
        got.append(flip(send, "blk", 1))
        message = shape((PART, FULL), BF16)
        wider = shape((PART + RIM, FULL), BF16)
        own, *wides = call(
            add_workers, [message, wider, wider], [VMEM] * 6, [], (1, 1), "add_workers",
        )(keep, *got, *rims)
        got_2, got_1 = flip(own, "blk", 2), flip(wides[0], "blk", 1)
        wide_3, got_2, across = tie((wides[1], got_2, swap(own, "col")))
        got_3 = flip(wide_3, "blk", 3)
        across = [across] + [swap(value, "col") for value in (got_1[:PART], got_2)]
        got_3, got_1, across = tie((got_3, got_1, across))
        got = [got_1, got_2, got_3]
        last = call(
            column_message, shape((PART + 64, FULL), BF16), [VMEM] * 3,
            [pltpu.VMEM((RIM, FULL), F32), pltpu.VMEM((64, HALF), F32)],
            (1, 1), "column_message",
        )(canvas.reshape(HIGH * WIDE, HALF), got[0], got[2])
        last = swap(last, "col")
        slab = (TILE_ROWS * BLOCK, 16, HALF)
        weights = [shape((9, HALF, FULL), F32)] * 2
        early, *outs = call(
            lay, [shape(grad_out.shape, BF16), shape(slab, F32)] + weights, [VMEM] * 9,
            [pltpu.VMEM((TILE_ROWS * BLOCK * 32, HALF), F32)], (1, 1), "lay",
        )(grad_out, canvas, own, *got, *across)
        grad_in, grad_second, grad_first = pl.pallas_call(
            finish,
            out_shape=[shape(grad_out.shape, BF16)] + weights,
            in_specs=[VMEM] * 2 + [HBM] * 3,
            out_specs=[HBM] * 3,
            scratch_shapes=[
                pltpu.VMEM((TILE_ROWS * BLOCK * 16 + 16, HALF), F32),
                pltpu.VMEM(slab, BF16),
                pltpu.VMEM((2, 9, ROWS, FULL), F32),
                pltpu.SemaphoreType.DMA((3,)),
            ],
            input_output_aliases={2: 0, 3: 1, 4: 2},
            compiler_params=pltpu.CompilerParams(vmem_limit_bytes=48 * 1024 * 1024),
            cost_estimate=pl.CostEstimate(flops=1, bytes_accessed=1, transcendentals=0),
            name="finish",
        )(outs[0], last, early, *outs[1:])
        return (grad_in, grad_first, grad_second)

    grad_first, grad_second = lax.psum((terms[0][1], terms[0][0]), ("blk", "col"))
    [canvas] = owner(at_owner)
    up, down = neighbours("blk")
    from_above = lax.ppermute(canvas[HIGH - 2 :].astype(BF16), "blk", up).astype(F32)
    from_below = lax.ppermute(canvas[:2].astype(BF16), "blk", down).astype(F32)
    inner = canvas[2 : HIGH - 2]
    inner = inner.at[:2].add(from_above).at[-2:].add(from_below)
    up, down = neighbours("col")
    from_left = lax.ppermute(inner[:, 32:34].astype(BF16), "col", up).astype(F32)
    from_right = lax.ppermute(inner[:, 34:36].astype(BF16), "col", down).astype(F32)
    inner = inner[:, :32].at[:, :2].add(from_left).at[:, -2:].add(from_right)
    grad_in = (grad_out.astype(F32) + inner).astype(BF16)
    return (grad_in, grad_first, grad_second)


def solution(mesh):
    return jax.shard_map(
        shards,
        mesh=mesh,
        in_specs=(
            P(("groups", "blk"), "col", "ch"),
            P(("groups", "col"), "blk", None, None, None, "ch"),
            P(("groups", "col"), "blk", None, None, None, "ch"),
            P(None, "ch", None),
            P(None, "ch", None),
            P(("groups", "col"), None, None),
        ),
        out_specs=(
            P(("groups", "blk"), "col", "ch"),
            P("groups", "ch", None),
            P("groups", "ch", None),
        ),
        check_vma=False,
    )
```

```python
import functools
import math

import jax
import jax.numpy as jnp
from jax import lax
from jax.experimental import pallas as pl
from jax.experimental.pallas import tpu as pltpu
from jax.sharding import PartitionSpec as P

BLOCK = 8
TILE_ROWS = 8
TILE_COLS = 4
TILE_BLOCKS = 32
PER_WORKER = 16
MIDDLE = 10
OUTER = 12
HALF = 128
FULL = 256
DEAD = -4096
HIGH = 68
RIM = 48
ROWS = 16
PART = 288
WIDE = 40

BF16 = jnp.bfloat16
F32 = jnp.float32
I32 = jnp.int32

VMEM = pl.BlockSpec(memory_space=pltpu.VMEM)
HBM = pl.BlockSpec(memory_space=pltpu.HBM)
SMEM = pl.BlockSpec(memory_space=pltpu.SMEM)


def call(body, outs, specs, scratch, cost, name):
    return pl.pallas_call(
        body,
        out_shape=outs,
        in_specs=specs,
        out_specs=jax.tree.map(lambda _: VMEM, outs),
        scratch_shapes=scratch,
        compiler_params=pltpu.CompilerParams(vmem_limit_bytes=48 * 1024 * 1024),
        cost_estimate=pl.CostEstimate(flops=cost[0], bytes_accessed=cost[1], transcendentals=0),
        name=name,
    )


def iota(shape, dim):
    return lax.broadcasted_iota(I32, shape, dim)


def one_hot(hits):
    return jnp.where(hits, 1.0, 0.0).astype(BF16)


def dot(a, b):
    return jnp.dot(a, b, preferred_element_type=F32)


def dot_nt(a, b):
    return lax.dot_general(a, b, (((1,), (1,)), ((), ())), preferred_element_type=F32)


def dot_tn(a, b):
    return lax.dot_general(a, b, (((0,), (0,)), ((), ())), preferred_element_type=F32)


def owner_table(routing, table, owners, capacity):
    me = lax.axis_index("blk")

    def clear(number, carry):
        table[number] = DEAD
        return carry

    lax.fori_loop(0, owners * capacity, clear, 0)

    def worker(number, carry):
        count = jnp.int32(0)
        for slot in range(PER_WORKER):
            code = routing[number, slot]
            hit = (code // TILE_BLOCKS) == me
            table[jnp.where(hit, number * capacity + count, owners * capacity)] = code % TILE_BLOCKS
            count = count + jnp.where(hit, 1, 0)
        return carry

    lax.fori_loop(0, owners, worker, 0)


def worker_codes(routing, counts, owners):
    me = lax.axis_index("blk")

    def clear(number, carry):
        counts[number] = 0
        return carry

    lax.fori_loop(0, owners, clear, 0)
    slots = []
    for slot in range(PER_WORKER):
        code = routing[me, slot]
        owner = code // TILE_BLOCKS
        rank = counts[owner]
        counts[owner] = rank + 1
        slots.append((owner, code % TILE_BLOCKS, rank))
    return slots


def views(refs, count):
    return list(refs) if len(refs) == count else [refs[0].at[k] for k in range(count)]


def partner(axis, step, permuted):
    return step ^ lax.axis_index(axis) if permuted else step


def pack_cotangents(owners, capacity, permuted, listed, source, *refs):
    outs, (places, tile, codes, arrived) = refs[:-4], refs[-4:]
    fetch = pltpu.make_async_copy(source, tile, arrived.at[0])
    fetch.start()
    lists = pltpu.make_async_copy(listed, codes, arrived.at[1])
    lists.start()
    lists.wait()
    hit = (codes[...] // TILE_BLOCKS) == lax.axis_index("blk")
    places[0] = jnp.where(hit, codes[...] % TILE_BLOCKS + 1, 0)
    before = (iota((PER_WORKER, PER_WORKER), 0) < iota((PER_WORKER, PER_WORKER), 1))
    places[1] = dot(one_hot(hit), one_hot(before)).astype(I32)
    rows = BLOCK * capacity
    row, lane = iota((rows, FULL), 0), iota((rows, FULL), 1)
    picks = []
    for step in range(owners):
        at = pl.ds(partner("blk", step, permuted), 1)
        same = places[1, at, :] == iota((rows, PER_WORKER), 0) % capacity
        place = jnp.sum(jnp.where(same, places[0, at, :], 0).astype(F32), axis=1, keepdims=True)
        target = (place.astype(I32) - 1) * BLOCK
        picks.append(one_hot(lane == target + row // capacity))
    pick = jnp.concatenate(picks, axis=0)
    fetch.wait()
    for u in range(0, BLOCK, 2):
        pair = [
            jnp.concatenate([tile[r, u + k] for r in range(TILE_ROWS)], axis=0) for k in range(2)
        ]
        moved = dot(pick, jnp.concatenate(pair, axis=1)).astype(BF16)
        for step, out in enumerate(views(outs, owners)):
            part = moved[step * rows : (step + 1) * rows]
            out[u] = part[:, :HALF]
            out[u + 1] = part[:, HALF:]


def outside_image(slots, owners, columns):
    column = lax.axis_index("col")
    row = iota((MIDDLE * PER_WORKER, HALF), 0)
    flags = jnp.zeros_like(row)
    for slot, (owner, place, rank) in enumerate(slots):
        block_row, block_col = place // TILE_COLS, place % TILE_COLS
        flag = (
            jnp.where((owner == 0) & (block_row == 0), 1, 0)
            + jnp.where((owner == owners - 1) & (block_row == TILE_ROWS - 1), 2, 0)
            + jnp.where((column == 0) & (block_col == 0), 4, 0)
            + jnp.where((column == columns - 1) & (block_col == TILE_COLS - 1), 8, 0)
        )
        flags = jnp.where(row % PER_WORKER == slot, flag, flags)
    across = row // PER_WORKER
    sides = (((flags & 4) != 0) & (across == 0)) | (((flags & 8) != 0) & (across == MIDDLE - 1))

    def here(m):
        if m == 0:
            return sides | ((flags & 1) != 0)
        if m == MIDDLE - 1:
            return sides | ((flags & 2) != 0)
        return sides

    return here


def pack_saved(owners, columns, capacity, wide, permuted, routing, saved, masked, *refs):
    outs, counts, table = refs[:-2], refs[-2], refs[-1]

    def clear(number, carry):
        table[number] = DEAD
        return carry

    lax.fori_loop(0, owners * capacity, clear, 0)
    slots = worker_codes(routing, counts, owners)
    rows = MIDDLE * PER_WORKER
    for slot, (owner, place, rank) in enumerate(slots):
        table[owner * capacity + rank] = slot
    outside = outside_image(slots, owners, columns)
    for m in range(MIDDLE):
        masked[m] = jnp.where(outside(m), 0.0, saved[m].astype(F32)).astype(BF16)
    size = wide * capacity
    row, lane = iota((size, FULL), 0), iota((size, FULL), 1)
    picks = []
    for step in range(owners):
        owner = partner("blk", step, permuted)
        target = jnp.full((size, FULL), DEAD, I32)
        for rank in range(capacity):
            target = jnp.where(row % capacity == rank, table[owner * capacity + rank], target)
        at = row // capacity
        picks.append(one_hot((lane == target + at * PER_WORKER) & (at < MIDDLE)))
    pick = jnp.concatenate(picks, axis=0)
    filler = jnp.zeros((FULL - rows, FULL), BF16)
    for m in range(0, MIDDLE, 2):
        pair = jnp.concatenate([masked[m], masked[m + 1]], axis=1)
        moved = dot(pick, jnp.concatenate([pair, filler], axis=0)).astype(BF16)
        for step, out in enumerate(views(outs, owners)):
            part = moved[step * size : (step + 1) * size]
            out[m] = part[:, :HALF]
            out[m + 1] = part[:, HALF:]


def ordered(own, other, axis):
    first = lax.axis_index("ch") == 0
    return jnp.concatenate(
        [jnp.where(first, own, other), jnp.where(first, other, own)], axis=axis
    )


def deal(value, kept, sent, grad, tap):
    low, high = value[: HALF // 2], value[HALF // 2 :]
    mine = lax.axis_index("col") == 0
    keep, send = jnp.where(mine, low, high), jnp.where(mine, high, low).astype(BF16)
    for k in range(4):
        step, rows = partner("blk", k, True), slice(k * ROWS, (k + 1) * ROWS)
        kept[step, grad, tap] = keep[rows]
        sent[step, grad, tap] = send[rows]


def emit(value, outs, grad, tap):
    if len(outs) == 2:
        deal(value, outs[0], outs[1], grad, tap)
    else:
        outs[0][grad, tap] = value


def spread(values, weight, total, places):
    height, extent = values.shape[:2]
    inputs = values[...].reshape(height * extent, FULL)
    width, step = weight.shape[1], places
    for dy in range(3):
        taps = jnp.concatenate([weight[3 * dy + dx] for dx in range(3)], axis=0)
        part = dot_nt(inputs, taps).reshape(height, extent, 3 * width)
        p, q, r = [part[:, :, dx * width : (dx + 1) * width] for dx in range(3)]
        sums = [
            p[:, :step],
            p[:, step : 2 * step] + q[:, :step],
            p[:, 2 * step :] + q[:, step : extent - step] + r[:, : extent - 2 * step],
            q[:, extent - step :] + r[:, extent - 2 * step : extent - step],
            r[:, extent - step :],
        ]
        at = 0
        for value in sums:
            size = value.shape[1]
            here = slice(at, at + size)
            if dy == 0:
                total[:height, here] = value
            else:
                total[dy : dy + height - 1, here] += value[:-1]
                total[dy + height - 1, here] = value[height - 1]
            at += size


def second_gradient(scale, owners, capacity, permuted, routing, *refs):
    parts = 1 if not permuted else owners
    own, other = views(refs[:parts], owners), views(refs[parts : 2 * parts], owners)
    masked, cot = refs[2 * parts : 2 * parts + 2]
    outs, counts = refs[2 * parts + 2 : -1], refs[-1]
    slots = worker_codes(routing, counts, owners)
    rows, inner = BLOCK * PER_WORKER, owners * BLOCK * capacity
    row, lane = iota((rows, inner), 0), iota((rows, inner), 1)
    target = jnp.full((rows, inner), DEAD, I32)
    for slot, (owner, place, rank) in enumerate(slots):
        step = partner("blk", owner, permuted)
        target = jnp.where(row % PER_WORKER == slot, step * (BLOCK * capacity) + rank, target)
    pick = one_hot(lane == target + (row // PER_WORKER) * capacity)
    for u in range(BLOCK):
        got = jnp.concatenate(
            [ordered(own[o][u], other[o][u], 1) for o in range(owners)], axis=0
        )
        cot[u] = dot(pick, got).astype(BF16)
    grads = cot[...].reshape(BLOCK * rows, FULL)
    turned = []
    for dx in range(3):
        window = masked[:, dx * PER_WORKER : (dx + BLOCK) * PER_WORKER].reshape(MIDDLE * rows, HALF)
        turned.append(jnp.maximum(window, jnp.zeros_like(window)).T)
    turned = jnp.concatenate(turned, axis=0)
    for dy in range(3):
        value = dot(turned[:, dy * rows : (dy + BLOCK) * rows], grads) * scale
        for dx in range(3):
            emit(value[dx * HALF : (dx + 1) * HALF], outs, 0, 3 * dy + dx)
    return slots


def first_gradient(
    scale, outside, cot, masked, saved_other, weight, weight_other, saved, *refs
):
    outs, (total, pre, full) = refs[:-3], refs[-3:]
    full[...] = ordered(weight[...], weight_other[...], 1)
    spread(cot, full, total, PER_WORKER)
    for m in range(MIDDLE):
        other = jnp.where(outside(m), 0.0, saved_other[m].astype(F32)).astype(BF16)
        live = ordered(masked[m], other, 1).astype(F32) > 0
        value = jnp.where(live, total[m], 0.0)
        pre[m] = value.astype(BF16).reshape(MIDDLE, PER_WORKER, FULL)
    size = MIDDLE * MIDDLE * PER_WORKER
    grads = pre[...].reshape(size, FULL)
    for dy in range(3):
        windows = [saved[dy : dy + MIDDLE, dx : dx + MIDDLE] for dx in range(3)]
        window = jnp.concatenate([w.reshape(size, HALF) for w in windows], axis=1)
        value = dot_tn(window, grads) * scale
        for dx in range(3):
            emit(value[dx * HALF : (dx + 1) * HALF], outs, 1, 3 * dy + dx)


def owner_spread(tile, tile_other, second, second_other, out, total, cot, full):
    row, lane = iota((FULL, FULL), 0), iota((FULL, FULL), 1)
    turn = one_hot(lane == (row % TILE_BLOCKS) * BLOCK + row // TILE_BLOCKS)
    for u in range(BLOCK):
        block = jnp.concatenate(
            [ordered(tile[r, u], tile_other[r, u], 1) for r in range(TILE_ROWS)], axis=0
        )
        cot[u] = dot(turn, block).astype(BF16)
    full[...] = ordered(second[...], second_other[...], 1)
    spread(cot, full, total, TILE_BLOCKS)
    out[...] = total[...].astype(BF16).reshape(out.shape)


def worker(scale, owners, columns, capacity, permuted, routing, *refs):
    parts = 1 if not permuted else owners
    inputs, refs = refs[: 2 * parts], refs[2 * parts :]
    (masked, saved_other, weight, weight_other, source), refs = refs[:5], refs[5:]
    if permuted:
        refs, sent = refs[:-1], refs[-1]
    outs, (counts, cot, total, pre, full, saved, arrived) = refs[:-7], refs[-7:]
    if permuted:
        kept, near, far = outs
        outs = (kept, sent)
    fetch = pltpu.make_async_copy(source, saved, arrived)
    fetch.start()
    slots = second_gradient(
        scale, owners, capacity, permuted, routing, *inputs, masked, cot, *outs, counts
    )
    fetch.wait()
    first_gradient(
        scale, outside_image(slots, owners, columns), cot, masked, saved_other, weight, weight_other,
        saved, *outs, total, pre, full,
    )
    if permuted:
        near[...] = sent[:2]
        far[...] = sent[2:]


def adjacent(step):
    me = lax.axis_index("blk")
    return (me ^ step) == me - 1, (me ^ step) == me + 1


def owner_canvas(owners, capacity, wide, permuted, routing, *refs):
    parts = 1 if not permuted else owners
    got, got_other = views(refs[:parts], owners), views(refs[parts : 2 * parts], owners)
    total, first, canvas = refs[2 * parts : 2 * parts + 3]
    rims, (table, pre, grown) = refs[2 * parts + 3 : -3], refs[-3:]
    owner_table(routing, table, owners, capacity)
    size, into = wide * capacity, MIDDLE * TILE_BLOCKS
    row, lane = iota((size, into), 0), iota((size, into), 1)
    picks = []
    for step in range(owners):
        worker = partner("blk", step, permuted)
        target = jnp.full((size, into), DEAD, I32)
        for rank in range(capacity):
            target = jnp.where(row % capacity == rank, table[worker * capacity + rank], target)
        at = row // capacity
        hits = (lane == target + at * TILE_BLOCKS) & (at < MIDDLE)
        picks.append(jnp.where(hits, 1.0, 0.0))
    pick = jnp.concatenate(picks, axis=0).T.astype(BF16)
    for m in range(MIDDLE):
        block = jnp.concatenate(
            [ordered(got[w][m], got_other[w][m], 1) for w in range(owners)], axis=0
        )
        value = jnp.where(dot(pick, block) > 0, total[m].reshape(into, FULL).astype(F32), 0.0)
        pre[m] = value.astype(BF16)
    spread(pre, first, grown, TILE_BLOCKS)
    height, depth = TILE_ROWS * WIDE, OUTER * TILE_BLOCKS
    row, lane = iota((height, depth), 0), iota((height, depth), 1)
    at_row, at_col = row // WIDE, row % WIDE
    n, place = lane // TILE_BLOCKS, lane % TILE_BLOCKS
    column = (place % TILE_COLS) * BLOCK + n - 2
    column = jnp.where(column < 0, column + 36, column)
    fold = one_hot((at_row == place // TILE_COLS) & (at_col == column))
    canvas[...] = jnp.zeros_like(canvas)
    for m in range(0, OUTER, 2):
        pair = jnp.concatenate(
            [grown[m + k].astype(BF16) for k in range(2)], axis=1
        )
        laid = dot(fold, pair).reshape(TILE_ROWS, WIDE, FULL)
        for r in range(TILE_ROWS):
            for k in range(2):
                canvas[r * BLOCK + m + k] += laid[r, :, k * HALF : (k + 1) * HALF]
    for k, rim in enumerate(rims):
        above, below = adjacent(2 * k + 1)
        top = jnp.concatenate([canvas[0], canvas[1]], axis=1)
        bottom = jnp.concatenate([canvas[HIGH - 2], canvas[HIGH - 1]], axis=1)
        here = jnp.where(below, bottom, jnp.where(above, top, 0.0))
        rim[...] = jnp.concatenate([here, jnp.zeros((RIM - WIDE, FULL), F32)], axis=0).astype(BF16)


def add_far(kept, got, *sends):
    for k, out in enumerate(sends):
        out[...] = (kept[2 + k] + got[k].astype(F32)).astype(BF16)


def add_near(kept, got, keep, send):
    keep[...] = kept[0] + got[0].astype(F32)
    send[...] = (kept[1] + got[1].astype(F32)).astype(BF16)


def add_workers(kept, got_3, got_2, got_1, rim_1, rim_3, out, out_1, out_3):
    value = kept[...]
    for part in (got_3, got_2, got_1):
        value = value + part[...].astype(F32)
    value = value.astype(BF16).reshape(PART, FULL)
    out[...] = value
    for message, rim in ((out_1, rim_1), (out_3, rim_3)):
        message[:PART] = value
        message[PART:] = rim[...]


def column_message(canvas, got_1, got_3, out, rim, strip):
    out[:PART] = got_3[:PART]
    for j in range(2):
        c = 32 + 2 * lax.axis_index("col") + j
        strip[...] = canvas[pl.ds(2 * WIDE + c, 64, stride=WIDE), :]
        for step, got in ((1, got_1), (3, got_3)):
            rim[...] = got[PART:].astype(F32)
            row = rim[pl.ds(c, 1), :]
            above, below = adjacent(step)
            top, bottom = jnp.where(above, row, 0.0), jnp.where(below, row, 0.0)
            strip[0:1] += top[:, :HALF]
            strip[1:2] += top[:, HALF:]
            strip[62:63] += bottom[:, :HALF]
            strip[63:64] += bottom[:, HALF:]
        out[PART:, j * HALF : (j + 1) * HALF] = strip[...].astype(BF16)


def gather_image(tile, canvas, got_1, got_3, total):
    rows = TILE_ROWS * BLOCK * 32
    total[...] = tile[...].reshape(rows, HALF).astype(F32) + canvas[
        2 : HIGH - 2, :32, :
    ].reshape(rows, HALF)
    for step, got in ((1, got_1), (3, got_3)):
        rim = got[PART : PART + 32].astype(F32)
        above, below = adjacent(step)
        top, bottom = jnp.where(above, rim, 0.0), jnp.where(below, rim, 0.0)
        total[0:32] += top[:, :HALF]
        total[32:64] += top[:, HALF:]
        total[rows - 64 : rows - 32] += bottom[:, :HALF]
        total[rows - 32 : rows] += bottom[:, HALF:]


def rows_at(number):
    column = lax.axis_index("col")
    place = (column if number < 4 else 1 - column) * 4 + partner("blk", number % 4, True)
    return pl.ds(pl.multiple_of(place * ROWS, ROWS), ROWS)


def lay(tile, canvas, *refs):
    parts, (image, slab), outs, total = refs[:-5], refs[-5:-3], refs[-3:-1], refs[-1]
    gather_image(tile, canvas, parts[1], parts[3], total)
    whole = total[...].reshape(image.shape)
    image[...] = whole.astype(BF16)
    slab[...] = jnp.where(lax.axis_index("col") == 0, whole[:, 16:], whole[:, :16])
    for number, part in zip((0, 1, 2, 3, 4, 5, 6), parts):
        value = part[:PART].astype(F32).reshape(2, 9, ROWS, FULL)
        for out, grad in zip(outs, (0, 1)):
            out[:, rows_at(number), :] = value[grad]


def finish(slab, last, old, old_0, old_1, image, out_0, out_1, total, side, laid, sems):
    copies = []
    laid[...] = last[:PART].astype(F32).reshape(2, 9, ROWS, FULL)
    for grad, dest in enumerate((out_0, out_1)):
        copies.append(
            pltpu.make_async_copy(laid.at[grad], dest.at[:, rows_at(7), :], sems.at[grad])
        )
        copies[-1].start()
    rows = TILE_ROWS * BLOCK * 16
    total[:rows] = slab[...].reshape(rows, HALF)
    strip = last[PART:].astype(F32)
    left = lax.axis_index("col") == 0
    at = jnp.where(left, 14, 0)
    for j in range(2):
        spot = (pl.ds(at + j, 64, stride=16), slice(None))
        total[spot] = total[spot] + strip[:, j * HALF : (j + 1) * HALF]
    side[...] = total[:rows].astype(BF16).reshape(side.shape)
    columns = pl.ds(pl.multiple_of(jnp.where(left, 16, 0), 16), 16)
    copies.append(pltpu.make_async_copy(side, image.at[:, columns, :], sems.at[2]))
    copies[-1].start()
    for copy in copies:
        copy.wait()


def swap(value, axis="ch"):
    return lax.ppermute(value, axis, [(0, 1), (1, 0)])


def flip(value, axis, step):
    size = lax.axis_size(axis)
    return lax.ppermute(value, axis, [(i, i ^ step) for i in range(size)])


def neighbours(axis):
    size = lax.axis_size(axis)
    up = [(i, (i + 1) % size) for i in range(size - 1)]
    return up, [(j, i) for i, j in up]


def shards(grad_out, saved_input, saved_pre, first_weight, second_weight, assignment):
    owners = lax.axis_size("blk")
    columns = lax.axis_size("col")
    capacity = max(2, TILE_BLOCKS // owners)
    wide = MIDDLE if (MIDDLE * capacity) % 16 == 0 else 16
    scale = 1.0 / math.sqrt(owners * columns * PER_WORKER * BLOCK * BLOCK)
    permuted = owners == 4 and columns == 2
    parts = owners if permuted else 1
    routing = assignment[0]
    shape = jax.ShapeDtypeStruct
    tables = [pltpu.SMEM((owners * capacity + 1,), I32)]
    counts = [pltpu.SMEM((owners,), I32)]

    def pieces(*dims):
        return [shape(dims, BF16)] * owners if permuted else [shape((owners,) + dims, BF16)]

    def exchange(values):
        if permuted:
            return list(values[:1]) + [flip(values[k], "blk", k) for k in (3, 2, 1)][::-1]
        return [lax.all_to_all(values[0], "blk", split_axis=0, concat_axis=0, tiled=True)]

    tie = lax.optimization_barrier
    tile = grad_out.reshape(TILE_ROWS, BLOCK, TILE_COLS * BLOCK, HALF)
    outgoing = call(
        functools.partial(pack_cotangents, owners, capacity, permuted),
        pieces(BLOCK, BLOCK * capacity, HALF),
        [HBM, HBM],
        [
            pltpu.VMEM((2,) + routing.shape, I32),
            pltpu.VMEM(tile.shape, BF16),
            pltpu.VMEM(routing.shape, I32),
            pltpu.SemaphoreType.DMA((2,)),
        ],
        (1, 1), "pack_cotangents",
    )(*[pltpu.with_memory_space_constraint(value, pltpu.HBM) for value in (routing, tile)])
    saved_slots = saved_pre[0, 0].transpose(1, 2, 0, 3)
    saved_slots = saved_slots.reshape(MIDDLE, MIDDLE * PER_WORKER, HALF)
    second_other, saved_other = swap(second_weight), swap(saved_slots)
    outgoing, saved_here = tie((outgoing, saved_slots))
    incoming = exchange(outgoing)

    second_other, saved_here = tie((second_other, saved_here))
    masked, *to_owners = call(
        functools.partial(pack_saved, owners, columns, capacity, wide, permuted),
        [shape((MIDDLE, MIDDLE * PER_WORKER, HALF), BF16)] + pieces(MIDDLE, wide * capacity, HALF),
        [SMEM, VMEM], counts + tables, (1, 1), "pack_saved",
    )(routing, saved_here)
    incoming_other = [swap(incoming[0])] if permuted else []
    incoming, to_owners, incoming_other = tie((incoming[::-1], to_owners[::-1], incoming_other))
    incoming, to_owners = incoming[::-1], to_owners[::-1]
    incoming_other += [swap(value) for value in incoming[len(incoming_other) :]]
    at_owner = exchange(to_owners)

    saved_tiles = saved_input[0, 0].transpose(1, 2, 0, 3)
    if permuted:
        part = (2, 9, ROWS, FULL)
        halved = [shape((4,) + part, F32)] + [shape((2,) + part, BF16)] * 2
    else:
        halved = [shape((2, 9, HALF, FULL), F32)]
    terms = call(
        functools.partial(worker, scale, owners, columns, capacity, permuted),
        halved,
        [SMEM] + [VMEM] * (2 * parts + 4) + [HBM],
        counts
        + [
            pltpu.VMEM((BLOCK, BLOCK * PER_WORKER, FULL), BF16),
            pltpu.VMEM((MIDDLE, MIDDLE * PER_WORKER, FULL), F32),
            pltpu.VMEM((MIDDLE, MIDDLE, PER_WORKER, FULL), BF16),
            pltpu.VMEM((9, FULL, FULL), BF16),
            pltpu.VMEM(saved_tiles.shape, BF16),
            pltpu.SemaphoreType.DMA,
        ]
        + ([pltpu.VMEM((4,) + part, BF16)] if permuted else []),
        (1, 1), "worker",
    )(
        routing, *incoming, *incoming_other, masked, saved_other, second_weight, second_other,
        pltpu.with_memory_space_constraint(saved_tiles, pltpu.HBM),
    )

    if permuted:
        kept, near, far = terms
        far, at_owner[2], at_owner[1] = tie((far, at_owner[2], at_owner[1]))
        far, tile_mine, tile_here = tie((far, tile, tile))
    else:
        terms, tile_mine, tile_here = tie((terms, tile, tile))
    total = call(
        owner_spread,
        shape((MIDDLE, MIDDLE, TILE_BLOCKS, FULL), BF16),
        [VMEM] * 4,
        [
            pltpu.VMEM((MIDDLE, MIDDLE * TILE_BLOCKS, FULL), F32),
            pltpu.VMEM((BLOCK, BLOCK * TILE_BLOCKS, FULL), BF16),
            pltpu.VMEM((9, FULL, FULL), BF16),
        ],
        (1, 1), "owner_spread",
    )(tile_here, swap(tile_mine), second_weight, second_other)

    def owner(at_owner):
        at_owner_other = [swap(value) for value in at_owner]
        return call(
            functools.partial(owner_canvas, owners, capacity, wide, permuted),
            [shape((HIGH, WIDE, HALF), F32)] + [shape((RIM, FULL), BF16)] * (2 if permuted else 0),
            [SMEM] + [VMEM] * (2 * len(at_owner) + 2),
            tables
            + [
                pltpu.VMEM((MIDDLE, MIDDLE * TILE_BLOCKS, FULL), BF16),
                pltpu.VMEM((OUTER, OUTER * TILE_BLOCKS, HALF), F32),
            ],
            (1, 1), "owner_canvas",
        )(routing, *at_owner, *at_owner_other, total, first_weight)

    if permuted:
        far_got, near_got = swap(far, "col"), swap(near, "col")
        total, far_got = tie((total, far_got))
        sends = call(add_far, [shape(part, BF16)] * 2, [VMEM] * 2, [], (1, 1), "add_far")(
            kept, far_got
        )
        sends, at_owner[3] = tie((sends[::-1], at_owner[3]))
        got = [flip(sends[0], "blk", 3), flip(sends[1], "blk", 2)]
        canvas, *rims = owner(at_owner)
        near_got, canvas = tie((near_got, canvas))
        keep, send = call(
            add_near, [shape(part, F32), shape(part, BF16)], [VMEM] * 2, [], (1, 1), "add_near",
        )(kept, near_got)
        got.append(flip(send, "blk", 1))
        message = shape((PART, FULL), BF16)
        wider = shape((PART + RIM, FULL), BF16)
        own, *wides = call(
            add_workers, [message, wider, wider], [VMEM] * 6, [], (1, 1), "add_workers",
        )(keep, *got, *rims)
        got_2, got_1 = flip(own, "blk", 2), flip(wides[0], "blk", 1)
        across, got_2, wide_3 = tie((swap(own, "col"), got_2, wides[1]))
        got_3 = flip(wide_3, "blk", 3)
        across = [across] + [swap(value, "col") for value in (got_1[:PART], got_2)]
        got_3, got_1, across = tie((got_3, got_1, across))
        got = [got_1, got_2, got_3]
        last = call(
            column_message, shape((PART + 64, FULL), BF16), [VMEM] * 3,
            [pltpu.VMEM((RIM, FULL), F32), pltpu.VMEM((64, HALF), F32)],
            (1, 1), "column_message",
        )(canvas.reshape(HIGH * WIDE, HALF), got[0], got[2])
        last = swap(last, "col")
        slab = (TILE_ROWS * BLOCK, 16, HALF)
        weights = [shape((9, HALF, FULL), F32)] * 2
        early, *outs = call(
            lay, [shape(grad_out.shape, BF16), shape(slab, F32)] + weights, [VMEM] * 9,
            [pltpu.VMEM((TILE_ROWS * BLOCK * 32, HALF), F32)], (1, 1), "lay",
        )(grad_out, canvas, own, *got, *across)
        grad_in, grad_second, grad_first = pl.pallas_call(
            finish,
            out_shape=[shape(grad_out.shape, BF16)] + weights,
            in_specs=[VMEM] * 2 + [HBM] * 3,
            out_specs=[HBM] * 3,
            scratch_shapes=[
                pltpu.VMEM((TILE_ROWS * BLOCK * 16 + 16, HALF), F32),
                pltpu.VMEM(slab, BF16),
                pltpu.VMEM((2, 9, ROWS, FULL), F32),
                pltpu.SemaphoreType.DMA((3,)),
            ],
            input_output_aliases={2: 0, 3: 1, 4: 2},
            compiler_params=pltpu.CompilerParams(vmem_limit_bytes=48 * 1024 * 1024),
            cost_estimate=pl.CostEstimate(flops=1, bytes_accessed=1, transcendentals=0),
            name="finish",
        )(outs[0], last, early, *outs[1:])
        return (grad_in, grad_first, grad_second)

    grad_first, grad_second = lax.psum((terms[0][1], terms[0][0]), ("blk", "col"))
    [canvas] = owner(at_owner)
    up, down = neighbours("blk")
    from_above = lax.ppermute(canvas[HIGH - 2 :].astype(BF16), "blk", up).astype(F32)
    from_below = lax.ppermute(canvas[:2].astype(BF16), "blk", down).astype(F32)
    inner = canvas[2 : HIGH - 2]
    inner = inner.at[:2].add(from_above).at[-2:].add(from_below)
    up, down = neighbours("col")
    from_left = lax.ppermute(inner[:, 32:34].astype(BF16), "col", up).astype(F32)
    from_right = lax.ppermute(inner[:, 34:36].astype(BF16), "col", down).astype(F32)
    inner = inner[:, :32].at[:, :2].add(from_left).at[:, -2:].add(from_right)
    grad_in = (grad_out.astype(F32) + inner).astype(BF16)
    return (grad_in, grad_first, grad_second)


def solution(mesh):
    return jax.shard_map(
        shards,
        mesh=mesh,
        in_specs=(
            P(("groups", "blk"), "col", "ch"),
            P(("groups", "col"), "blk", None, None, None, "ch"),
            P(("groups", "col"), "blk", None, None, None, "ch"),
            P(None, "ch", None),
            P(None, "ch", None),
            P(("groups", "col"), None, None),
        ),
        out_specs=(
            P(("groups", "blk"), "col", "ch"),
            P("groups", "ch", None),
            P("groups", "ch", None),
        ),
        check_vma=False,
    )
```

```python
import functools
import math

import jax
import jax.numpy as jnp
from jax import lax
from jax.experimental import pallas as pl
from jax.experimental.pallas import tpu as pltpu
from jax.sharding import PartitionSpec as P

BLOCK = 8
TILE_ROWS = 8
TILE_COLS = 4
TILE_BLOCKS = 32
PER_WORKER = 16
MIDDLE = 10
OUTER = 12
HALF = 128
FULL = 256
DEAD = -4096
HIGH = 68
RIM = 48
ROWS = 16
PART = 288
WIDE = 40

BF16 = jnp.bfloat16
F32 = jnp.float32
I32 = jnp.int32

VMEM = pl.BlockSpec(memory_space=pltpu.VMEM)
HBM = pl.BlockSpec(memory_space=pltpu.HBM)
SMEM = pl.BlockSpec(memory_space=pltpu.SMEM)


def call(body, outs, specs, scratch, cost, name):
    return pl.pallas_call(
        body,
        out_shape=outs,
        in_specs=specs,
        out_specs=jax.tree.map(lambda _: VMEM, outs),
        scratch_shapes=scratch,
        compiler_params=pltpu.CompilerParams(vmem_limit_bytes=48 * 1024 * 1024),
        cost_estimate=pl.CostEstimate(flops=cost[0], bytes_accessed=cost[1], transcendentals=0),
        name=name,
    )


def iota(shape, dim):
    return lax.broadcasted_iota(I32, shape, dim)


def one_hot(hits):
    return jnp.where(hits, 1.0, 0.0).astype(BF16)


def dot(a, b):
    return jnp.dot(a, b, preferred_element_type=F32)


def dot_nt(a, b):
    return lax.dot_general(a, b, (((1,), (1,)), ((), ())), preferred_element_type=F32)


def dot_tn(a, b):
    return lax.dot_general(a, b, (((0,), (0,)), ((), ())), preferred_element_type=F32)


def owner_table(routing, table, owners, capacity):
    me = lax.axis_index("blk")

    def clear(number, carry):
        table[number] = DEAD
        return carry

    lax.fori_loop(0, owners * capacity, clear, 0)

    def worker(number, carry):
        count = jnp.int32(0)
        for slot in range(PER_WORKER):
            code = routing[number, slot]
            hit = (code // TILE_BLOCKS) == me
            table[jnp.where(hit, number * capacity + count, owners * capacity)] = code % TILE_BLOCKS
            count = count + jnp.where(hit, 1, 0)
        return carry

    lax.fori_loop(0, owners, worker, 0)


def worker_codes(routing, counts, owners):
    me = lax.axis_index("blk")

    def clear(number, carry):
        counts[number] = 0
        return carry

    lax.fori_loop(0, owners, clear, 0)
    slots = []
    for slot in range(PER_WORKER):
        code = routing[me, slot]
        owner = code // TILE_BLOCKS
        rank = counts[owner]
        counts[owner] = rank + 1
        slots.append((owner, code % TILE_BLOCKS, rank))
    return slots


def views(refs, count):
    return list(refs) if len(refs) == count else [refs[0].at[k] for k in range(count)]


def partner(axis, step, permuted):
    return step ^ lax.axis_index(axis) if permuted else step


def pack_cotangents(owners, capacity, permuted, listed, source, *refs):
    outs, (places, tile, codes, arrived) = refs[:-4], refs[-4:]
    fetch = pltpu.make_async_copy(source, tile, arrived.at[0])
    fetch.start()
    lists = pltpu.make_async_copy(listed, codes, arrived.at[1])
    lists.start()
    lists.wait()
    hit = (codes[...] // TILE_BLOCKS) == lax.axis_index("blk")
    places[0] = jnp.where(hit, codes[...] % TILE_BLOCKS + 1, 0)
    before = (iota((PER_WORKER, PER_WORKER), 0) < iota((PER_WORKER, PER_WORKER), 1))
    places[1] = dot(one_hot(hit), one_hot(before)).astype(I32)
    rows = BLOCK * capacity
    row, lane = iota((rows, FULL), 0), iota((rows, FULL), 1)
    picks = []
    for step in range(owners):
        at = pl.ds(partner("blk", step, permuted), 1)
        same = places[1, at, :] == iota((rows, PER_WORKER), 0) % capacity
        place = jnp.sum(jnp.where(same, places[0, at, :], 0).astype(F32), axis=1, keepdims=True)
        target = (place.astype(I32) - 1) * BLOCK
        picks.append(one_hot(lane == target + row // capacity))
    pick = jnp.concatenate(picks, axis=0)
    fetch.wait()
    for u in range(0, BLOCK, 2):
        pair = [
            jnp.concatenate([tile[r, u + k] for r in range(TILE_ROWS)], axis=0) for k in range(2)
        ]
        moved = dot(pick, jnp.concatenate(pair, axis=1)).astype(BF16)
        for step, out in enumerate(views(outs, owners)):
            part = moved[step * rows : (step + 1) * rows]
            out[u] = part[:, :HALF]
            out[u + 1] = part[:, HALF:]


def outside_image(slots, owners, columns):
    column = lax.axis_index("col")
    row = iota((MIDDLE * PER_WORKER, HALF), 0)
    flags = jnp.zeros_like(row)
    for slot, (owner, place, rank) in enumerate(slots):
        block_row, block_col = place // TILE_COLS, place % TILE_COLS
        flag = (
            jnp.where((owner == 0) & (block_row == 0), 1, 0)
            + jnp.where((owner == owners - 1) & (block_row == TILE_ROWS - 1), 2, 0)
            + jnp.where((column == 0) & (block_col == 0), 4, 0)
            + jnp.where((column == columns - 1) & (block_col == TILE_COLS - 1), 8, 0)
        )
        flags = jnp.where(row % PER_WORKER == slot, flag, flags)
    across = row // PER_WORKER
    sides = (((flags & 4) != 0) & (across == 0)) | (((flags & 8) != 0) & (across == MIDDLE - 1))

    def here(m):
        if m == 0:
            return sides | ((flags & 1) != 0)
        if m == MIDDLE - 1:
            return sides | ((flags & 2) != 0)
        return sides

    return here


def pack_saved(owners, columns, capacity, wide, permuted, routing, saved, masked, *refs):
    outs, counts, table = refs[:-2], refs[-2], refs[-1]

    def clear(number, carry):
        table[number] = DEAD
        return carry

    lax.fori_loop(0, owners * capacity, clear, 0)
    slots = worker_codes(routing, counts, owners)
    rows = MIDDLE * PER_WORKER
    for slot, (owner, place, rank) in enumerate(slots):
        table[owner * capacity + rank] = slot
    outside = outside_image(slots, owners, columns)
    for m in range(MIDDLE):
        masked[m] = jnp.where(outside(m), 0.0, saved[m].astype(F32)).astype(BF16)
    size = wide * capacity
    row, lane = iota((size, FULL), 0), iota((size, FULL), 1)
    picks = []
    for step in range(owners):
        owner = partner("blk", step, permuted)
        target = jnp.full((size, FULL), DEAD, I32)
        for rank in range(capacity):
            target = jnp.where(row % capacity == rank, table[owner * capacity + rank], target)
        at = row // capacity
        picks.append(one_hot((lane == target + at * PER_WORKER) & (at < MIDDLE)))
    pick = jnp.concatenate(picks, axis=0)
    filler = jnp.zeros((FULL - rows, FULL), BF16)
    for m in range(0, MIDDLE, 2):
        pair = jnp.concatenate([masked[m], masked[m + 1]], axis=1)
        moved = dot(pick, jnp.concatenate([pair, filler], axis=0)).astype(BF16)
        for step, out in enumerate(views(outs, owners)):
            part = moved[step * size : (step + 1) * size]
            out[m] = part[:, :HALF]
            out[m + 1] = part[:, HALF:]


def ordered(own, other, axis):
    first = lax.axis_index("ch") == 0
    return jnp.concatenate(
        [jnp.where(first, own, other), jnp.where(first, other, own)], axis=axis
    )


def deal(value, kept, sent, grad, tap):
    low, high = value[: HALF // 2], value[HALF // 2 :]
    mine = lax.axis_index("col") == 0
    keep, send = jnp.where(mine, low, high), jnp.where(mine, high, low).astype(BF16)
    for k in range(4):
        step, rows = partner("blk", k, True), slice(k * ROWS, (k + 1) * ROWS)
        kept[step, grad, tap] = keep[rows]
        sent[step, grad, tap] = send[rows]


def emit(value, outs, grad, tap):
    if len(outs) == 2:
        deal(value, outs[0], outs[1], grad, tap)
    else:
        outs[0][grad, tap] = value


def spread(values, weight, total, places):
    height, extent = values.shape[:2]
    inputs = values[...].reshape(height * extent, FULL)
    width, step = weight.shape[1], places
    for dy in range(3):
        taps = jnp.concatenate([weight[3 * dy + dx] for dx in range(3)], axis=0)
        part = dot_nt(inputs, taps).reshape(height, extent, 3 * width)
        p, q, r = [part[:, :, dx * width : (dx + 1) * width] for dx in range(3)]
        sums = [
            p[:, :step],
            p[:, step : 2 * step] + q[:, :step],
            p[:, 2 * step :] + q[:, step : extent - step] + r[:, : extent - 2 * step],
            q[:, extent - step :] + r[:, extent - 2 * step : extent - step],
            r[:, extent - step :],
        ]
        at = 0
        for value in sums:
            size = value.shape[1]
            here = slice(at, at + size)
            if dy == 0:
                total[:height, here] = value
            else:
                total[dy : dy + height - 1, here] += value[:-1]
                total[dy + height - 1, here] = value[height - 1]
            at += size


def second_gradient(scale, owners, capacity, permuted, routing, *refs):
    parts = 1 if not permuted else owners
    own, other = views(refs[:parts], owners), views(refs[parts : 2 * parts], owners)
    masked, cot = refs[2 * parts : 2 * parts + 2]
    outs, counts = refs[2 * parts + 2 : -1], refs[-1]
    slots = worker_codes(routing, counts, owners)
    rows, inner = BLOCK * PER_WORKER, owners * BLOCK * capacity
    row, lane = iota((rows, inner), 0), iota((rows, inner), 1)
    target = jnp.full((rows, inner), DEAD, I32)
    for slot, (owner, place, rank) in enumerate(slots):
        step = partner("blk", owner, permuted)
        target = jnp.where(row % PER_WORKER == slot, step * (BLOCK * capacity) + rank, target)
    pick = one_hot(lane == target + (row // PER_WORKER) * capacity)
    for u in range(BLOCK):
        got = jnp.concatenate(
            [ordered(own[o][u], other[o][u], 1) for o in range(owners)], axis=0
        )
        cot[u] = dot(pick, got).astype(BF16)
    grads = cot[...].reshape(BLOCK * rows, FULL)
    turned = []
    for dx in range(3):
        window = masked[:, dx * PER_WORKER : (dx + BLOCK) * PER_WORKER].reshape(MIDDLE * rows, HALF)
        turned.append(jnp.maximum(window, jnp.zeros_like(window)).T)
    turned = jnp.concatenate(turned, axis=0)
    for dy in range(3):
        value = dot(turned[:, dy * rows : (dy + BLOCK) * rows], grads) * scale
        for dx in range(3):
            emit(value[dx * HALF : (dx + 1) * HALF], outs, 0, 3 * dy + dx)
    return slots


def first_gradient(
    scale, outside, cot, masked, saved_other, weight, weight_other, saved, *refs
):
    outs, (total, pre, full) = refs[:-3], refs[-3:]
    full[...] = ordered(weight[...], weight_other[...], 1)
    spread(cot, full, total, PER_WORKER)
    for m in range(MIDDLE):
        other = jnp.where(outside(m), 0.0, saved_other[m].astype(F32)).astype(BF16)
        live = ordered(masked[m], other, 1).astype(F32) > 0
        value = jnp.where(live, total[m], 0.0)
        pre[m] = value.astype(BF16).reshape(MIDDLE, PER_WORKER, FULL)
    size = MIDDLE * MIDDLE * PER_WORKER
    grads = pre[...].reshape(size, FULL)
    for dy in range(3):
        windows = [saved[dy : dy + MIDDLE, dx : dx + MIDDLE] for dx in range(3)]
        window = jnp.concatenate([w.reshape(size, HALF) for w in windows], axis=1)
        value = dot_tn(window, grads) * scale
        for dx in range(3):
            emit(value[dx * HALF : (dx + 1) * HALF], outs, 1, 3 * dy + dx)


def owner_spread(tile, tile_other, second, second_other, out, total, cot, full):
    row, lane = iota((FULL, FULL), 0), iota((FULL, FULL), 1)
    turn = one_hot(lane == (row % TILE_BLOCKS) * BLOCK + row // TILE_BLOCKS)
    for u in range(BLOCK):
        block = jnp.concatenate(
            [ordered(tile[r, u], tile_other[r, u], 1) for r in range(TILE_ROWS)], axis=0
        )
        cot[u] = dot(turn, block).astype(BF16)
    full[...] = ordered(second[...], second_other[...], 1)
    spread(cot, full, total, TILE_BLOCKS)
    out[...] = total[...].astype(BF16).reshape(out.shape)


def worker(scale, owners, columns, capacity, permuted, routing, *refs):
    parts = 1 if not permuted else owners
    inputs, refs = refs[: 2 * parts], refs[2 * parts :]
    (masked, saved_other, weight, weight_other, source), refs = refs[:5], refs[5:]
    if permuted:
        refs, sent = refs[:-1], refs[-1]
    outs, (counts, cot, total, pre, full, saved, arrived) = refs[:-7], refs[-7:]
    if permuted:
        kept, near, far = outs
        outs = (kept, sent)
    fetch = pltpu.make_async_copy(source, saved, arrived)
    fetch.start()
    slots = second_gradient(
        scale, owners, capacity, permuted, routing, *inputs, masked, cot, *outs, counts
    )
    fetch.wait()
    first_gradient(
        scale, outside_image(slots, owners, columns), cot, masked, saved_other, weight, weight_other,
        saved, *outs, total, pre, full,
    )
    if permuted:
        near[...] = sent[:2]
        far[...] = sent[2:]


def adjacent(step):
    me = lax.axis_index("blk")
    return (me ^ step) == me - 1, (me ^ step) == me + 1


def owner_canvas(owners, capacity, wide, permuted, routing, *refs):
    parts = 1 if not permuted else owners
    got, got_other = views(refs[:parts], owners), views(refs[parts : 2 * parts], owners)
    total, first, canvas = refs[2 * parts : 2 * parts + 3]
    rims, (table, pre, grown) = refs[2 * parts + 3 : -3], refs[-3:]
    owner_table(routing, table, owners, capacity)
    size, into = wide * capacity, MIDDLE * TILE_BLOCKS
    row, lane = iota((size, into), 0), iota((size, into), 1)
    picks = []
    for step in range(owners):
        worker = partner("blk", step, permuted)
        target = jnp.full((size, into), DEAD, I32)
        for rank in range(capacity):
            target = jnp.where(row % capacity == rank, table[worker * capacity + rank], target)
        at = row // capacity
        hits = (lane == target + at * TILE_BLOCKS) & (at < MIDDLE)
        picks.append(jnp.where(hits, 1.0, 0.0))
    pick = jnp.concatenate(picks, axis=0).T.astype(BF16)
    for m in range(MIDDLE):
        block = jnp.concatenate(
            [ordered(got[w][m], got_other[w][m], 1) for w in range(owners)], axis=0
        )
        value = jnp.where(dot(pick, block) > 0, total[m].reshape(into, FULL).astype(F32), 0.0)
        pre[m] = value.astype(BF16)
    spread(pre, first, grown, TILE_BLOCKS)
    height, depth = TILE_ROWS * WIDE, OUTER * TILE_BLOCKS
    row, lane = iota((height, depth), 0), iota((height, depth), 1)
    at_row, at_col = row // WIDE, row % WIDE
    n, place = lane // TILE_BLOCKS, lane % TILE_BLOCKS
    column = (place % TILE_COLS) * BLOCK + n - 2
    column = jnp.where(column < 0, column + 36, column)
    fold = one_hot((at_row == place // TILE_COLS) & (at_col == column))
    canvas[...] = jnp.zeros_like(canvas)
    for m in range(0, OUTER, 2):
        pair = jnp.concatenate(
            [grown[m + k].astype(BF16) for k in range(2)], axis=1
        )
        laid = dot(fold, pair).reshape(TILE_ROWS, WIDE, FULL)
        for r in range(TILE_ROWS):
            for k in range(2):
                canvas[r * BLOCK + m + k] += laid[r, :, k * HALF : (k + 1) * HALF]
    for k, rim in enumerate(rims):
        above, below = adjacent(2 * k + 1)
        top = jnp.concatenate([canvas[0], canvas[1]], axis=1)
        bottom = jnp.concatenate([canvas[HIGH - 2], canvas[HIGH - 1]], axis=1)
        here = jnp.where(below, bottom, jnp.where(above, top, 0.0))
        rim[...] = jnp.concatenate([here, jnp.zeros((RIM - WIDE, FULL), F32)], axis=0).astype(BF16)


def add_far(kept, got, *sends):
    for k, out in enumerate(sends):
        out[...] = (kept[2 + k] + got[k].astype(F32)).astype(BF16)


def add_near(kept, got, keep, send):
    keep[...] = kept[0] + got[0].astype(F32)
    send[...] = (kept[1] + got[1].astype(F32)).astype(BF16)


def add_workers(kept, got_3, got_2, got_1, rim_1, rim_3, out, out_1, out_3):
    value = kept[...]
    for part in (got_3, got_2, got_1):
        value = value + part[...].astype(F32)
    value = value.astype(BF16).reshape(PART, FULL)
    out[...] = value
    for message, rim in ((out_1, rim_1), (out_3, rim_3)):
        message[:PART] = value
        message[PART:] = rim[...]


def column_message(canvas, got_1, got_3, out, rim, strip):
    out[:PART] = got_3[:PART]
    for j in range(2):
        c = 32 + 2 * lax.axis_index("col") + j
        strip[...] = canvas[pl.ds(2 * WIDE + c, 64, stride=WIDE), :]
        for step, got in ((1, got_1), (3, got_3)):
            rim[...] = got[PART:].astype(F32)
            row = rim[pl.ds(c, 1), :]
            above, below = adjacent(step)
            top, bottom = jnp.where(above, row, 0.0), jnp.where(below, row, 0.0)
            strip[0:1] += top[:, :HALF]
            strip[1:2] += top[:, HALF:]
            strip[62:63] += bottom[:, :HALF]
            strip[63:64] += bottom[:, HALF:]
        out[PART:, j * HALF : (j + 1) * HALF] = strip[...].astype(BF16)


def gather_image(tile, canvas, got_1, got_3, total):
    rows = TILE_ROWS * BLOCK * 32
    total[...] = tile[...].reshape(rows, HALF).astype(F32) + canvas[
        2 : HIGH - 2, :32, :
    ].reshape(rows, HALF)
    for step, got in ((1, got_1), (3, got_3)):
        rim = got[PART : PART + 32].astype(F32)
        above, below = adjacent(step)
        top, bottom = jnp.where(above, rim, 0.0), jnp.where(below, rim, 0.0)
        total[0:32] += top[:, :HALF]
        total[32:64] += top[:, HALF:]
        total[rows - 64 : rows - 32] += bottom[:, :HALF]
        total[rows - 32 : rows] += bottom[:, HALF:]


def rows_at(number):
    column = lax.axis_index("col")
    place = (column if number < 4 else 1 - column) * 4 + partner("blk", number % 4, True)
    return pl.ds(pl.multiple_of(place * ROWS, ROWS), ROWS)


def lay(tile, canvas, *refs):
    parts, (image, slab), outs, total = refs[:-5], refs[-5:-3], refs[-3:-1], refs[-1]
    gather_image(tile, canvas, parts[1], parts[3], total)
    whole = total[...].reshape(image.shape)
    image[...] = whole.astype(BF16)
    slab[...] = jnp.where(lax.axis_index("col") == 0, whole[:, 16:], whole[:, :16])
    for number, part in zip((0, 1, 2, 3, 4, 5, 6), parts):
        value = part[:PART].astype(F32).reshape(2, 9, ROWS, FULL)
        for out, grad in zip(outs, (0, 1)):
            out[:, rows_at(number), :] = value[grad]


def finish(slab, last, old, old_0, old_1, image, out_0, out_1, total, side, laid, sems):
    copies = []
    laid[...] = last[:PART].astype(F32).reshape(2, 9, ROWS, FULL)
    for grad, dest in enumerate((out_0, out_1)):
        copies.append(
            pltpu.make_async_copy(laid.at[grad], dest.at[:, rows_at(7), :], sems.at[grad])
        )
        copies[-1].start()
    rows = TILE_ROWS * BLOCK * 16
    total[:rows] = slab[...].reshape(rows, HALF)
    strip = last[PART:].astype(F32)
    left = lax.axis_index("col") == 0
    at = jnp.where(left, 14, 0)
    for j in range(2):
        spot = (pl.ds(at + j, 64, stride=16), slice(None))
        total[spot] = total[spot] + strip[:, j * HALF : (j + 1) * HALF]
    side[...] = total[:rows].astype(BF16).reshape(side.shape)
    columns = pl.ds(pl.multiple_of(jnp.where(left, 16, 0), 16), 16)
    copies.append(pltpu.make_async_copy(side, image.at[:, columns, :], sems.at[2]))
    copies[-1].start()
    for copy in copies:
        copy.wait()


def swap(value, axis="ch"):
    return lax.ppermute(value, axis, [(0, 1), (1, 0)])


def flip(value, axis, step):
    size = lax.axis_size(axis)
    return lax.ppermute(value, axis, [(i, i ^ step) for i in range(size)])


def neighbours(axis):
    size = lax.axis_size(axis)
    up = [(i, (i + 1) % size) for i in range(size - 1)]
    return up, [(j, i) for i, j in up]


def shards(grad_out, saved_input, saved_pre, first_weight, second_weight, assignment):
    owners = lax.axis_size("blk")
    columns = lax.axis_size("col")
    capacity = max(2, TILE_BLOCKS // owners)
    wide = MIDDLE if (MIDDLE * capacity) % 16 == 0 else 16
    scale = 1.0 / math.sqrt(owners * columns * PER_WORKER * BLOCK * BLOCK)
    permuted = owners == 4 and columns == 2
    parts = owners if permuted else 1
    routing = assignment[0]
    shape = jax.ShapeDtypeStruct
    tables = [pltpu.SMEM((owners * capacity + 1,), I32)]
    counts = [pltpu.SMEM((owners,), I32)]

    def pieces(*dims):
        return [shape(dims, BF16)] * owners if permuted else [shape((owners,) + dims, BF16)]

    def exchange(values):
        if permuted:
            return list(values[:1]) + [flip(values[k], "blk", k) for k in (3, 2, 1)][::-1]
        return [lax.all_to_all(values[0], "blk", split_axis=0, concat_axis=0, tiled=True)]

    tie = lax.optimization_barrier
    tile = grad_out.reshape(TILE_ROWS, BLOCK, TILE_COLS * BLOCK, HALF)
    outgoing = call(
        functools.partial(pack_cotangents, owners, capacity, permuted),
        pieces(BLOCK, BLOCK * capacity, HALF),
        [HBM, HBM],
        [
            pltpu.VMEM((2,) + routing.shape, I32),
            pltpu.VMEM(tile.shape, BF16),
            pltpu.VMEM(routing.shape, I32),
            pltpu.SemaphoreType.DMA((2,)),
        ],
        (1, 1), "pack_cotangents",
    )(*[pltpu.with_memory_space_constraint(value, pltpu.HBM) for value in (routing, tile)])
    saved_slots = saved_pre[0, 0].transpose(1, 2, 0, 3)
    saved_slots = saved_slots.reshape(MIDDLE, MIDDLE * PER_WORKER, HALF)
    second_other, saved_other = swap(second_weight), swap(saved_slots)
    outgoing, saved_here = tie((outgoing, saved_slots))
    incoming = exchange(outgoing)

    second_other, saved_here = tie((second_other, saved_here))
    masked, *to_owners = call(
        functools.partial(pack_saved, owners, columns, capacity, wide, permuted),
        [shape((MIDDLE, MIDDLE * PER_WORKER, HALF), BF16)] + pieces(MIDDLE, wide * capacity, HALF),
        [SMEM, VMEM], counts + tables, (1, 1), "pack_saved",
    )(routing, saved_here)
    incoming_other = [swap(incoming[0])] if permuted else []
    incoming, to_owners, incoming_other = tie((incoming[::-1], to_owners[::-1], incoming_other))
    incoming, to_owners = incoming[::-1], to_owners[::-1]
    incoming_other += [swap(value) for value in incoming[len(incoming_other) :]]
    at_owner = exchange(to_owners)

    saved_tiles = saved_input[0, 0].transpose(1, 2, 0, 3)
    if permuted:
        part = (2, 9, ROWS, FULL)
        halved = [shape((4,) + part, F32)] + [shape((2,) + part, BF16)] * 2
    else:
        halved = [shape((2, 9, HALF, FULL), F32)]
    terms = call(
        functools.partial(worker, scale, owners, columns, capacity, permuted),
        halved,
        [SMEM] + [VMEM] * (2 * parts + 4) + [HBM],
        counts
        + [
            pltpu.VMEM((BLOCK, BLOCK * PER_WORKER, FULL), BF16),
            pltpu.VMEM((MIDDLE, MIDDLE * PER_WORKER, FULL), F32),
            pltpu.VMEM((MIDDLE, MIDDLE, PER_WORKER, FULL), BF16),
            pltpu.VMEM((9, FULL, FULL), BF16),
            pltpu.VMEM(saved_tiles.shape, BF16),
            pltpu.SemaphoreType.DMA,
        ]
        + ([pltpu.VMEM((4,) + part, BF16)] if permuted else []),
        (1, 1), "worker",
    )(
        routing, *incoming, *incoming_other, masked, saved_other, second_weight, second_other,
        pltpu.with_memory_space_constraint(saved_tiles, pltpu.HBM),
    )

    if permuted:
        kept, near, far = terms
        far, at_owner[1], at_owner[2] = tie((far, at_owner[1], at_owner[2]))
        far, tile_mine, tile_here = tie((far, tile, tile))
    else:
        terms, tile_mine, tile_here = tie((terms, tile, tile))
    total = call(
        owner_spread,
        shape((MIDDLE, MIDDLE, TILE_BLOCKS, FULL), BF16),
        [VMEM] * 4,
        [
            pltpu.VMEM((MIDDLE, MIDDLE * TILE_BLOCKS, FULL), F32),
            pltpu.VMEM((BLOCK, BLOCK * TILE_BLOCKS, FULL), BF16),
            pltpu.VMEM((9, FULL, FULL), BF16),
        ],
        (1, 1), "owner_spread",
    )(tile_here, swap(tile_mine), second_weight, second_other)

    def owner(at_owner):
        at_owner_other = [swap(value) for value in at_owner]
        return call(
            functools.partial(owner_canvas, owners, capacity, wide, permuted),
            [shape((HIGH, WIDE, HALF), F32)] + [shape((RIM, FULL), BF16)] * (2 if permuted else 0),
            [SMEM] + [VMEM] * (2 * len(at_owner) + 2),
            tables
            + [
                pltpu.VMEM((MIDDLE, MIDDLE * TILE_BLOCKS, FULL), BF16),
                pltpu.VMEM((OUTER, OUTER * TILE_BLOCKS, HALF), F32),
            ],
            (1, 1), "owner_canvas",
        )(routing, *at_owner, *at_owner_other, total, first_weight)

    if permuted:
        far_got, near_got = swap(far, "col"), swap(near, "col")
        total, far_got = tie((total, far_got))
        sends = call(add_far, [shape(part, BF16)] * 2, [VMEM] * 2, [], (1, 1), "add_far")(
            kept, far_got
        )
        sends, at_owner[3] = tie((sends[::-1], at_owner[3]))
        got = [flip(sends[0], "blk", 3), flip(sends[1], "blk", 2)]
        canvas, *rims = owner(at_owner)
        near_got, canvas = tie((near_got, canvas))
        keep, send = call(
            add_near, [shape(part, F32), shape(part, BF16)], [VMEM] * 2, [], (1, 1), "add_near",
        )(kept, near_got)
        got.append(flip(send, "blk", 1))
        message = shape((PART, FULL), BF16)
        wider = shape((PART + RIM, FULL), BF16)
        own, *wides = call(
            add_workers, [message, wider, wider], [VMEM] * 6, [], (1, 1), "add_workers",
        )(keep, *got, *rims)
        got_2, got_1 = flip(own, "blk", 2), flip(wides[0], "blk", 1)
        across, got_2, wide_3 = tie((swap(own, "col"), got_2, wides[1]))
        got_3 = flip(wide_3, "blk", 3)
        across = [across] + [swap(value, "col") for value in (got_1[:PART], got_2)]
        got_3, got_1, across = tie((got_3, got_1, across))
        got = [got_1, got_2, got_3]
        last = call(
            column_message, shape((PART + 64, FULL), BF16), [VMEM] * 3,
            [pltpu.VMEM((RIM, FULL), F32), pltpu.VMEM((64, HALF), F32)],
            (1, 1), "column_message",
        )(canvas.reshape(HIGH * WIDE, HALF), got[0], got[2])
        last = swap(last, "col")
        slab = (TILE_ROWS * BLOCK, 16, HALF)
        weights = [shape((9, HALF, FULL), F32)] * 2
        early, *outs = call(
            lay, [shape(grad_out.shape, BF16), shape(slab, F32)] + weights, [VMEM] * 9,
            [pltpu.VMEM((TILE_ROWS * BLOCK * 32, HALF), F32)], (1, 1), "lay",
        )(grad_out, canvas, own, *got, *across)
        grad_in, grad_second, grad_first = pl.pallas_call(
            finish,
            out_shape=[shape(grad_out.shape, BF16)] + weights,
            in_specs=[VMEM] * 2 + [HBM] * 3,
            out_specs=[HBM] * 3,
            scratch_shapes=[
                pltpu.VMEM((TILE_ROWS * BLOCK * 16 + 16, HALF), F32),
                pltpu.VMEM(slab, BF16),
                pltpu.VMEM((2, 9, ROWS, FULL), F32),
                pltpu.SemaphoreType.DMA((3,)),
            ],
            input_output_aliases={2: 0, 3: 1, 4: 2},
            compiler_params=pltpu.CompilerParams(vmem_limit_bytes=48 * 1024 * 1024),
            cost_estimate=pl.CostEstimate(flops=1, bytes_accessed=1, transcendentals=0),
            name="finish",
        )(outs[0], last, early, *outs[1:])
        return (grad_in, grad_first, grad_second)

    grad_first, grad_second = lax.psum((terms[0][1], terms[0][0]), ("blk", "col"))
    [canvas] = owner(at_owner)
    up, down = neighbours("blk")
    from_above = lax.ppermute(canvas[HIGH - 2 :].astype(BF16), "blk", up).astype(F32)
    from_below = lax.ppermute(canvas[:2].astype(BF16), "blk", down).astype(F32)
    inner = canvas[2 : HIGH - 2]
    inner = inner.at[:2].add(from_above).at[-2:].add(from_below)
    up, down = neighbours("col")
    from_left = lax.ppermute(inner[:, 32:34].astype(BF16), "col", up).astype(F32)
    from_right = lax.ppermute(inner[:, 34:36].astype(BF16), "col", down).astype(F32)
    inner = inner[:, :32].at[:, :2].add(from_left).at[:, -2:].add(from_right)
    grad_in = (grad_out.astype(F32) + inner).astype(BF16)
    return (grad_in, grad_first, grad_second)


def solution(mesh):
    return jax.shard_map(
        shards,
        mesh=mesh,
        in_specs=(
            P(("groups", "blk"), "col", "ch"),
            P(("groups", "col"), "blk", None, None, None, "ch"),
            P(("groups", "col"), "blk", None, None, None, "ch"),
            P(None, "ch", None),
            P(None, "ch", None),
            P(("groups", "col"), None, None),
        ),
        out_specs=(
            P(("groups", "blk"), "col", "ch"),
            P("groups", "ch", None),
            P("groups", "ch", None),
        ),
        check_vma=False,
    )
```

```python
import functools
import math

import jax
import jax.numpy as jnp
from jax import lax
from jax.experimental import pallas as pl
from jax.experimental.pallas import tpu as pltpu
from jax.sharding import PartitionSpec as P

BLOCK = 8
TILE_ROWS = 8
TILE_COLS = 4
TILE_BLOCKS = 32
PER_WORKER = 16
MIDDLE = 10
OUTER = 12
HALF = 128
FULL = 256
DEAD = -4096
HIGH = 68
RIM = 48
ROWS = 16
PART = 288
WIDE = 40

BF16 = jnp.bfloat16
F32 = jnp.float32
I32 = jnp.int32

VMEM = pl.BlockSpec(memory_space=pltpu.VMEM)
HBM = pl.BlockSpec(memory_space=pltpu.HBM)
SMEM = pl.BlockSpec(memory_space=pltpu.SMEM)


def call(body, outs, specs, scratch, cost, name):
    return pl.pallas_call(
        body,
        out_shape=outs,
        in_specs=specs,
        out_specs=jax.tree.map(lambda _: VMEM, outs),
        scratch_shapes=scratch,
        compiler_params=pltpu.CompilerParams(vmem_limit_bytes=48 * 1024 * 1024),
        cost_estimate=pl.CostEstimate(flops=cost[0], bytes_accessed=cost[1], transcendentals=0),
        name=name,
    )


def iota(shape, dim):
    return lax.broadcasted_iota(I32, shape, dim)


def one_hot(hits):
    return jnp.where(hits, 1.0, 0.0).astype(BF16)


def dot(a, b):
    return jnp.dot(a, b, preferred_element_type=F32)


def dot_nt(a, b):
    return lax.dot_general(a, b, (((1,), (1,)), ((), ())), preferred_element_type=F32)


def dot_tn(a, b):
    return lax.dot_general(a, b, (((0,), (0,)), ((), ())), preferred_element_type=F32)


def owner_table(routing, table, owners, capacity):
    me = lax.axis_index("blk")

    def clear(number, carry):
        table[number] = DEAD
        return carry

    lax.fori_loop(0, owners * capacity, clear, 0)

    def worker(number, carry):
        count = jnp.int32(0)
        for slot in range(PER_WORKER):
            code = routing[number, slot]
            hit = (code // TILE_BLOCKS) == me
            table[jnp.where(hit, number * capacity + count, owners * capacity)] = code % TILE_BLOCKS
            count = count + jnp.where(hit, 1, 0)
        return carry

    lax.fori_loop(0, owners, worker, 0)


def worker_codes(routing, counts, owners):
    me = lax.axis_index("blk")

    def clear(number, carry):
        counts[number] = 0
        return carry

    lax.fori_loop(0, owners, clear, 0)
    slots = []
    for slot in range(PER_WORKER):
        code = routing[me, slot]
        owner = code // TILE_BLOCKS
        rank = counts[owner]
        counts[owner] = rank + 1
        slots.append((owner, code % TILE_BLOCKS, rank))
    return slots


def views(refs, count):
    return list(refs) if len(refs) == count else [refs[0].at[k] for k in range(count)]


def partner(axis, step, permuted):
    return step ^ lax.axis_index(axis) if permuted else step


def pack_cotangents(owners, capacity, permuted, listed, source, *refs):
    outs, (places, tile, codes, arrived) = refs[:-4], refs[-4:]
    fetch = pltpu.make_async_copy(source, tile, arrived.at[0])
    fetch.start()
    lists = pltpu.make_async_copy(listed, codes, arrived.at[1])
    lists.start()
    lists.wait()
    hit = (codes[...] // TILE_BLOCKS) == lax.axis_index("blk")
    places[0] = jnp.where(hit, codes[...] % TILE_BLOCKS + 1, 0)
    before = (iota((PER_WORKER, PER_WORKER), 0) < iota((PER_WORKER, PER_WORKER), 1))
    places[1] = dot(one_hot(hit), one_hot(before)).astype(I32)
    rows = BLOCK * capacity
    row, lane = iota((rows, FULL), 0), iota((rows, FULL), 1)
    picks = []
    for step in range(owners):
        at = pl.ds(partner("blk", step, permuted), 1)
        same = places[1, at, :] == iota((rows, PER_WORKER), 0) % capacity
        place = jnp.sum(jnp.where(same, places[0, at, :], 0).astype(F32), axis=1, keepdims=True)
        target = (place.astype(I32) - 1) * BLOCK
        picks.append(one_hot(lane == target + row // capacity))
    pick = jnp.concatenate(picks, axis=0)
    fetch.wait()
    for u in range(0, BLOCK, 2):
        pair = [
            jnp.concatenate([tile[r, u + k] for r in range(TILE_ROWS)], axis=0) for k in range(2)
        ]
        moved = dot(pick, jnp.concatenate(pair, axis=1)).astype(BF16)
        for step, out in enumerate(views(outs, owners)):
            part = moved[step * rows : (step + 1) * rows]
            out[u] = part[:, :HALF]
            out[u + 1] = part[:, HALF:]


def outside_image(slots, owners, columns):
    column = lax.axis_index("col")
    row = iota((MIDDLE * PER_WORKER, HALF), 0)
    flags = jnp.zeros_like(row)
    for slot, (owner, place, rank) in enumerate(slots):
        block_row, block_col = place // TILE_COLS, place % TILE_COLS
        flag = (
            jnp.where((owner == 0) & (block_row == 0), 1, 0)
            + jnp.where((owner == owners - 1) & (block_row == TILE_ROWS - 1), 2, 0)
            + jnp.where((column == 0) & (block_col == 0), 4, 0)
            + jnp.where((column == columns - 1) & (block_col == TILE_COLS - 1), 8, 0)
        )
        flags = jnp.where(row % PER_WORKER == slot, flag, flags)
    across = row // PER_WORKER
    sides = (((flags & 4) != 0) & (across == 0)) | (((flags & 8) != 0) & (across == MIDDLE - 1))

    def here(m):
        if m == 0:
            return sides | ((flags & 1) != 0)
        if m == MIDDLE - 1:
            return sides | ((flags & 2) != 0)
        return sides

    return here


def pack_saved(owners, columns, capacity, wide, permuted, routing, saved, masked, *refs):
    outs, counts, table = refs[:-2], refs[-2], refs[-1]

    def clear(number, carry):
        table[number] = DEAD
        return carry

    lax.fori_loop(0, owners * capacity, clear, 0)
    slots = worker_codes(routing, counts, owners)
    rows = MIDDLE * PER_WORKER
    for slot, (owner, place, rank) in enumerate(slots):
        table[owner * capacity + rank] = slot
    outside = outside_image(slots, owners, columns)
    for m in range(MIDDLE):
        masked[m] = jnp.where(outside(m), 0.0, saved[m].astype(F32)).astype(BF16)
    size = wide * capacity
    row, lane = iota((size, FULL), 0), iota((size, FULL), 1)
    picks = []
    for step in range(owners):
        owner = partner("blk", step, permuted)
        target = jnp.full((size, FULL), DEAD, I32)
        for rank in range(capacity):
            target = jnp.where(row % capacity == rank, table[owner * capacity + rank], target)
        at = row // capacity
        picks.append(one_hot((lane == target + at * PER_WORKER) & (at < MIDDLE)))
    pick = jnp.concatenate(picks, axis=0)
    filler = jnp.zeros((FULL - rows, FULL), BF16)
    for m in range(0, MIDDLE, 2):
        pair = jnp.concatenate([masked[m], masked[m + 1]], axis=1)
        moved = dot(pick, jnp.concatenate([pair, filler], axis=0)).astype(BF16)
        for step, out in enumerate(views(outs, owners)):
            part = moved[step * size : (step + 1) * size]
            out[m] = part[:, :HALF]
            out[m + 1] = part[:, HALF:]


def ordered(own, other, axis):
    first = lax.axis_index("ch") == 0
    return jnp.concatenate(
        [jnp.where(first, own, other), jnp.where(first, other, own)], axis=axis
    )


def deal(value, kept, sent, grad, tap):
    low, high = value[: HALF // 2], value[HALF // 2 :]
    mine = lax.axis_index("col") == 0
    keep, send = jnp.where(mine, low, high), jnp.where(mine, high, low).astype(BF16)
    for k in range(4):
        step, rows = partner("blk", k, True), slice(k * ROWS, (k + 1) * ROWS)
        kept[step, grad, tap] = keep[rows]
        sent[step, grad, tap] = send[rows]


def emit(value, outs, grad, tap):
    if len(outs) == 2:
        deal(value, outs[0], outs[1], grad, tap)
    else:
        outs[0][grad, tap] = value


def spread(values, weight, total, places):
    height, extent = values.shape[:2]
    inputs = values[...].reshape(height * extent, FULL)
    width, step = weight.shape[1], places
    for dy in range(3):
        taps = jnp.concatenate([weight[3 * dy + dx] for dx in range(3)], axis=0)
        part = dot_nt(inputs, taps).reshape(height, extent, 3 * width)
        p, q, r = [part[:, :, dx * width : (dx + 1) * width] for dx in range(3)]
        sums = [
            p[:, :step],
            p[:, step : 2 * step] + q[:, :step],
            p[:, 2 * step :] + q[:, step : extent - step] + r[:, : extent - 2 * step],
            q[:, extent - step :] + r[:, extent - 2 * step : extent - step],
            r[:, extent - step :],
        ]
        at = 0
        for value in sums:
            size = value.shape[1]
            here = slice(at, at + size)
            if dy == 0:
                total[:height, here] = value
            else:
                total[dy : dy + height - 1, here] += value[:-1]
                total[dy + height - 1, here] = value[height - 1]
            at += size


def second_gradient(scale, owners, capacity, permuted, routing, *refs):
    parts = 1 if not permuted else owners
    own, other = views(refs[:parts], owners), views(refs[parts : 2 * parts], owners)
    masked, cot = refs[2 * parts : 2 * parts + 2]
    outs, counts = refs[2 * parts + 2 : -1], refs[-1]
    slots = worker_codes(routing, counts, owners)
    rows, inner = BLOCK * PER_WORKER, owners * BLOCK * capacity
    row, lane = iota((rows, inner), 0), iota((rows, inner), 1)
    target = jnp.full((rows, inner), DEAD, I32)
    for slot, (owner, place, rank) in enumerate(slots):
        step = partner("blk", owner, permuted)
        target = jnp.where(row % PER_WORKER == slot, step * (BLOCK * capacity) + rank, target)
    pick = one_hot(lane == target + (row // PER_WORKER) * capacity)
    for u in range(BLOCK):
        got = jnp.concatenate(
            [ordered(own[o][u], other[o][u], 1) for o in range(owners)], axis=0
        )
        cot[u] = dot(pick, got).astype(BF16)
    grads = cot[...].reshape(BLOCK * rows, FULL)
    turned = []
    for dx in range(3):
        window = masked[:, dx * PER_WORKER : (dx + BLOCK) * PER_WORKER].reshape(MIDDLE * rows, HALF)
        turned.append(jnp.maximum(window, jnp.zeros_like(window)).T)
    turned = jnp.concatenate(turned, axis=0)
    for dy in range(3):
        value = dot(turned[:, dy * rows : (dy + BLOCK) * rows], grads) * scale
        for dx in range(3):
            emit(value[dx * HALF : (dx + 1) * HALF], outs, 0, 3 * dy + dx)
    return slots


def first_gradient(
    scale, outside, cot, masked, saved_other, weight, weight_other, saved, *refs
):
    outs, (total, pre, full) = refs[:-3], refs[-3:]
    full[...] = ordered(weight[...], weight_other[...], 1)
    spread(cot, full, total, PER_WORKER)
    for m in range(MIDDLE):
        other = jnp.where(outside(m), 0.0, saved_other[m].astype(F32)).astype(BF16)
        live = ordered(masked[m], other, 1).astype(F32) > 0
        value = jnp.where(live, total[m], 0.0)
        pre[m] = value.astype(BF16).reshape(MIDDLE, PER_WORKER, FULL)
    size = MIDDLE * MIDDLE * PER_WORKER
    grads = pre[...].reshape(size, FULL)
    for dy in range(3):
        windows = [saved[dy : dy + MIDDLE, dx : dx + MIDDLE] for dx in range(3)]
        window = jnp.concatenate([w.reshape(size, HALF) for w in windows], axis=1)
        value = dot_tn(window, grads) * scale
        for dx in range(3):
            emit(value[dx * HALF : (dx + 1) * HALF], outs, 1, 3 * dy + dx)


def owner_spread(tile, tile_other, second, second_other, out, total, cot, full):
    row, lane = iota((FULL, FULL), 0), iota((FULL, FULL), 1)
    turn = one_hot(lane == (row % TILE_BLOCKS) * BLOCK + row // TILE_BLOCKS)
    for u in range(BLOCK):
        block = jnp.concatenate(
            [ordered(tile[r, u], tile_other[r, u], 1) for r in range(TILE_ROWS)], axis=0
        )
        cot[u] = dot(turn, block).astype(BF16)
    full[...] = ordered(second[...], second_other[...], 1)
    spread(cot, full, total, TILE_BLOCKS)
    out[...] = total[...].astype(BF16).reshape(out.shape)


def worker(scale, owners, columns, capacity, permuted, routing, *refs):
    parts = 1 if not permuted else owners
    inputs, refs = refs[: 2 * parts], refs[2 * parts :]
    (masked, saved_other, weight, weight_other, source), refs = refs[:5], refs[5:]
    if permuted:
        refs, sent = refs[:-1], refs[-1]
    outs, (counts, cot, total, pre, full, saved, arrived) = refs[:-7], refs[-7:]
    if permuted:
        kept, near, far = outs
        outs = (kept, sent)
    fetch = pltpu.make_async_copy(source, saved, arrived)
    fetch.start()
    slots = second_gradient(
        scale, owners, capacity, permuted, routing, *inputs, masked, cot, *outs, counts
    )
    fetch.wait()
    first_gradient(
        scale, outside_image(slots, owners, columns), cot, masked, saved_other, weight, weight_other,
        saved, *outs, total, pre, full,
    )
    if permuted:
        near[...] = sent[:2]
        far[...] = sent[2:]


def adjacent(step):
    me = lax.axis_index("blk")
    return (me ^ step) == me - 1, (me ^ step) == me + 1


def owner_canvas(owners, capacity, wide, permuted, routing, *refs):
    parts = 1 if not permuted else owners
    got, got_other = views(refs[:parts], owners), views(refs[parts : 2 * parts], owners)
    total, first, canvas = refs[2 * parts : 2 * parts + 3]
    rims, (table, pre, grown) = refs[2 * parts + 3 : -3], refs[-3:]
    owner_table(routing, table, owners, capacity)
    size, into = wide * capacity, MIDDLE * TILE_BLOCKS
    row, lane = iota((size, into), 0), iota((size, into), 1)
    picks = []
    for step in range(owners):
        worker = partner("blk", step, permuted)
        target = jnp.full((size, into), DEAD, I32)
        for rank in range(capacity):
            target = jnp.where(row % capacity == rank, table[worker * capacity + rank], target)
        at = row // capacity
        hits = (lane == target + at * TILE_BLOCKS) & (at < MIDDLE)
        picks.append(jnp.where(hits, 1.0, 0.0))
    pick = jnp.concatenate(picks, axis=0).T.astype(BF16)
    for m in range(MIDDLE):
        block = jnp.concatenate(
            [ordered(got[w][m], got_other[w][m], 1) for w in range(owners)], axis=0
        )
        value = jnp.where(dot(pick, block) > 0, total[m].reshape(into, FULL).astype(F32), 0.0)
        pre[m] = value.astype(BF16)
    spread(pre, first, grown, TILE_BLOCKS)
    height, depth = TILE_ROWS * WIDE, OUTER * TILE_BLOCKS
    row, lane = iota((height, depth), 0), iota((height, depth), 1)
    at_row, at_col = row // WIDE, row % WIDE
    n, place = lane // TILE_BLOCKS, lane % TILE_BLOCKS
    column = (place % TILE_COLS) * BLOCK + n - 2
    column = jnp.where(column < 0, column + 36, column)
    fold = one_hot((at_row == place // TILE_COLS) & (at_col == column))
    canvas[...] = jnp.zeros_like(canvas)
    for m in range(0, OUTER, 2):
        pair = jnp.concatenate(
            [grown[m + k].astype(BF16) for k in range(2)], axis=1
        )
        laid = dot(fold, pair).reshape(TILE_ROWS, WIDE, FULL)
        for r in range(TILE_ROWS):
            for k in range(2):
                canvas[r * BLOCK + m + k] += laid[r, :, k * HALF : (k + 1) * HALF]
    for k, rim in enumerate(rims):
        above, below = adjacent(2 * k + 1)
        top = jnp.concatenate([canvas[0], canvas[1]], axis=1)
        bottom = jnp.concatenate([canvas[HIGH - 2], canvas[HIGH - 1]], axis=1)
        here = jnp.where(below, bottom, jnp.where(above, top, 0.0))
        rim[...] = jnp.concatenate([here, jnp.zeros((RIM - WIDE, FULL), F32)], axis=0).astype(BF16)


def add_far(kept, got, *sends):
    for k, out in enumerate(sends):
        out[...] = (kept[2 + k] + got[k].astype(F32)).astype(BF16)


def add_near(kept, got, keep, send):
    keep[...] = kept[0] + got[0].astype(F32)
    send[...] = (kept[1] + got[1].astype(F32)).astype(BF16)


def add_workers(kept, got_2, got_3, got_1, rim_1, rim_3, out, out_1, out_3):
    value = kept[...]
    for part in (got_2, got_3, got_1):
        value = value + part[...].astype(F32)
    value = value.astype(BF16).reshape(PART, FULL)
    out[...] = value
    for message, rim in ((out_1, rim_1), (out_3, rim_3)):
        message[:PART] = value
        message[PART:] = rim[...]


def column_message(canvas, got_1, got_3, out, rim, strip):
    out[:PART] = got_3[:PART]
    for j in range(2):
        c = 32 + 2 * lax.axis_index("col") + j
        strip[...] = canvas[pl.ds(2 * WIDE + c, 64, stride=WIDE), :]
        for step, got in ((1, got_1), (3, got_3)):
            rim[...] = got[PART:].astype(F32)
            row = rim[pl.ds(c, 1), :]
            above, below = adjacent(step)
            top, bottom = jnp.where(above, row, 0.0), jnp.where(below, row, 0.0)
            strip[0:1] += top[:, :HALF]
            strip[1:2] += top[:, HALF:]
            strip[62:63] += bottom[:, :HALF]
            strip[63:64] += bottom[:, HALF:]
        out[PART:, j * HALF : (j + 1) * HALF] = strip[...].astype(BF16)


def gather_image(tile, canvas, got_1, got_3, total):
    rows = TILE_ROWS * BLOCK * 32
    total[...] = tile[...].reshape(rows, HALF).astype(F32) + canvas[
        2 : HIGH - 2, :32, :
    ].reshape(rows, HALF)
    for step, got in ((1, got_1), (3, got_3)):
        rim = got[PART : PART + 32].astype(F32)
        above, below = adjacent(step)
        top, bottom = jnp.where(above, rim, 0.0), jnp.where(below, rim, 0.0)
        total[0:32] += top[:, :HALF]
        total[32:64] += top[:, HALF:]
        total[rows - 64 : rows - 32] += bottom[:, :HALF]
        total[rows - 32 : rows] += bottom[:, HALF:]


def rows_at(number):
    column = lax.axis_index("col")
    place = (column if number < 4 else 1 - column) * 4 + partner("blk", number % 4, True)
    return pl.ds(pl.multiple_of(place * ROWS, ROWS), ROWS)


def lay(tile, canvas, *refs):
    parts, (image, slab), outs, total = refs[:-5], refs[-5:-3], refs[-3:-1], refs[-1]
    gather_image(tile, canvas, parts[1], parts[3], total)
    whole = total[...].reshape(image.shape)
    image[...] = whole.astype(BF16)
    slab[...] = jnp.where(lax.axis_index("col") == 0, whole[:, 16:], whole[:, :16])
    for number, part in zip((0, 1, 2, 3, 4, 5, 6), parts):
        value = part[:PART].astype(F32).reshape(2, 9, ROWS, FULL)
        for out, grad in zip(outs, (0, 1)):
            out[:, rows_at(number), :] = value[grad]


def finish(slab, last, old, old_0, old_1, image, out_0, out_1, total, side, laid, sems):
    copies = []
    laid[...] = last[:PART].astype(F32).reshape(2, 9, ROWS, FULL)
    for grad, dest in enumerate((out_0, out_1)):
        copies.append(
            pltpu.make_async_copy(laid.at[grad], dest.at[:, rows_at(7), :], sems.at[grad])
        )
        copies[-1].start()
    rows = TILE_ROWS * BLOCK * 16
    total[:rows] = slab[...].reshape(rows, HALF)
    strip = last[PART:].astype(F32)
    left = lax.axis_index("col") == 0
    at = jnp.where(left, 14, 0)
    for j in range(2):
        spot = (pl.ds(at + j, 64, stride=16), slice(None))
        total[spot] = total[spot] + strip[:, j * HALF : (j + 1) * HALF]
    side[...] = total[:rows].astype(BF16).reshape(side.shape)
    columns = pl.ds(pl.multiple_of(jnp.where(left, 16, 0), 16), 16)
    copies.append(pltpu.make_async_copy(side, image.at[:, columns, :], sems.at[2]))
    copies[-1].start()
    for copy in copies:
        copy.wait()


def swap(value, axis="ch"):
    return lax.ppermute(value, axis, [(0, 1), (1, 0)])


def flip(value, axis, step):
    size = lax.axis_size(axis)
    return lax.ppermute(value, axis, [(i, i ^ step) for i in range(size)])


def neighbours(axis):
    size = lax.axis_size(axis)
    up = [(i, (i + 1) % size) for i in range(size - 1)]
    return up, [(j, i) for i, j in up]


def shards(grad_out, saved_input, saved_pre, first_weight, second_weight, assignment):
    owners = lax.axis_size("blk")
    columns = lax.axis_size("col")
    capacity = max(2, TILE_BLOCKS // owners)
    wide = MIDDLE if (MIDDLE * capacity) % 16 == 0 else 16
    scale = 1.0 / math.sqrt(owners * columns * PER_WORKER * BLOCK * BLOCK)
    permuted = owners == 4 and columns == 2
    parts = owners if permuted else 1
    routing = assignment[0]
    shape = jax.ShapeDtypeStruct
    tables = [pltpu.SMEM((owners * capacity + 1,), I32)]
    counts = [pltpu.SMEM((owners,), I32)]

    def pieces(*dims):
        return [shape(dims, BF16)] * owners if permuted else [shape((owners,) + dims, BF16)]

    def exchange(values):
        if permuted:
            return list(values[:1]) + [flip(values[k], "blk", k) for k in (3, 2, 1)][::-1]
        return [lax.all_to_all(values[0], "blk", split_axis=0, concat_axis=0, tiled=True)]

    tie = lax.optimization_barrier
    tile = grad_out.reshape(TILE_ROWS, BLOCK, TILE_COLS * BLOCK, HALF)
    outgoing = call(
        functools.partial(pack_cotangents, owners, capacity, permuted),
        pieces(BLOCK, BLOCK * capacity, HALF),
        [HBM, HBM],
        [
            pltpu.VMEM((2,) + routing.shape, I32),
            pltpu.VMEM(tile.shape, BF16),
            pltpu.VMEM(routing.shape, I32),
            pltpu.SemaphoreType.DMA((2,)),
        ],
        (1, 1), "pack_cotangents",
    )(*[pltpu.with_memory_space_constraint(value, pltpu.HBM) for value in (routing, tile)])
    saved_slots = saved_pre[0, 0].transpose(1, 2, 0, 3)
    saved_slots = saved_slots.reshape(MIDDLE, MIDDLE * PER_WORKER, HALF)
    second_other, saved_other = swap(second_weight), swap(saved_slots)
    outgoing, saved_here = tie((outgoing, saved_slots))
    incoming = exchange(outgoing)

    second_other, saved_here = tie((second_other, saved_here))
    masked, *to_owners = call(
        functools.partial(pack_saved, owners, columns, capacity, wide, permuted),
        [shape((MIDDLE, MIDDLE * PER_WORKER, HALF), BF16)] + pieces(MIDDLE, wide * capacity, HALF),
        [SMEM, VMEM], counts + tables, (1, 1), "pack_saved",
    )(routing, saved_here)
    incoming_other = [swap(incoming[0])] if permuted else []
    incoming, to_owners, incoming_other = tie((incoming[::-1], to_owners[::-1], incoming_other))
    incoming, to_owners = incoming[::-1], to_owners[::-1]
    incoming_other += [swap(value) for value in incoming[len(incoming_other) :]]
    at_owner = exchange(to_owners)

    saved_tiles = saved_input[0, 0].transpose(1, 2, 0, 3)
    if permuted:
        part = (2, 9, ROWS, FULL)
        halved = [shape((4,) + part, F32)] + [shape((2,) + part, BF16)] * 2
    else:
        halved = [shape((2, 9, HALF, FULL), F32)]
    terms = call(
        functools.partial(worker, scale, owners, columns, capacity, permuted),
        halved,
        [SMEM] + [VMEM] * (2 * parts + 4) + [HBM],
        counts
        + [
            pltpu.VMEM((BLOCK, BLOCK * PER_WORKER, FULL), BF16),
            pltpu.VMEM((MIDDLE, MIDDLE * PER_WORKER, FULL), F32),
            pltpu.VMEM((MIDDLE, MIDDLE, PER_WORKER, FULL), BF16),
            pltpu.VMEM((9, FULL, FULL), BF16),
            pltpu.VMEM(saved_tiles.shape, BF16),
            pltpu.SemaphoreType.DMA,
        ]
        + ([pltpu.VMEM((4,) + part, BF16)] if permuted else []),
        (1, 1), "worker",
    )(
        routing, *incoming, *incoming_other, masked, saved_other, second_weight, second_other,
        pltpu.with_memory_space_constraint(saved_tiles, pltpu.HBM),
    )

    if permuted:
        kept, near, far = terms
        far, at_owner[2], at_owner[1] = tie((far, at_owner[2], at_owner[1]))
        far, tile_mine, tile_here = tie((far, tile, tile))
    else:
        terms, tile_mine, tile_here = tie((terms, tile, tile))
    total = call(
        owner_spread,
        shape((MIDDLE, MIDDLE, TILE_BLOCKS, FULL), BF16),
        [VMEM] * 4,
        [
            pltpu.VMEM((MIDDLE, MIDDLE * TILE_BLOCKS, FULL), F32),
            pltpu.VMEM((BLOCK, BLOCK * TILE_BLOCKS, FULL), BF16),
            pltpu.VMEM((9, FULL, FULL), BF16),
        ],
        (1, 1), "owner_spread",
    )(tile_here, swap(tile_mine), second_weight, second_other)

    def owner(at_owner):
        at_owner_other = [swap(value) for value in at_owner]
        return call(
            functools.partial(owner_canvas, owners, capacity, wide, permuted),
            [shape((HIGH, WIDE, HALF), F32)] + [shape((RIM, FULL), BF16)] * (2 if permuted else 0),
            [SMEM] + [VMEM] * (2 * len(at_owner) + 2),
            tables
            + [
                pltpu.VMEM((MIDDLE, MIDDLE * TILE_BLOCKS, FULL), BF16),
                pltpu.VMEM((OUTER, OUTER * TILE_BLOCKS, HALF), F32),
            ],
            (1, 1), "owner_canvas",
        )(routing, *at_owner, *at_owner_other, total, first_weight)

    if permuted:
        far_got, near_got = swap(far, "col"), swap(near, "col")
        total, far_got = tie((total, far_got))
        sends = call(add_far, [shape(part, BF16)] * 2, [VMEM] * 2, [], (1, 1), "add_far")(
            kept, far_got
        )
        sends, at_owner[3] = tie((sends[::-1], at_owner[3]))
        got = [flip(sends[1], "blk", 2), flip(sends[0], "blk", 3)]
        canvas, *rims = owner(at_owner)
        near_got, canvas = tie((near_got, canvas))
        keep, send = call(
            add_near, [shape(part, F32), shape(part, BF16)], [VMEM] * 2, [], (1, 1), "add_near",
        )(kept, near_got)
        got.append(flip(send, "blk", 1))
        message = shape((PART, FULL), BF16)
        wider = shape((PART + RIM, FULL), BF16)
        own, *wides = call(
            add_workers, [message, wider, wider], [VMEM] * 6, [], (1, 1), "add_workers",
        )(keep, *got, *rims)
        got_2, got_1 = flip(own, "blk", 2), flip(wides[0], "blk", 1)
        across, got_2, wide_3 = tie((swap(own, "col"), got_2, wides[1]))
        got_3 = flip(wide_3, "blk", 3)
        across = [across] + [swap(value, "col") for value in (got_1[:PART], got_2)]
        got_3, got_1, across = tie((got_3, got_1, across))
        got = [got_1, got_2, got_3]
        last = call(
            column_message, shape((PART + 64, FULL), BF16), [VMEM] * 3,
            [pltpu.VMEM((RIM, FULL), F32), pltpu.VMEM((64, HALF), F32)],
            (1, 1), "column_message",
        )(canvas.reshape(HIGH * WIDE, HALF), got[0], got[2])
        last = swap(last, "col")
        slab = (TILE_ROWS * BLOCK, 16, HALF)
        weights = [shape((9, HALF, FULL), F32)] * 2
        early, *outs = call(
            lay, [shape(grad_out.shape, BF16), shape(slab, F32)] + weights, [VMEM] * 9,
            [pltpu.VMEM((TILE_ROWS * BLOCK * 32, HALF), F32)], (1, 1), "lay",
        )(grad_out, canvas, own, *got, *across)
        grad_in, grad_second, grad_first = pl.pallas_call(
            finish,
            out_shape=[shape(grad_out.shape, BF16)] + weights,
            in_specs=[VMEM] * 2 + [HBM] * 3,
            out_specs=[HBM] * 3,
            scratch_shapes=[
                pltpu.VMEM((TILE_ROWS * BLOCK * 16 + 16, HALF), F32),
                pltpu.VMEM(slab, BF16),
                pltpu.VMEM((2, 9, ROWS, FULL), F32),
                pltpu.SemaphoreType.DMA((3,)),
            ],
            input_output_aliases={2: 0, 3: 1, 4: 2},
            compiler_params=pltpu.CompilerParams(vmem_limit_bytes=48 * 1024 * 1024),
            cost_estimate=pl.CostEstimate(flops=1, bytes_accessed=1, transcendentals=0),
            name="finish",
        )(outs[0], last, early, *outs[1:])
        return (grad_in, grad_first, grad_second)

    grad_first, grad_second = lax.psum((terms[0][1], terms[0][0]), ("blk", "col"))
    [canvas] = owner(at_owner)
    up, down = neighbours("blk")
    from_above = lax.ppermute(canvas[HIGH - 2 :].astype(BF16), "blk", up).astype(F32)
    from_below = lax.ppermute(canvas[:2].astype(BF16), "blk", down).astype(F32)
    inner = canvas[2 : HIGH - 2]
    inner = inner.at[:2].add(from_above).at[-2:].add(from_below)
    up, down = neighbours("col")
    from_left = lax.ppermute(inner[:, 32:34].astype(BF16), "col", up).astype(F32)
    from_right = lax.ppermute(inner[:, 34:36].astype(BF16), "col", down).astype(F32)
    inner = inner[:, :32].at[:, :2].add(from_left).at[:, -2:].add(from_right)
    grad_in = (grad_out.astype(F32) + inner).astype(BF16)
    return (grad_in, grad_first, grad_second)


def solution(mesh):
    return jax.shard_map(
        shards,
        mesh=mesh,
        in_specs=(
            P(("groups", "blk"), "col", "ch"),
            P(("groups", "col"), "blk", None, None, None, "ch"),
            P(("groups", "col"), "blk", None, None, None, "ch"),
            P(None, "ch", None),
            P(None, "ch", None),
            P(("groups", "col"), None, None),
        ),
        out_specs=(
            P(("groups", "blk"), "col", "ch"),
            P("groups", "ch", None),
            P("groups", "ch", None),
        ),
        check_vma=False,
    )
```
